32 devices in a mesh: rep: 4 (over y, x), fsdp: 8 (over z, core).
Axes of the slice: x: 2, y: 2, z: 4, core: 2. Of those that a mesh axis runs over, the one named last changes fastest.
Arguments:
- hidden_in: bfloat16 [16384, 1536], P(('rep', 'fsdp')), may hold values from -6 to 6
- lengths: int32 [32, 2], P(('rep', 'fsdp')), may hold values from 128 to 384, as said below
- norm_gain: bfloat16 [1536], P('fsdp'), may hold values from 0.5 to 1.5
- in_weight: bfloat16 [1536, 6448], P('fsdp'), may hold values from -0.15625 to 0.15625
- conv_weight: bfloat16 [4, 3328], P(None, 'fsdp'), may hold values from -3 to 3
- conv_bias: bfloat16 [3328], P('fsdp'), may hold values from -0.5 to 0.5
- dt_bias: bfloat16 [48], P('fsdp'), may hold values from -6 to -3
- a_log: bfloat16 [48], P('fsdp'), may hold values from 0 to 1.3984375
- skip_gain: bfloat16 [48], P('fsdp'), may hold values from 0.5 to 1.5
- gate_gain: bfloat16 [3072], P('fsdp'), may hold values from 0.5 to 1.5
- out_weight: bfloat16 [3072, 1536], P(None, 'fsdp'), may hold values from -0.109375 to 0.109375
- cotangent: bfloat16 [16384, 1536], P(('rep', 'fsdp')), may hold values from -12 to 12
Outputs:
- mixed: bfloat16 [16384, 1536], P(('rep', 'fsdp'))
- grad_hidden: float32 [16384, 1536], P(('rep', 'fsdp'))
- grad_norm_gain: float32 [1536], P('fsdp')
- grad_in_weight: float32 [1536, 6448], P('fsdp')
- grad_conv_weight: float32 [4, 3328], P(None, 'fsdp')
- grad_conv_bias: float32 [3328], P('fsdp')
- grad_dt_bias: float32 [48], P('fsdp')
- grad_a_log: float32 [48], P('fsdp')
- grad_skip_gain: float32 [48], P('fsdp')
- grad_gate_gain: float32 [3072], P('fsdp')
- grad_out_weight: float32 [3072, 1536], P(None, 'fsdp')
The draws below stay inside these ranges and needn't reach their ends.
Inputs may be any that keep to these rules, and one draw needn't show every extreme that they name: Each row gives the lengths of the two sequences of one device's block of 512 token slots, which fill its first rows in order; the remaining rows are padding. Every block fills at least half of its rows, and in some block a first sequence of 128 tokens and a second one fill all rows.
All inputs are finite; a program needn't handle non-finite values.
Results may differ from the reference program's by a relative error of at most 0.0068.
Values may be sent and summed in bfloat16 or wider, within the bound.
No kernel may reach another device: no remote copies, remote signals or barrier semaphores. Data moves between devices by JAX's collectives and lax.ppermute only.
A program may use at most 256 MiB of HBM per device.

```python
import jax
import jax.numpy as jnp
from jax import lax

D = 1536
HEADS = 48
CONV = 4
TOK_DEV = 512
MIN_LEN = 128
D_INNER = 3072
CHANNELS = 3328
PROJ = 6448
BLOCKS = 32
TOKENS = 16384


def draw_lengths(key, part):
    key = jax.random.fold_in(key, 11)
    first_key, second_key, third_key = jax.random.split(key, 3)
    padding = jax.random.randint(first_key, (BLOCKS,), 0, TOK_DEV // 2 + 1)
    filled = jax.random.randint(second_key, (), 0, BLOCKS)
    devices = jnp.arange(BLOCKS, dtype=jnp.int32)
    padding = jnp.where(devices == filled, 0, padding)
    used_rows = TOK_DEV - padding
    random_bits = jax.random.randint(third_key, (BLOCKS,), 0, 1 << 20)
    first_length = MIN_LEN + random_bits % (used_rows - 2 * MIN_LEN + 1)
    first_length = jnp.where(devices == filled, MIN_LEN, first_length)
    return jnp.stack([first_length, used_rows - first_length], axis=1).astype(jnp.int32)


def strengthened(drawn, own_key, source, target, blocks, factor):
    def block_of(axis_at):
        return (jnp.arange(drawn.shape[axis_at]) // (drawn.shape[axis_at] // blocks)).reshape((-1,) + (1,) * (drawn.ndim - 1 - axis_at))

    first = jax.random.permutation(own_key, blocks)[block_of(target)]
    second = (block_of(target) + blocks // 2) % blocks
    return jnp.where((block_of(source) == first) | (block_of(source) == second), factor * drawn, drawn)


def block_scale(rng, shape, cuts, low, high):
    def one(axis_at, parts):
        heights = jax.random.uniform(jax.random.fold_in(jax.random.fold_in(rng, 6), axis_at), (parts,), jnp.float32, low / len(cuts), high / len(cuts))
        return jnp.repeat(jnp.exp(heights), shape[axis_at] // parts).reshape((-1,) + (1,) * (len(shape) - axis_at - 1))

    level = one(*cuts[0])
    for cut in cuts[1:]:
        level = level * one(*cut)
    return level


def scatter_about(key, shape, scale, reach, pieces=(), kind=jnp.bfloat16):
    values = scale * jax.random.normal(key, shape, jnp.float32)
    if pieces:
        values = values * block_scale(key, shape, pieces, -0.22, 0.18)
    return jnp.clip(values, -reach, reach).astype(kind)


def heavy_noise(stream_key, dims, spread, reach, cuts, heavy, kind=jnp.bfloat16):
    values = spread * jax.random.normal(stream_key, dims, jnp.float32)
    if cuts:
        values = values * block_scale(stream_key, dims, cuts, -0.22, 0.18)
    return jnp.clip(strengthened(values, jax.random.fold_in(stream_key, 3), *heavy), -reach, reach).astype(kind)


def setup_inputs(seed: int = 0) -> dict:
    seeds = jax.random.split(jax.random.key(seed), 13)
    hidden_in = scatter_about(seeds[0], (TOKENS, D), 1.0, 6.0, ((0, 32),))
    lengths = draw_lengths(jax.random.fold_in(seeds[12], 71), 0)
    norm_gain = jnp.clip(1.0 + 0.1 * jax.random.normal(seeds[2], (D,), jnp.float32), 0.5, 1.5).astype(jnp.bfloat16)
    in_weight = scatter_about(seeds[3], (D, PROJ), D ** -0.5, 0.15625, ((0, 8),))
    conv_weight = scatter_about(seeds[4], (CONV, CHANNELS), CONV ** -0.5, 3.0, ((1, 8),))
    conv_bias = jnp.clip(jax.random.uniform(seeds[5], (CHANNELS,), jnp.float32, -0.5, 0.5) * block_scale(seeds[5], (CHANNELS,), ((0, 8),), -0.4, 0.0), -0.5, 0.5).astype(jnp.bfloat16)
    dt_bias = jnp.clip(-6.0 + 3.0 * jax.random.uniform(seeds[6], (HEADS,), jnp.float32) ** block_scale(seeds[6], (HEADS,), ((0, 8),), -0.2, 0.2), -6.0, -3.0).astype(jnp.bfloat16)
    a_log = jnp.clip(1.3984375 * jax.random.uniform(seeds[7], (HEADS,), jnp.float32) ** block_scale(seeds[7], (HEADS,), ((0, 8),), -0.2, 0.2), 0.0, 1.3984375).astype(jnp.bfloat16)
    skip_gain = jnp.clip(0.5 + 1.0 * jax.random.uniform(seeds[8], (HEADS,), jnp.float32) ** block_scale(seeds[8], (HEADS,), ((0, 8),), -0.2, 0.2), 0.5, 1.5).astype(jnp.bfloat16)
    gate_gain = jnp.clip(1.0 + 0.1 * jax.random.normal(seeds[9], (D_INNER,), jnp.float32), 0.5, 1.5).astype(jnp.bfloat16)
    out_weight = scatter_about(seeds[10], (D_INNER, D), D_INNER ** -0.5, 0.109375, ((1, 8),))
    cotangent = heavy_noise(seeds[11], (TOKENS, D), 1.0, 12.0, ((0, 32),), (0, 1, 32, 2.75))
    return {"hidden_in": hidden_in, "lengths": lengths, "norm_gain": norm_gain, "in_weight": in_weight, "conv_weight": conv_weight, "conv_bias": conv_bias, "dt_bias": dt_bias, "a_log": a_log, "skip_gain": skip_gain, "gate_gain": gate_gain, "out_weight": out_weight, "cotangent": cotangent}


highest = lax.Precision.HIGHEST
epsilon = 1e-05

@jax.custom_vjp
def low(v):
    return lax.optimization_barrier(v.astype(jnp.bfloat16)).astype(jnp.float32)

@jax.custom_vjp
def low_back(v):
    return v

def low_keep(v):
    return (low(v), None)

def low_pass(kept, grad):
    return (grad,)

def back_keep(v):
    return (v, None)

def back_low(kept, grad):
    return (low(grad),)
low.defvjp(low_keep, low_pass)
low_back.defvjp(back_keep, back_low)

def segments_of(lengths_row, token_count):
    seq_ends = jnp.cumsum(lengths_row).astype(jnp.int32)
    positions = jnp.arange(token_count, dtype=jnp.int32)
    return (positions[:, None] >= seq_ends[None, :]).sum(axis=1).astype(jnp.int32)

def normalize(inputs, scales):
    factor = lax.rsqrt(lax.optimization_barrier(jnp.mean(inputs * inputs, axis=-1, keepdims=True)) + epsilon)
    return inputs * factor * scales

def convolve(channels_in, segment, kernel, offsets):
    taps = kernel.shape[0]
    result = offsets + kernel[taps - 1] * channels_in
    for delay in range(1, taps):
        shifted = jnp.concatenate([jnp.zeros((delay, channels_in.shape[1]), channels_in.dtype), channels_in[:-delay]], 0)
        earlier = jnp.concatenate([jnp.full((delay,), -1, jnp.int32), segment[:-delay]])
        result = result + kernel[taps - 1 - delay] * jnp.where((earlier == segment)[:, None], shifted, 0.0)
    return jax.nn.silu(result)

def quadratic(values, keys, queries, rates, steps, segment, skip):
    token_count = values.shape[0]
    positions = jnp.arange(token_count, dtype=jnp.int32)
    allowed = (positions[:, None] >= positions[None, :]) & (segment[:, None] == segment[None, :])
    running = jnp.cumsum(rates, axis=0)
    scores = jnp.dot(queries, keys.T, precision=highest)
    decay = jnp.exp(jnp.where(allowed[:, :, None], running[:, None, :] - running[None, :, :], -jnp.inf))
    weights = scores[:, :, None] * decay * steps[None, :, :]
    return jnp.einsum('tsh,shp->thp', weights, values, precision=highest) + skip[None, :, None] * values

def mixer(projected, segment, kernel, offsets, step_bias, decay_log, skip, gate_scale):
    inner = gate_scale.shape[0]
    channels = offsets.shape[0]
    heads = step_bias.shape[0]
    state_size = (channels - inner) // 2
    gate = projected[:, :inner]
    conv_in = projected[:, inner:inner + channels]
    step_raw = projected[:, inner + channels:]
    conv_out = convolve(conv_in, segment, kernel, offsets)
    steps = jax.nn.softplus(step_raw + step_bias)
    rates = -jnp.exp(decay_log) * steps
    values = conv_out[:, :inner].reshape(-1, heads, inner // heads)
    keys = conv_out[:, inner:inner + state_size]
    queries = conv_out[:, inner + state_size:]
    ssd_out = quadratic(values, keys, queries, rates, steps, segment, skip).reshape(-1, inner)
    return normalize(ssd_out * jax.nn.silu(gate), gate_scale)

def reference(hidden_in, lengths, norm_gain, in_weight, conv_weight, conv_bias, dt_bias, a_log, skip_gain, gate_gain, out_weight, cotangent):
    segment = jax.vmap(lambda lengths_row: segments_of(lengths_row, TOK_DEV))(lengths)
    is_valid = segment < 2

    def forward(hidden, n_gain, w_in, kernel, offsets, step_bias, decay_log, skip, gate_scale, w_out):

        def one_block(triple):
            token_rows, block_segment, keep_rows = triple
            normed = low(normalize(token_rows, n_gain))
            projected = low_back(jnp.dot(normed, w_in, precision=highest))
            branch = low(mixer(projected, block_segment, kernel, offsets, step_bias, decay_log, skip, gate_scale))
            summed = token_rows + jnp.dot(branch, w_out, precision=highest)
            return jnp.where(keep_rows[:, None], summed, 0.0)
        outputs = lax.map(jax.checkpoint(one_block), (hidden.reshape(BLOCKS, TOK_DEV, D), segment, is_valid))
        return outputs.reshape(TOKENS, D)
    floats = tuple((a.astype(jnp.float32) for a in (hidden_in, norm_gain, in_weight, conv_weight, conv_bias, dt_bias, a_log, skip_gain, gate_gain, out_weight)))
    result, pull = jax.vjp(forward, *floats)
    grads = pull(cotangent.astype(jnp.float32))
    return (result.astype(jnp.bfloat16), grads[0], grads[1], grads[2], grads[3], grads[4], grads[5], grads[6], grads[7], grads[8], grads[9])
```

```python
import functools

import jax
import jax.numpy as jnp
from jax import lax
from jax.experimental import pallas as pl
from jax.experimental.pallas import tpu as pltpu
from jax.sharding import PartitionSpec as P

EPS = 1e-05
CHUNK = 128
LANES = 128
HIGHEST = lax.Precision.HIGHEST
F32 = jnp.float32
BF16 = jnp.bfloat16


def dot(left, right, precision=None):
    return lax.dot_general(
        left, right, (((1,), (0,)), ((), ())), precision=precision, preferred_element_type=F32
    )


def dot_nt(left, right):
    return lax.dot_general(left, right, (((1,), (1,)), ((), ())), preferred_element_type=F32)


def sigmoid(v):
    return 1.0 / (1.0 + jnp.exp(-v))


def softplus(v):
    return jnp.maximum(v, 0.0) + jnp.log1p(jnp.exp(-jnp.abs(v)))


def begin_of(position, first, both):
    return jnp.where(position >= both, both, jnp.where(position >= first, first, 0))


def iotas(rows, columns):
    return (
        lax.broadcasted_iota(jnp.int32, (rows, columns), 0),
        lax.broadcasted_iota(jnp.int32, (rows, columns), 1),
    )


def conv_tile(u_ref, cw_ref, start, columns, masks):
    inputs = [u_ref[start : start + CHUNK, columns]]
    for delay in range(1, 4):
        if start:
            shifted = u_ref[start - delay : start - delay + CHUNK, columns]
        else:
            shifted = pltpu.roll(inputs[0], delay, 0)
        inputs.append(jnp.where(masks[delay - 1], shifted, 0.0))
    pre = cw_ref[4:5, columns] + cw_ref[3:4, columns] * inputs[0]
    for delay in range(1, 4):
        pre = pre + cw_ref[3 - delay : 4 - delay, columns] * inputs[delay]
    return pre, inputs


def chunk_rates(dt_ref, hp_ref, start):
    raw = dt_ref[start : start + CHUNK, :] + hp_ref[0:1, :]
    step = softplus(raw)
    rate = -jnp.exp(hp_ref[1:2, :]) * step
    row, column = iotas(CHUNK, CHUNK)
    running = dot((row >= column).astype(F32), rate, HIGHEST)
    return raw, step, rate, running


def pair_of(low, matrix, head):
    return jnp.where(low, matrix[:, head : head + 1], matrix[:, head + 1 : head + 2])


def forward_kernel(heads, size, len_ref, u_ref, dt_ref, kq_ref, cw_ref, hp_ref, y_ref, st_ref, state):
    block = pl.program_id(0)
    first = len_ref[block, 0]
    both = first + len_ref[block, 1]
    tokens = u_ref.shape[0]
    chunks = tokens // CHUNK
    row, column = iotas(CHUNK, CHUNK)
    low = column < size
    low_row = low[0:1, :]
    for ci in range(chunks):
        start = ci * CHUNK
        position = row + start
        begin = begin_of(position, first, both)
        masks = [position - delay >= begin for delay in range(1, 4)]
        raw, step, rate, running = chunk_rates(dt_ref, hp_ref, start)
        running_t = running.T
        keys = kq_ref[start : start + CHUNK, :LANES]
        queries = kq_ref[start : start + CHUNK, LANES:]
        keys_t = keys.astype(F32).T.astype(BF16)
        allowed = (column <= row) & (column + start >= begin)
        scores = jnp.where(allowed, dot_nt(queries, keys), 0.0)
        last_begin = begin_of(start + CHUNK - 1, first, both)
        source = position >= last_begin
        reached = begin < start
        ending = running[CHUNK - 1 : CHUNK, :]
        kept = jnp.where(last_begin < start, jnp.exp(ending), 0.0)
        for pair in range(heads // 2):
            h = 2 * pair
            columns = slice(pair * LANES, (pair + 1) * LANES)
            pre, _ = conv_tile(u_ref, cw_ref, start, columns, masks)
            values = pre * sigmoid(pre)
            scaled = values * pair_of(low, step, h)
            weights = []
            for head in (h, h + 1):
                gap = running[:, head : head + 1] - running_t[head : head + 1, :]
                weights.append((scores * jnp.exp(jnp.minimum(gap, 0.0))).astype(BF16))
            stacked = jnp.concatenate(
                [jnp.where(low, scaled, 0.0), jnp.where(low, 0.0, scaled)], axis=0
            ).astype(BF16)
            out = dot(jnp.concatenate(weights, axis=1), stacked)
            out = out + cw_ref[5:6, columns] * values
            across = pair_of(low, running, h)
            if ci:
                carried = dot(queries, state[:, columns].astype(BF16))
                out = out + jnp.where(reached, carried * jnp.exp(across), 0.0)
            y_ref[start : start + CHUNK, columns] = out
            if ci < chunks - 1:
                left = pair_of(low_row, ending, h) - across
                source_in = jnp.where(source, scaled * jnp.exp(left), 0.0).astype(BF16)
                fresh = dot(keys_t, source_in)
                if ci:
                    fresh = fresh + state[:, columns] * pair_of(low_row, kept, h)
                state[:, columns] = fresh
                st_ref[0, ci, :, columns] = fresh.astype(BF16)


def backward_kernel(
    heads,
    size,
    first_head,
    len_ref,
    u_ref,
    dt_ref,
    kq_ref,
    dy_ref,
    st_ref,
    cw_ref,
    hp_ref,
    du_ref,
    ddt_ref,
    dkq_ref,
    cg_ref,
    hg_ref,
    d_state,
    d_pre,
    out_in,
    source_in,
):
    block = pl.program_id(0)
    first = len_ref[block, 0]
    both = first + len_ref[block, 1]
    tokens, width = u_ref.shape
    chunks = tokens // CHUNK
    row, column = iotas(CHUNK, CHUNK)
    low = column < size
    low_row = low[0:1, :]
    wide_row, wide_column = iotas(2 * CHUNK, LANES)
    pick_row, pick_column = iotas(16, 2 * CHUNK)

    @pl.when(block == 0)
    def _():
        cg_ref[...] = jnp.zeros_like(cg_ref)
        hg_ref[...] = jnp.zeros_like(hg_ref)

    d_pre[tokens : tokens + 8, :] = jnp.zeros((8, width), F32)
    for ci in reversed(range(chunks)):
        start = ci * CHUNK
        has_later = ci < chunks - 1
        position = row + start
        begin = begin_of(position, first, both)
        masks = [position - delay >= begin for delay in range(1, 4)]
        ahead = [begin_of(position + delay, first, both) <= position for delay in range(1, 4)]
        raw, step, rate, running = chunk_rates(dt_ref, hp_ref, start)
        running_t = running.T
        keys = kq_ref[start : start + CHUNK, :LANES]
        queries = kq_ref[start : start + CHUNK, LANES:]
        allowed = (row <= column) & (position >= begin_of(column + start, first, both))
        scores = jnp.where(allowed, dot_nt(keys, queries), 0.0)
        last_begin = begin_of(start + CHUNK - 1, first, both)
        source = position >= last_begin
        reached = begin < start
        ending = running[CHUNK - 1 : CHUNK, :]
        kept = jnp.where(last_begin < start, jnp.exp(ending), 0.0)
        d_scores = jnp.zeros((CHUNK, CHUNK), F32)
        later_sums = jnp.zeros((16, CHUNK), F32)
        early_sums = jnp.zeros((CHUNK, LANES), F32)
        out_sums = jnp.zeros((CHUNK, LANES), F32)
        source_sums = jnp.zeros((CHUNK, LANES), F32)
        direct_sums = jnp.zeros((CHUNK, LANES), F32)
        kept_sums = jnp.zeros((8, LANES), F32)
        for pair in range(heads // 2):
            h = first_head + 2 * pair
            columns = slice(pair * LANES, (pair + 1) * LANES)
            to_head = (column == h + (row >= size).astype(jnp.int32)).astype(BF16)
            pre, inputs = conv_tile(u_ref, cw_ref, start, columns, masks)
            gate = sigmoid(pre)
            values = pre * gate
            steps = pair_of(low, step, h)
            scaled = values * steps
            d_out = dy_ref[start : start + CHUNK, columns].astype(F32)
            d_low = d_out.astype(BF16)
            stacked = jnp.concatenate(
                [jnp.where(low, scaled, 0.0), jnp.where(low, 0.0, scaled)], axis=0
            ).astype(BF16)
            d_weights = dot_nt(stacked, d_low)
            weights, products = [], []
            for at, head in enumerate((h, h + 1)):
                gap = running_t[head : head + 1, :] - running[:, head : head + 1]
                decay = jnp.exp(jnp.minimum(gap, 0.0))
                d_decayed = decay * d_weights[at * CHUNK : (at + 1) * CHUNK]
                d_scores = d_scores + d_decayed
                products.append((scores * d_decayed).astype(BF16))
                weights.append((scores * decay).astype(BF16))
            early = wide_column == h + (wide_row >= CHUNK).astype(jnp.int32)
            early_sums = early_sums + dot(jnp.concatenate(products, axis=1), early.astype(BF16))
            later = pick_row == h + (pick_column >= CHUNK).astype(jnp.int32)
            later_sums = later_sums + dot(later.astype(BF16), jnp.concatenate(products, axis=0))
            d_stacked = jnp.concatenate(
                [jnp.where(low, d_out, 0.0), jnp.where(low, 0.0, d_out)], axis=0
            ).astype(BF16)
            d_scaled = dot(jnp.concatenate(weights, axis=1), d_stacked)
            across = pair_of(low, running, h)
            if has_later:
                left = jnp.exp(pair_of(low_row, ending, h) - across)
                left = jnp.where(source, left, 0.0)
                d_state_here = d_state[:, columns]
                d_source = dot(keys, d_state_here.astype(BF16)) * left
                d_scaled = d_scaled + d_source
                source_sums = source_sums + dot((scaled * d_source).astype(BF16), to_head)
                source_in[:, columns] = (scaled * left).astype(BF16)
            if ci:
                before = st_ref[0, ci - 1, :, columns]
                d_reach = jnp.where(reached, d_out * jnp.exp(across), 0.0)
                out_sums = out_sums + dot((d_reach * dot(queries, before)).astype(BF16), to_head)
                out_in[:, columns] = d_reach.astype(BF16)
                if has_later:
                    held = jnp.sum(d_state_here * before.astype(F32), axis=0, keepdims=True)
                    held = held * pair_of(low_row, kept, h)
                    kept_sums = kept_sums + dot(
                        jnp.broadcast_to(held, (8, LANES)), to_head.astype(F32), HIGHEST
                    )
            direct_sums = direct_sums + dot((d_scaled * values).astype(BF16), to_head)
            d_values = d_scaled * steps + cw_ref[5:6, columns] * d_out
            cg_ref[5:6, columns] += jnp.sum(d_out * values, axis=0, keepdims=True)
            d_here = d_values * (gate * (1.0 + pre * (1.0 - gate)))
            d_pre[start : start + CHUNK, columns] = d_here
            d_in = cw_ref[3:4, columns] * d_here
            for delay in range(1, 4):
                shifted = d_pre[start + delay : start + delay + CHUNK, columns]
                d_in = d_in + cw_ref[3 - delay : 4 - delay, columns] * jnp.where(
                    ahead[delay - 1], shifted, 0.0
                )
            du_ref[start : start + CHUNK, columns] = d_in.astype(BF16)
            for delay in range(4):
                cg_ref[3 - delay : 4 - delay, columns] += jnp.sum(
                    inputs[delay] * d_here, axis=0, keepdims=True
                )
            cg_ref[4:5, columns] += jnp.sum(d_here, axis=0, keepdims=True)
        d_scores = jnp.where(allowed, d_scores, 0.0)
        d_keys = dot(d_scores.astype(BF16), queries)
        d_queries = dot(d_scores.T.astype(BF16), keys)
        d_running = (
            jnp.concatenate([later_sums, jnp.zeros((CHUNK - 16, CHUNK), F32)], axis=0).T
            - early_sums
            + out_sums
            - source_sums
        )
        if has_later:
            d_keys = d_keys + dot_nt(source_in[...], d_state[...].astype(BF16))
            at_end = jnp.sum(source_sums, axis=0, keepdims=True) + kept_sums[0:1, :]
            d_running = d_running + jnp.where(row == CHUNK - 1, at_end, 0.0)
        if ci:
            d_queries = d_queries + dot_nt(out_in[...], st_ref[0, ci - 1])
            queries_t = queries.astype(F32).T.astype(BF16)
            for pair in range(heads // 2):
                columns = slice(pair * LANES, (pair + 1) * LANES)
                fresh = dot(queries_t, out_in[:, columns])
                if has_later:
                    fresh = fresh + d_state[:, columns] * pair_of(low_row, kept, first_head + 2 * pair)
                d_state[:, columns] = fresh
        dkq_ref[start : start + CHUNK, :LANES] = d_keys
        dkq_ref[start : start + CHUNK, LANES:] = d_queries
        d_rate = dot((row <= column).astype(F32), d_running, HIGHEST)
        d_step = direct_sums - jnp.exp(hp_ref[1:2, :]) * d_rate
        d_raw = d_step * sigmoid(raw)
        ddt_ref[start : start + CHUNK, :] = d_raw.astype(BF16)
        hg_ref[0:1, :] += jnp.sum(d_raw, axis=0, keepdims=True)
        hg_ref[1:2, :] += jnp.sum(d_rate * rate, axis=0, keepdims=True)


def prepare_kernel(heads, size, state, at_ref, in_ref, out_ref, mine_ref, other_ref):
    x, core = at_ref[0], at_ref[1]
    inner = out_ref.shape[0]
    width = heads * size
    steps_at = 2 * inner + 2 * state
    steps = in_ref[:, steps_at : steps_at + 4 * heads].astype(F32)
    rows = steps.shape[0]
    steps = jnp.concatenate([steps, jnp.zeros((rows, LANES - 4 * heads), F32)], axis=1)
    column = lax.broadcasted_iota(jnp.int32, (rows, LANES), 1)
    for ref, c in ((mine_ref, core), (other_ref, 1 - core)):
        p = 2 * x + c
        keys_at = pl.multiple_of(2 * inner + c * state, LANES)
        ref[:, :state] = in_ref[:, pl.ds(keys_at, state)]
        values_at = pl.multiple_of(inner + p * width, LANES)
        ref[:, state : state + width] = in_ref[:, pl.ds(values_at, width)]
        drawn = pltpu.roll(steps, lax.rem(LANES - heads * p, LANES), 1)
        drawn = jnp.where(column < heads, drawn, 0.0).astype(BF16)
        ref[:, state + width : state + width + LANES] = drawn
        at = state + width + LANES
        gate_at = pl.multiple_of(p * width, LANES)
        ref[:, at : at + width] = in_ref[:, pl.ds(gate_at, width)]
        ref[:, at + width : at + 2 * width] = out_ref[pl.ds(gate_at, width), :].T


def prepare_call(heads, size, state, place, in_weight, out_weight):
    rows = in_weight.shape[0]
    columns = state + LANES + 3 * heads * size
    return pl.pallas_call(
        functools.partial(prepare_kernel, heads, size, state),
        in_specs=[
            pl.BlockSpec(memory_space=pltpu.SMEM),
            pl.BlockSpec(memory_space=pltpu.VMEM),
            pl.BlockSpec(memory_space=pltpu.VMEM),
        ],
        out_specs=[pl.BlockSpec(memory_space=pltpu.VMEM)] * 2,
        out_shape=[jax.ShapeDtypeStruct((rows, columns), BF16)] * 2,
        compiler_params=pltpu.CompilerParams(vmem_limit_bytes=24 * 1024 * 1024),
        name="prepare_weights",
    )(place, in_weight, out_weight)


def assemble_rows(links_shape, at_ref, own_ref, core_ref, pieces, whole_ref):
    sides, groups = links_shape
    a, g, c = at_ref[0], at_ref[1], at_ref[2]
    rows = own_ref.shape[0]
    part = 2 * rows // sides
    base = g * (2 * rows)
    whole_ref[pl.ds(pl.multiple_of(base + c * rows, 16), rows), :] = own_ref[...]
    whole_ref[pl.ds(pl.multiple_of(base + (1 - c) * rows, 16), rows), :] = core_ref[...]
    for k in range(1, groups):
        base = lax.rem(g + groups - k, groups) * (2 * rows)
        for j, ref in enumerate(pieces):
            at = base + lax.rem(a + sides - j, sides) * part
            whole_ref[pl.ds(pl.multiple_of(at, 16), part), :] = ref[(k - 1) * part : k * part, :]


def project_kernel(links_shape, at_ref, own_ref, core_ref, *refs):
    sides = links_shape[0]
    pieces, (rows_ref, whole_ref, out_ref) = refs[:sides], refs[sides:]

    @pl.when(pl.program_id(0) == 0)
    def _():
        assemble_rows(links_shape, at_ref, own_ref, core_ref, pieces, whole_ref)

    out_ref[...] = dot(rows_ref[...], whole_ref[...])


def whole_spec(array):
    return pl.BlockSpec(array.shape, lambda b: (0,) * array.ndim)


def project_call(links_shape, place, own, core, pieces, rows, tokens):
    columns, depth = own.shape[1], rows.shape[1]
    operands = [own, core, *pieces]
    return pl.pallas_call(
        functools.partial(project_kernel, links_shape),
        grid=(rows.shape[0] // tokens,),
        in_specs=[pl.BlockSpec(memory_space=pltpu.SMEM)]
        + [whole_spec(array) for array in operands]
        + [pl.BlockSpec((tokens, depth), lambda b: (b, 0))],
        out_specs=[
            pl.BlockSpec((depth, columns), lambda b: (0, 0)),
            pl.BlockSpec((tokens, columns), lambda b: (b, 0)),
        ],
        out_shape=[
            jax.ShapeDtypeStruct((depth, columns), BF16),
            jax.ShapeDtypeStruct((rows.shape[0], columns), F32),
        ],
        compiler_params=pltpu.CompilerParams(vmem_limit_bytes=40 * 1024 * 1024),
        cost_estimate=pl.CostEstimate(
            flops=2 * rows.size * columns, bytes_accessed=2 * rows.size, transcendentals=0
        ),
        name="project",
    )(place, *operands, rows)


def branch_back_kernel(links_shape, at_ref, own_ref, core_ref, *refs):
    sides = links_shape[0]
    pieces = refs[:sides]
    rows_refs = refs[sides : sides + 4]
    gate_ref, ssd_ref, cw_ref, whole_ref, out_ref, sums_ref = refs[sides + 4 :]
    block = pl.program_id(0)

    @pl.when(block == 0)
    def _():
        assemble_rows(links_shape, at_ref, own_ref, core_ref, pieces, whole_ref)

    for at, rows_ref in enumerate(rows_refs):

        @pl.when(block == at)
        def _():
            out_ref[...] = dot(rows_ref[...], whole_ref[...])

    tokens, width = out_ref.shape
    sums_ref[...] = jnp.zeros_like(sums_ref)
    for start in range(0, tokens, CHUNK):
        squares = jnp.zeros((CHUNK, LANES), F32)
        products = jnp.zeros((CHUNK, LANES), F32)
        for left in range(0, width, LANES):
            tile = (slice(start, start + CHUNK), slice(left, left + LANES))
            gate = gate_ref[tile]
            gated = ssd_ref[tile] * (gate * sigmoid(gate))
            squares = squares + gated * gated
            products = products + gated * (cw_ref[6:7, left : left + LANES] * out_ref[tile])
        sums_ref[0:1, start : start + CHUNK] = jnp.sum(squares.T, axis=0, keepdims=True)
        sums_ref[1:2, start : start + CHUNK] = jnp.sum(products.T, axis=0, keepdims=True)


def branch_back_call(links_shape, place, own, core, pieces, rows, gate, ssd_out, conv_rows):
    columns = own.shape[1]
    tokens, depth = rows[0].shape
    operands = [own, core, *pieces, *rows]
    return pl.pallas_call(
        functools.partial(branch_back_kernel, links_shape),
        grid=(4,),
        in_specs=[pl.BlockSpec(memory_space=pltpu.SMEM)]
        + [whole_spec(array) for array in operands]
        + [
            pl.BlockSpec((tokens, columns), lambda b: (b, 0)),
            pl.BlockSpec((tokens, columns), lambda b: (b, 0)),
            pl.BlockSpec((8, columns), lambda b: (0, 0)),
        ],
        out_specs=[
            pl.BlockSpec((depth, columns), lambda b: (0, 0)),
            pl.BlockSpec((tokens, columns), lambda b: (b, 0)),
            pl.BlockSpec((8, tokens), lambda b: (0, b)),
        ],
        out_shape=[
            jax.ShapeDtypeStruct((depth, columns), BF16),
            jax.ShapeDtypeStruct((4 * tokens, columns), F32),
            jax.ShapeDtypeStruct((8, 4 * tokens), F32),
        ],
        compiler_params=pltpu.CompilerParams(vmem_limit_bytes=56 * 1024 * 1024),
        cost_estimate=pl.CostEstimate(
            flops=8 * tokens * depth * columns, bytes_accessed=8 * tokens * depth, transcendentals=0
        ),
        name="branch_back",
    )(place, *operands, gate, ssd_out, conv_rows)


def gating_back_kernel(
    inner, sums_ref, core_ref, side_ref, both_ref, gate_ref, ssd_ref, db_ref, cw_ref,
    branch_ref, dgate_ref, dssd_ref, gain_ref
):
    @pl.when(pl.program_id(0) == 0)
    def _():
        gain_ref[...] = jnp.zeros_like(gain_ref)

    sums = sums_ref[...] + core_ref[...] + side_ref[...] + both_ref[...]
    scale_row = lax.rsqrt(sums[0:1, :] * (1.0 / inner) + EPS)
    cross_row = scale_row * scale_row * scale_row * (sums[1:2, :] * (1.0 / inner))
    tokens, width = gate_ref.shape
    for start in range(0, tokens, CHUNK):
        stacked = jnp.concatenate(
            [scale_row[:, start : start + CHUNK], cross_row[:, start : start + CHUNK],
             jnp.zeros((CHUNK - 2, CHUNK), F32)], axis=0
        ).T
        scale, cross = stacked[:, 0:1], stacked[:, 1:2]
        for left in range(0, width, LANES):
            columns = slice(left, left + LANES)
            tile = (slice(start, start + CHUNK), columns)
            gate, ssd, d_branch = gate_ref[tile], ssd_ref[tile], db_ref[tile]
            gain = cw_ref[6:7, columns]
            sig = sigmoid(gate)
            act = gate * sig
            gated = ssd * act
            scaled = gated * scale
            branch_ref[tile] = (scaled * gain).astype(BF16)
            gain_ref[0:1, columns] += jnp.sum(d_branch * scaled, axis=0, keepdims=True)
            d_gated = scale * (gain * d_branch) - gated * cross
            dssd_ref[tile] = d_gated * act
            dgate_ref[tile] = (d_gated * ssd * (sig * (1.0 + gate * (1.0 - sig)))).astype(BF16)


def gating_back_call(inner, sums, gate, ssd_out, d_branch, conv_rows):
    rows, columns = gate.shape
    tokens = rows // 4
    block = pl.BlockSpec((tokens, columns), lambda b: (b, 0))
    order = [lambda b: (0, b)]
    order.append(lambda b: (0, b + 1 - 2 * lax.rem(b, 2)))
    order.append(lambda b: (0, lax.rem(b + 2, 4)))
    order.append(lambda b: (0, 3 - b))
    return pl.pallas_call(
        functools.partial(gating_back_kernel, inner),
        grid=(4,),
        in_specs=[pl.BlockSpec((8, tokens), index) for index in order]
        + [block, block, block, pl.BlockSpec((8, columns), lambda b: (0, 0))],
        out_specs=[block, block, block, pl.BlockSpec((8, columns), lambda b: (0, 0))],
        out_shape=[
            jax.ShapeDtypeStruct((rows, columns), BF16),
            jax.ShapeDtypeStruct((rows, columns), BF16),
            jax.ShapeDtypeStruct((rows, columns), F32),
            jax.ShapeDtypeStruct((8, columns), F32),
        ],
        compiler_params=pltpu.CompilerParams(vmem_limit_bytes=40 * 1024 * 1024),
        cost_estimate=pl.CostEstimate(
            flops=20 * rows * columns, bytes_accessed=20 * rows * columns, transcendentals=0
        ),
        name="gating_back",
    )(*sums, gate, ssd_out, d_branch, conv_rows)


def normalize_kernel(*refs):
    rows_refs, (gain_ref, normed_ref, scale_ref) = refs[:4], refs[4:]
    for at, rows_ref in enumerate(rows_refs):

        @pl.when(pl.program_id(0) == at)
        def _():
            depth = rows_ref.shape[1]
            for start in range(0, rows_ref.shape[0], 64):
                rows = rows_ref[start : start + 64, :].astype(F32)
                mean = jnp.sum(rows * rows, axis=1, keepdims=True) * (1.0 / depth)
                scale = lax.rsqrt(mean + EPS)
                normed = rows * scale * gain_ref[0:1, :]
                normed_ref[start : start + 64, :] = normed.astype(BF16)
                scale_ref[start : start + 64, :] = jnp.broadcast_to(scale, (64, LANES))


def normalize_call(blocks, gain):
    tokens, depth = blocks[0].shape
    return pl.pallas_call(
        normalize_kernel,
        grid=(4,),
        in_specs=[whole_spec(block) for block in blocks] + [whole_spec(gain)],
        out_specs=[
            pl.BlockSpec((tokens, depth), lambda b: (b, 0)),
            pl.BlockSpec((tokens, LANES), lambda b: (b, 0)),
        ],
        out_shape=[
            jax.ShapeDtypeStruct((4 * tokens, depth), BF16),
            jax.ShapeDtypeStruct((4 * tokens, LANES), F32),
        ],
        compiler_params=pltpu.CompilerParams(vmem_limit_bytes=40 * 1024 * 1024),
        name="normalize",
    )(*blocks, gain)


def weight_grad_kernel(links_shape, at_ref, left_ref, right_ref, *refs):
    sides = links_shape[0]
    outs, scratch = refs[:sides], refs[sides]
    scratch[...] = lax.dot_general(
        left_ref[...], right_ref[...], (((0,), (0,)), ((), ())), preferred_element_type=F32
    ).astype(BF16)
    chips, part = outs[0].shape[0], outs[0].shape[1]
    for chip in range(chips):
        for j, out in enumerate(outs):
            at = (chip * sides + lax.rem(at_ref[0] + j, sides)) * part
            out[chip] = scratch[pl.ds(pl.multiple_of(at, 16), part), :]


def weight_grad_call(links_shape, place, left, right):
    sides, groups = links_shape
    tokens, depth = left.shape
    columns = right.shape[1]
    rows = depth // groups
    part = rows // sides
    chips = 1
    while chips * rows % LANES:
        chips += 1
    return pl.pallas_call(
        functools.partial(weight_grad_kernel, links_shape),
        grid=(groups // chips,),
        in_specs=[
            pl.BlockSpec(memory_space=pltpu.SMEM),
            pl.BlockSpec((tokens, chips * rows), lambda b: (0, b)),
            pl.BlockSpec((tokens, columns), lambda b: (0, 0)),
        ],
        out_specs=[pl.BlockSpec((chips, part, columns), lambda b: (b, 0, 0))] * sides,
        out_shape=[jax.ShapeDtypeStruct((groups, part, columns), BF16)] * sides,
        scratch_shapes=[pltpu.VMEM((chips * rows, columns), BF16)],
        compiler_params=pltpu.CompilerParams(vmem_limit_bytes=40 * 1024 * 1024),
        cost_estimate=pl.CostEstimate(
            flops=2 * left.size * columns, bytes_accessed=2 * left.size, transcendentals=0
        ),
        name="weight_grad",
    )(place, left, right)


def forward_call(heads, size, lengths, conv_in, keys_queries, conv_rows, head_rows):
    blocks = lengths.shape[0]
    total = conv_in.shape[0]
    tokens = total // blocks
    width = heads * size
    state = keys_queries.shape[1] // 2
    boundaries = tokens // CHUNK - 1
    return pl.pallas_call(
        functools.partial(forward_kernel, heads, size),
        grid=(blocks,),
        in_specs=[
            pl.BlockSpec(memory_space=pltpu.SMEM),
            pl.BlockSpec((tokens, width), lambda b: (b, 0)),
            pl.BlockSpec((tokens, LANES), lambda b: (b, width // LANES)),
            pl.BlockSpec((tokens, 2 * state), lambda b: (b, 0)),
            pl.BlockSpec((8, width), lambda b: (0, 0)),
            pl.BlockSpec((8, LANES), lambda b: (0, 0)),
        ],
        out_specs=[
            pl.BlockSpec((tokens, width), lambda b: (b, 0)),
            pl.BlockSpec((1, boundaries, state, width), lambda b: (b, 0, 0, 0)),
        ],
        out_shape=[
            jax.ShapeDtypeStruct((total, width), F32),
            jax.ShapeDtypeStruct((blocks, boundaries, state, width), BF16),
        ],
        scratch_shapes=[pltpu.VMEM((state, width), F32)],
        compiler_params=pltpu.CompilerParams(vmem_limit_bytes=40 * 1024 * 1024),
        cost_estimate=pl.CostEstimate(
            flops=blocks * 3_000_000_000, bytes_accessed=blocks * 8_000_000, transcendentals=0
        ),
        name="ssd_forward",
    )(lengths, conv_in, conv_in, keys_queries, conv_rows, head_rows)


def backward_call(
    heads, size, part, lengths, conv_in, keys_queries, d_out, states, conv_rows, head_rows
):
    blocks = lengths.shape[0]
    total = conv_in.shape[0]
    tokens = total // blocks
    width = heads * size
    steps_at = d_out.shape[1] // LANES
    state = keys_queries.shape[1] // 2
    boundaries = tokens // CHUNK - 1
    return pl.pallas_call(
        functools.partial(backward_kernel, heads, size, part * heads),
        grid=(blocks,),
        in_specs=[
            pl.BlockSpec(memory_space=pltpu.SMEM),
            pl.BlockSpec((tokens, width), lambda b: (b, part)),
            pl.BlockSpec((tokens, LANES), lambda b: (b, steps_at)),
            pl.BlockSpec((tokens, 2 * state), lambda b: (b, 0)),
            pl.BlockSpec((tokens, width), lambda b: (b, part)),
            pl.BlockSpec((1, boundaries, state, width), lambda b: (b, 0, 0, part)),
            pl.BlockSpec((8, width), lambda b: (0, part)),
            pl.BlockSpec((8, LANES), lambda b: (0, 0)),
        ],
        out_specs=[
            pl.BlockSpec((tokens, width), lambda b: (b, 0)),
            pl.BlockSpec((tokens, LANES), lambda b: (b, 0)),
            pl.BlockSpec((tokens, 2 * state), lambda b: (b, 0)),
            pl.BlockSpec((8, width), lambda b: (0, 0)),
            pl.BlockSpec((8, LANES), lambda b: (0, 0)),
        ],
        out_shape=[
            jax.ShapeDtypeStruct((total, width), BF16),
            jax.ShapeDtypeStruct((total, LANES), BF16),
            jax.ShapeDtypeStruct((total, 2 * state), F32),
            jax.ShapeDtypeStruct((8, width), F32),
            jax.ShapeDtypeStruct((8, LANES), F32),
        ],
        scratch_shapes=[
            pltpu.VMEM((state, width), F32),
            pltpu.VMEM((tokens + 8, width), F32),
            pltpu.VMEM((CHUNK, width), BF16),
            pltpu.VMEM((CHUNK, width), BF16),
        ],
        compiler_params=pltpu.CompilerParams(vmem_limit_bytes=48 * 1024 * 1024),
        cost_estimate=pl.CostEstimate(
            flops=blocks * 6_000_000_000, bytes_accessed=blocks * 8_000_000, transcendentals=0
        ),
        name="ssd_backward",
    )(lengths, conv_in, conv_in, keys_queries, d_out, states, conv_rows, head_rows)


def after(values):
    return lax.optimization_barrier(values)


def phase(sends, work=None, arguments=()):
    values, arguments = after(([value for _, value in sends], arguments))
    moved = [send(value) for (send, _), value in zip(sends, values)]
    done = work(*arguments) if work else ()
    return after((moved, done))


def total(first, others):
    result = first.astype(F32)
    for other in others:
        result = result + other.astype(F32)
    return result


class Links:
    def __init__(self, reps, shards):
        self.reps, self.shards = reps, shards
        self.sides, self.groups = reps // 2, shards // 2
        rep, shard = lax.axis_index("rep"), lax.axis_index("fsdp")
        self.rep, self.shard = rep, shard
        self.a, self.x = rep // 2, rep % 2
        self.g, self.c = shard // 2, shard % 2

    def send(self, value, target):
        pairs = []
        for r in range(self.reps):
            for f in range(self.shards):
                to_r, to_f = target(r, f)
                pairs.append((r * self.shards + f, to_r * self.shards + to_f))
        return lax.ppermute(value, ("rep", "fsdp"), pairs)

    def core(self, value):
        return self.send(value, lambda r, f: (r, f ^ 1))

    def side(self, value):
        return self.send(value, lambda r, f: (r ^ 1, f))

    def corner(self, value):
        return self.send(value, lambda r, f: (r ^ 1, f ^ 1))

    def along_a(self, value, by):
        return self.send(value, lambda r, f: (((r // 2 + by) % self.sides) * 2 + r % 2, f))

    def along_g(self, value, by):
        return self.send(value, lambda r, f: (r, ((f // 2 + by) % self.groups) * 2 + f % 2))

    def flip(self, value, bit_of_rep, bit_of_shard):
        return self.send(value, lambda r, f: (r ^ bit_of_rep, f ^ bit_of_shard))

    def round_g(self, piece):
        return [self.along_g(piece, k) for k in range(1, self.groups)]

    def piece_of(self, mine, from_core):
        if self.sides == 2:
            return jnp.where(self.a == self.c, mine, from_core)
        is_high = self.c == 1
        chip = jnp.concatenate(
            [jnp.where(is_high, from_core, mine), jnp.where(is_high, mine, from_core)], axis=0
        )
        part = chip.shape[0] // self.sides
        return lax.dynamic_slice_in_dim(chip, self.a * part, part, 0)

    def round_a(self, joined):
        return [self.along_a(joined, j) for j in range(1, self.sides)]

    def assemble(self, mine, from_core, joined, rounds):
        rows, columns = mine.shape
        part = 2 * rows // self.sides
        whole = jnp.zeros((rows * self.shards, columns), mine.dtype)
        base = self.g * 2 * rows
        whole = lax.dynamic_update_slice_in_dim(whole, mine, base + self.c * rows, 0)
        whole = lax.dynamic_update_slice_in_dim(whole, from_core, base + (1 - self.c) * rows, 0)
        for k in range(1, self.groups):
            base = ((self.g - k) % self.groups) * 2 * rows
            for j, pieces in enumerate([joined] + rounds):
                piece = pieces[(k - 1) * part : k * part]
                at = base + ((self.a - j) % self.sides) * part
                whole = lax.dynamic_update_slice_in_dim(whole, piece, at, 0)
        return whole

    def parts_for_a(self, view):
        axis = view.ndim - 3
        mine = lax.dynamic_index_in_dim(view, self.a, axis, keepdims=False)
        others = [
            lax.dynamic_index_in_dim(view, (self.a + j) % self.sides, axis, keepdims=False)
            for j in range(1, self.sides)
        ]
        return mine, others

    def parts_for_g(self, view):
        mine = lax.dynamic_index_in_dim(view, self.g, 0, keepdims=False)
        others = [
            lax.dynamic_index_in_dim(view, (self.g + k) % self.groups, 0, keepdims=False)
            for k in range(1, self.groups)
        ]
        return mine, others

    def send_a(self, others):
        return [self.along_a(part, j + 1) for j, part in enumerate(others)]

    def send_g(self, others):
        return [self.along_g(part, k + 1) for k, part in enumerate(others)]

    def chips_of(self, partial):
        rows = partial.shape[0] // (self.groups * self.sides)
        return partial.reshape(self.groups, self.sides, rows, partial.shape[1])

    def spread_a(self, piece):
        return [self.along_a(piece, j) for j in range(1, self.sides)]

    def join_a(self, piece, others):
        if self.sides == 2:
            is_high = self.a == 1
            return jnp.concatenate(
                [jnp.where(is_high, others[0], piece), jnp.where(is_high, piece, others[0])],
                axis=0,
            )
        part = piece.shape[0]
        chip = jnp.zeros((part * self.sides, piece.shape[1]), piece.dtype)
        for j, value in enumerate([piece] + others):
            at = ((self.a - j) % self.sides) * part
            chip = lax.dynamic_update_slice_in_dim(chip, value, at, 0)
        return chip

    def join_x(self, piece, other):
        is_far = self.x == 1
        return jnp.concatenate(
            [jnp.where(is_far, other, piece), jnp.where(is_far, piece, other)], axis=1
        )

    def rows_of_core(self, chip):
        rows = chip.shape[0] // 2
        is_high = self.c == 1
        mine = jnp.where(is_high, chip[rows:], chip[:rows])
        return mine, jnp.where(is_high, chip[:rows], chip[rows:])

    def shares(self, mine, from_core):
        columns = mine.shape[1] // 2
        is_high = self.c == 1
        low = jnp.where(is_high, from_core, mine)
        high = jnp.where(is_high, mine, from_core)
        return [low[:, :columns], high[:, :columns], low[:, columns:], high[:, columns:]]

    def sum_all(self, value):
        bit = 1
        while bit < self.shards:
            value = value + self.flip(value, 0, bit)
            bit *= 2
        bit = 1
        while bit < self.reps:
            value = value + self.flip(value, bit, 0)
            bit *= 2
        return value

    def group_blocks(self, value):
        far = self.side(value)
        return [value, self.core(value), far, self.core(far)]

    def core_sum(self, partials, link_type):
        tokens = partials.shape[0] // 2
        return partials[:tokens].astype(F32) + self.core(
            partials[tokens:].astype(link_type)
        ).astype(F32)


def shift_rows(values, by):
    zeros = jnp.zeros((values.shape[0], abs(by), values.shape[2]), values.dtype)
    if by > 0:
        return jnp.concatenate([zeros, values[:, :-by]], axis=1)
    return jnp.concatenate([values[:, -by:], zeros], axis=1)


def causal_conv(inputs, begin, taps, bias):
    position = jnp.arange(inputs.shape[1], dtype=jnp.int32)[None, :]
    result = bias + taps[3] * inputs
    shifted = [inputs]
    for delay in range(1, 4):
        inside = (position - delay >= begin)[..., None]
        shifted.append(jnp.where(inside, shift_rows(inputs, delay), 0.0))
        result = result + taps[3 - delay] * shifted[delay]
    return result, shifted


def causal_conv_back(d_result, begin, taps):
    position = jnp.arange(d_result.shape[1], dtype=jnp.int32)[None, :]
    d_inputs = taps[3] * d_result
    for delay in range(1, 4):
        inside = (position - delay >= begin)[..., None]
        moved = shift_rows(jnp.where(inside, d_result, 0.0), -delay)
        d_inputs = d_inputs + taps[3 - delay] * moved
    return d_inputs


def per_device(
    reps,
    shards,
    hidden_in,
    lengths,
    norm_gain,
    in_weight,
    conv_weight,
    conv_bias,
    dt_bias,
    a_log,
    skip_gain,
    gate_gain,
    out_weight,
    cotangent,
):
    links = Links(reps, shards)
    tokens, depth = hidden_in.shape
    inner = gate_gain.shape[0] * shards
    channels = conv_bias.shape[0] * shards
    all_heads = dt_bias.shape[0] * shards
    state = (channels - inner) // 2
    size = inner // all_heads
    heads, width = all_heads // 4, inner // 4
    x, c = links.x, links.c
    p = 2 * x + c

    is_high = c == 1
    far_hidden = links.side(hidden_in)
    mine, for_core = prepare_call(
        heads, size, state, jnp.stack([x, c]).astype(jnp.int32), in_weight, out_weight
    )
    ends = jnp.cumsum(lengths[0])
    positions = jnp.arange(tokens, dtype=jnp.int32)
    is_valid = (positions < ends[1])[:, None]
    back_own = jnp.where(is_valid, cotangent, jnp.zeros_like(cotangent))

    small_in = [conv_weight, conv_bias, norm_gain, gate_gain, dt_bias, a_log, skip_gain]
    sizes = [piece.size for piece in small_in]
    length = sum(sizes)
    padded = -(-length // LANES) * LANES
    packed = jnp.concatenate([piece.reshape(-1) for piece in small_in])
    packed = jnp.pad(packed, (0, padded - length)).reshape(1, padded)
    def parameters(far_pairs):
        gathered = jnp.zeros((shards, padded), BF16)
        gathered = lax.dynamic_update_slice_in_dim(gathered, pair_packed, links.g * 2, 0)
        for k in range(1, links.groups):
            at = ((links.g - k) % links.groups) * 2
            gathered = lax.dynamic_update_slice_in_dim(gathered, far_pairs[k - 1], at, 0)
        gathered = gathered.astype(F32)
        offsets = [sum(sizes[:i]) for i in range(len(sizes) + 1)]
        parts = [gathered[:, offsets[i] : offsets[i + 1]] for i in range(len(sizes))]
        taps = parts[0].reshape(shards, 4, -1).transpose(1, 0, 2).reshape(4, channels)
        bias = parts[1].reshape(channels)
        n_gain = parts[2].reshape(depth)
        g_gain = parts[3].reshape(inner)
        head_params = jnp.stack([parts[i].reshape(-1) for i in (4, 5, 6)])

        def of_group(array, step):
            return lax.dynamic_slice_in_dim(array, p * step, step, array.ndim - 1)

        head_here = of_group(head_params, heads)
        head_rows = jnp.pad(head_here, ((0, 5), (0, LANES - heads)))
        conv_rows = jnp.concatenate(
            [
                of_group(taps[:, :inner], width),
                of_group(bias[:inner], width)[None],
                jnp.repeat(head_here[2], size)[None],
                of_group(g_gain, width)[None],
                jnp.zeros((1, width), F32),
            ],
            axis=0,
        )
        return taps, bias, n_gain, head_rows, conv_rows

    split_a, split_b = state + width + LANES, state + 2 * width + LANES

    def columns(start, stop):
        return mine[:, start:stop], from_core[:, start:stop]

    def turn(k):
        return lambda value: links.along_g(value, k)

    def rounds(joined):
        return [(lambda value, j=j: links.along_a(value, j), joined) for j in range(1, links.sides)]

    others = list(range(1, links.groups))
    few = len(others) // 2
    (from_core, packed_core, lengths_core), _ = phase(
        [(links.core, for_core), (links.core, packed), (links.core, lengths)]
    )
    piece = links.piece_of(mine, from_core)
    pair_packed = jnp.concatenate(
        [jnp.where(is_high, packed_core, packed), jnp.where(is_high, packed, packed_core)], axis=0
    )
    first = piece[:, :split_a]
    moved, _ = phase(
        [(turn(k), first) for k in others[:1]] + [(turn(k), pair_packed) for k in others]
    )
    z_first, small_far = moved[:1], moved[1:]

    moved, parameters_here = phase(
        [(turn(k), first) for k in others[1:]] + [(links.core, hidden_in)], parameters, (small_far,)
    )
    z_first, core_hidden = z_first + moved[:-1], moved[-1]
    taps, bias, n_gain, head_rows, conv_rows = parameters_here
    n_rows = jnp.broadcast_to(n_gain[None], (8, depth))
    z_kq = jnp.concatenate([part[:, :state] for part in z_first], axis=0)
    z_values = jnp.concatenate([part[:, state:] for part in z_first], axis=0)
    gate_part = piece[:, split_a:split_b]

    far_hidden, z_kq, z_values = after((far_hidden, z_kq, z_values))
    moved, _ = phase(
        rounds(z_kq)
        + [(turn(k), gate_part) for k in others[: few + 0]]
        + [(links.core, far_hidden)]
    )
    y_kq, z_gate, far_core_hidden = moved[: links.sides - 1], moved[links.sides - 1 : -1], moved[-1]
    w_kq = links.assemble(*columns(0, state), z_kq, y_kq)
    kq_columns = inner + c * state
    pair_lengths = jnp.concatenate([lengths, lengths_core], axis=0)
    pair_ends = jnp.cumsum(pair_lengths, axis=1)
    position = positions[None, :]
    begin = jnp.where(
        position >= pair_ends[:, 1:],
        pair_ends[:, 1:],
        jnp.where(position >= pair_ends[:, :1], pair_ends[:, :1], 0),
    )
    kq_taps = lax.dynamic_slice_in_dim(taps, kq_columns, state, 1)
    kq_bias = lax.dynamic_slice_in_dim(bias, kq_columns, state, 0)

    def keys_or_queries(w_kq, core_hidden, far_hidden, far_core_hidden):
        normed, scale = normalize_call(
            [hidden_in, core_hidden, far_hidden, far_core_hidden], n_rows
        )
        kq_in = dot(normed[: 2 * tokens], w_kq).reshape(2, tokens, state)
        kq_pre, kq_shifted = causal_conv(kq_in, begin, kq_taps, kq_bias)
        return scale[:tokens, :1], normed, kq_pre, kq_shifted

    moved, (scale_own, normed, kq_pre, kq_shifted) = phase(
        [(turn(k), gate_part) for k in others[few:-1]] + rounds(z_values),
        keys_or_queries,
        (w_kq, core_hidden, far_hidden, far_core_hidden),
    )
    z_gate, y_values = z_gate + moved[: 1 - links.sides], moved[1 - links.sides :]
    counts = jnp.stack([pair_lengths // 32, pair_lengths % 32], axis=2).reshape(2, 4).astype(BF16)
    counts = jnp.pad(counts, ((0, 14), (0, state - 4)))
    kq_near = jax.nn.silu(kq_pre).astype(BF16).reshape(2 * tokens, state)
    place = jnp.stack([links.a, links.g, c]).astype(jnp.int32)
    links_shape = (links.sides, links.groups)

    def project(start, stop, joined, rounds_of_it):
        operands = (*columns(start, stop), [joined, *rounds_of_it], normed)
        return functools.partial(project_call, links_shape, place, tokens=tokens), operands

    moved, (w_values, conv_in) = phase(
        [(turn(k), gate_part) for k in others[-1:]]
        + [(links.side, jnp.concatenate([kq_near, counts], axis=0))],
        *project(state, split_a, z_values, y_values),
    )
    z_gate, kq_far = z_gate + moved[:1], moved[1]
    all_counts = jnp.concatenate([counts[:2, :4], kq_far[2 * tokens : 2 * tokens + 2, :4]], axis=0)
    all_counts = all_counts.astype(jnp.int32)
    all_lengths = all_counts[:, 0::2] * 32 + all_counts[:, 1::2]
    kq_half = jnp.concatenate([kq_near, kq_far[: 2 * tokens]], axis=0)
    z_gate = jnp.concatenate(z_gate, axis=0)

    (kq_core,), _ = phase([(links.core, kq_half)])
    kq_core = kq_core.reshape(2, 2, tokens, state)[:, ::-1].reshape(4 * tokens, state)
    keys_queries = jnp.concatenate(
        [jnp.where(is_high, kq_core, kq_half), jnp.where(is_high, kq_half, kq_core)], axis=1
    )
    far_back = links.side(back_own)
    moved, (ssd_out, states) = phase(
        rounds(z_gate) + [(turn(k), piece[:, split_b:]) for k in others],
        functools.partial(forward_call, heads, size),
        (all_lengths, conv_in, keys_queries, conv_rows, head_rows),
    )
    y_gate, z_out = moved[: links.sides - 1], moved[links.sides - 1 :]
    z_out = jnp.concatenate(z_out, axis=0)

    moved, (w_gate, gate) = phase(
        rounds(z_out) + [(links.core, back_own)], *project(split_a, split_b, z_gate, y_gate)
    )
    y_out, core_back = moved[:-1], moved[-1]
    (far_core_back,), _ = phase([(links.core, far_back)])
    back_blocks = [back_own, core_back, far_back, far_core_back]
    w_out, d_branch, sums = branch_back_call(
        links_shape, place, *columns(split_b, split_b + width), [z_out, *y_out], back_blocks,
        gate, ssd_out, conv_rows,
    )
    moved, back = phase(
        [(links.core, sums), (links.side, sums), (links.corner, sums)],
        lambda *blocks: jnp.concatenate(blocks, axis=0),
        back_blocks,
    )
    branch, d_gate, d_ssd, gain_rows = gating_back_call(
        inner, [sums, *moved], gate, ssd_out, d_branch, conv_rows
    )
    grad_gate_gain = gain_rows[0]

    def weight_grad(left, right):
        return lax.dot_general(
            left, right, (((0,), (0,)), ((), ())), preferred_element_type=F32
        ).astype(BF16)

    half = heads // 2
    by_g = width // (3 * LANES) * 2 * LANES
    far_rows, near_rows = slice(2 * tokens, None), slice(0, 2 * tokens)

    def backward(part, d_out):
        return backward_call(
            half, size, part, all_lengths, conv_in, keys_queries, d_out, states, conv_rows, head_rows
        )

    def a_sends(parts):
        return [
            (lambda value, j=j: links.along_a(value, j + 1), part) for j, part in enumerate(parts)
        ]

    def g_sends(parts):
        return [(turn(k + 1), part) for k, part in enumerate(parts)]

    g_out_z = weight_grad(back, branch[:, :by_g])
    mixed_parts = dot_nt(branch, w_out).astype(BF16).reshape(2, 2, tokens, depth)
    def grad_parts(left, right):
        parts = weight_grad_call(links_shape, place, left, right)
        return parts[0], parts[1:]

    gate_mine, gate_others = grad_parts(normed, d_gate)
    out_y_mine, out_y_others = grad_parts(back, branch[:, by_g:])
    first_mine = jnp.concatenate([gate_mine, out_y_mine], axis=2)
    first_others = [jnp.concatenate(p, axis=2) for p in zip(gate_others, out_y_others)]
    out_mine, out_others = links.parts_for_g(g_out_z.reshape(links.groups, -1, by_g))
    moved, (d_in_0, d_steps_0, d_kq_0, conv_grads_0, head_grads_0) = phase(
        a_sends(first_others) + g_sends(out_others) + [(links.core, mixed_parts[:, 1])],
        functools.partial(backward, 0),
        (d_ssd,),
    )
    count_a, count_g = links.sides - 1, links.groups - 1
    first_held = total(first_mine, moved[:count_a]).astype(BF16)
    out_chip = total(out_mine, moved[count_a:-1]).astype(BF16)
    mixed_sum = mixed_parts[:, 0].astype(F32) + moved[-1].astype(F32)
    first_mine, first_others = links.parts_for_g(first_held)
    values_mine, values_others = grad_parts(normed, d_in_0)
    moved, (d_in_1, d_steps_1, d_kq_1, conv_grads_1, head_grads_1) = phase(
        g_sends(first_others) + a_sends(values_others) + [(links.side, mixed_sum[1].astype(BF16))],
        functools.partial(backward, 1),
        (d_ssd,),
    )
    first_piece = total(first_mine, moved[:count_g]).astype(BF16)
    held_0 = total(values_mine, moved[count_g:-1]).astype(BF16)
    mixed = hidden_in.astype(F32) + mixed_sum[0] + moved[-1].astype(F32)
    mixed = jnp.where(is_valid, mixed, 0.0).astype(BF16)

    d_kq_parts = (d_kq_0 + d_kq_1).reshape(2, 2, tokens, 2 * state)
    d_kq_mine = jnp.where(is_high, d_kq_parts[..., state:], d_kq_parts[..., :state])
    d_kq_core = jnp.where(is_high, d_kq_parts[..., :state], d_kq_parts[..., state:])
    d_kq_core = d_kq_core[:, ::-1].astype(BF16)
    d_steps = d_steps_0 + d_steps_1
    d_rest = jnp.concatenate([d_in_0, d_in_1, d_steps], axis=1)

    def d_normed_of(d_gate_rows, d_rest_rows):
        return (dot_nt(d_gate_rows, w_gate) + dot_nt(d_rest_rows, w_values)).astype(BF16)

    values_mine, values_others = grad_parts(normed, d_in_1)
    out_mine, out_others = links.parts_for_a(out_chip.reshape(links.sides, -1, by_g))
    moved, d_far = phase(
        [(links.core, d_kq_core)]
        + a_sends(values_others)
        + a_sends(out_others)
        + [(links.side, first_piece)],
        d_normed_of,
        (d_gate[far_rows], d_rest[far_rows]),
    )
    d_kq_sum = d_kq_mine + moved[0].astype(F32)
    held_1 = total(values_mine, moved[1 : 1 + count_a]).astype(BF16)
    out_piece = total(out_mine, moved[1 + count_a : -1]).astype(BF16)
    first_x = links.join_x(first_piece, moved[-1])

    values_mine, values_others = links.parts_for_g(jnp.concatenate([held_0, held_1], axis=2))
    d_far = d_far.reshape(2, tokens, depth)
    moved, d_near = phase(
        [(links.side, d_kq_sum[1].astype(BF16)), (links.core, d_far[1])] + g_sends(values_others),
        d_normed_of,
        (d_gate[near_rows], d_rest[near_rows]),
    )
    d_kq = d_kq_sum[0] + moved[0].astype(F32)
    d_far = total(d_far[0], [moved[1]]).astype(BF16)
    values_piece = total(values_mine, moved[2:]).astype(BF16)

    kq_sig = sigmoid(kq_pre)
    d_kq_pre = d_kq * (kq_sig * (1.0 + kq_pre * (1.0 - kq_sig)))
    d_kq_in = causal_conv_back(d_kq_pre, begin, kq_taps).astype(BF16).reshape(2 * tokens, state)
    last_piece = jnp.concatenate([out_piece, values_piece], axis=1)
    moved, _ = phase([(links.side, d_kq_in), (links.side, last_piece)] + rounds(first_x))
    quarter = state // 2
    d_kq_all = jnp.concatenate([d_kq_in, moved[0]], axis=0)
    d_tail = jnp.concatenate(
        [
            jnp.where(x == 1, d_kq_all[:, quarter:], d_kq_all[:, :quarter]),
            d_steps[:, :heads],
            jnp.zeros((4 * tokens, LANES - quarter - heads), BF16),
        ],
        axis=1,
    )
    tail_mine, tail_others = grad_parts(normed, d_tail)
    last_x = links.join_x(last_piece, moved[1])
    first_rows = links.rows_of_core(links.join_a(first_x, moved[2:]))
    d_near = (d_near.astype(F32) + dot_nt(d_kq_in, w_kq)).astype(BF16).reshape(2, tokens, depth)
    far_d = links.side(d_far)

    moved, _ = phase(
        a_sends(tail_others)
        + rounds(last_x)
        + [(links.core, first_rows[1]), (links.core, d_near[1])]
    )
    tail_held = total(tail_mine, moved[:count_a]).astype(BF16)
    last_rows = links.rows_of_core(links.join_a(last_x, moved[count_a : 2 * count_a]))
    first_shares = links.shares(first_rows[0], moved[-2])
    d_near = total(d_near[0], [moved[-1]])

    tail_mine, tail_others = links.parts_for_g(tail_held)
    moved, _ = phase(g_sends(tail_others) + [(links.core, last_rows[1])])
    tail_piece = total(tail_mine, moved[:-1]).astype(BF16)
    last_shares = links.shares(last_rows[0], moved[-1])
    moved, _ = phase(rounds(tail_piece))
    tail_rows = links.rows_of_core(links.join_a(tail_piece, moved))
    moved, _ = phase([(links.core, tail_rows[1])])
    tail_both = jnp.concatenate(
        [jnp.where(is_high, moved[0], tail_rows[0]), jnp.where(is_high, tail_rows[0], moved[0])],
        axis=1,
    )
    (tail_far,), _ = phase([(links.side, tail_both)])
    tail_low = jnp.where(x == 1, tail_far, tail_both)
    tail_high = jnp.where(x == 1, tail_both, tail_far)
    tail_shares = [tail_low[:, :LANES], tail_low[:, LANES:], tail_high[:, :LANES], tail_high[:, LANES:]]
    d_normed = d_near + far_d.astype(F32)

    own_hidden, own_scale = hidden_in.astype(F32), scale_own
    weighted = n_gain * d_normed
    inner_mean = jnp.mean(own_hidden * weighted, axis=-1, keepdims=True)
    grad_hidden = (
        back_own.astype(F32)
        + own_scale * weighted
        - own_hidden * (own_scale * own_scale * own_scale * inner_mean)
    )

    conv_grads = jnp.concatenate([conv_grads_0, conv_grads_1], axis=1)
    head_grads = head_grads_0 + head_grads_1
    small = jnp.zeros((8, channels), F32)
    small = lax.dynamic_update_slice(small, conv_grads[:5], (0, p * width))
    d_kq_rows = [jnp.sum(kq_shifted[delay] * d_kq_pre, axis=(0, 1)) for delay in (3, 2, 1, 0)]
    d_kq_rows = jnp.stack(d_kq_rows + [jnp.sum(d_kq_pre, axis=(0, 1))])
    small = lax.dynamic_update_slice(small, d_kq_rows, (0, kq_columns))
    small = lax.dynamic_update_slice(small, grad_gate_gain[None], (5, p * width))
    grad_skip = conv_grads[5].reshape(heads, size).sum(axis=1)
    head_all = jnp.stack([head_grads[0, :heads], head_grads[1, :heads], grad_skip])
    small_heads = jnp.zeros((3, all_heads), F32)
    small_heads = lax.dynamic_update_slice(small_heads, head_all, (0, p * heads))
    small = lax.dynamic_update_slice(small, small_heads.reshape(1, -1), (7, 0))
    small = links.sum_all(small)

    def own_slice(array, count):
        return lax.dynamic_slice_in_dim(array, links.shard * count, count, array.ndim - 1)

    grad_conv = own_slice(small[:5], channels // shards)
    grad_heads = own_slice(small[7, : 3 * all_heads].reshape(3, all_heads), all_heads // shards)

    grad_in = jnp.concatenate(
        [share[:, :width] for share in first_shares]
        + [share[:, by_g:] for share in last_shares]
        + [tail_shares[i][:, :quarter] for i in (0, 2, 1, 3)]
        + [share[:, quarter : quarter + heads] for share in tail_shares],
        axis=1,
    ).astype(F32)
    out_parts = [
        part
        for first, last in zip(first_shares, last_shares)
        for part in (last[:, :by_g], first[:, width:])
    ]
    grad_norm = jnp.sum(grad_in * in_weight.astype(F32), axis=1) / norm_gain.astype(F32)
    grad_out = jnp.concatenate(out_parts, axis=1).astype(F32).T
    return (
        mixed,
        grad_hidden,
        grad_norm,
        grad_in,
        grad_conv[:4],
        grad_conv[4],
        grad_heads[0],
        grad_heads[1],
        grad_heads[2],
        own_slice(small[5, :inner], inner // shards),
        grad_out,
    )


def solution(mesh):
    return jax.shard_map(
        functools.partial(per_device, mesh.shape["rep"], mesh.shape["fsdp"]),
        mesh=mesh,
        in_specs=(
            P(("rep", "fsdp"), None),
            P(("rep", "fsdp"), None),
            P("fsdp"),
            P("fsdp", None),
            P(None, "fsdp"),
            P("fsdp"),
            P("fsdp"),
            P("fsdp"),
            P("fsdp"),
            P("fsdp"),
            P(None, "fsdp"),
            P(("rep", "fsdp"), None),
        ),
        out_specs=(
            P(("rep", "fsdp"), None),
            P(("rep", "fsdp"), None),
            P("fsdp"),
            P("fsdp", None),
            P(None, "fsdp"),
            P("fsdp"),
            P("fsdp"),
            P("fsdp"),
            P("fsdp"),
            P("fsdp"),
            P(None, "fsdp"),
        ),
        check_vma=False,
    )
```

```python
import functools

import jax
import jax.numpy as jnp
from jax import lax
from jax.experimental import pallas as pl
from jax.experimental.pallas import tpu as pltpu
from jax.sharding import PartitionSpec as P

EPS = 1e-05
CHUNK = 128
LANES = 128
HIGHEST = lax.Precision.HIGHEST
F32 = jnp.float32
BF16 = jnp.bfloat16


def dot(left, right, precision=None):
    return lax.dot_general(
        left, right, (((1,), (0,)), ((), ())), precision=precision, preferred_element_type=F32
    )


def dot_nt(left, right):
    return lax.dot_general(left, right, (((1,), (1,)), ((), ())), preferred_element_type=F32)


def sigmoid(v):
    return 1.0 / (1.0 + jnp.exp(-v))


def softplus(v):
    return jnp.maximum(v, 0.0) + jnp.log1p(jnp.exp(-jnp.abs(v)))


def begin_of(position, first, both):
    return jnp.where(position >= both, both, jnp.where(position >= first, first, 0))


def iotas(rows, columns):
    return (
        lax.broadcasted_iota(jnp.int32, (rows, columns), 0),
        lax.broadcasted_iota(jnp.int32, (rows, columns), 1),
    )


def conv_tile(u_ref, cw_ref, start, columns, masks):
    inputs = [u_ref[start : start + CHUNK, columns]]
    for delay in range(1, 4):
        if start:
            shifted = u_ref[start - delay : start - delay + CHUNK, columns]
        else:
            shifted = pltpu.roll(inputs[0], delay, 0)
        inputs.append(jnp.where(masks[delay - 1], shifted, 0.0))
    pre = cw_ref[4:5, columns] + cw_ref[3:4, columns] * inputs[0]
    for delay in range(1, 4):
        pre = pre + cw_ref[3 - delay : 4 - delay, columns] * inputs[delay]
    return pre, inputs


def chunk_rates(dt_ref, hp_ref, start):
    raw = dt_ref[start : start + CHUNK, :] + hp_ref[0:1, :]
    step = softplus(raw)
    rate = -jnp.exp(hp_ref[1:2, :]) * step
    row, column = iotas(CHUNK, CHUNK)
    running = dot((row >= column).astype(F32), rate, HIGHEST)
    return raw, step, rate, running


def pair_of(low, matrix, head):
    return jnp.where(low, matrix[:, head : head + 1], matrix[:, head + 1 : head + 2])


def forward_kernel(heads, size, len_ref, u_ref, dt_ref, kq_ref, cw_ref, hp_ref, y_ref, st_ref, state):
    block = pl.program_id(0)
    first = len_ref[block, 0]
    both = first + len_ref[block, 1]
    tokens = u_ref.shape[0]
    chunks = tokens // CHUNK
    row, column = iotas(CHUNK, CHUNK)
    low = column < size
    low_row = low[0:1, :]
    for ci in range(chunks):
        start = ci * CHUNK
        position = row + start
        begin = begin_of(position, first, both)
        masks = [position - delay >= begin for delay in range(1, 4)]
        raw, step, rate, running = chunk_rates(dt_ref, hp_ref, start)
        running_t = running.T
        keys = kq_ref[start : start + CHUNK, :LANES]
        queries = kq_ref[start : start + CHUNK, LANES:]
        keys_t = keys.astype(F32).T.astype(BF16)
        allowed = (column <= row) & (column + start >= begin)
        scores = jnp.where(allowed, dot_nt(queries, keys), 0.0)
        last_begin = begin_of(start + CHUNK - 1, first, both)
        source = position >= last_begin
        reached = begin < start
        ending = running[CHUNK - 1 : CHUNK, :]
        kept = jnp.where(last_begin < start, jnp.exp(ending), 0.0)
        for pair in range(heads // 2):
            h = 2 * pair
            columns = slice(pair * LANES, (pair + 1) * LANES)
            pre, _ = conv_tile(u_ref, cw_ref, start, columns, masks)
            values = pre * sigmoid(pre)
            scaled = values * pair_of(low, step, h)
            weights = []
            for head in (h, h + 1):
                gap = running[:, head : head + 1] - running_t[head : head + 1, :]
                weights.append((scores * jnp.exp(jnp.minimum(gap, 0.0))).astype(BF16))
            stacked = jnp.concatenate(
                [jnp.where(low, scaled, 0.0), jnp.where(low, 0.0, scaled)], axis=0
            ).astype(BF16)
            out = dot(jnp.concatenate(weights, axis=1), stacked)
            out = out + cw_ref[5:6, columns] * values
            across = pair_of(low, running, h)
            if ci:
                carried = dot(queries, state[:, columns].astype(BF16))
                out = out + jnp.where(reached, carried * jnp.exp(across), 0.0)
            y_ref[start : start + CHUNK, columns] = out
            if ci < chunks - 1:
                left = pair_of(low_row, ending, h) - across
                source_in = jnp.where(source, scaled * jnp.exp(left), 0.0).astype(BF16)
                fresh = dot(keys_t, source_in)
                if ci:
                    fresh = fresh + state[:, columns] * pair_of(low_row, kept, h)
                state[:, columns] = fresh
                st_ref[0, ci, :, columns] = fresh.astype(BF16)


def backward_kernel(
    heads,
    size,
    first_head,
    first_block,
    len_ref,
    u_ref,
    dt_ref,
    kq_ref,
    dy_ref,
    st_ref,
    cw_ref,
    hp_ref,
    du_ref,
    ddt_ref,
    dkq_ref,
    cg_ref,
    hg_ref,
    d_state,
    d_pre,
    out_in,
    source_in,
):
    block = pl.program_id(0)
    first = len_ref[first_block + block, 0]
    both = first + len_ref[first_block + block, 1]
    tokens, width = u_ref.shape
    chunks = tokens // CHUNK
    row, column = iotas(CHUNK, CHUNK)
    low = column < size
    low_row = low[0:1, :]
    wide_row, wide_column = iotas(2 * CHUNK, LANES)
    pick_row, pick_column = iotas(16, 2 * CHUNK)

    @pl.when(block == 0)
    def _():
        cg_ref[...] = jnp.zeros_like(cg_ref)
        hg_ref[...] = jnp.zeros_like(hg_ref)

    d_pre[tokens : tokens + 8, :] = jnp.zeros((8, width), F32)
    for ci in reversed(range(chunks)):
        start = ci * CHUNK
        has_later = ci < chunks - 1
        position = row + start
        begin = begin_of(position, first, both)
        masks = [position - delay >= begin for delay in range(1, 4)]
        ahead = [begin_of(position + delay, first, both) <= position for delay in range(1, 4)]
        raw, step, rate, running = chunk_rates(dt_ref, hp_ref, start)
        running_t = running.T
        keys = kq_ref[start : start + CHUNK, :LANES]
        queries = kq_ref[start : start + CHUNK, LANES:]
        allowed = (row <= column) & (position >= begin_of(column + start, first, both))
        scores = jnp.where(allowed, dot_nt(keys, queries), 0.0)
        last_begin = begin_of(start + CHUNK - 1, first, both)
        source = position >= last_begin
        reached = begin < start
        ending = running[CHUNK - 1 : CHUNK, :]
        kept = jnp.where(last_begin < start, jnp.exp(ending), 0.0)
        d_scores = jnp.zeros((CHUNK, CHUNK), F32)
        later_sums = jnp.zeros((16, CHUNK), F32)
        early_sums = jnp.zeros((CHUNK, LANES), F32)
        out_sums = jnp.zeros((CHUNK, LANES), F32)
        source_sums = jnp.zeros((CHUNK, LANES), F32)
        direct_sums = jnp.zeros((CHUNK, LANES), F32)
        kept_sums = jnp.zeros((8, LANES), F32)
        for pair in range(heads // 2):
            h = first_head + 2 * pair
            columns = slice(pair * LANES, (pair + 1) * LANES)
            to_head = (column == h + (row >= size).astype(jnp.int32)).astype(BF16)
            pre, inputs = conv_tile(u_ref, cw_ref, start, columns, masks)
            gate = sigmoid(pre)
            values = pre * gate
            steps = pair_of(low, step, h)
            scaled = values * steps
            d_out = dy_ref[start : start + CHUNK, columns].astype(F32)
            d_low = d_out.astype(BF16)
            stacked = jnp.concatenate(
                [jnp.where(low, scaled, 0.0), jnp.where(low, 0.0, scaled)], axis=0
            ).astype(BF16)
            d_weights = dot_nt(stacked, d_low)
            weights, products = [], []
            for at, head in enumerate((h, h + 1)):
                gap = running_t[head : head + 1, :] - running[:, head : head + 1]
                decay = jnp.exp(jnp.minimum(gap, 0.0))
                d_decayed = decay * d_weights[at * CHUNK : (at + 1) * CHUNK]
                d_scores = d_scores + d_decayed
                products.append((scores * d_decayed).astype(BF16))
                weights.append((scores * decay).astype(BF16))
            early = wide_column == h + (wide_row >= CHUNK).astype(jnp.int32)
            early_sums = early_sums + dot(jnp.concatenate(products, axis=1), early.astype(BF16))
            later = pick_row == h + (pick_column >= CHUNK).astype(jnp.int32)
            later_sums = later_sums + dot(later.astype(BF16), jnp.concatenate(products, axis=0))
            d_stacked = jnp.concatenate(
                [jnp.where(low, d_out, 0.0), jnp.where(low, 0.0, d_out)], axis=0
            ).astype(BF16)
            d_scaled = dot(jnp.concatenate(weights, axis=1), d_stacked)
            across = pair_of(low, running, h)
            if has_later:
                left = jnp.exp(pair_of(low_row, ending, h) - across)
                left = jnp.where(source, left, 0.0)
                d_state_here = d_state[:, columns]
                d_source = dot(keys, d_state_here.astype(BF16)) * left
                d_scaled = d_scaled + d_source
                source_sums = source_sums + dot((scaled * d_source).astype(BF16), to_head)
                source_in[:, columns] = (scaled * left).astype(BF16)
            if ci:
                before = st_ref[0, ci - 1, :, columns]
                d_reach = jnp.where(reached, d_out * jnp.exp(across), 0.0)
                out_sums = out_sums + dot((d_reach * dot(queries, before)).astype(BF16), to_head)
                out_in[:, columns] = d_reach.astype(BF16)
                if has_later:
                    held = jnp.sum(d_state_here * before.astype(F32), axis=0, keepdims=True)
                    held = held * pair_of(low_row, kept, h)
                    kept_sums = kept_sums + dot(
                        jnp.broadcast_to(held, (8, LANES)), to_head.astype(F32), HIGHEST
                    )
            direct_sums = direct_sums + dot((d_scaled * values).astype(BF16), to_head)
            d_values = d_scaled * steps + cw_ref[5:6, columns] * d_out
            cg_ref[5:6, columns] += jnp.sum(d_out * values, axis=0, keepdims=True)
            d_here = d_values * (gate * (1.0 + pre * (1.0 - gate)))
            d_pre[start : start + CHUNK, columns] = d_here
            d_in = cw_ref[3:4, columns] * d_here
            for delay in range(1, 4):
                shifted = d_pre[start + delay : start + delay + CHUNK, columns]
                d_in = d_in + cw_ref[3 - delay : 4 - delay, columns] * jnp.where(
                    ahead[delay - 1], shifted, 0.0
                )
            du_ref[start : start + CHUNK, columns] = d_in.astype(BF16)
            for delay in range(4):
                cg_ref[3 - delay : 4 - delay, columns] += jnp.sum(
                    inputs[delay] * d_here, axis=0, keepdims=True
                )
            cg_ref[4:5, columns] += jnp.sum(d_here, axis=0, keepdims=True)
        d_scores = jnp.where(allowed, d_scores, 0.0)
        d_keys = dot(d_scores.astype(BF16), queries)
        d_queries = dot(d_scores.T.astype(BF16), keys)
        d_running = (
            jnp.concatenate([later_sums, jnp.zeros((CHUNK - 16, CHUNK), F32)], axis=0).T
            - early_sums
            + out_sums
            - source_sums
        )
        if has_later:
            d_keys = d_keys + dot_nt(source_in[...], d_state[...].astype(BF16))
            at_end = jnp.sum(source_sums, axis=0, keepdims=True) + kept_sums[0:1, :]
            d_running = d_running + jnp.where(row == CHUNK - 1, at_end, 0.0)
        if ci:
            d_queries = d_queries + dot_nt(out_in[...], st_ref[0, ci - 1])
            queries_t = queries.astype(F32).T.astype(BF16)
            for pair in range(heads // 2):
                columns = slice(pair * LANES, (pair + 1) * LANES)
                fresh = dot(queries_t, out_in[:, columns])
                if has_later:
                    fresh = fresh + d_state[:, columns] * pair_of(low_row, kept, first_head + 2 * pair)
                d_state[:, columns] = fresh
        dkq_ref[start : start + CHUNK, :LANES] = d_keys
        dkq_ref[start : start + CHUNK, LANES:] = d_queries
        d_rate = dot((row <= column).astype(F32), d_running, HIGHEST)
        d_step = direct_sums - jnp.exp(hp_ref[1:2, :]) * d_rate
        d_raw = d_step * sigmoid(raw)
        ddt_ref[start : start + CHUNK, :] = d_raw.astype(BF16)
        hg_ref[0:1, :] += jnp.sum(d_raw, axis=0, keepdims=True)
        hg_ref[1:2, :] += jnp.sum(d_rate * rate, axis=0, keepdims=True)


def prepare_first_kernel(heads, size, state, at_ref, in_ref, mine_ref, other_ref):
    x, core = at_ref[0], at_ref[1]
    width = heads * size
    inner = 4 * width
    steps_at = 2 * inner + 2 * state
    steps = in_ref[:, steps_at : steps_at + 4 * heads].astype(F32)
    rows = steps.shape[0]
    steps = jnp.concatenate([steps, jnp.zeros((rows, LANES - 4 * heads), F32)], axis=1)
    column = lax.broadcasted_iota(jnp.int32, (rows, LANES), 1)
    for ref, c in ((mine_ref, core), (other_ref, 1 - core)):
        p = 2 * x + c
        values_at = pl.multiple_of(inner + p * width, LANES)
        ref[:, :width] = in_ref[:, pl.ds(values_at, width)]
        drawn = pltpu.roll(steps, lax.rem(LANES - heads * p, LANES), 1)
        ref[:, width : width + LANES] = jnp.where(column < heads, drawn, 0.0).astype(BF16)
        keys_at = pl.multiple_of(2 * inner + c * state, LANES)
        ref[:, width + LANES : width + LANES + state] = in_ref[:, pl.ds(keys_at, state)]


def prepare_last_kernel(width, at_ref, in_ref, out_ref, mine_ref, other_ref):
    x, core = at_ref[0], at_ref[1]
    for ref, c in ((mine_ref, core), (other_ref, 1 - core)):
        at = pl.multiple_of((2 * x + c) * width, LANES)
        ref[:, :width] = in_ref[:, pl.ds(at, width)]
        ref[:, width:] = out_ref[pl.ds(at, width), :].T


def prepare_call(kernel, columns, place, *weights):
    rows = weights[0].shape[0]
    return pl.pallas_call(
        kernel,
        in_specs=[pl.BlockSpec(memory_space=pltpu.SMEM)]
        + [pl.BlockSpec(memory_space=pltpu.VMEM)] * len(weights),
        out_specs=[pl.BlockSpec(memory_space=pltpu.VMEM)] * 2,
        out_shape=[jax.ShapeDtypeStruct((rows, columns), BF16)] * 2,
        compiler_params=pltpu.CompilerParams(vmem_limit_bytes=24 * 1024 * 1024),
        name="prepare",
    )(place, *weights)


def unpack_kernel(sizes, heads, size, state, at_ref, small_ref, n_ref, conv_ref, head_ref, kq_ref, all_ref):
    conv_size, gate_size, norm_size, head_size = sizes
    x, c = at_ref[0], at_ref[1]
    p = 2 * x + c
    shards = small_ref.shape[0] // 8
    width = heads * size

    def joined(first_row, rows, at, part, columns):
        padded = -(-columns // LANES) * LANES
        lanes = -(-part // LANES) * LANES
        lane = lax.broadcasted_iota(jnp.int32, (8, lanes), 1)
        result = jnp.zeros((8, padded), F32)
        for f in range(shards):
            rows_here = small_ref[8 * f : 8 * f + 8, at : at + lanes].astype(F32)
            rows_here = jnp.where(lane < part, rows_here, 0.0)
            if padded > lanes:
                rows_here = jnp.concatenate(
                    [rows_here, jnp.zeros((8, padded - lanes), F32)], axis=1
                )
            result = result + pltpu.roll(rows_here, (part * f) % padded, 1)
        return result[first_row : first_row + rows]

    conv_all = joined(0, 5, 0, conv_size, conv_size * shards)
    gate_all = joined(5, 1, 0, gate_size, gate_size * shards)
    norm_all = joined(6, 1, 0, norm_size, norm_size * shards)
    n_ref[...] = jnp.broadcast_to(norm_all, n_ref.shape)
    all_ref[...] = jnp.zeros_like(all_ref)
    all_ref[0:5, : conv_all.shape[1]] = conv_all
    all_ref[6:7, : gate_all.shape[1]] = gate_all
    conv_ref[...] = all_ref[:, pl.ds(pl.multiple_of(p * width, LANES), width)]
    kq_at = 4 * width + c * state
    kq_ref[...] = all_ref[:, pl.ds(pl.multiple_of(kq_at, LANES), state)]
    column = lax.broadcasted_iota(jnp.int32, (8, LANES), 1)
    head_ref[...] = jnp.zeros_like(head_ref)
    for row in range(3):
        values = joined(7, 1, row * LANES, head_size, head_size * shards)
        values = jnp.broadcast_to(values, (8, LANES))
        values = pltpu.roll(values, lax.rem(LANES - heads * p, LANES), 1)
        head_ref[row : row + 1, :] = jnp.where(column < heads, values, 0.0)[0:1]
    row_at, column_at = iotas(LANES, width)
    spread = (row_at == column_at // size).astype(F32)
    conv_ref[5:6, :] = dot(head_ref[...], spread, HIGHEST)[2:3]


def unpack_call(sizes, heads, size, state, place, small):
    shards = small.shape[0] // 8
    depth, width = sizes[2] * shards, heads * size
    columns = -(-sizes[0] * shards // LANES) * LANES
    return pl.pallas_call(
        functools.partial(unpack_kernel, sizes, heads, size, state),
        in_specs=[
            pl.BlockSpec(memory_space=pltpu.SMEM),
            pl.BlockSpec(memory_space=pltpu.VMEM),
        ],
        out_specs=[pl.BlockSpec(memory_space=pltpu.VMEM)] * 4,
        out_shape=[
            jax.ShapeDtypeStruct((8, depth), F32),
            jax.ShapeDtypeStruct((8, width), F32),
            jax.ShapeDtypeStruct((8, LANES), F32),
            jax.ShapeDtypeStruct((8, state), F32),
        ],
        scratch_shapes=[pltpu.VMEM((8, columns), F32)],
        compiler_params=pltpu.CompilerParams(vmem_limit_bytes=24 * 1024 * 1024),
        name="unpack",
    )(place, small)


def assemble_rows(links_shape, at_ref, own_ref, core_ref, pieces, whole_ref):
    sides, groups = links_shape
    a, g, c = at_ref[0], at_ref[1], at_ref[2]
    rows = own_ref.shape[0]
    part = 2 * rows // sides
    base = g * (2 * rows)
    whole_ref[pl.ds(pl.multiple_of(base + c * rows, 16), rows), :] = own_ref[...]
    whole_ref[pl.ds(pl.multiple_of(base + (1 - c) * rows, 16), rows), :] = core_ref[...]
    for k in range(1, groups):
        base = lax.rem(g + groups - k, groups) * (2 * rows)
        for j in range(sides):
            at = base + lax.rem(a + sides - j, sides) * part
            piece = pieces[(k - 1) * sides + j]
            whole_ref[pl.ds(pl.multiple_of(at, 16), part), :] = piece[...]


def project_kernel(links_shape, at_ref, own_ref, core_ref, *refs):
    pieces, (rows_ref, whole_ref, out_ref) = refs[:-3], refs[-3:]

    @pl.when(pl.program_id(0) == 0)
    def _():
        assemble_rows(links_shape, at_ref, own_ref, core_ref, pieces, whole_ref)

    out_ref[...] = dot(rows_ref[...], whole_ref[...])


def whole_spec(array):
    return pl.BlockSpec(array.shape, lambda b: (0,) * array.ndim)


def columns_spec(array, width, index):
    if array.shape[1] == width:
        index = 0
    return pl.BlockSpec((array.shape[0], width), lambda b: (0, index))


def project_call(links_shape, width, index, blocks, tokens, place, parts, rows):
    depth = rows.shape[1]
    return pl.pallas_call(
        functools.partial(project_kernel, links_shape),
        grid=(blocks,),
        in_specs=[pl.BlockSpec(memory_space=pltpu.SMEM)]
        + [columns_spec(array, width, index) for array in parts]
        + [pl.BlockSpec((tokens, depth), lambda b: (b, 0))],
        out_specs=[
            pl.BlockSpec((depth, width), lambda b: (0, 0)),
            pl.BlockSpec((tokens, width), lambda b: (b, 0)),
        ],
        out_shape=[
            jax.ShapeDtypeStruct((depth, width), BF16),
            jax.ShapeDtypeStruct((blocks * tokens, width), F32),
        ],
        compiler_params=pltpu.CompilerParams(vmem_limit_bytes=40 * 1024 * 1024),
        cost_estimate=pl.CostEstimate(
            flops=2 * rows.size * width, bytes_accessed=2 * rows.size, transcendentals=0
        ),
        name="project",
    )(place, *parts, rows)


def branch_back_kernel(links_shape, at_ref, own_ref, core_ref, *refs):
    pieces, rows_refs = refs[:-10], refs[-10:-6]
    gate_ref, ssd_ref, cw_ref, whole_ref, out_ref, sums_ref = refs[-6:]
    block = pl.program_id(0)

    @pl.when(block == 0)
    def _():
        assemble_rows(links_shape, at_ref, own_ref, core_ref, pieces, whole_ref)

    for at, rows_ref in enumerate(rows_refs):

        @pl.when(block == at)
        def _():
            out_ref[...] = dot(rows_ref[...], whole_ref[...])

    tokens, width = out_ref.shape
    sums_ref[...] = jnp.zeros_like(sums_ref)
    for start in range(0, tokens, CHUNK):
        squares = jnp.zeros((CHUNK, LANES), F32)
        products = jnp.zeros((CHUNK, LANES), F32)
        for left in range(0, width, LANES):
            tile = (slice(start, start + CHUNK), slice(left, left + LANES))
            gate = gate_ref[tile]
            gated = ssd_ref[tile] * (gate * sigmoid(gate))
            squares = squares + gated * gated
            products = products + gated * (cw_ref[6:7, left : left + LANES] * out_ref[tile])
        sums_ref[0:1, start : start + CHUNK] = jnp.sum(squares.T, axis=0, keepdims=True)
        sums_ref[1:2, start : start + CHUNK] = jnp.sum(products.T, axis=0, keepdims=True)


def branch_back_call(links_shape, width, index, place, parts, rows, gate, ssd_out, conv_rows):
    tokens, depth = rows[0].shape
    block = pl.BlockSpec((tokens, width), lambda b: (b, 0))
    return pl.pallas_call(
        functools.partial(branch_back_kernel, links_shape),
        grid=(4,),
        in_specs=[pl.BlockSpec(memory_space=pltpu.SMEM)]
        + [columns_spec(array, width, index) for array in parts]
        + [whole_spec(array) for array in rows]
        + [block, block, pl.BlockSpec((8, width), lambda b: (0, 0))],
        out_specs=[
            pl.BlockSpec((depth, width), lambda b: (0, 0)),
            block,
            pl.BlockSpec((8, tokens), lambda b: (0, b)),
        ],
        out_shape=[
            jax.ShapeDtypeStruct((depth, width), BF16),
            jax.ShapeDtypeStruct((4 * tokens, width), F32),
            jax.ShapeDtypeStruct((8, 4 * tokens), F32),
        ],
        compiler_params=pltpu.CompilerParams(vmem_limit_bytes=56 * 1024 * 1024),
        cost_estimate=pl.CostEstimate(
            flops=8 * tokens * depth * width, bytes_accessed=8 * tokens * depth, transcendentals=0
        ),
        name="branch_back",
    )(place, *parts, *rows, gate, ssd_out, conv_rows)


def gating_back_kernel(
    inner, sums_ref, core_ref, side_ref, both_ref, gate_ref, ssd_ref, db_ref, cw_ref,
    branch_ref, dgate_ref, dssd_ref, gain_ref
):
    @pl.when(pl.program_id(0) == 0)
    def _():
        gain_ref[...] = jnp.zeros_like(gain_ref)

    sums = sums_ref[...] + core_ref[...] + side_ref[...] + both_ref[...]
    scale_row = lax.rsqrt(sums[0:1, :] * (1.0 / inner) + EPS)
    cross_row = scale_row * scale_row * scale_row * (sums[1:2, :] * (1.0 / inner))
    tokens, width = gate_ref.shape
    for start in range(0, tokens, CHUNK):
        stacked = jnp.concatenate(
            [scale_row[:, start : start + CHUNK], cross_row[:, start : start + CHUNK],
             jnp.zeros((CHUNK - 2, CHUNK), F32)], axis=0
        ).T
        scale, cross = stacked[:, 0:1], stacked[:, 1:2]
        for left in range(0, width, LANES):
            columns = slice(left, left + LANES)
            tile = (slice(start, start + CHUNK), columns)
            gate, ssd, d_branch = gate_ref[tile], ssd_ref[tile], db_ref[tile]
            gain = cw_ref[6:7, columns]
            sig = sigmoid(gate)
            act = gate * sig
            gated = ssd * act
            scaled = gated * scale
            branch_ref[tile] = (scaled * gain).astype(BF16)
            gain_ref[0:1, columns] += jnp.sum(d_branch * scaled, axis=0, keepdims=True)
            d_gated = scale * (gain * d_branch) - gated * cross
            dssd_ref[tile] = d_gated * act
            dgate_ref[tile] = (d_gated * ssd * (sig * (1.0 + gate * (1.0 - sig)))).astype(BF16)


def gating_back_call(inner, sums, gate, ssd_out, d_branch, conv_rows):
    rows, columns = gate.shape
    tokens = rows // 4
    block = pl.BlockSpec((tokens, columns), lambda b: (b, 0))
    order = [lambda b: (0, b)]
    order.append(lambda b: (0, b + 1 - 2 * lax.rem(b, 2)))
    order.append(lambda b: (0, lax.rem(b + 2, 4)))
    order.append(lambda b: (0, 3 - b))
    return pl.pallas_call(
        functools.partial(gating_back_kernel, inner),
        grid=(4,),
        in_specs=[pl.BlockSpec((8, tokens), index) for index in order]
        + [block, block, block, pl.BlockSpec((8, columns), lambda b: (0, 0))],
        out_specs=[block, block, block, pl.BlockSpec((8, columns), lambda b: (0, 0))],
        out_shape=[
            jax.ShapeDtypeStruct((rows, columns), BF16),
            jax.ShapeDtypeStruct((rows, columns), BF16),
            jax.ShapeDtypeStruct((rows, columns), F32),
            jax.ShapeDtypeStruct((8, columns), F32),
        ],
        compiler_params=pltpu.CompilerParams(vmem_limit_bytes=40 * 1024 * 1024),
        cost_estimate=pl.CostEstimate(
            flops=20 * rows * columns, bytes_accessed=20 * rows * columns, transcendentals=0
        ),
        name="gating_back",
    )(*sums, gate, ssd_out, d_branch, conv_rows)


def normalize_kernel(*refs):
    rows_refs, (gain_ref, normed_ref, scale_ref) = refs[:4], refs[4:]
    for at, rows_ref in enumerate(rows_refs):

        @pl.when(pl.program_id(0) == at)
        def _():
            depth = rows_ref.shape[1]
            for start in range(0, rows_ref.shape[0], 64):
                rows = rows_ref[start : start + 64, :].astype(F32)
                mean = jnp.sum(rows * rows, axis=1, keepdims=True) * (1.0 / depth)
                scale = lax.rsqrt(mean + EPS)
                normed = rows * scale * gain_ref[0:1, :]
                normed_ref[start : start + 64, :] = normed.astype(BF16)
                scale_ref[start : start + 64, :] = jnp.broadcast_to(scale, (64, LANES))


def normalize_call(blocks, gain):
    tokens, depth = blocks[0].shape
    return pl.pallas_call(
        normalize_kernel,
        grid=(4,),
        in_specs=[whole_spec(block) for block in blocks] + [whole_spec(gain)],
        out_specs=[
            pl.BlockSpec((tokens, depth), lambda b: (b, 0)),
            pl.BlockSpec((tokens, LANES), lambda b: (b, 0)),
        ],
        out_shape=[
            jax.ShapeDtypeStruct((4 * tokens, depth), BF16),
            jax.ShapeDtypeStruct((4 * tokens, LANES), F32),
        ],
        compiler_params=pltpu.CompilerParams(vmem_limit_bytes=40 * 1024 * 1024),
        name="normalize",
    )(*blocks, gain)


def weight_grad_kernel(links_shape, groups_of_terms, over_a, at_ref, *refs):
    sides, groups = links_shape
    count = sum(len(terms) for terms in groups_of_terms)
    left_count = 1 + max(left_at for terms in groups_of_terms for left_at, _ in terms)
    lefts, rights = refs[:left_count], refs[left_count : left_count + count]
    outs, scratch = refs[left_count + count : -1], refs[-1]
    at_column, at_term = 0, 0
    for terms in groups_of_terms:
        result = None
        for left_at, first_row in terms:
            right = rights[at_term][...]
            term = lax.dot_general(
                lefts[left_at][first_row : first_row + right.shape[0], :],
                right,
                (((0,), (0,)), ((), ())),
                preferred_element_type=F32,
            )
            result = term if result is None else result + term
            at_term += 1
        width = result.shape[1]
        scratch[:, at_column : at_column + width] = result.astype(BF16)
        at_column += width
    if over_a:
        chips, part = outs[0].shape[0], outs[0].shape[1]
        for chip in range(chips):
            for j, out in enumerate(outs):
                at = (chip * sides + lax.rem(at_ref[0] + j, sides)) * part
                out[chip] = scratch[pl.ds(pl.multiple_of(at, 16), part), :]
        return
    rows = outs[0].shape[0]
    chips = scratch.shape[0] // rows
    for chip in range(chips):
        turn = lax.rem(pl.program_id(0) * chips + chip + groups - at_ref[1], groups)
        for k, out in enumerate(outs):

            @pl.when(turn == k)
            def _():
                out[...] = scratch[chip * rows : (chip + 1) * rows, :]


def weight_grad_call(links_shape, over_a, place, groups_of_terms):
    sides, groups = links_shape
    terms = [term for group in groups_of_terms for term in group]
    depth = terms[0][0].shape[1]
    columns = sum(group[0][5] for group in groups_of_terms)
    rows = depth // groups
    part = rows // sides
    chips = 1
    while chips * rows % LANES:
        chips += 1
    lefts = []
    for term in terms:
        if not any(term[0] is left for left in lefts):
            lefts.append(term[0])

    def left_at(term):
        return [term[0] is left for left in lefts].index(True)

    def left_spec(left):
        return pl.BlockSpec((left.shape[0], chips * rows), lambda b: (0, b))

    def right_spec(term):
        return pl.BlockSpec((term[1], term[5]), lambda b: (term[4], term[6]))

    if over_a:
        out_specs = [pl.BlockSpec((chips, part, columns), lambda b: (b, 0, 0))] * sides
        out_shape = [jax.ShapeDtypeStruct((groups, part, columns), BF16)] * sides
    else:
        out_specs = [pl.BlockSpec((rows, columns), lambda b: (0, 0))] * groups
        out_shape = [jax.ShapeDtypeStruct((rows, columns), BF16)] * groups
    shapes = tuple(
        tuple((left_at(term), term[1] * term[2]) for term in group) for group in groups_of_terms
    )
    return pl.pallas_call(
        functools.partial(weight_grad_kernel, links_shape, shapes, over_a),
        grid=(groups // chips,),
        in_specs=[pl.BlockSpec(memory_space=pltpu.SMEM)]
        + [left_spec(left) for left in lefts]
        + [right_spec(term) for term in terms],
        out_specs=out_specs,
        out_shape=out_shape,
        scratch_shapes=[pltpu.VMEM((chips * rows, columns), BF16)],
        compiler_params=pltpu.CompilerParams(vmem_limit_bytes=48 * 1024 * 1024),
        cost_estimate=pl.CostEstimate(
            flops=2 * terms[0][1] * depth * columns,
            bytes_accessed=2 * terms[0][1] * depth,
            transcendentals=0,
        ),
        name="weight_grad",
    )(place, *lefts, *[term[3] for term in terms])


def combine_kernel(groups, at_ref, *refs):
    parts, outs = refs[:-groups], refs[-groups:]
    result = parts[0][0].astype(F32)
    for part in parts[1:]:
        result = result + part[0].astype(F32)
    turn = lax.rem(pl.program_id(0) + groups - at_ref[1], groups)
    for k, out in enumerate(outs):

        @pl.when(turn == k)
        def _():
            out[...] = result.astype(BF16)


def combine_call(groups, place, parts):
    rows, columns = parts[0].shape[1:]
    return pl.pallas_call(
        functools.partial(combine_kernel, groups),
        grid=(groups,),
        in_specs=[pl.BlockSpec(memory_space=pltpu.SMEM)]
        + [pl.BlockSpec((1, rows, columns), lambda b: (b, 0, 0))] * len(parts),
        out_specs=[pl.BlockSpec((rows, columns), lambda b: (0, 0))] * groups,
        out_shape=[jax.ShapeDtypeStruct((rows, columns), BF16)] * groups,
        compiler_params=pltpu.CompilerParams(vmem_limit_bytes=24 * 1024 * 1024),
        name="combine",
    )(place, *parts)


def forward_call(heads, size, lengths, conv_in, keys_queries, conv_rows, head_rows):
    blocks = lengths.shape[0]
    total = conv_in.shape[0]
    tokens = total // blocks
    width = heads * size
    state = keys_queries.shape[1] // 2
    boundaries = tokens // CHUNK - 1
    return pl.pallas_call(
        functools.partial(forward_kernel, heads, size),
        grid=(blocks,),
        in_specs=[
            pl.BlockSpec(memory_space=pltpu.SMEM),
            pl.BlockSpec((tokens, width), lambda b: (b, 0)),
            pl.BlockSpec((tokens, LANES), lambda b: (b, width // LANES)),
            pl.BlockSpec((tokens, 2 * state), lambda b: (b, 0)),
            pl.BlockSpec((8, width), lambda b: (0, 0)),
            pl.BlockSpec((8, LANES), lambda b: (0, 0)),
        ],
        out_specs=[
            pl.BlockSpec((tokens, width), lambda b: (b, 0)),
            pl.BlockSpec((1, boundaries, state, width), lambda b: (b, 0, 0, 0)),
        ],
        out_shape=[
            jax.ShapeDtypeStruct((total, width), F32),
            jax.ShapeDtypeStruct((blocks, boundaries, state, width), BF16),
        ],
        scratch_shapes=[pltpu.VMEM((state, width), F32)],
        compiler_params=pltpu.CompilerParams(vmem_limit_bytes=40 * 1024 * 1024),
        cost_estimate=pl.CostEstimate(
            flops=blocks * 3_000_000_000, bytes_accessed=blocks * 8_000_000, transcendentals=0
        ),
        name="ssd_forward",
    )(lengths, conv_in, conv_in, keys_queries, conv_rows, head_rows)


def backward_call(
    heads, size, first_head, first_block, blocks,
    lengths, conv_in, keys_queries, d_out, states, conv_rows, head_rows
):
    tokens = conv_in.shape[0] // lengths.shape[0]
    total = blocks * tokens
    width = heads * size
    part = first_head * size // width
    steps_at = d_out.shape[1] // LANES
    state = keys_queries.shape[1] // 2
    boundaries = tokens // CHUNK - 1

    def rows_of(columns, index):
        return pl.BlockSpec((tokens, columns), lambda b: (first_block + b, index))

    return pl.pallas_call(
        functools.partial(backward_kernel, heads, size, first_head, first_block),
        grid=(blocks,),
        in_specs=[
            pl.BlockSpec(memory_space=pltpu.SMEM),
            rows_of(width, part),
            rows_of(LANES, steps_at),
            rows_of(2 * state, 0),
            rows_of(width, part),
            pl.BlockSpec(
                (1, boundaries, state, width), lambda b: (first_block + b, 0, 0, part)
            ),
            pl.BlockSpec((8, width), lambda b: (0, part)),
            pl.BlockSpec((8, LANES), lambda b: (0, 0)),
        ],
        out_specs=[
            pl.BlockSpec((tokens, width), lambda b: (b, 0)),
            pl.BlockSpec((tokens, LANES), lambda b: (b, 0)),
            pl.BlockSpec((tokens, 2 * state), lambda b: (b, 0)),
            pl.BlockSpec((8, width), lambda b: (0, 0)),
            pl.BlockSpec((8, LANES), lambda b: (0, 0)),
        ],
        out_shape=[
            jax.ShapeDtypeStruct((total, width), BF16),
            jax.ShapeDtypeStruct((total, LANES), BF16),
            jax.ShapeDtypeStruct((total, 2 * state), F32),
            jax.ShapeDtypeStruct((8, width), F32),
            jax.ShapeDtypeStruct((8, LANES), F32),
        ],
        scratch_shapes=[
            pltpu.VMEM((state, width), F32),
            pltpu.VMEM((tokens + 8, width), F32),
            pltpu.VMEM((CHUNK, width), BF16),
            pltpu.VMEM((CHUNK, width), BF16),
        ],
        compiler_params=pltpu.CompilerParams(vmem_limit_bytes=48 * 1024 * 1024),
        cost_estimate=pl.CostEstimate(
            flops=blocks * heads * 1_000_000_000,
            bytes_accessed=blocks * 8_000_000,
            transcendentals=0,
        ),
        name="ssd_backward",
    )(lengths, conv_in, conv_in, keys_queries, d_out, states, conv_rows, head_rows)


def after(values):
    return lax.optimization_barrier(values)


def phase(sends, work=None, arguments=(), until=None):
    values, arguments = after(([value for _, value in sends], arguments))
    moved = [send(value) for (send, _), value in zip(sends, values)]
    done = work(*arguments) if work else ()
    moved, done, until = after((moved, done, until))
    return (moved, done) if until is None else (moved, done, until)


def total(first, others):
    result = first.astype(F32)
    for other in others:
        result = result + other.astype(F32)
    return result


class Links:
    def __init__(self, reps, shards):
        self.reps, self.shards = reps, shards
        self.sides, self.groups = reps // 2, shards // 2
        rep, shard = lax.axis_index("rep"), lax.axis_index("fsdp")
        self.rep, self.shard = rep, shard
        self.a, self.x = rep // 2, rep % 2
        self.g, self.c = shard // 2, shard % 2

    def send(self, value, target):
        pairs = []
        for r in range(self.reps):
            for f in range(self.shards):
                to_r, to_f = target(r, f)
                pairs.append((r * self.shards + f, to_r * self.shards + to_f))
        return lax.ppermute(value, ("rep", "fsdp"), pairs)

    def core(self, value):
        return self.send(value, lambda r, f: (r, f ^ 1))

    def side(self, value):
        return self.send(value, lambda r, f: (r ^ 1, f))

    def corner(self, value):
        return self.send(value, lambda r, f: (r ^ 1, f ^ 1))

    def along_a(self, value, by):
        return self.send(value, lambda r, f: (((r // 2 + by) % self.sides) * 2 + r % 2, f))

    def along_g(self, value, by):
        return self.send(value, lambda r, f: (r, ((f // 2 + by) % self.groups) * 2 + f % 2))

    def diagonal(self, value, by):
        return self.send(
            value, lambda r, f: (((r // 2 + by) % self.sides) * 2 + (r % 2 ^ 1), f)
        )

    def flip(self, value, bit_of_rep, bit_of_shard):
        return self.send(value, lambda r, f: (r ^ bit_of_rep, f ^ bit_of_shard))

    def round_g(self, piece):
        return [self.along_g(piece, k) for k in range(1, self.groups)]

    def piece_of(self, mine, from_core):
        if self.sides == 2:
            return jnp.where(self.a == self.c, mine, from_core)
        is_high = self.c == 1
        chip = jnp.concatenate(
            [jnp.where(is_high, from_core, mine), jnp.where(is_high, mine, from_core)], axis=0
        )
        part = chip.shape[0] // self.sides
        return lax.dynamic_slice_in_dim(chip, self.a * part, part, 0)

    def round_a(self, joined):
        return [self.along_a(joined, j) for j in range(1, self.sides)]

    def assemble(self, mine, from_core, joined, rounds):
        rows, columns = mine.shape
        part = 2 * rows // self.sides
        whole = jnp.zeros((rows * self.shards, columns), mine.dtype)
        base = self.g * 2 * rows
        whole = lax.dynamic_update_slice_in_dim(whole, mine, base + self.c * rows, 0)
        whole = lax.dynamic_update_slice_in_dim(whole, from_core, base + (1 - self.c) * rows, 0)
        for k in range(1, self.groups):
            base = ((self.g - k) % self.groups) * 2 * rows
            for j, pieces in enumerate([joined] + rounds):
                piece = pieces[(k - 1) * part : k * part]
                at = base + ((self.a - j) % self.sides) * part
                whole = lax.dynamic_update_slice_in_dim(whole, piece, at, 0)
        return whole

    def parts_for_a(self, view):
        axis = view.ndim - 3
        mine = lax.dynamic_index_in_dim(view, self.a, axis, keepdims=False)
        others = [
            lax.dynamic_index_in_dim(view, (self.a + j) % self.sides, axis, keepdims=False)
            for j in range(1, self.sides)
        ]
        return mine, others

    def parts_for_g(self, view):
        mine = lax.dynamic_index_in_dim(view, self.g, 0, keepdims=False)
        others = [
            lax.dynamic_index_in_dim(view, (self.g + k) % self.groups, 0, keepdims=False)
            for k in range(1, self.groups)
        ]
        return mine, others

    def send_a(self, others):
        return [self.along_a(part, j + 1) for j, part in enumerate(others)]

    def send_g(self, others):
        return [self.along_g(part, k + 1) for k, part in enumerate(others)]

    def chips_of(self, partial):
        rows = partial.shape[0] // (self.groups * self.sides)
        return partial.reshape(self.groups, self.sides, rows, partial.shape[1])

    def spread_a(self, piece):
        return [self.along_a(piece, j) for j in range(1, self.sides)]

    def join_a(self, piece, others):
        if self.sides == 2:
            is_high = self.a == 1
            return jnp.concatenate(
                [jnp.where(is_high, others[0], piece), jnp.where(is_high, piece, others[0])],
                axis=0,
            )
        part = piece.shape[0]
        chip = jnp.zeros((part * self.sides, piece.shape[1]), piece.dtype)
        for j, value in enumerate([piece] + others):
            at = ((self.a - j) % self.sides) * part
            chip = lax.dynamic_update_slice_in_dim(chip, value, at, 0)
        return chip

    def join_x(self, piece, other):
        is_far = self.x == 1
        return jnp.concatenate(
            [jnp.where(is_far, other, piece), jnp.where(is_far, piece, other)], axis=1
        )

    def rows_of_core(self, chip):
        rows = chip.shape[0] // 2
        is_high = self.c == 1
        mine = jnp.where(is_high, chip[rows:], chip[:rows])
        return mine, jnp.where(is_high, chip[:rows], chip[rows:])

    def shares(self, mine, from_core):
        columns = mine.shape[1] // 2
        is_high = self.c == 1
        low = jnp.where(is_high, from_core, mine)
        high = jnp.where(is_high, mine, from_core)
        return [low[:, :columns], high[:, :columns], low[:, columns:], high[:, columns:]]

    def sum_all(self, value):
        bit = 1
        while bit < self.shards:
            value = value + self.flip(value, 0, bit)
            bit *= 2
        bit = 1
        while bit < self.reps:
            value = value + self.flip(value, bit, 0)
            bit *= 2
        return value

    def group_blocks(self, value):
        far = self.side(value)
        return [value, self.core(value), far, self.core(far)]

    def core_sum(self, partials, link_type):
        tokens = partials.shape[0] // 2
        return partials[:tokens].astype(F32) + self.core(
            partials[tokens:].astype(link_type)
        ).astype(F32)


def shift_rows(values, by):
    zeros = jnp.zeros((values.shape[0], abs(by), values.shape[2]), values.dtype)
    if by > 0:
        return jnp.concatenate([zeros, values[:, :-by]], axis=1)
    return jnp.concatenate([values[:, -by:], zeros], axis=1)


def causal_conv(inputs, begin, taps, bias):
    position = jnp.arange(inputs.shape[1], dtype=jnp.int32)[None, :]
    result = bias + taps[3] * inputs
    shifted = [inputs]
    for delay in range(1, 4):
        inside = (position - delay >= begin)[..., None]
        shifted.append(jnp.where(inside, shift_rows(inputs, delay), 0.0))
        result = result + taps[3 - delay] * shifted[delay]
    return result, shifted


def causal_conv_back(d_result, begin, taps):
    position = jnp.arange(d_result.shape[1], dtype=jnp.int32)[None, :]
    d_inputs = taps[3] * d_result
    for delay in range(1, 4):
        inside = (position - delay >= begin)[..., None]
        moved = shift_rows(jnp.where(inside, d_result, 0.0), -delay)
        d_inputs = d_inputs + taps[3 - delay] * moved
    return d_inputs


def per_device(
    reps,
    shards,
    hidden_in,
    lengths,
    norm_gain,
    in_weight,
    conv_weight,
    conv_bias,
    dt_bias,
    a_log,
    skip_gain,
    gate_gain,
    out_weight,
    cotangent,
):
    links = Links(reps, shards)
    tokens, depth = hidden_in.shape
    inner = gate_gain.shape[0] * shards
    channels = conv_bias.shape[0] * shards
    all_heads = dt_bias.shape[0] * shards
    state = (channels - inner) // 2
    size = inner // all_heads
    heads, width = all_heads // 4, inner // 4
    x, c = links.x, links.c
    p = 2 * x + c

    is_high, is_far = c == 1, x == 1
    far_hidden = links.side(hidden_in)
    ends = jnp.cumsum(lengths[0])
    positions = jnp.arange(tokens, dtype=jnp.int32)
    is_valid = (positions < ends[1])[:, None]
    back_own = jnp.where(is_valid, cotangent, jnp.zeros_like(cotangent))
    sides, groups = links.sides, links.groups
    links_shape = (sides, groups)
    place = jnp.stack([links.a, links.g, c]).astype(jnp.int32)

    lanes = max(conv_weight.shape[1], gate_gain.shape[0], norm_gain.shape[0], 3 * LANES)
    lanes = -(-lanes // LANES) * LANES

    def pack(conv_weight, conv_bias, gate_gain, norm_gain, *head_values):
        heads_row = jnp.concatenate(
            [jnp.pad(v, (0, LANES - v.shape[0])) for v in head_values]
        )
        rows = [conv_bias, gate_gain, norm_gain, heads_row[:lanes]]
        rows = [jnp.pad(row, (0, lanes - row.shape[0]))[None] for row in rows]
        taps_rows = jnp.pad(conv_weight, ((0, 0), (0, lanes - conv_weight.shape[1])))
        return jnp.concatenate([taps_rows, *rows], axis=0)

    small_in = (conv_weight, conv_bias, gate_gain, norm_gain, dt_bias, a_log, skip_gain)
    sizes = (conv_bias.shape[0], gate_gain.shape[0], norm_gain.shape[0], dt_bias.shape[0])

    first_columns, last_columns = width + LANES + state, 2 * width
    core_place = jnp.stack([x, c]).astype(jnp.int32)
    mine_a, for_core_a = prepare_call(
        functools.partial(prepare_first_kernel, heads, size, state),
        first_columns,
        core_place,
        in_weight,
    )

    def hops(pieces, stage):
        sends = [(stage, 1, pieces[stage - 1])]
        if groups - stage != stage:
            sends.append((groups - stage, groups - 1, pieces[(groups - stage + 1) % groups]))
        return sends

    def hop_sends(pieces, stage):
        return [
            ((lambda value, by=by: links.along_g(value, by)), value)
            for _, by, value in hops(pieces, stage)
        ]

    def landed(pieces, stage, values):
        at = [k for k, _, _ in hops(pieces, stage)]
        return {**pieces, **dict(zip(at, values))}

    def rounds(piece):
        return [(lambda value, j=j: links.along_a(value, j), piece) for j in range(1, sides)]

    def doubled(value, bit, other):
        upper = (links.shard // bit) % 2 == 1
        return jnp.concatenate(
            [jnp.where(upper, other, value), jnp.where(upper, value, other)], axis=0
        )

    def swap(bit):
        return lambda value: links.flip(value, 0, bit)

    (from_core_a,), packed = phase([(links.core, for_core_a)], pack, small_in)
    pieces_a = {0: links.piece_of(mine_a, from_core_a)}

    def prepare_last(packed, in_weight, out_weight):
        small_pair = doubled(packed, 1, links.core(packed))
        small_four = doubled(small_pair, 2, links.flip(small_pair, 0, 2))
        kernel = functools.partial(prepare_last_kernel, width)
        last = prepare_call(kernel, last_columns, core_place, in_weight, out_weight)
        return small_four, last

    moved, (small_all, (mine_b, for_core_b)) = phase(
        hop_sends(pieces_a, 1) + [(links.core, lengths)],
        prepare_last,
        (packed, in_weight, out_weight),
    )
    lengths_core = moved[-1]
    pieces_a = landed(pieces_a, 1, moved[:-1])
    y_a = {}
    firsts = [k for k in pieces_a if k]
    sends = [send for k in firsts for send in rounds(pieces_a[k])]
    moved, _ = phase(
        hop_sends(pieces_a, 2) + [(swap(4), small_all), (links.core, for_core_b)] + sends
    )
    for at, k in enumerate(reversed(firsts)):
        stop = len(moved) - at * (sides - 1)
        y_a[k] = moved[stop - (sides - 1) : stop]
    hop_count = len(hops(pieces_a, 2))
    small_all = doubled(small_all, 4, moved[hop_count])
    from_core_b = moved[hop_count + 1]
    pieces_b = {0: links.piece_of(mine_b, from_core_b)}
    pieces_a = landed(pieces_a, 2, moved[:hop_count])
    bit = 8
    while bit < shards:
        small_all = doubled(small_all, bit, links.flip(small_all, 0, bit))
        bit *= 2
    for stage in range(3, groups // 2 + 1):
        values = [send(value) for send, value in hop_sends(pieces_a, stage)]
        pieces_a = landed(pieces_a, stage, values)
    pieces_a, pieces_b, far_hidden = after((pieces_a, pieces_b, far_hidden))
    rest = [k for k in pieces_a if k and k not in y_a]
    b_firsts = [send(value) for send, value in hop_sends(pieces_b, 1)]
    sends = [send for k in rest for send in rounds(pieces_a[k])]
    moved, parameters_here = phase(
        sends + [(links.core, hidden_in), (links.core, far_hidden)],
        functools.partial(unpack_call, sizes, heads, size, state, core_place),
        (small_all,),
    )
    core_hidden, far_core_hidden = moved[-2:]
    for at, k in enumerate(rest):
        y_a[k] = moved[at * (sides - 1) : (at + 1) * (sides - 1)]
    n_rows, conv_rows, head_rows, kq_rows = parameters_here
    n_gain = n_rows[0]

    def parts_of(mine, from_core, pieces, rounds_of):
        parts = [mine, from_core]
        for k in range(1, groups):
            parts += [pieces[k], *rounds_of[k]]
        return parts

    parts_a = parts_of(mine_a, from_core_a, pieces_a, y_a)
    pair_lengths = jnp.concatenate([lengths, lengths_core], axis=0)
    pair_ends = jnp.cumsum(pair_lengths, axis=1)
    position = positions[None, :]
    begin = jnp.where(
        position >= pair_ends[:, 1:],
        pair_ends[:, 1:],
        jnp.where(position >= pair_ends[:, :1], pair_ends[:, :1], 0),
    )
    kq_columns = inner + c * state
    kq_taps, kq_bias = kq_rows[:4], kq_rows[4]
    normed, scale = normalize_call([hidden_in, core_hidden, far_hidden, far_core_hidden], n_rows)
    scale_own = scale[:tokens, :1]
    kq_index = (width + LANES) // state
    w_kq, kq_in = project_call(links_shape, state, kq_index, 2, tokens, place, parts_a, normed)
    kq_pre, kq_shifted = causal_conv(kq_in.reshape(2, tokens, state), begin, kq_taps, kq_bias)
    counts = jnp.stack([pair_lengths // 32, pair_lengths % 32], axis=2).reshape(2, 4).astype(BF16)
    counts = jnp.pad(counts, ((0, 14), (0, state - 4)))
    kq_near = jax.nn.silu(kq_pre).astype(BF16).reshape(2 * tokens, state)
    moved, (w_values, conv_in), b_firsts = phase(
        [(links.side, jnp.concatenate([kq_near, counts], axis=0))],
        functools.partial(project_call, links_shape, width + LANES, 0, 4, tokens, place),
        (parts_a, normed),
        b_firsts,
    )
    pieces_b = landed(pieces_b, 1, b_firsts)
    kq_far = moved[0]
    all_counts = jnp.concatenate([counts[:2, :4], kq_far[2 * tokens : 2 * tokens + 2, :4]], axis=0)
    all_counts = all_counts.astype(jnp.int32)
    all_lengths = all_counts[:, 0::2] * 32 + all_counts[:, 1::2]
    kq_half = jnp.concatenate([kq_near, kq_far[: 2 * tokens]], axis=0)

    kq_half, pieces_b, back_own = after((kq_half, pieces_b, back_own))
    firsts = [k for k in pieces_b if k]
    b_seconds = [send(value) for send, value in hop_sends(pieces_b, 2)]
    y_firsts = [[send(value) for send, value in rounds(pieces_b[k])] for k in firsts]
    (kq_core,), _ = phase([(links.core, kq_half)])
    kq_core = kq_core.reshape(2, 2, tokens, state)[:, ::-1].reshape(4 * tokens, state)
    keys_queries = jnp.concatenate(
        [jnp.where(is_high, kq_core, kq_half), jnp.where(is_high, kq_half, kq_core)], axis=1
    )
    cuts = [slice(0, tokens // 2), slice(tokens // 2, tokens)]
    moved, (ssd_out, states), (b_seconds, y_firsts) = phase(
        [(links.side, back_own[cuts[0]])],
        functools.partial(forward_call, heads, size),
        (all_lengths, conv_in, keys_queries, conv_rows, head_rows),
        (b_seconds, y_firsts),
    )
    far_back = [moved[0]]
    y_b = dict(zip(firsts, y_firsts))
    pieces_b = landed(pieces_b, 2, b_seconds)
    for stage in range(3, groups // 2 + 1):
        values = [send(value) for send, value in hop_sends(pieces_b, stage)]
        pieces_b = landed(pieces_b, stage, values)
    rest = [k for k in pieces_b if k and k not in y_b]
    gate_sends = [send for k in rest for send in rounds(pieces_b[k][:, :width])]
    out_sends = [send for k in rest for send in rounds(pieces_b[k][:, width:])]
    moved, _ = phase(
        gate_sends
        + [(links.core, back_own), (links.side, back_own[cuts[1]]), (links.core, far_back[0])]
    )
    core_back = moved[-3]
    far_back.append(moved[-2])
    far_core_back = [moved[-1]]
    moved = moved[:-3]

    def last_parts(values):
        latest = {k: values[at * (sides - 1) : (at + 1) * (sides - 1)] for at, k in enumerate(rest)}
        return parts_of(mine_b, from_core_b, pieces_b, {**y_b, **latest})

    moved, (w_gate, gate) = phase(
        out_sends + [(links.core, far_back[1])],
        functools.partial(project_call, links_shape, width, 0, 4, tokens, place),
        (last_parts(moved), normed),
    )
    far_core_back.append(moved[-1])
    moved = moved[:-1]
    back_blocks = [
        back_own,
        core_back,
        jnp.concatenate(far_back, axis=0),
        jnp.concatenate(far_core_back, axis=0),
    ]
    w_out, d_branch, sums = branch_back_call(
        links_shape, width, 1, place, last_parts(moved), back_blocks, gate, ssd_out, conv_rows
    )
    moved, _ = phase([(links.core, sums), (links.side, sums), (links.corner, sums)])
    branch, d_gate, d_ssd, gain_rows = gating_back_call(
        inner, [sums, *moved], gate, ssd_out, d_branch, conv_rows
    )
    grad_gate_gain = gain_rows[0]

    by_g = width // (3 * LANES) * 2 * LANES
    most = heads // 3 * 2
    less = heads - most
    most_width, less_width = most * size, less * size
    rows_all = 4 * tokens

    def backward(first_head, count, first_block, blocks, d_out):
        return backward_call(
            count, size, first_head, first_block, blocks,
            all_lengths, conv_in, keys_queries, d_out, states, conv_rows, head_rows,
        )

    def turn(k):
        return lambda value: links.along_g(value, k)

    def a_sends(parts):
        return [
            (lambda value, j=j: links.along_a(value, j + 1), part) for j, part in enumerate(parts)
        ]

    def g_sends(parts):
        return [(turn(k + 1), part) for k, part in enumerate(parts)]

    def start(sends):
        return [send(value) for send, value in sends]

    count_a, count_g = sides - 1, groups - 1
    mixed_parts = dot_nt(branch, w_out).astype(BF16).reshape(2, 2, tokens, depth)
    mixed_keep, mixed_send = mixed_parts[:, 0], mixed_parts[:, 1]

    def first_grads(normed, d_gate, back_blocks, branch):
        def out_terms(columns, index):
            return [
                (block, tokens, 0, branch, at, columns, index)
                for at, block in enumerate(back_blocks)
            ]

        first = weight_grad_call(
            links_shape, True, place,
            [
                [(normed, rows_all, 0, d_gate, 0, width, 0)],
                out_terms(width - by_g, by_g // (width - by_g)),
            ],
        )
        return first, weight_grad_call(links_shape, False, place, [out_terms(by_g, 0)])

    moved, (first_parts, out_parts) = phase(
        [(links.core, mixed_send)], first_grads, (normed, d_gate, back_blocks, branch)
    )
    mixed_sum = mixed_keep.astype(F32) + moved[0].astype(F32)
    moved, (d_in_0, d_steps_0, d_kq_0, conv_grads_0, head_grads_0) = phase(
        a_sends(first_parts[1:])
        + g_sends(out_parts[1:])
        + [(links.side, mixed_sum[1].astype(BF16))],
        functools.partial(backward, 0, most, 0, 4),
        (d_ssd,),
    )
    mixed = hidden_in.astype(F32) + mixed_sum[0] + moved[-1].astype(F32)
    mixed = jnp.where(is_valid, mixed, 0.0).astype(BF16)
    first_held = combine_call(groups, place, [first_parts[0], *moved[:count_a]])
    values_0 = weight_grad_call(
        links_shape, True, place, [[(normed, rows_all, 0, d_in_0, 0, most_width, 0)]]
    )
    out_chip = total(out_parts[0], moved[count_a:-1]).astype(BF16)
    out_mine, out_others = links.parts_for_a(out_chip.reshape(sides, -1, by_g))
    first_held, values_0, d_ssd, mixed, out_mine, out_others = after(
        (first_held, values_0, d_ssd, mixed, out_mine, out_others)
    )
    first_sends = g_sends(first_held[1:])
    first_sends = first_sends[:1] + first_sends[-1:] + first_sends[1:-1]

    def back_project(first_row, d_in_1, d_steps):
        rows = slice(first_row, first_row + 2 * tokens)
        d_rest = jnp.concatenate([d_in_0[rows], d_in_1, d_steps], axis=1)
        return dot_nt(d_gate[rows], w_gate) + dot_nt(d_rest, w_values)

    def far_work(d_ssd):
        results = backward(most, less, 2, 2, d_ssd)
        d_steps = d_steps_0[2 * tokens :] + results[1]
        return results, d_steps, back_project(2 * tokens, results[0], d_steps).astype(BF16)

    moved, (results, d_steps_far, d_far_parts) = phase(
        a_sends(values_0[1:]) + first_sends[:2], far_work, (d_ssd,)
    )
    first_far = moved[count_a:]
    d_in_far, _, d_kq_far, conv_grads_far, head_grads_far = results
    held_0 = combine_call(groups, place, [values_0[0], *moved[:count_a]])
    held_sends = g_sends(held_0[1:])
    held_sends = held_sends[:1] + held_sends[-1:] + held_sends[1:-1]

    def halves(first_rows, second_rows):
        rows = (first_rows + second_rows).reshape(2, tokens, 2 * state)
        mine = jnp.where(is_high, rows[..., state:], rows[..., :state])
        other = jnp.where(is_high, rows[..., :state], rows[..., state:])
        return mine, other[::-1].astype(BF16)

    kq_far_mine, kq_far_core = halves(d_kq_0[2 * tokens :], d_kq_far)
    moved, _ = phase([(links.core, kq_far_core), (links.core, d_far_parts[tokens:])])
    kq_far_sum = (kq_far_mine + moved[0].astype(F32)).astype(BF16)
    d_far = (d_far_parts[:tokens].astype(F32) + moved[1].astype(F32)).astype(BF16)
    moved, results = phase(
        [(links.side, kq_far_sum)]
        + first_sends[2:]
        + [(links.side, d_far[cuts[0]])]
        + a_sends(out_others),
        functools.partial(backward, most, less, 0, 2),
        (d_ssd,),
    )
    d_in_near, d_steps_near, d_kq_near, conv_grads_near, head_grads_near = results
    kq_from_side = moved[0]
    first_far = first_far + moved[1 : count_g - 1]
    far_d = [moved[count_g - 1]]
    out_piece = total(out_mine, moved[count_g:]).astype(BF16)
    first_piece = total(first_held[0], first_far).astype(BF16)
    first_piece = jnp.concatenate([first_piece, out_piece], axis=1)
    kq_near_mine, kq_near_core = halves(d_kq_0[: 2 * tokens], d_kq_near)

    d_steps_near = d_steps_0[: 2 * tokens] + d_steps_near
    d_steps = jnp.concatenate([d_steps_near, d_steps_far], axis=0)
    moved, d_near = phase(
        [(links.core, kq_near_core)] + held_sends[:1],
        functools.partial(back_project, 0),
        (d_in_near, d_steps_near),
    )
    held_far = moved[1:]
    d_kq = kq_near_mine + moved[0].astype(F32) + kq_from_side.astype(F32)
    kq_sig = sigmoid(kq_pre)
    d_kq_pre = d_kq * (kq_sig * (1.0 + kq_pre * (1.0 - kq_sig)))
    d_kq_in = causal_conv_back(d_kq_pre, begin, kq_taps).astype(BF16).reshape(2 * tokens, state)
    half_rows = 2 * tokens

    def last_grads(normed, d_in_near, d_in_far, d_steps, d_kq_in):
        last = weight_grad_call(
            links_shape, True, place,
            [
                [
                    (normed, half_rows, 0, d_in_near, 0, less_width, 0),
                    (normed, half_rows, 1, d_in_far, 0, less_width, 0),
                ],
                [
                    (normed, half_rows, 0, d_steps, 0, LANES, 0),
                    (normed, half_rows, 1, d_steps, 1, LANES, 0),
                ],
                [(normed, half_rows, 0, d_kq_in, 0, state, 0)],
            ],
        )
        return last, dot_nt(d_kq_in, w_kq)

    moved, (last_parts_here, kq_part) = phase(
        rounds(first_piece) + held_sends[1:],
        last_grads,
        (normed, d_in_near, d_in_far, d_steps, d_kq_in),
    )
    first_y = moved[:count_a]
    held_far = held_far + moved[count_a:]
    held_piece = total(held_0[0], held_far).astype(BF16)
    first_rows = links.rows_of_core(links.join_a(first_piece, first_y))
    d_near = d_near + kq_part
    d_near_keep, d_near_send = d_near[:tokens], d_near[tokens:].astype(BF16)

    conv_grads = jnp.concatenate([conv_grads_0, conv_grads_far + conv_grads_near], axis=1)
    head_grads = head_grads_0 + head_grads_far + head_grads_near
    d_kq_rows = [jnp.sum(kq_shifted[delay] * d_kq_pre, axis=(0, 1)) for delay in (3, 2, 1, 0)]
    d_kq_rows = jnp.stack(d_kq_rows + [jnp.sum(d_kq_pre, axis=(0, 1))])
    small = jnp.zeros((8, channels), F32)
    small = lax.dynamic_update_slice(small, conv_grads[:5], (0, p * width))
    small = lax.dynamic_update_slice(small, d_kq_rows, (0, kq_columns))
    small = lax.dynamic_update_slice(small, grad_gate_gain[None], (5, p * width))
    grad_skip = conv_grads[5].reshape(heads, size).sum(axis=1)
    head_all = jnp.stack([head_grads[0, :heads], head_grads[1, :heads], grad_skip])
    small_heads = jnp.zeros((3, all_heads), F32)
    small_heads = lax.dynamic_update_slice(small_heads, head_all, (0, p * heads))
    small = lax.dynamic_update_slice(small, small_heads.reshape(1, -1), (7, 0))

    moved, _ = phase(
        a_sends(last_parts_here[1:])
        + [(links.side, d_far[cuts[1]]), (links.core, d_near_send), (links.core, small)]
        + [(links.core, first_rows[1])]
    )
    far_d.append(moved[count_a])
    d_near = d_near_keep + moved[count_a + 1].astype(F32)
    small = small + moved[count_a + 2]
    first_mine, first_core = first_rows[0], moved[-1]
    first_both = jnp.concatenate(
        [jnp.where(is_high, first_core, first_mine), jnp.where(is_high, first_mine, first_core)],
        axis=1,
    )
    last_held = combine_call(groups, place, [last_parts_here[0], *moved[:count_a]])
    first_half = first_both.shape[1] // 2
    moved, _ = phase(
        g_sends(last_held[1:])
        + [(links.side, first_both[:, :first_half])]
        + rounds(held_piece)
    )
    first_other = [moved[count_g]]
    last_piece = total(last_held[0], moved[:count_g]).astype(BF16)
    held_rows = links.rows_of_core(links.join_a(held_piece, moved[count_g + 1 :]))

    def final_norm(d_near, far_d):
        d_normed = d_near + far_d.astype(F32)
        own_hidden, own_scale = hidden_in.astype(F32), scale_own
        weighted = n_gain * d_normed
        inner_mean = jnp.mean(own_hidden * weighted, axis=-1, keepdims=True)
        return (
            back_own.astype(F32)
            + own_scale * weighted
            - own_hidden * (own_scale * own_scale * own_scale * inner_mean)
        )

    diagonals = [(lambda value, j=j: links.diagonal(value, j), last_piece) for j in range(1, sides)]
    moved, _ = phase(
        rounds(last_piece)
        + [(links.side, last_piece), (links.core, held_rows[1]), (swap(2), small)]
        + diagonals
    )
    same_x = links.join_a(last_piece, moved[:count_a])
    held_core, small = moved[count_a + 1], small + moved[count_a + 2]
    other_x = links.join_a(moved[count_a], moved[count_a + 3 :])
    at_kq = less_width + LANES
    kq_both = same_x[:, at_kq:].astype(F32) + other_x[:, at_kq:].astype(F32)
    last_rows = links.rows_of_core(
        jnp.concatenate(
            [
                jnp.where(is_far, other_x, same_x)[:, :at_kq],
                jnp.where(is_far, same_x, other_x)[:, :at_kq],
                kq_both.astype(BF16),
            ],
            axis=1,
        )
    )
    held_both = jnp.concatenate(
        [jnp.where(is_high, held_core, held_rows[0]), jnp.where(is_high, held_rows[0], held_core)],
        axis=1,
    )
    moved, grad_hidden = phase(
        [(links.side, first_both[:, first_half:]), (links.side, held_both)]
        + [(links.core, last_rows[1]), (swap(4), small)],
        final_norm,
        (d_near, jnp.concatenate(far_d, axis=0)),
    )
    small = small + moved[3]
    bit = 8
    while bit < shards:
        small = small + links.flip(small, 0, bit)
        bit *= 2
    first_other = jnp.concatenate([first_other[0], moved[0]], axis=1)
    held_other, last_core = moved[1], moved[2]
    first_low = jnp.where(is_far, first_other, first_both)
    first_high = jnp.where(is_far, first_both, first_other)
    held_low = jnp.where(is_far, held_other, held_both)
    held_high = jnp.where(is_far, held_both, held_other)
    low = jnp.where(is_high, last_core, last_rows[0])
    high = jnp.where(is_high, last_rows[0], last_core)
    first_width = width + (width - by_g) + by_g
    first_shares = [
        first_low[:, :first_width], first_low[:, first_width:],
        first_high[:, :first_width], first_high[:, first_width:],
    ]
    held_shares = [
        held_low[:, :most_width], held_low[:, most_width:],
        held_high[:, :most_width], held_high[:, most_width:],
    ]
    last_shares = [
        low[:, :at_kq], high[:, :at_kq], low[:, at_kq : 2 * at_kq], high[:, at_kq : 2 * at_kq]
    ]
    kq_shares = [low[:, 2 * at_kq :], high[:, 2 * at_kq :]]
    moved, _ = phase(
        [(links.side, small)]
        + rounds(small)
        + [(lambda value, j=j: links.diagonal(value, j), small) for j in range(1, sides)]
    )
    small = total(small, moved)

    def own_slice(array, count):
        return lax.dynamic_slice_in_dim(array, links.shard * count, count, array.ndim - 1)

    grad_conv = own_slice(small[:5], channels // shards)
    grad_heads = own_slice(small[7, : 3 * all_heads].reshape(3, all_heads), all_heads // shards)

    grad_in = jnp.concatenate(
        [share[:, :width] for share in first_shares]
        + [part for pair in zip(held_shares, last_shares) for part in (pair[0], pair[1][:, :less_width])]
        + kq_shares
        + [share[:, less_width : less_width + heads] for share in last_shares],
        axis=1,
    ).astype(F32)
    out_shares = [
        part
        for share in first_shares
        for part in (share[:, 2 * width - by_g :], share[:, width : 2 * width - by_g])
    ]
    grad_norm = jnp.sum(grad_in * in_weight.astype(F32), axis=1) / norm_gain.astype(F32)
    grad_out = jnp.concatenate(out_shares, axis=1).astype(F32).T
    return (
        mixed,
        grad_hidden,
        grad_norm,
        grad_in,
        grad_conv[:4],
        grad_conv[4],
        grad_heads[0],
        grad_heads[1],
        grad_heads[2],
        own_slice(small[5, :inner], inner // shards),
        grad_out,
    )


def solution(mesh):
    return jax.shard_map(
        functools.partial(per_device, mesh.shape["rep"], mesh.shape["fsdp"]),
        mesh=mesh,
        in_specs=(
            P(("rep", "fsdp"), None),
            P(("rep", "fsdp"), None),
            P("fsdp"),
            P("fsdp", None),
            P(None, "fsdp"),
            P("fsdp"),
            P("fsdp"),
            P("fsdp"),
            P("fsdp"),
            P("fsdp"),
            P(None, "fsdp"),
            P(("rep", "fsdp"), None),
        ),
        out_specs=(
            P(("rep", "fsdp"), None),
            P(("rep", "fsdp"), None),
            P("fsdp"),
            P("fsdp", None),
            P(None, "fsdp"),
            P("fsdp"),
            P("fsdp"),
            P("fsdp"),
            P("fsdp"),
            P("fsdp"),
            P(None, "fsdp"),
        ),
        check_vma=False,
    )
```

```python
import functools

import jax
import jax.numpy as jnp
from jax import lax
from jax.experimental import pallas as pl
from jax.experimental.pallas import tpu as pltpu
from jax.sharding import PartitionSpec as P

EPS = 1e-05
CHUNK = 128
LANES = 128
HIGHEST = lax.Precision.HIGHEST
F32 = jnp.float32
BF16 = jnp.bfloat16


def dot(left, right, precision=None):
    return lax.dot_general(
        left, right, (((1,), (0,)), ((), ())), precision=precision, preferred_element_type=F32
    )


def dot_nt(left, right):
    return lax.dot_general(left, right, (((1,), (1,)), ((), ())), preferred_element_type=F32)


def sigmoid(v):
    return 0.5 * jnp.tanh(0.5 * v) + 0.5


def softplus(v):
    return jnp.maximum(v, 0.0) + jnp.log1p(jnp.exp(-jnp.abs(v)))


def begin_of(position, first, both):
    return jnp.where(position >= both, both, jnp.where(position >= first, first, 0))


def iotas(rows, columns):
    return (
        lax.broadcasted_iota(jnp.int32, (rows, columns), 0),
        lax.broadcasted_iota(jnp.int32, (rows, columns), 1),
    )


def conv_tile(u_ref, cw_ref, start, columns, masks):
    inputs = [u_ref[start : start + CHUNK, columns]]
    for delay in range(1, 4):
        if start:
            shifted = u_ref[start - delay : start - delay + CHUNK, columns]
        else:
            shifted = pltpu.roll(inputs[0], delay, 0)
        inputs.append(jnp.where(masks[delay - 1], shifted, 0.0))
    pre = cw_ref[4:5, columns] + cw_ref[3:4, columns] * inputs[0]
    for delay in range(1, 4):
        pre = pre + cw_ref[3 - delay : 4 - delay, columns] * inputs[delay]
    return pre


def chunk_rates(dt_ref, hp_ref, start):
    raw = dt_ref[start : start + CHUNK, :] + hp_ref[0:1, :]
    step = softplus(raw)
    rate = -jnp.exp(hp_ref[1:2, :]) * step
    row, column = iotas(CHUNK, CHUNK)
    running = dot((row >= column).astype(F32), rate, HIGHEST)
    return raw, step, rate, running


def pair_of(low, matrix, head):
    return jnp.where(low, matrix[:, head : head + 1], matrix[:, head + 1 : head + 2])


def forward_kernel(heads, size, first_block, len_ref, u_ref, dt_ref, kq_ref, cw_ref, hp_ref, *refs):
    y_ref, st_ref, pre_ref, state = refs[-4:]
    block = first_block + pl.program_id(0)
    first = len_ref[block, 0]
    both = first + len_ref[block, 1]
    tokens = u_ref.shape[0]
    chunks = tokens // CHUNK
    row, column = iotas(CHUNK, CHUNK)
    low = column < size
    low_row = low[0:1, :]
    for ci in range(chunks):
        start = ci * CHUNK
        position = row + start
        begin = begin_of(position, first, both)
        masks = [position - delay >= begin for delay in range(1, 4)]
        raw, step, rate, running = chunk_rates(dt_ref, hp_ref, start)
        running_t = running.T
        keys = kq_ref[start : start + CHUNK, :LANES]
        queries = kq_ref[start : start + CHUNK, LANES:]
        keys_t = keys.astype(F32).T.astype(BF16)
        allowed = (column <= row) & (column + start >= begin)
        scores = jnp.where(allowed, dot_nt(queries, keys), 0.0)
        last_begin = begin_of(start + CHUNK - 1, first, both)
        source = position >= last_begin
        reached = begin < start
        ending = running[CHUNK - 1 : CHUNK, :]
        kept = jnp.where(last_begin < start, jnp.exp(ending), 0.0)
        for pair in range(heads // 2):
            h = 2 * pair
            columns = slice(pair * LANES, (pair + 1) * LANES)
            pre = conv_tile(u_ref, cw_ref, start, columns, masks)
            pre_ref[start : start + CHUNK, columns] = pre
            values = pre * sigmoid(pre)
            scaled = values * pair_of(low, step, h)
            weights = []
            for head in (h, h + 1):
                gap = running[:, head : head + 1] - running_t[head : head + 1, :]
                weights.append((scores * jnp.exp(jnp.minimum(gap, 0.0))).astype(BF16))
            stacked = jnp.concatenate(
                [jnp.where(low, scaled, 0.0), jnp.where(low, 0.0, scaled)], axis=0
            ).astype(BF16)
            out = dot(jnp.concatenate(weights, axis=1), stacked)
            out = out + cw_ref[5:6, columns] * values
            across = pair_of(low, running, h)
            if ci:
                carried = dot(queries, state[:, columns].astype(BF16))
                out = out + jnp.where(reached, carried * jnp.exp(across), 0.0)
            y_ref[start : start + CHUNK, columns] = out
            if ci < chunks - 1:
                left = pair_of(low_row, ending, h) - across
                source_in = jnp.where(source, scaled * jnp.exp(left), 0.0).astype(BF16)
                fresh = dot(keys_t, source_in)
                if ci:
                    fresh = fresh + state[:, columns] * pair_of(low_row, kept, h)
                state[:, columns] = fresh
                st_ref[0, ci, :, columns] = fresh.astype(BF16)


def backward_kernel(
    heads,
    size,
    first_head,
    first_block,
    len_ref,
    at_ref,
    u_ref,
    pre_ref,
    dt_ref,
    kq_ref,
    dy_ref,
    st_ref,
    cw_ref,
    hp_ref,
    *refs,
):
    added = refs[:-10]
    du_ref, ddt_ref, mine_ref, other_ref, cg_ref, hg_ref = refs[-10:-4]
    d_state, d_pre, out_in, source_in = refs[-4:]
    is_high = at_ref[1] == 1
    block = pl.program_id(0)
    first = len_ref[first_block + block, 0]
    both = first + len_ref[first_block + block, 1]
    tokens, width = u_ref.shape
    chunks = tokens // CHUNK
    row, column = iotas(CHUNK, CHUNK)
    low = column < size
    low_row = low[0:1, :]
    wide_row, wide_column = iotas(2 * CHUNK, LANES)
    pick_row, pick_column = iotas(16, 2 * CHUNK)

    @pl.when(block == 0)
    def _():
        cg_ref[...] = jnp.zeros_like(cg_ref)
        hg_ref[...] = jnp.zeros_like(hg_ref)

    d_pre[tokens : tokens + 8, :] = jnp.zeros((8, width), F32)
    for ci in reversed(range(chunks)):
        start = ci * CHUNK
        has_later = ci < chunks - 1
        position = row + start
        begin = begin_of(position, first, both)
        ahead = [begin_of(position + delay, first, both) <= position for delay in range(1, 4)]
        raw, step, rate, running = chunk_rates(dt_ref, hp_ref, start)
        running_t = running.T
        keys = kq_ref[start : start + CHUNK, :LANES]
        queries = kq_ref[start : start + CHUNK, LANES:]
        allowed = (row <= column) & (position >= begin_of(column + start, first, both))
        scores = jnp.where(allowed, dot_nt(keys, queries), 0.0)
        last_begin = begin_of(start + CHUNK - 1, first, both)
        source = position >= last_begin
        reached = begin < start
        ending = running[CHUNK - 1 : CHUNK, :]
        kept = jnp.where(last_begin < start, jnp.exp(ending), 0.0)
        d_scores = jnp.zeros((CHUNK, CHUNK), F32)
        later_sums = jnp.zeros((16, CHUNK), F32)
        early_sums = jnp.zeros((CHUNK, LANES), F32)
        out_sums = jnp.zeros((CHUNK, LANES), F32)
        source_sums = jnp.zeros((CHUNK, LANES), F32)
        direct_sums = jnp.zeros((CHUNK, LANES), F32)
        kept_sums = jnp.zeros((8, LANES), F32)
        for pair in range(heads // 2):
            h = first_head + 2 * pair
            columns = slice(pair * LANES, (pair + 1) * LANES)
            to_head = (column == h + (row >= size).astype(jnp.int32)).astype(BF16)
            pre = pre_ref[start : start + CHUNK, columns]
            inputs = u_ref[start : start + CHUNK, columns]
            gate = sigmoid(pre)
            values = pre * gate
            steps = pair_of(low, step, h)
            scaled = values * steps
            d_out = dy_ref[start : start + CHUNK, columns].astype(F32)
            d_low = d_out.astype(BF16)
            stacked = jnp.concatenate(
                [jnp.where(low, scaled, 0.0), jnp.where(low, 0.0, scaled)], axis=0
            ).astype(BF16)
            d_weights = dot_nt(stacked, d_low)
            weights, products = [], []
            for at, head in enumerate((h, h + 1)):
                gap = running_t[head : head + 1, :] - running[:, head : head + 1]
                decay = jnp.exp(jnp.minimum(gap, 0.0))
                d_decayed = decay * d_weights[at * CHUNK : (at + 1) * CHUNK]
                d_scores = d_scores + d_decayed
                products.append((scores * d_decayed).astype(BF16))
                weights.append((scores * decay).astype(BF16))
            early = wide_column == h + (wide_row >= CHUNK).astype(jnp.int32)
            early_sums = early_sums + dot(jnp.concatenate(products, axis=1), early.astype(BF16))
            later = pick_row == h + (pick_column >= CHUNK).astype(jnp.int32)
            later_sums = later_sums + dot(later.astype(BF16), jnp.concatenate(products, axis=0))
            d_stacked = jnp.concatenate(
                [jnp.where(low, d_out, 0.0), jnp.where(low, 0.0, d_out)], axis=0
            ).astype(BF16)
            d_scaled = dot(jnp.concatenate(weights, axis=1), d_stacked)
            across = pair_of(low, running, h)
            if has_later:
                left = jnp.exp(pair_of(low_row, ending, h) - across)
                left = jnp.where(source, left, 0.0)
                d_state_here = d_state[:, columns]
                d_source = dot(keys, d_state_here.astype(BF16)) * left
                d_scaled = d_scaled + d_source
                source_sums = source_sums + dot((scaled * d_source).astype(BF16), to_head)
                source_in[:, columns] = (scaled * left).astype(BF16)
            if ci:
                before = st_ref[0, ci - 1, :, columns]
                d_reach = jnp.where(reached, d_out * jnp.exp(across), 0.0)
                out_sums = out_sums + dot((d_reach * dot(queries, before)).astype(BF16), to_head)
                out_in[:, columns] = d_reach.astype(BF16)
                if has_later:
                    held = jnp.sum(d_state_here * before.astype(F32), axis=0, keepdims=True)
                    held = held * pair_of(low_row, kept, h)
                    kept_sums = kept_sums + dot(
                        jnp.broadcast_to(held, (8, LANES)), to_head.astype(F32), HIGHEST
                    )
            direct_sums = direct_sums + dot((d_scaled * values).astype(BF16), to_head)
            d_values = d_scaled * steps + cw_ref[5:6, columns] * d_out
            cg_ref[5:6, columns] += jnp.sum(d_out * values, axis=0, keepdims=True)
            d_here = d_values * (gate * (1.0 + pre * (1.0 - gate)))
            d_pre[start : start + CHUNK, columns] = d_here
            d_in = cw_ref[3:4, columns] * d_here
            cg_ref[3:4, columns] += jnp.sum(inputs * d_here, axis=0, keepdims=True)
            for delay in range(1, 4):
                shifted = d_pre[start + delay : start + delay + CHUNK, columns]
                shifted = jnp.where(ahead[delay - 1], shifted, 0.0)
                d_in = d_in + cw_ref[3 - delay : 4 - delay, columns] * shifted
                cg_ref[3 - delay : 4 - delay, columns] += jnp.sum(
                    inputs * shifted, axis=0, keepdims=True
                )
            du_ref[start : start + CHUNK, columns] = d_in.astype(BF16)
            cg_ref[4:5, columns] += jnp.sum(d_here, axis=0, keepdims=True)
        d_scores = jnp.where(allowed, d_scores, 0.0)
        d_keys = dot(d_scores.astype(BF16), queries)
        d_queries = dot(d_scores.T.astype(BF16), keys)
        d_running = (
            jnp.concatenate([later_sums, jnp.zeros((CHUNK - 16, CHUNK), F32)], axis=0).T
            - early_sums
            + out_sums
            - source_sums
        )
        if has_later:
            d_keys = d_keys + dot_nt(source_in[...], d_state[...].astype(BF16))
            at_end = jnp.sum(source_sums, axis=0, keepdims=True) + kept_sums[0:1, :]
            d_running = d_running + jnp.where(row == CHUNK - 1, at_end, 0.0)
        if ci:
            d_queries = d_queries + dot_nt(out_in[...], st_ref[0, ci - 1])
            queries_t = queries.astype(F32).T.astype(BF16)
            for pair in range(heads // 2):
                columns = slice(pair * LANES, (pair + 1) * LANES)
                fresh = dot(queries_t, out_in[:, columns])
                if has_later:
                    fresh = fresh + d_state[:, columns] * pair_of(low_row, kept, first_head + 2 * pair)
                d_state[:, columns] = fresh
        here = slice(start, start + CHUNK)
        mine = jnp.where(is_high, d_queries, d_keys)
        other = jnp.where(is_high, d_keys, d_queries)
        if added:
            mine, other = mine + added[0][here, :], other + added[1][here, :]
        mine_ref[here, :] = mine.astype(mine_ref.dtype)
        other_ref[here, :] = other.astype(other_ref.dtype)
        d_rate = dot((row <= column).astype(F32), d_running, HIGHEST)
        d_step = direct_sums - jnp.exp(hp_ref[1:2, :]) * d_rate
        d_raw = d_step * sigmoid(raw)
        ddt_ref[start : start + CHUNK, :] = d_raw.astype(BF16)
        hg_ref[0:1, :] += jnp.sum(d_raw, axis=0, keepdims=True)
        hg_ref[1:2, :] += jnp.sum(d_rate * rate, axis=0, keepdims=True)


def prepare_first_kernel(heads, size, state, at_ref, in_ref, mine_ref, other_ref):
    x, core = at_ref[0], at_ref[1]
    width = heads * size
    inner = 4 * width
    steps_at = 2 * inner + 2 * state
    steps = in_ref[:, steps_at : steps_at + 4 * heads].astype(F32)
    rows = steps.shape[0]
    steps = jnp.concatenate([steps, jnp.zeros((rows, LANES - 4 * heads), F32)], axis=1)
    column = lax.broadcasted_iota(jnp.int32, (rows, LANES), 1)
    for ref, c in ((mine_ref, core), (other_ref, 1 - core)):
        p = 2 * x + c
        values_at = pl.multiple_of(inner + p * width, LANES)
        ref[:, :width] = in_ref[:, pl.ds(values_at, width)]
        drawn = pltpu.roll(steps, lax.rem(LANES - heads * p, LANES), 1)
        ref[:, width : width + LANES] = jnp.where(column < heads, drawn, 0.0).astype(BF16)
        keys_at = pl.multiple_of(2 * inner + c * state, LANES)
        ref[:, width + LANES : width + LANES + state] = in_ref[:, pl.ds(keys_at, state)]


def prepare_last_kernel(width, at_ref, in_ref, out_ref, mine_ref, other_ref):
    x, core = at_ref[0], at_ref[1]
    for ref, c in ((mine_ref, core), (other_ref, 1 - core)):
        at = pl.multiple_of((2 * x + c) * width, LANES)
        ref[:, :width] = in_ref[:, pl.ds(at, width)]
        ref[:, width:] = out_ref[:, pl.ds(at, width)]


def prepare_call(kernel, columns, place, *weights):
    rows = weights[0].shape[0]
    return pl.pallas_call(
        kernel,
        in_specs=[pl.BlockSpec(memory_space=pltpu.SMEM)]
        + [pl.BlockSpec(memory_space=pltpu.VMEM)] * len(weights),
        out_specs=[pl.BlockSpec(memory_space=pltpu.VMEM)] * 2,
        out_shape=[jax.ShapeDtypeStruct((rows, columns), BF16)] * 2,
        compiler_params=pltpu.CompilerParams(vmem_limit_bytes=24 * 1024 * 1024),
        name="prepare",
    )(place, *weights)


def unpack_kernel(sizes, heads, size, state, at_ref, small_ref, n_ref, conv_ref, head_ref, kq_ref, all_ref):
    conv_size, gate_size, norm_size, head_size = sizes
    x, c = at_ref[0], at_ref[1]
    p = 2 * x + c
    shards = small_ref.shape[0] // 8
    width = heads * size

    def joined(first_row, rows, at, part, columns):
        padded = -(-columns // LANES) * LANES
        lanes = -(-part // LANES) * LANES
        lane = lax.broadcasted_iota(jnp.int32, (8, lanes), 1)
        result = jnp.zeros((8, padded), F32)
        for f in range(shards):
            rows_here = small_ref[8 * f : 8 * f + 8, at : at + lanes].astype(F32)
            rows_here = jnp.where(lane < part, rows_here, 0.0)
            if padded > lanes:
                rows_here = jnp.concatenate(
                    [rows_here, jnp.zeros((8, padded - lanes), F32)], axis=1
                )
            result = result + pltpu.roll(rows_here, (part * f) % padded, 1)
        return result[first_row : first_row + rows]

    conv_all = joined(0, 5, 0, conv_size, conv_size * shards)
    gate_all = joined(5, 1, 0, gate_size, gate_size * shards)
    norm_all = joined(6, 1, 0, norm_size, norm_size * shards)
    n_ref[...] = jnp.broadcast_to(norm_all, n_ref.shape)
    all_ref[...] = jnp.zeros_like(all_ref)
    all_ref[0:5, : conv_all.shape[1]] = conv_all
    all_ref[6:7, : gate_all.shape[1]] = gate_all
    conv_ref[...] = all_ref[:, pl.ds(pl.multiple_of(p * width, LANES), width)]
    kq_at = 4 * width + c * state
    kq_ref[...] = all_ref[:, pl.ds(pl.multiple_of(kq_at, LANES), state)]
    column = lax.broadcasted_iota(jnp.int32, (8, LANES), 1)
    head_ref[...] = jnp.zeros_like(head_ref)
    for row in range(3):
        values = joined(7, 1, row * LANES, head_size, head_size * shards)
        values = jnp.broadcast_to(values, (8, LANES))
        values = pltpu.roll(values, lax.rem(LANES - heads * p, LANES), 1)
        head_ref[row : row + 1, :] = jnp.where(column < heads, values, 0.0)[0:1]
    row_at, column_at = iotas(LANES, width)
    spread = (row_at == column_at // size).astype(F32)
    conv_ref[5:6, :] = dot(head_ref[...], spread, HIGHEST)[2:3]


def unpack_call(sizes, heads, size, state, place, small):
    shards = small.shape[0] // 8
    depth, width = sizes[2] * shards, heads * size
    columns = -(-sizes[0] * shards // LANES) * LANES
    return pl.pallas_call(
        functools.partial(unpack_kernel, sizes, heads, size, state),
        in_specs=[
            pl.BlockSpec(memory_space=pltpu.SMEM),
            pl.BlockSpec(memory_space=pltpu.VMEM),
        ],
        out_specs=[pl.BlockSpec(memory_space=pltpu.VMEM)] * 4,
        out_shape=[
            jax.ShapeDtypeStruct((8, depth), F32),
            jax.ShapeDtypeStruct((8, width), F32),
            jax.ShapeDtypeStruct((8, LANES), F32),
            jax.ShapeDtypeStruct((8, state), F32),
        ],
        scratch_shapes=[pltpu.VMEM((8, columns), F32)],
        compiler_params=pltpu.CompilerParams(vmem_limit_bytes=24 * 1024 * 1024),
        name="unpack",
    )(place, small)


def assemble_rows(links_shape, at_ref, own_ref, core_ref, pieces, whole_ref):
    sides, groups = links_shape
    a, g, c = at_ref[0], at_ref[1], at_ref[2]
    rows = own_ref.shape[0]
    part = 2 * rows // sides
    base = g * (2 * rows)
    whole_ref[pl.ds(pl.multiple_of(base + c * rows, 16), rows), :] = own_ref[...]
    whole_ref[pl.ds(pl.multiple_of(base + (1 - c) * rows, 16), rows), :] = core_ref[...]
    for k in range(1, groups):
        base = lax.rem(g + groups - k, groups) * (2 * rows)
        for j in range(sides):
            at = base + lax.rem(a + sides - j, sides) * part
            piece = pieces[(k - 1) * sides + j]
            whole_ref[pl.ds(pl.multiple_of(at, 16), part), :] = piece[...]


def project_kernel(links_shape, at_ref, own_ref, core_ref, *refs):
    pieces, (rows_ref, whole_ref, out_ref) = refs[:-3], refs[-3:]

    @pl.when(pl.program_id(0) == 0)
    def _():
        assemble_rows(links_shape, at_ref, own_ref, core_ref, pieces, whole_ref)

    out_ref[...] = dot(rows_ref[...], whole_ref[...])


def whole_spec(array):
    return pl.BlockSpec(array.shape, lambda b: (0,) * array.ndim)


def columns_spec(array, width, index):
    if array.shape[1] == width:
        index = 0
    return pl.BlockSpec((array.shape[0], width), lambda b: (0, index))


def project_call(links_shape, width, index, blocks, tokens, place, parts, rows):
    depth = rows.shape[1]
    return pl.pallas_call(
        functools.partial(project_kernel, links_shape),
        grid=(blocks,),
        in_specs=[pl.BlockSpec(memory_space=pltpu.SMEM)]
        + [columns_spec(array, width, index) for array in parts]
        + [pl.BlockSpec((tokens, depth), lambda b: (b, 0))],
        out_specs=[
            pl.BlockSpec((depth, width), lambda b: (0, 0)),
            pl.BlockSpec((tokens, width), lambda b: (b, 0)),
        ],
        out_shape=[
            jax.ShapeDtypeStruct((depth, width), BF16),
            jax.ShapeDtypeStruct((blocks * tokens, width), F32),
        ],
        compiler_params=pltpu.CompilerParams(vmem_limit_bytes=40 * 1024 * 1024),
        cost_estimate=pl.CostEstimate(
            flops=2 * rows.size * width, bytes_accessed=2 * rows.size, transcendentals=0
        ),
        name="project",
    )(place, *parts, rows)


def branch_back_kernel(links_shape, at_ref, own_ref, core_ref, *refs):
    pieces, rows_refs = refs[:-10], refs[-10:-6]
    gate_ref, ssd_ref, cw_ref, whole_ref, out_ref, sums_ref = refs[-6:]
    block = pl.program_id(0)

    @pl.when(block == 0)
    def _():
        assemble_rows(links_shape, at_ref, own_ref, core_ref, pieces, whole_ref)

    for at, rows_ref in enumerate(rows_refs):

        @pl.when(block == at)
        def _():
            out_ref[...] = dot(rows_ref[...], whole_ref[...])

    tokens, width = out_ref.shape
    sums_ref[...] = jnp.zeros_like(sums_ref)
    for start in range(0, tokens, CHUNK):
        squares = jnp.zeros((CHUNK, LANES), F32)
        products = jnp.zeros((CHUNK, LANES), F32)
        for left in range(0, width, LANES):
            tile = (slice(start, start + CHUNK), slice(left, left + LANES))
            gate = gate_ref[tile]
            gated = ssd_ref[tile] * (gate * sigmoid(gate))
            squares = squares + gated * gated
            products = products + gated * (cw_ref[6:7, left : left + LANES] * out_ref[tile])
        sums_ref[0:1, start : start + CHUNK] = jnp.sum(squares.T, axis=0, keepdims=True)
        sums_ref[1:2, start : start + CHUNK] = jnp.sum(products.T, axis=0, keepdims=True)


def branch_back_call(links_shape, width, index, place, parts, rows, gate, ssd_out, conv_rows):
    tokens, depth = rows[0].shape
    block = pl.BlockSpec((tokens, width), lambda b: (b, 0))
    return pl.pallas_call(
        functools.partial(branch_back_kernel, links_shape),
        grid=(4,),
        in_specs=[pl.BlockSpec(memory_space=pltpu.SMEM)]
        + [columns_spec(array, width, index) for array in parts]
        + [whole_spec(array) for array in rows]
        + [block, block, pl.BlockSpec((8, width), lambda b: (0, 0))],
        out_specs=[
            pl.BlockSpec((depth, width), lambda b: (0, 0)),
            block,
            pl.BlockSpec((8, tokens), lambda b: (0, b)),
        ],
        out_shape=[
            jax.ShapeDtypeStruct((depth, width), BF16),
            jax.ShapeDtypeStruct((4 * tokens, width), F32),
            jax.ShapeDtypeStruct((8, 4 * tokens), F32),
        ],
        compiler_params=pltpu.CompilerParams(vmem_limit_bytes=56 * 1024 * 1024),
        cost_estimate=pl.CostEstimate(
            flops=8 * tokens * depth * width, bytes_accessed=8 * tokens * depth, transcendentals=0
        ),
        name="branch_back",
    )(place, *parts, *rows, gate, ssd_out, conv_rows)


def gating_back_kernel(
    inner, sums_ref, core_ref, side_ref, both_ref, gate_ref, ssd_ref, db_ref, cw_ref,
    branch_ref, dgate_ref, dssd_ref, gain_ref
):
    @pl.when(pl.program_id(0) == 0)
    def _():
        gain_ref[...] = jnp.zeros_like(gain_ref)

    sums = sums_ref[...] + core_ref[...] + side_ref[...] + both_ref[...]
    scale_row = lax.rsqrt(sums[0:1, :] * (1.0 / inner) + EPS)
    cross_row = scale_row * scale_row * scale_row * (sums[1:2, :] * (1.0 / inner))
    tokens, width = gate_ref.shape
    for start in range(0, tokens, CHUNK):
        stacked = jnp.concatenate(
            [scale_row[:, start : start + CHUNK], cross_row[:, start : start + CHUNK],
             jnp.zeros((CHUNK - 2, CHUNK), F32)], axis=0
        ).T
        scale, cross = stacked[:, 0:1], stacked[:, 1:2]
        for left in range(0, width, LANES):
            columns = slice(left, left + LANES)
            tile = (slice(start, start + CHUNK), columns)
            gate, ssd, d_branch = gate_ref[tile], ssd_ref[tile], db_ref[tile]
            gain = cw_ref[6:7, columns]
            sig = sigmoid(gate)
            act = gate * sig
            gated = ssd * act
            scaled = gated * scale
            branch_ref[tile] = (scaled * gain).astype(BF16)
            gain_ref[0:1, columns] += jnp.sum(d_branch * scaled, axis=0, keepdims=True)
            d_gated = scale * (gain * d_branch) - gated * cross
            dssd_ref[tile] = d_gated * act
            dgate_ref[tile] = (d_gated * ssd * (sig * (1.0 + gate * (1.0 - sig)))).astype(BF16)


def gating_back_call(inner, sums, gate, ssd_out, d_branch, conv_rows):
    rows, columns = gate.shape
    tokens = rows // 4
    block = pl.BlockSpec((tokens, columns), lambda b: (b, 0))
    order = [lambda b: (0, b)]
    order.append(lambda b: (0, b + 1 - 2 * lax.rem(b, 2)))
    order.append(lambda b: (0, lax.rem(b + 2, 4)))
    order.append(lambda b: (0, 3 - b))
    return pl.pallas_call(
        functools.partial(gating_back_kernel, inner),
        grid=(4,),
        in_specs=[pl.BlockSpec((8, tokens), index) for index in order]
        + [block, block, block, pl.BlockSpec((8, columns), lambda b: (0, 0))],
        out_specs=[block, block, block, pl.BlockSpec((8, columns), lambda b: (0, 0))],
        out_shape=[
            jax.ShapeDtypeStruct((rows, columns), BF16),
            jax.ShapeDtypeStruct((rows, columns), BF16),
            jax.ShapeDtypeStruct((rows, columns), F32),
            jax.ShapeDtypeStruct((8, columns), F32),
        ],
        compiler_params=pltpu.CompilerParams(vmem_limit_bytes=40 * 1024 * 1024),
        cost_estimate=pl.CostEstimate(
            flops=20 * rows * columns, bytes_accessed=20 * rows * columns, transcendentals=0
        ),
        name="gating_back",
    )(*sums, gate, ssd_out, d_branch, conv_rows)


def normalize_kernel(*refs):
    rows_refs, (gain_ref, normed_ref, scale_ref) = refs[:4], refs[4:]
    for at, rows_ref in enumerate(rows_refs):

        @pl.when(pl.program_id(0) == at)
        def _():
            depth = rows_ref.shape[1]
            for start in range(0, rows_ref.shape[0], 64):
                rows = rows_ref[start : start + 64, :].astype(F32)
                mean = jnp.sum(rows * rows, axis=1, keepdims=True) * (1.0 / depth)
                scale = lax.rsqrt(mean + EPS)
                normed = rows * scale * gain_ref[0:1, :]
                normed_ref[start : start + 64, :] = normed.astype(BF16)
                scale_ref[start : start + 64, :] = jnp.broadcast_to(scale, (64, LANES))


def normalize_call(blocks, gain):
    tokens, depth = blocks[0].shape
    return pl.pallas_call(
        normalize_kernel,
        grid=(4,),
        in_specs=[whole_spec(block) for block in blocks] + [whole_spec(gain)],
        out_specs=[
            pl.BlockSpec((tokens, depth), lambda b: (b, 0)),
            pl.BlockSpec((tokens, LANES), lambda b: (b, 0)),
        ],
        out_shape=[
            jax.ShapeDtypeStruct((4 * tokens, depth), BF16),
            jax.ShapeDtypeStruct((4 * tokens, LANES), F32),
        ],
        compiler_params=pltpu.CompilerParams(vmem_limit_bytes=40 * 1024 * 1024),
        name="normalize",
    )(*blocks, gain)


def weight_grad_kernel(links_shape, groups_of_terms, over_a, at_ref, *refs):
    sides, groups = links_shape
    count = sum(len(terms) for terms in groups_of_terms)
    left_count = 1 + max(left_at for terms in groups_of_terms for left_at, _ in terms)
    lefts, rights = refs[:left_count], refs[left_count : left_count + count]
    outs, scratch = refs[left_count + count : -1], refs[-1]
    at_column, at_term = 0, 0
    for terms in groups_of_terms:
        result = None
        for left_at, first_row in terms:
            right = rights[at_term][...]
            term = lax.dot_general(
                lefts[left_at][first_row : first_row + right.shape[0], :],
                right,
                (((0,), (0,)), ((), ())),
                preferred_element_type=F32,
            )
            result = term if result is None else result + term
            at_term += 1
        width = result.shape[1]
        scratch[:, at_column : at_column + width] = result.astype(BF16)
        at_column += width
    if over_a:
        chips, part = outs[0].shape[0], outs[0].shape[1]
        for chip in range(chips):
            for j, out in enumerate(outs):
                at = (chip * sides + lax.rem(at_ref[0] + j, sides)) * part
                out[chip] = scratch[pl.ds(pl.multiple_of(at, 16), part), :]
        return
    rows = outs[0].shape[0]
    chips = scratch.shape[0] // rows
    for chip in range(chips):
        turn = lax.rem(pl.program_id(0) * chips + chip + groups - at_ref[1], groups)
        for k, out in enumerate(outs):

            @pl.when(turn == k)
            def _():
                out[...] = scratch[chip * rows : (chip + 1) * rows, :]


def weight_grad_call(links_shape, over_a, place, groups_of_terms):
    sides, groups = links_shape
    terms = [term for group in groups_of_terms for term in group]
    depth = terms[0][0].shape[1]
    columns = sum(group[0][5] for group in groups_of_terms)
    rows = depth // groups
    part = rows // sides
    chips = 1
    while chips * rows % LANES:
        chips += 1
    lefts = []
    for term in terms:
        if not any(term[0] is left for left in lefts):
            lefts.append(term[0])

    def left_at(term):
        return [term[0] is left for left in lefts].index(True)

    def left_spec(left):
        return pl.BlockSpec((left.shape[0], chips * rows), lambda b: (0, b))

    def right_spec(term):
        return pl.BlockSpec((term[1], term[5]), lambda b: (term[4], term[6]))

    if over_a:
        out_specs = [pl.BlockSpec((chips, part, columns), lambda b: (b, 0, 0))] * sides
        out_shape = [jax.ShapeDtypeStruct((groups, part, columns), BF16)] * sides
    else:
        out_specs = [pl.BlockSpec((rows, columns), lambda b: (0, 0))] * groups
        out_shape = [jax.ShapeDtypeStruct((rows, columns), BF16)] * groups
    shapes = tuple(
        tuple((left_at(term), term[1] * term[2]) for term in group) for group in groups_of_terms
    )
    return pl.pallas_call(
        functools.partial(weight_grad_kernel, links_shape, shapes, over_a),
        grid=(groups // chips,),
        in_specs=[pl.BlockSpec(memory_space=pltpu.SMEM)]
        + [left_spec(left) for left in lefts]
        + [right_spec(term) for term in terms],
        out_specs=out_specs,
        out_shape=out_shape,
        scratch_shapes=[pltpu.VMEM((chips * rows, columns), BF16)],
        compiler_params=pltpu.CompilerParams(vmem_limit_bytes=48 * 1024 * 1024),
        cost_estimate=pl.CostEstimate(
            flops=2 * terms[0][1] * depth * columns,
            bytes_accessed=2 * terms[0][1] * depth,
            transcendentals=0,
        ),
        name="weight_grad",
    )(place, *lefts, *[term[3] for term in terms])


def combine_kernel(groups, at_ref, *refs):
    parts, outs = refs[:-groups], refs[-groups:]
    result = parts[0][0].astype(F32)
    for part in parts[1:]:
        result = result + part[0].astype(F32)
    turn = lax.rem(pl.program_id(0) + groups - at_ref[1], groups)
    for k, out in enumerate(outs):

        @pl.when(turn == k)
        def _():
            out[...] = result.astype(BF16)


def combine_call(groups, place, parts):
    rows, columns = parts[0].shape[1:]
    return pl.pallas_call(
        functools.partial(combine_kernel, groups),
        grid=(groups,),
        in_specs=[pl.BlockSpec(memory_space=pltpu.SMEM)]
        + [pl.BlockSpec((1, rows, columns), lambda b: (b, 0, 0))] * len(parts),
        out_specs=[pl.BlockSpec((rows, columns), lambda b: (0, 0))] * groups,
        out_shape=[jax.ShapeDtypeStruct((rows, columns), BF16)] * groups,
        compiler_params=pltpu.CompilerParams(vmem_limit_bytes=24 * 1024 * 1024),
        name="combine",
    )(place, *parts)


def keys_back_kernel(len_ref, mine_ref, core_ref, side_ref, in_ref, rows_ref, d_ref, grads_ref):
    block = pl.program_id(0)
    first = len_ref[block, 0]
    both = first + len_ref[block, 1]
    tokens, columns = in_ref.shape
    position = lax.broadcasted_iota(jnp.int32, (tokens, columns), 0)
    begin = begin_of(position, first, both)
    inside = [position - delay >= begin for delay in range(1, 4)]
    inputs = [in_ref[...]]
    for delay in range(1, 4):
        shifted = pltpu.roll(inputs[0], delay, 0)
        inputs.append(jnp.where(inside[delay - 1], shifted, 0.0))
    pre = rows_ref[4:5, :] + rows_ref[3:4, :] * inputs[0]
    for delay in range(1, 4):
        pre = pre + rows_ref[3 - delay : 4 - delay, :] * inputs[delay]
    sig = sigmoid(pre)
    d_out = mine_ref[...] + core_ref[...].astype(F32) + side_ref[...].astype(F32)
    d_pre = d_out * (sig * (1.0 + pre * (1.0 - sig)))
    d_in = rows_ref[3:4, :] * d_pre
    for delay in range(1, 4):
        moved = pltpu.roll(jnp.where(inside[delay - 1], d_pre, 0.0), tokens - delay, 0)
        d_in = d_in + rows_ref[3 - delay : 4 - delay, :] * moved
    d_ref[...] = d_in.astype(BF16)

    @pl.when(block == 0)
    def _():
        grads_ref[...] = jnp.zeros_like(grads_ref)

    for delay in range(4):
        grads_ref[3 - delay : 4 - delay, :] += jnp.sum(
            inputs[delay] * d_pre, axis=0, keepdims=True
        )
    grads_ref[4:5, :] += jnp.sum(d_pre, axis=0, keepdims=True)


def keys_back_call(lengths, parts, inputs, rows):
    total, columns = inputs.shape
    block = pl.BlockSpec((total // 2, columns), lambda b: (b, 0))
    small = pl.BlockSpec((8, columns), lambda b: (0, 0))
    return pl.pallas_call(
        keys_back_kernel,
        grid=(2,),
        in_specs=[pl.BlockSpec(memory_space=pltpu.SMEM)] + [block] * 4 + [small],
        out_specs=[block, small],
        out_shape=[
            jax.ShapeDtypeStruct((total, columns), BF16),
            jax.ShapeDtypeStruct((8, columns), F32),
        ],
        compiler_params=pltpu.CompilerParams(vmem_limit_bytes=24 * 1024 * 1024),
        name="keys_back",
    )(lengths, *parts, inputs, rows)


def small_kernel(heads, size, at_ref, *refs):
    convs, head_refs, (gain_ref, kq_ref, out_ref) = refs[:3], refs[3:6], refs[6:]
    p = 2 * at_ref[0] + at_ref[1]
    width = heads * size
    most, less = convs[0].shape[1], convs[1].shape[1]
    out_ref[...] = jnp.zeros_like(out_ref)
    rest = convs[1][...] + convs[2][...]
    at = pl.multiple_of(p * width, LANES)
    out_ref[0:5, pl.ds(at, most)] = convs[0][0:5, :]
    out_ref[0:5, pl.ds(pl.multiple_of(at + most, LANES), less)] = rest[0:5, :]
    kq_at = pl.multiple_of(4 * width + at_ref[1] * kq_ref.shape[1], LANES)
    out_ref[0:5, pl.ds(kq_at, kq_ref.shape[1])] = kq_ref[0:5, :]
    out_ref[5:6, pl.ds(at, width)] = gain_ref[0:1, :]
    skip = jnp.concatenate([convs[0][...], rest], axis=1)
    row, column = iotas(width, LANES)
    skip = dot(skip, (row // size == column).astype(F32), HIGHEST)
    sums = head_refs[0][...] + head_refs[1][...] + head_refs[2][...]
    for field, values in enumerate((sums[0:1], sums[1:2], skip[5:6])):
        values = jnp.broadcast_to(values, (8, LANES))
        lane = lax.broadcasted_iota(jnp.int32, (8, LANES), 1)
        values = pltpu.roll(jnp.where(lane < heads, values, 0.0), heads * p, 1)
        out_ref[7:8, field * LANES : (field + 1) * LANES] = values[0:1]


def small_call(heads, size, channels, place, convs, head_grads, gains, kq_grads):
    operands = [*convs, *head_grads, gains, kq_grads]
    return pl.pallas_call(
        functools.partial(small_kernel, heads, size),
        in_specs=[pl.BlockSpec(memory_space=pltpu.SMEM)]
        + [pl.BlockSpec(memory_space=pltpu.VMEM)] * len(operands),
        out_specs=pl.BlockSpec(memory_space=pltpu.VMEM),
        out_shape=jax.ShapeDtypeStruct((8, channels), F32),
        compiler_params=pltpu.CompilerParams(vmem_limit_bytes=24 * 1024 * 1024),
        name="small_gradients",
    )(place, *operands)


def final_kernel(heads, size, most, by_g, at_ref, *refs):
    first_both, first_other, held_both, held_other, last_mine, last_core = refs[:6]
    weight_ref, gain_ref, in_ref, out_ref, norm_ref = refs[6:]
    far, high = at_ref[0] == 1, at_ref[1] == 1
    width = heads * size
    less = width - most
    rows = in_ref.shape[0]
    at_values, at_keys = 4 * width, 8 * width
    state = last_mine.shape[1] - 2 * (less + LANES)
    at_steps = at_keys + 2 * state
    norm = jnp.zeros((rows, 1), F32)

    def put(at, values):
        stop = at + values.shape[1]
        in_ref[:, at:stop] = values
        weight = weight_ref[:, at:stop].astype(F32)
        return jnp.sum(values * weight, axis=1, keepdims=True)

    def share(both, other, p, count, start, stop):
        columns = slice((p % 2) * count + start, (p % 2) * count + stop)
        take_other = far if p < 2 else jnp.logical_not(far)
        return jnp.where(take_other, other[:, columns], both[:, columns]).astype(F32)

    def last_share(core, start, stop):
        take_core = high if core == 0 else jnp.logical_not(high)
        columns = slice(start, stop)
        return jnp.where(take_core, last_core[:, columns], last_mine[:, columns]).astype(F32)

    steps = jnp.zeros((rows, LANES), F32)
    lane = lax.broadcasted_iota(jnp.int32, (rows, LANES), 1)
    for p in range(4):
        first = functools.partial(share, first_both, first_other, p, 2 * width)
        norm = norm + put(p * width, first(0, width))
        out_ref[:, p * width : p * width + by_g] = first(2 * width - by_g, 2 * width)
        out_ref[:, p * width + by_g : (p + 1) * width] = first(width, 2 * width - by_g)
        at = at_values + p * width
        norm = norm + put(at, share(held_both, held_other, p, most, 0, most))
        left = (p // 2) * (less + LANES)
        norm = norm + put(at + most, last_share(p % 2, left, left + less))
        drawn = last_share(p % 2, left + less, left + less + LANES)
        steps = steps + pltpu.roll(jnp.where(lane < heads, drawn, 0.0), heads * p, 1)
    for core in range(2):
        at = 2 * (less + LANES)
        norm = norm + put(at_keys + core * state, last_share(core, at, at + state))
    norm = norm + put(at_steps, steps[:, : 4 * heads])
    norm_ref[...] = norm / gain_ref[...]


def final_call(heads, size, most, by_g, place, shares, weight, gain):
    rows, columns = weight.shape
    operands = [*shares, weight, gain]
    return pl.pallas_call(
        functools.partial(final_kernel, heads, size, most, by_g),
        in_specs=[pl.BlockSpec(memory_space=pltpu.SMEM)]
        + [pl.BlockSpec(memory_space=pltpu.VMEM)] * len(operands),
        out_specs=[pl.BlockSpec(memory_space=pltpu.VMEM)] * 3,
        out_shape=[
            jax.ShapeDtypeStruct((rows, columns), F32),
            jax.ShapeDtypeStruct((rows, 4 * heads * size), F32),
            jax.ShapeDtypeStruct((rows, 1), F32),
        ],
        compiler_params=pltpu.CompilerParams(vmem_limit_bytes=40 * 1024 * 1024),
        cost_estimate=pl.CostEstimate(
            flops=5_000_000_000, bytes_accessed=16_000_000, transcendentals=0
        ),
        name="owner_gradients",
    )(place, *operands)


def forward_call(
    heads, size, first_block, blocks, lengths, conv_in, keys_queries, conv_rows, head_rows, before=()
):
    total = conv_in.shape[0]
    tokens = total // lengths.shape[0]
    width = heads * size
    state = keys_queries.shape[1] // 2
    boundaries = tokens // CHUNK - 1
    return pl.pallas_call(
        functools.partial(forward_kernel, heads, size, first_block),
        grid=(blocks,),
        in_specs=[
            pl.BlockSpec(memory_space=pltpu.SMEM),
            pl.BlockSpec((tokens, width), lambda b: (first_block + b, 0)),
            pl.BlockSpec((tokens, LANES), lambda b: (first_block + b, width // LANES)),
            pl.BlockSpec((tokens, 2 * state), lambda b: (first_block + b, 0)),
            pl.BlockSpec((8, width), lambda b: (0, 0)),
            pl.BlockSpec((8, LANES), lambda b: (0, 0)),
        ]
        + [pl.BlockSpec(memory_space=pl.ANY)] * len(before),
        out_specs=[
            pl.BlockSpec((tokens, width), lambda b: (first_block + b, 0)),
            pl.BlockSpec((1, boundaries, state, width), lambda b: (first_block + b, 0, 0, 0)),
            pl.BlockSpec((tokens, width), lambda b: (first_block + b, 0)),
        ],
        out_shape=[
            jax.ShapeDtypeStruct((total, width), F32),
            jax.ShapeDtypeStruct((lengths.shape[0], boundaries, state, width), BF16),
            jax.ShapeDtypeStruct((total, width), F32),
        ],
        scratch_shapes=[pltpu.VMEM((state, width), F32)],
        input_output_aliases={6 + at: at for at in range(len(before))},
        compiler_params=pltpu.CompilerParams(vmem_limit_bytes=40 * 1024 * 1024),
        cost_estimate=pl.CostEstimate(
            flops=blocks * 3_000_000_000, bytes_accessed=blocks * 8_000_000, transcendentals=0
        ),
        name="ssd_forward",
    )(lengths, conv_in, conv_in, keys_queries, conv_rows, head_rows, *before)


def backward_call(
    heads, size, first_head, first_block, blocks,
    lengths, place, conv_in, conv_pre, keys_queries, d_out, states, conv_rows, head_rows, before=()
):
    tokens = conv_in.shape[0] // lengths.shape[0]
    total = blocks * tokens
    width = heads * size
    part = first_head * size // width
    steps_at = d_out.shape[1] // LANES
    state = keys_queries.shape[1] // 2
    boundaries = tokens // CHUNK - 1

    def rows_of(columns, index):
        return pl.BlockSpec((tokens, columns), lambda b: (first_block + b, index))

    def swapped(b):
        return b + 1 - 2 * lax.rem(b, 2)

    return pl.pallas_call(
        functools.partial(backward_kernel, heads, size, first_head, first_block),
        grid=(blocks,),
        in_specs=[
            pl.BlockSpec(memory_space=pltpu.SMEM),
            pl.BlockSpec(memory_space=pltpu.SMEM),
            rows_of(width, part),
            rows_of(width, part),
            rows_of(LANES, steps_at),
            rows_of(2 * state, 0),
            rows_of(width, part),
            pl.BlockSpec(
                (1, boundaries, state, width), lambda b: (first_block + b, 0, 0, part)
            ),
            pl.BlockSpec((8, width), lambda b: (0, part)),
            pl.BlockSpec((8, LANES), lambda b: (0, 0)),
        ]
        + [
            rows_of(state, 0),
            pl.BlockSpec((tokens, state), lambda b: (swapped(first_block + b), 0)),
        ][: len(before)],
        out_specs=[
            pl.BlockSpec((tokens, width), lambda b: (b, 0)),
            pl.BlockSpec((tokens, LANES), lambda b: (b, 0)),
            pl.BlockSpec((tokens, state), lambda b: (b, 0)),
            pl.BlockSpec((tokens, state), lambda b: (swapped(b), 0)),
            pl.BlockSpec((8, width), lambda b: (0, 0)),
            pl.BlockSpec((8, LANES), lambda b: (0, 0)),
        ],
        out_shape=[
            jax.ShapeDtypeStruct((total, width), BF16),
            jax.ShapeDtypeStruct((total, LANES), BF16),
            jax.ShapeDtypeStruct((total, state), F32),
            jax.ShapeDtypeStruct((total, state), BF16 if before else F32),
            jax.ShapeDtypeStruct((8, width), F32),
            jax.ShapeDtypeStruct((8, LANES), F32),
        ],
        scratch_shapes=[
            pltpu.VMEM((state, width), F32),
            pltpu.VMEM((tokens + 8, width), F32),
            pltpu.VMEM((CHUNK, width), BF16),
            pltpu.VMEM((CHUNK, width), BF16),
        ],
        compiler_params=pltpu.CompilerParams(vmem_limit_bytes=48 * 1024 * 1024),
        cost_estimate=pl.CostEstimate(
            flops=blocks * heads * 1_000_000_000,
            bytes_accessed=blocks * 8_000_000,
            transcendentals=0,
        ),
        name="ssd_backward",
    )(lengths, place, conv_in, conv_pre, conv_in, keys_queries, d_out, states, conv_rows, head_rows, *before)


def after(values):
    return lax.optimization_barrier(values)


def phase(sends, work=None, arguments=(), until=None):
    values, arguments = after(([value for _, value in sends], arguments))
    moved = [send(value) for (send, _), value in zip(sends, values)]
    done = work(*arguments) if work else ()
    moved, done, until = after((moved, done, until))
    return (moved, done) if until is None else (moved, done, until)


def total(first, others):
    result = first.astype(F32)
    for other in others:
        result = result + other.astype(F32)
    return result


class Links:
    def __init__(self, reps, shards):
        self.reps, self.shards = reps, shards
        self.sides, self.groups = reps // 2, shards // 2
        rep, shard = lax.axis_index("rep"), lax.axis_index("fsdp")
        self.rep, self.shard = rep, shard
        self.a, self.x = rep // 2, rep % 2
        self.g, self.c = shard // 2, shard % 2

    def send(self, value, target):
        pairs = []
        for r in range(self.reps):
            for f in range(self.shards):
                to_r, to_f = target(r, f)
                pairs.append((r * self.shards + f, to_r * self.shards + to_f))
        return lax.ppermute(value, ("rep", "fsdp"), pairs)

    def core(self, value):
        return self.send(value, lambda r, f: (r, f ^ 1))

    def side(self, value):
        return self.send(value, lambda r, f: (r ^ 1, f))

    def corner(self, value):
        return self.send(value, lambda r, f: (r ^ 1, f ^ 1))

    def along_a(self, value, by):
        return self.send(value, lambda r, f: (((r // 2 + by) % self.sides) * 2 + r % 2, f))

    def along_g(self, value, by):
        return self.send(value, lambda r, f: (r, ((f // 2 + by) % self.groups) * 2 + f % 2))

    def diagonal(self, value, by):
        return self.send(
            value, lambda r, f: (((r // 2 + by) % self.sides) * 2 + (r % 2 ^ 1), f)
        )

    def flip(self, value, bit_of_rep, bit_of_shard):
        return self.send(value, lambda r, f: (r ^ bit_of_rep, f ^ bit_of_shard))

    def round_g(self, piece):
        return [self.along_g(piece, k) for k in range(1, self.groups)]

    def piece_of(self, mine, from_core):
        if self.sides == 2:
            return jnp.where(self.a == self.c, mine, from_core)
        is_high = self.c == 1
        chip = jnp.concatenate(
            [jnp.where(is_high, from_core, mine), jnp.where(is_high, mine, from_core)], axis=0
        )
        part = chip.shape[0] // self.sides
        return lax.dynamic_slice_in_dim(chip, self.a * part, part, 0)

    def round_a(self, joined):
        return [self.along_a(joined, j) for j in range(1, self.sides)]

    def assemble(self, mine, from_core, joined, rounds):
        rows, columns = mine.shape
        part = 2 * rows // self.sides
        whole = jnp.zeros((rows * self.shards, columns), mine.dtype)
        base = self.g * 2 * rows
        whole = lax.dynamic_update_slice_in_dim(whole, mine, base + self.c * rows, 0)
        whole = lax.dynamic_update_slice_in_dim(whole, from_core, base + (1 - self.c) * rows, 0)
        for k in range(1, self.groups):
            base = ((self.g - k) % self.groups) * 2 * rows
            for j, pieces in enumerate([joined] + rounds):
                piece = pieces[(k - 1) * part : k * part]
                at = base + ((self.a - j) % self.sides) * part
                whole = lax.dynamic_update_slice_in_dim(whole, piece, at, 0)
        return whole

    def parts_for_a(self, view):
        axis = view.ndim - 3
        mine = lax.dynamic_index_in_dim(view, self.a, axis, keepdims=False)
        others = [
            lax.dynamic_index_in_dim(view, (self.a + j) % self.sides, axis, keepdims=False)
            for j in range(1, self.sides)
        ]
        return mine, others

    def parts_for_g(self, view):
        mine = lax.dynamic_index_in_dim(view, self.g, 0, keepdims=False)
        others = [
            lax.dynamic_index_in_dim(view, (self.g + k) % self.groups, 0, keepdims=False)
            for k in range(1, self.groups)
        ]
        return mine, others

    def send_a(self, others):
        return [self.along_a(part, j + 1) for j, part in enumerate(others)]

    def send_g(self, others):
        return [self.along_g(part, k + 1) for k, part in enumerate(others)]

    def chips_of(self, partial):
        rows = partial.shape[0] // (self.groups * self.sides)
        return partial.reshape(self.groups, self.sides, rows, partial.shape[1])

    def spread_a(self, piece):
        return [self.along_a(piece, j) for j in range(1, self.sides)]

    def join_a(self, piece, others):
        if self.sides == 2:
            is_high = self.a == 1
            return jnp.concatenate(
                [jnp.where(is_high, others[0], piece), jnp.where(is_high, piece, others[0])],
                axis=0,
            )
        part = piece.shape[0]
        chip = jnp.zeros((part * self.sides, piece.shape[1]), piece.dtype)
        for j, value in enumerate([piece] + others):
            at = ((self.a - j) % self.sides) * part
            chip = lax.dynamic_update_slice_in_dim(chip, value, at, 0)
        return chip

    def join_x(self, piece, other):
        is_far = self.x == 1
        return jnp.concatenate(
            [jnp.where(is_far, other, piece), jnp.where(is_far, piece, other)], axis=1
        )

    def rows_of_core(self, chip):
        rows = chip.shape[0] // 2
        is_high = self.c == 1
        mine = jnp.where(is_high, chip[rows:], chip[:rows])
        return mine, jnp.where(is_high, chip[:rows], chip[rows:])

    def shares(self, mine, from_core):
        columns = mine.shape[1] // 2
        is_high = self.c == 1
        low = jnp.where(is_high, from_core, mine)
        high = jnp.where(is_high, mine, from_core)
        return [low[:, :columns], high[:, :columns], low[:, columns:], high[:, columns:]]

    def sum_all(self, value):
        bit = 1
        while bit < self.shards:
            value = value + self.flip(value, 0, bit)
            bit *= 2
        bit = 1
        while bit < self.reps:
            value = value + self.flip(value, bit, 0)
            bit *= 2
        return value

    def group_blocks(self, value):
        far = self.side(value)
        return [value, self.core(value), far, self.core(far)]

    def core_sum(self, partials, link_type):
        tokens = partials.shape[0] // 2
        return partials[:tokens].astype(F32) + self.core(
            partials[tokens:].astype(link_type)
        ).astype(F32)


def shift_rows(values, by):
    zeros = jnp.zeros((values.shape[0], abs(by), values.shape[2]), values.dtype)
    if by > 0:
        return jnp.concatenate([zeros, values[:, :-by]], axis=1)
    return jnp.concatenate([values[:, -by:], zeros], axis=1)


def causal_conv(inputs, begin, taps, bias):
    position = jnp.arange(inputs.shape[1], dtype=jnp.int32)[None, :]
    result = bias + taps[3] * inputs
    shifted = [inputs]
    for delay in range(1, 4):
        inside = (position - delay >= begin)[..., None]
        shifted.append(jnp.where(inside, shift_rows(inputs, delay), 0.0))
        result = result + taps[3 - delay] * shifted[delay]
    return result, shifted


def causal_conv_back(d_result, begin, taps):
    position = jnp.arange(d_result.shape[1], dtype=jnp.int32)[None, :]
    d_inputs = taps[3] * d_result
    for delay in range(1, 4):
        inside = (position - delay >= begin)[..., None]
        moved = shift_rows(jnp.where(inside, d_result, 0.0), -delay)
        d_inputs = d_inputs + taps[3 - delay] * moved
    return d_inputs


def per_device(
    reps,
    shards,
    hidden_in,
    lengths,
    norm_gain,
    in_weight,
    conv_weight,
    conv_bias,
    dt_bias,
    a_log,
    skip_gain,
    gate_gain,
    out_weight,
    cotangent,
):
    links = Links(reps, shards)
    tokens, depth = hidden_in.shape
    inner = gate_gain.shape[0] * shards
    channels = conv_bias.shape[0] * shards
    all_heads = dt_bias.shape[0] * shards
    state = (channels - inner) // 2
    size = inner // all_heads
    heads, width = all_heads // 4, inner // 4
    x, c = links.x, links.c
    p = 2 * x + c

    is_high, is_far = c == 1, x == 1
    far_hidden = links.side(hidden_in)
    ends = jnp.cumsum(lengths[0])
    positions = jnp.arange(tokens, dtype=jnp.int32)
    is_valid = (positions < ends[1])[:, None]
    back_own = jnp.where(is_valid, cotangent, jnp.zeros_like(cotangent))
    sides, groups = links.sides, links.groups
    links_shape = (sides, groups)
    place = jnp.stack([links.a, links.g, c]).astype(jnp.int32)

    lanes = max(conv_weight.shape[1], gate_gain.shape[0], norm_gain.shape[0], 3 * LANES)
    lanes = -(-lanes // LANES) * LANES

    def pack(conv_weight, conv_bias, gate_gain, norm_gain, *head_values):
        heads_row = jnp.concatenate(
            [jnp.pad(v, (0, LANES - v.shape[0])) for v in head_values]
        )
        rows = [conv_bias, gate_gain, norm_gain, heads_row[:lanes]]
        rows = [jnp.pad(row, (0, lanes - row.shape[0]))[None] for row in rows]
        taps_rows = jnp.pad(conv_weight, ((0, 0), (0, lanes - conv_weight.shape[1])))
        return jnp.concatenate([taps_rows, *rows], axis=0)

    small_in = (conv_weight, conv_bias, gate_gain, norm_gain, dt_bias, a_log, skip_gain)
    sizes = (conv_bias.shape[0], gate_gain.shape[0], norm_gain.shape[0], dt_bias.shape[0])

    first_columns, last_columns = width + LANES + state, 2 * width
    core_place = jnp.stack([x, c]).astype(jnp.int32)
    mine_a, for_core_a = prepare_call(
        functools.partial(prepare_first_kernel, heads, size, state),
        first_columns,
        core_place,
        in_weight,
    )

    def hops(pieces, stage):
        sends = [(stage, 1, pieces[stage - 1])]
        if groups - stage != stage:
            sends.append((groups - stage, groups - 1, pieces[(groups - stage + 1) % groups]))
        return sends

    def hop_sends(pieces, stage):
        return [
            ((lambda value, by=by: links.along_g(value, by)), value)
            for _, by, value in hops(pieces, stage)
        ]

    def landed(pieces, stage, values):
        at = [k for k, _, _ in hops(pieces, stage)]
        return {**pieces, **dict(zip(at, values))}

    def rounds(piece):
        return [(lambda value, j=j: links.along_a(value, j), piece) for j in range(1, sides)]

    def doubled(value, bit, other):
        upper = (links.shard // bit) % 2 == 1
        return jnp.concatenate(
            [jnp.where(upper, other, value), jnp.where(upper, value, other)], axis=0
        )

    def swap(bit):
        return lambda value: links.flip(value, 0, bit)

    (from_core_a,), packed = phase([(links.core, for_core_a)], pack, small_in)
    pieces_a = {0: links.piece_of(mine_a, from_core_a)}

    def prepare_last(packed, in_weight, out_weight):
        small_pair = doubled(packed, 1, links.core(packed))
        small_four = doubled(small_pair, 2, links.flip(small_pair, 0, 2))
        kernel = functools.partial(prepare_last_kernel, width)
        last = prepare_call(kernel, last_columns, core_place, in_weight, out_weight)
        return small_four, last

    moved, (small_all, (mine_b, for_core_b)) = phase(
        hop_sends(pieces_a, 1) + [(links.core, lengths)],
        prepare_last,
        (packed, in_weight, out_weight.T),
    )
    lengths_core = moved[-1]
    pieces_a = landed(pieces_a, 1, moved[:-1])
    firsts = [k for k in pieces_a if k]
    early, late = firsts[:1], firsts[1:]
    early_sends = [send for k in early for send in rounds(pieces_a[k])]
    moved, _ = phase(
        hop_sends(pieces_a, 2)
        + [(swap(4), small_all), (links.core, for_core_b)]
        + early_sends
    )
    hop_count = len(hops(pieces_a, 2))
    small_all = doubled(small_all, 4, moved[hop_count])
    from_core_b = moved[hop_count + 1]
    y_moved = moved[hop_count + 2 :]
    pieces_a = landed(pieces_a, 2, moved[:hop_count])
    pieces_b = {0: links.piece_of(mine_b, from_core_b)}
    bit = 8
    while bit < shards:
        small_all = doubled(small_all, bit, links.flip(small_all, 0, bit))
        bit *= 2
    for stage in range(3, groups // 2 + 1):
        values = [send(value) for send, value in hop_sends(pieces_a, stage)]
        pieces_a = landed(pieces_a, stage, values)
    pieces_a, pieces_b, far_hidden = after((pieces_a, pieces_b, far_hidden))
    late = late + [k for k in pieces_a if k and k not in firsts]
    late_sends = [send for k in late for send in rounds(pieces_a[k])]
    b_firsts = [send(value) for send, value in hop_sends(pieces_b, 1)]
    moved, parameters_here = phase(
        late_sends + [(links.core, hidden_in), (links.core, far_hidden)],
        functools.partial(unpack_call, sizes, heads, size, state, core_place),
        (small_all,),
    )
    core_hidden, far_core_hidden = moved[-2:]
    y_moved = y_moved + moved[:-2]
    y_a = {
        k: y_moved[at * (sides - 1) : (at + 1) * (sides - 1)] for at, k in enumerate(early + late)
    }
    n_rows, conv_rows, head_rows, kq_rows = parameters_here
    n_gain = n_rows[0]

    def parts_of(mine, from_core, pieces, rounds_of):
        parts = [mine, from_core]
        for k in range(1, groups):
            parts += [pieces[k], *rounds_of[k]]
        return parts

    parts_a = parts_of(mine_a, from_core_a, pieces_a, y_a)
    pair_lengths = jnp.concatenate([lengths, lengths_core], axis=0)
    pair_ends = jnp.cumsum(pair_lengths, axis=1)
    position = positions[None, :]
    begin = jnp.where(
        position >= pair_ends[:, 1:],
        pair_ends[:, 1:],
        jnp.where(position >= pair_ends[:, :1], pair_ends[:, :1], 0),
    )
    kq_columns = inner + c * state
    kq_taps, kq_bias = kq_rows[:4], kq_rows[4]
    normed, scale = normalize_call([hidden_in, core_hidden, far_hidden, far_core_hidden], n_rows)
    scale_own = scale[:tokens, :1]
    kq_index = (width + LANES) // state
    w_kq, kq_in = project_call(links_shape, state, kq_index, 2, tokens, place, parts_a, normed)
    kq_pre, kq_shifted = causal_conv(kq_in.reshape(2, tokens, state), begin, kq_taps, kq_bias)
    counts = jnp.stack([pair_lengths // 32, pair_lengths % 32], axis=2).reshape(2, 4).astype(BF16)
    counts = jnp.pad(counts, ((0, 14), (0, state - 4)))
    kq_near = jax.nn.silu(kq_pre).astype(BF16).reshape(2 * tokens, state)
    count = tokens // 4
    cuts = [slice(at, at + count) for at in range(0, tokens, count)]
    moved, (w_values, conv_in), b_firsts = phase(
        [
            (links.side, jnp.concatenate([kq_near, counts], axis=0)),
            (links.side, back_own[cuts[0]]),
        ],
        functools.partial(project_call, links_shape, width + LANES, 0, 4, tokens, place),
        (parts_a, normed),
        b_firsts,
    )
    pieces_b = landed(pieces_b, 1, b_firsts)
    kq_far, far_back = moved[0], [moved[1]]
    all_counts = jnp.concatenate([counts[:2, :4], kq_far[2 * tokens : 2 * tokens + 2, :4]], axis=0)
    all_counts = all_counts.astype(jnp.int32)
    all_lengths = all_counts[:, 0::2] * 32 + all_counts[:, 1::2]
    kq_half = jnp.concatenate([kq_near, kq_far[: 2 * tokens]], axis=0)

    (kq_core,), _ = phase([(links.core, kq_half)])
    kq_core = kq_core.reshape(2, 2, tokens, state)[:, ::-1].reshape(4 * tokens, state)
    keys_queries = jnp.concatenate(
        [jnp.where(is_high, kq_core, kq_half), jnp.where(is_high, kq_half, kq_core)], axis=1
    )
    firsts = [k for k in pieces_b if k]
    hop_count = len(hops(pieces_b, 2))
    moved, before = phase(
        hop_sends(pieces_b, 2)
        + rounds(pieces_b[firsts[0]])
        + [(links.side, back_own[cuts[1]]), (links.core, back_own)],
        functools.partial(forward_call, heads, size, 0, 2),
        (all_lengths, conv_in, keys_queries, conv_rows, head_rows),
    )
    y_b = {firsts[0]: moved[hop_count:-2]}
    far_back.append(moved[-2])
    core_back = moved[-1]
    pieces_b = landed(pieces_b, 2, moved[:hop_count])
    for stage in range(3, groups // 2 + 1):
        values = [send(value) for send, value in hop_sends(pieces_b, stage)]
        pieces_b = landed(pieces_b, stage, values)
    rest = [k for k in pieces_b if k and k not in firsts]
    moved, (ssd_out, states, conv_pre) = phase(
        [send for k in firsts[1:] for send in rounds(pieces_b[k])]
        + [(links.side, back_own[cuts[2]])],
        functools.partial(forward_call, heads, size, 2, 2),
        (all_lengths, conv_in, keys_queries, conv_rows, head_rows, before),
    )
    far_back.append(moved[-1])
    for at, k in enumerate(firsts[1:]):
        y_b[k] = moved[at * (sides - 1) : (at + 1) * (sides - 1)]
    gate_sends = [send for k in rest for send in rounds(pieces_b[k][:, :width])]
    out_sends = [send for k in rest for send in rounds(pieces_b[k][:, width:])]
    most_back = jnp.concatenate(far_back, axis=0)
    moved, _ = phase(
        gate_sends + [(links.side, back_own[cuts[3]]), (links.core, most_back)]
    )
    gate_moved, last_back, far_core_back = moved[:-2], moved[-2], moved[-1]

    def last_parts(values):
        latest = {k: values[at * (sides - 1) : (at + 1) * (sides - 1)] for at, k in enumerate(rest)}
        return parts_of(mine_b, from_core_b, pieces_b, {**y_b, **latest})

    moved, (w_gate, gate) = phase(
        out_sends + [(links.core, last_back)],
        functools.partial(project_call, links_shape, width, 0, 4, tokens, place),
        (last_parts(gate_moved), normed),
    )
    out_moved, last_core_back = moved[:-1], moved[-1]
    back_blocks = [
        back_own,
        core_back,
        jnp.concatenate([most_back, last_back], axis=0),
        jnp.concatenate([far_core_back, last_core_back], axis=0),
    ]
    w_out, d_branch, sums = branch_back_call(
        links_shape, width, 1, place, last_parts(out_moved), back_blocks, gate, ssd_out, conv_rows
    )
    moved, _ = phase([(links.core, sums), (links.side, sums), (links.corner, sums)])
    branch, d_gate, d_ssd, gain_rows = gating_back_call(
        inner, [sums, *moved], gate, ssd_out, d_branch, conv_rows
    )

    by_g = width // (3 * LANES) * 2 * LANES
    most = heads // 3 * 2
    less = heads - most
    most_width, less_width = most * size, less * size
    rows_all = 4 * tokens

    def backward(first_head, count, first_block, blocks, d_out, *before):
        return backward_call(
            count, size, first_head, first_block, blocks, all_lengths, core_place,
            conv_in, conv_pre, keys_queries, d_out, states, conv_rows, head_rows, before,
        )

    def turn(k):
        return lambda value: links.along_g(value, k)

    def a_sends(parts):
        return [
            (lambda value, j=j: links.along_a(value, j + 1), part) for j, part in enumerate(parts)
        ]

    def g_sends(parts):
        return [(turn(k + 1), part) for k, part in enumerate(parts)]

    def start(sends):
        return [send(value) for send, value in sends]

    count_a, count_g = sides - 1, groups - 1
    mixed_parts = dot_nt(branch, w_out).astype(BF16).reshape(2, 2, tokens, depth)
    mixed_keep, mixed_send = mixed_parts[:, 0], mixed_parts[:, 1]

    def first_grads(normed, d_gate, back_blocks, branch):
        def out_terms(columns, index):
            return [
                (block, tokens, 0, branch, at, columns, index)
                for at, block in enumerate(back_blocks)
            ]

        first = weight_grad_call(
            links_shape, True, place,
            [
                [(normed, rows_all, 0, d_gate, 0, width, 0)],
                out_terms(width - by_g, by_g // (width - by_g)),
            ],
        )
        return first, weight_grad_call(links_shape, False, place, [out_terms(by_g, 0)])

    moved, (first_parts, out_parts) = phase(
        [(links.core, mixed_send)], first_grads, (normed, d_gate, back_blocks, branch)
    )
    mixed_sum = mixed_keep.astype(F32) + moved[0].astype(F32)
    moved, (d_in_0, d_steps_0, kq_mine_0, kq_other_0, conv_grads_0, head_grads_0) = phase(
        a_sends(first_parts[1:])
        + g_sends(out_parts[1:])
        + [(links.side, mixed_sum[1].astype(BF16))],
        functools.partial(backward, 0, most, 0, 4),
        (d_ssd,),
    )
    mixed = hidden_in.astype(F32) + mixed_sum[0] + moved[-1].astype(F32)
    mixed = jnp.where(is_valid, mixed, 0.0).astype(BF16)
    first_held = combine_call(groups, place, [first_parts[0], *moved[:count_a]])
    values_0 = weight_grad_call(
        links_shape, True, place, [[(normed, rows_all, 0, d_in_0, 0, most_width, 0)]]
    )
    out_chip = total(out_parts[0], moved[count_a:-1]).astype(BF16)
    out_mine, out_others = links.parts_for_a(out_chip.reshape(sides, -1, by_g))
    first_held, values_0, d_ssd, mixed, out_mine, out_others = after(
        (first_held, values_0, d_ssd, mixed, out_mine, out_others)
    )
    first_sends = g_sends(first_held[1:])
    first_sends = first_sends[:1] + first_sends[-1:] + first_sends[1:-1]

    def back_project(first_row, d_in_1, d_steps):
        rows = slice(first_row, first_row + 2 * tokens)
        d_rest = jnp.concatenate([d_in_0[rows], d_in_1, d_steps], axis=1)
        return dot_nt(d_gate[rows], w_gate) + dot_nt(d_rest, w_values)

    def far_work(d_ssd):
        results = backward(most, less, 2, 2, d_ssd, kq_mine_0, kq_other_0)
        d_steps = d_steps_0[2 * tokens :] + results[1]
        return results, d_steps, back_project(2 * tokens, results[0], d_steps).astype(BF16)

    moved, (results, d_steps_far, d_far_parts) = phase(
        a_sends(values_0[1:]) + first_sends[:2], far_work, (d_ssd,)
    )
    first_far = moved[count_a:]
    d_in_far, _, kq_far_mine, kq_far_core, conv_grads_far, head_grads_far = results
    held_0 = combine_call(groups, place, [values_0[0], *moved[:count_a]])
    held_sends = g_sends(held_0[1:])
    held_sends = held_sends[:1] + held_sends[-1:] + held_sends[1:-1]

    moved, _ = phase([(links.core, kq_far_core), (links.core, d_far_parts[tokens:])])
    kq_far_sum = (kq_far_mine + moved[0].astype(F32)).astype(BF16)
    d_far = (d_far_parts[:tokens].astype(F32) + moved[1].astype(F32)).astype(BF16)
    moved, results = phase(
        [(links.side, kq_far_sum)]
        + first_sends[2:]
        + [(links.side, d_far[: tokens // 2])]
        + a_sends(out_others),
        functools.partial(backward, most, less, 0, 2),
        (d_ssd, kq_mine_0, kq_other_0),
    )
    d_in_near, d_steps_near, kq_near_mine, kq_near_core, conv_grads_near, head_grads_near = results
    kq_from_side = moved[0]
    first_far = first_far + moved[1 : count_g - 1]
    far_d = [moved[count_g - 1]]
    out_piece = total(out_mine, moved[count_g:]).astype(BF16)
    first_piece = total(first_held[0], first_far).astype(BF16)
    first_piece = jnp.concatenate([first_piece, out_piece], axis=1)
    d_steps_near = d_steps_0[: 2 * tokens] + d_steps_near
    d_steps = jnp.concatenate([d_steps_near, d_steps_far], axis=0)
    moved, d_near = phase(
        [(links.core, kq_near_core)] + held_sends[:1],
        functools.partial(back_project, 0),
        (d_in_near, d_steps_near),
    )
    held_far = moved[1:]
    d_kq_in, kq_grads = keys_back_call(
        all_lengths, [kq_near_mine, moved[0], kq_from_side], kq_in, kq_rows
    )
    half_rows = 2 * tokens

    def last_grads(normed, d_in_near, d_in_far, d_steps, d_kq_in):
        last = weight_grad_call(
            links_shape, True, place,
            [
                [
                    (normed, half_rows, 0, d_in_near, 0, less_width, 0),
                    (normed, half_rows, 1, d_in_far, 0, less_width, 0),
                ],
                [
                    (normed, half_rows, 0, d_steps, 0, LANES, 0),
                    (normed, half_rows, 1, d_steps, 1, LANES, 0),
                ],
                [(normed, half_rows, 0, d_kq_in, 0, state, 0)],
            ],
        )
        return last

    moved, last_parts_here = phase(
        rounds(first_piece) + held_sends[1:],
        last_grads,
        (normed, d_in_near, d_in_far, d_steps, d_kq_in),
    )
    first_y = moved[:count_a]
    held_far = held_far + moved[count_a:]
    held_piece = total(held_0[0], held_far).astype(BF16)
    first_rows = links.rows_of_core(links.join_a(first_piece, first_y))
    d_near_keep = d_near[:tokens] + dot_nt(d_kq_in[:tokens], w_kq)
    d_near_send = (d_near[tokens:] + dot_nt(d_kq_in[tokens:], w_kq)).astype(BF16)
    small = small_call(
        heads, size, channels, core_place,
        [conv_grads_0, conv_grads_far, conv_grads_near],
        [head_grads_0, head_grads_far, head_grads_near],
        gain_rows, kq_grads,
    )
    moved, _ = phase(
        a_sends(last_parts_here[1:])
        + [(links.side, d_far[tokens // 2 :]), (links.core, d_near_send), (links.core, small)]
        + [(links.core, first_rows[1])]
    )
    far_d.append(moved[count_a])
    d_near = d_near_keep + moved[count_a + 1].astype(F32)
    small = small + moved[count_a + 2]
    first_mine, first_core = first_rows[0], moved[-1]
    first_both = jnp.concatenate(
        [jnp.where(is_high, first_core, first_mine), jnp.where(is_high, first_mine, first_core)],
        axis=1,
    )
    last_held = combine_call(groups, place, [last_parts_here[0], *moved[:count_a]])
    first_half = first_both.shape[1] // (3 * LANES) * 2 * LANES
    moved, _ = phase(
        g_sends(last_held[1:])
        + [(links.side, first_both[:, :first_half])]
        + rounds(held_piece)
    )
    first_other = [moved[count_g]]
    last_piece = total(last_held[0], moved[:count_g]).astype(BF16)
    held_rows = links.rows_of_core(links.join_a(held_piece, moved[count_g + 1 :]))

    def final_norm(d_near, far_d):
        d_normed = d_near + far_d.astype(F32)
        own_hidden, own_scale = hidden_in.astype(F32), scale_own
        weighted = n_gain * d_normed
        inner_mean = jnp.mean(own_hidden * weighted, axis=-1, keepdims=True)
        return (
            back_own.astype(F32)
            + own_scale * weighted
            - own_hidden * (own_scale * own_scale * own_scale * inner_mean)
        )

    diagonals = [(lambda value, j=j: links.diagonal(value, j), last_piece) for j in range(1, sides)]
    moved, _ = phase(
        rounds(last_piece)
        + [(links.side, last_piece), (links.core, held_rows[1]), (swap(2), small)]
        + diagonals
        + [(links.side, first_both[:, first_half:])]
    )
    first_other.append(moved.pop())
    same_x = links.join_a(last_piece, moved[:count_a])
    held_core, small = moved[count_a + 1], small + moved[count_a + 2]
    other_x = links.join_a(moved[count_a], moved[count_a + 3 :])
    at_kq = less_width + LANES
    kq_both = same_x[:, at_kq:].astype(F32) + other_x[:, at_kq:].astype(F32)
    last_rows = links.rows_of_core(
        jnp.concatenate(
            [
                jnp.where(is_far, other_x, same_x)[:, :at_kq],
                jnp.where(is_far, same_x, other_x)[:, :at_kq],
                kq_both.astype(BF16),
            ],
            axis=1,
        )
    )
    held_both = jnp.concatenate(
        [jnp.where(is_high, held_core, held_rows[0]), jnp.where(is_high, held_rows[0], held_core)],
        axis=1,
    )
    moved, grad_hidden = phase(
        [(links.side, held_both), (links.core, last_rows[1]), (swap(4), small)],
        final_norm,
        (d_near, jnp.concatenate(far_d, axis=0)),
    )
    small = small + moved[2]
    bit = 8
    while bit < shards:
        small = small + links.flip(small, 0, bit)
        bit *= 2
    first_other = jnp.concatenate(first_other, axis=1)
    held_other, last_core = moved[0], moved[1]
    moved, (grad_in, grad_out, grad_norm) = phase(
        [(links.side, small)]
        + rounds(small)
        + [(lambda value, j=j: links.diagonal(value, j), small) for j in range(1, sides)],
        functools.partial(final_call, heads, size, most_width, by_g, core_place),
        (
            [first_both, first_other, held_both, held_other, last_rows[0], last_core],
            in_weight,
            norm_gain.astype(F32)[:, None],
        ),
    )
    small = total(small, moved)

    def own_slice(array, count):
        return lax.dynamic_slice_in_dim(array, links.shard * count, count, array.ndim - 1)

    grad_conv = own_slice(small[:5], channels // shards)
    grad_heads = [
        own_slice(small[7, field * LANES : field * LANES + all_heads], all_heads // shards)
        for field in range(3)
    ]
    return (
        mixed,
        grad_hidden,
        grad_norm[:, 0],
        grad_in,
        grad_conv[:4],
        grad_conv[4],
        grad_heads[0],
        grad_heads[1],
        grad_heads[2],
        own_slice(small[5, :inner], inner // shards),
        grad_out.T,
    )


def solution(mesh):
    return jax.shard_map(
        functools.partial(per_device, mesh.shape["rep"], mesh.shape["fsdp"]),
        mesh=mesh,
        in_specs=(
            P(("rep", "fsdp"), None),
            P(("rep", "fsdp"), None),
            P("fsdp"),
            P("fsdp", None),
            P(None, "fsdp"),
            P("fsdp"),
            P("fsdp"),
            P("fsdp"),
            P("fsdp"),
            P("fsdp"),
            P(None, "fsdp"),
            P(("rep", "fsdp"), None),
        ),
        out_specs=(
            P(("rep", "fsdp"), None),
            P(("rep", "fsdp"), None),
            P("fsdp"),
            P("fsdp", None),
            P(None, "fsdp"),
            P("fsdp"),
            P("fsdp"),
            P("fsdp"),
            P("fsdp"),
            P("fsdp"),
            P(None, "fsdp"),
        ),
        check_vma=False,
    )
```

```python
import functools

import jax
import jax.numpy as jnp
from jax import lax
from jax.experimental import pallas as pl
from jax.experimental.pallas import tpu as pltpu
from jax.sharding import PartitionSpec as P

EPS = 1e-05
CHUNK = 128
LANES = 128
HIGHEST = lax.Precision.HIGHEST
F32 = jnp.float32
BF16 = jnp.bfloat16


def dot(left, right, precision=None):
    return lax.dot_general(
        left, right, (((1,), (0,)), ((), ())), precision=precision, preferred_element_type=F32
    )


def dot_nt(left, right):
    return lax.dot_general(left, right, (((1,), (1,)), ((), ())), preferred_element_type=F32)


def sigmoid(v):
    return 0.5 * jnp.tanh(0.5 * v) + 0.5


def softplus(v):
    return jnp.maximum(v, 0.0) + jnp.log1p(jnp.exp(-jnp.abs(v)))


def begin_of(position, first, both):
    return jnp.where(position >= both, both, jnp.where(position >= first, first, 0))


def iotas(rows, columns):
    return (
        lax.broadcasted_iota(jnp.int32, (rows, columns), 0),
        lax.broadcasted_iota(jnp.int32, (rows, columns), 1),
    )


def conv_tile(u_ref, cw_ref, start, columns, masks):
    inputs = [u_ref[start : start + CHUNK, columns]]
    for delay in range(1, 4):
        if start:
            shifted = u_ref[start - delay : start - delay + CHUNK, columns]
        else:
            shifted = pltpu.roll(inputs[0], delay, 0)
        inputs.append(jnp.where(masks[delay - 1], shifted, 0.0))
    pre = cw_ref[4:5, columns] + cw_ref[3:4, columns] * inputs[0]
    for delay in range(1, 4):
        pre = pre + cw_ref[3 - delay : 4 - delay, columns] * inputs[delay]
    return pre


def chunk_rates(dt_ref, hp_ref, start):
    raw = dt_ref[start : start + CHUNK, :] + hp_ref[0:1, :]
    step = softplus(raw)
    rate = -jnp.exp(hp_ref[1:2, :]) * step
    row, column = iotas(CHUNK, CHUNK)
    running = dot((row >= column).astype(F32), rate, HIGHEST)
    return raw, step, rate, running


def pair_of(low, matrix, head):
    return jnp.where(low, matrix[:, head : head + 1], matrix[:, head + 1 : head + 2])


def forward_kernel(heads, size, first_block, len_ref, u_ref, dt_ref, kq_ref, cw_ref, hp_ref, *refs):
    y_ref, st_ref, pre_ref, state = refs[-4:]
    block = first_block + pl.program_id(0)
    first = len_ref[block, 0]
    both = first + len_ref[block, 1]
    tokens = u_ref.shape[0]
    chunks = tokens // CHUNK
    row, column = iotas(CHUNK, CHUNK)
    low = column < size
    low_row = low[0:1, :]
    for ci in range(chunks):
        start = ci * CHUNK
        position = row + start
        begin = begin_of(position, first, both)
        masks = [position - delay >= begin for delay in range(1, 4)]
        raw, step, rate, running = chunk_rates(dt_ref, hp_ref, start)
        running_t = running.T
        keys = kq_ref[start : start + CHUNK, :LANES]
        queries = kq_ref[start : start + CHUNK, LANES:]
        keys_t = keys.astype(F32).T.astype(BF16)
        allowed = (column <= row) & (column + start >= begin)
        scores = jnp.where(allowed, dot_nt(queries, keys), 0.0)
        last_begin = begin_of(start + CHUNK - 1, first, both)
        source = position >= last_begin
        reached = begin < start
        ending = running[CHUNK - 1 : CHUNK, :]
        kept = jnp.where(last_begin < start, jnp.exp(ending), 0.0)
        for pair in range(heads // 2):
            h = 2 * pair
            columns = slice(pair * LANES, (pair + 1) * LANES)
            pre = conv_tile(u_ref, cw_ref, start, columns, masks)
            pre_ref[start : start + CHUNK, columns] = pre
            values = pre * sigmoid(pre)
            scaled = values * pair_of(low, step, h)
            weights = []
            for head in (h, h + 1):
                gap = running[:, head : head + 1] - running_t[head : head + 1, :]
                weights.append((scores * jnp.exp(jnp.minimum(gap, 0.0))).astype(BF16))
            stacked = jnp.concatenate(
                [jnp.where(low, scaled, 0.0), jnp.where(low, 0.0, scaled)], axis=0
            ).astype(BF16)
            out = dot(jnp.concatenate(weights, axis=1), stacked)
            out = out + cw_ref[5:6, columns] * values
            across = pair_of(low, running, h)
            if ci:
                carried = dot(queries, state[:, columns].astype(BF16))
                out = out + jnp.where(reached, carried * jnp.exp(across), 0.0)
            y_ref[start : start + CHUNK, columns] = out
            if ci < chunks - 1:
                left = pair_of(low_row, ending, h) - across
                source_in = jnp.where(source, scaled * jnp.exp(left), 0.0).astype(BF16)
                fresh = dot(keys_t, source_in)
                if ci:
                    fresh = fresh + state[:, columns] * pair_of(low_row, kept, h)
                state[:, columns] = fresh
                st_ref[0, ci, :, columns] = fresh.astype(BF16)


def backward_kernel(
    heads,
    size,
    first_head,
    first_block,
    len_ref,
    at_ref,
    u_ref,
    pre_ref,
    dt_ref,
    kq_ref,
    dy_ref,
    st_ref,
    cw_ref,
    hp_ref,
    *refs,
):
    added = refs[:-10]
    du_ref, ddt_ref, mine_ref, other_ref, cg_ref, hg_ref = refs[-10:-4]
    d_state, d_pre, out_in, source_in = refs[-4:]
    is_high = at_ref[1] == 1
    block = pl.program_id(0)
    first = len_ref[first_block + block, 0]
    both = first + len_ref[first_block + block, 1]
    tokens, width = u_ref.shape
    chunks = tokens // CHUNK
    row, column = iotas(CHUNK, CHUNK)
    low = column < size
    low_row = low[0:1, :]
    wide_row, wide_column = iotas(2 * CHUNK, LANES)
    pick_row, pick_column = iotas(16, 2 * CHUNK)

    @pl.when(block == 0)
    def _():
        cg_ref[...] = jnp.zeros_like(cg_ref)
        hg_ref[...] = jnp.zeros_like(hg_ref)

    d_pre[tokens : tokens + 8, :] = jnp.zeros((8, width), F32)
    for ci in reversed(range(chunks)):
        start = ci * CHUNK
        has_later = ci < chunks - 1
        position = row + start
        begin = begin_of(position, first, both)
        ahead = [begin_of(position + delay, first, both) <= position for delay in range(1, 4)]
        raw, step, rate, running = chunk_rates(dt_ref, hp_ref, start)
        running_t = running.T
        keys = kq_ref[start : start + CHUNK, :LANES]
        queries = kq_ref[start : start + CHUNK, LANES:]
        allowed = (row <= column) & (position >= begin_of(column + start, first, both))
        scores = jnp.where(allowed, dot_nt(keys, queries), 0.0)
        last_begin = begin_of(start + CHUNK - 1, first, both)
        source = position >= last_begin
        reached = begin < start
        ending = running[CHUNK - 1 : CHUNK, :]
        kept = jnp.where(last_begin < start, jnp.exp(ending), 0.0)
        d_scores = jnp.zeros((CHUNK, CHUNK), F32)
        later_sums = jnp.zeros((16, CHUNK), F32)
        early_sums = jnp.zeros((CHUNK, LANES), F32)
        out_sums = jnp.zeros((CHUNK, LANES), F32)
        source_sums = jnp.zeros((CHUNK, LANES), F32)
        direct_sums = jnp.zeros((CHUNK, LANES), F32)
        kept_sums = jnp.zeros((8, LANES), F32)
        for pair in range(heads // 2):
            h = first_head + 2 * pair
            columns = slice(pair * LANES, (pair + 1) * LANES)
            to_head = (column == h + (row >= size).astype(jnp.int32)).astype(BF16)
            pre = pre_ref[start : start + CHUNK, columns]
            inputs = u_ref[start : start + CHUNK, columns]
            gate = sigmoid(pre)
            values = pre * gate
            steps = pair_of(low, step, h)
            scaled = values * steps
            d_out = dy_ref[start : start + CHUNK, columns].astype(F32)
            d_low = d_out.astype(BF16)
            stacked = jnp.concatenate(
                [jnp.where(low, scaled, 0.0), jnp.where(low, 0.0, scaled)], axis=0
            ).astype(BF16)
            d_weights = dot_nt(stacked, d_low)
            weights, products = [], []
            for at, head in enumerate((h, h + 1)):
                gap = running_t[head : head + 1, :] - running[:, head : head + 1]
                decay = jnp.exp(jnp.minimum(gap, 0.0))
                d_decayed = decay * d_weights[at * CHUNK : (at + 1) * CHUNK]
                d_scores = d_scores + d_decayed
                products.append((scores * d_decayed).astype(BF16))
                weights.append((scores * decay).astype(BF16))
            early = wide_column == h + (wide_row >= CHUNK).astype(jnp.int32)
            early_sums = early_sums + dot(jnp.concatenate(products, axis=1), early.astype(BF16))
            later = pick_row == h + (pick_column >= CHUNK).astype(jnp.int32)
            later_sums = later_sums + dot(later.astype(BF16), jnp.concatenate(products, axis=0))
            d_stacked = jnp.concatenate(
                [jnp.where(low, d_out, 0.0), jnp.where(low, 0.0, d_out)], axis=0
            ).astype(BF16)
            d_scaled = dot(jnp.concatenate(weights, axis=1), d_stacked)
            across = pair_of(low, running, h)
            if has_later:
                left = jnp.exp(pair_of(low_row, ending, h) - across)
                left = jnp.where(source, left, 0.0)
                d_state_here = d_state[:, columns]
                d_source = dot(keys, d_state_here.astype(BF16)) * left
                d_scaled = d_scaled + d_source
                source_sums = source_sums + dot((scaled * d_source).astype(BF16), to_head)
                source_in[:, columns] = (scaled * left).astype(BF16)
            if ci:
                before = st_ref[0, ci - 1, :, columns]
                d_reach = jnp.where(reached, d_out * jnp.exp(across), 0.0)
                out_sums = out_sums + dot((d_reach * dot(queries, before)).astype(BF16), to_head)
                out_in[:, columns] = d_reach.astype(BF16)
                if has_later:
                    held = jnp.sum(d_state_here * before.astype(F32), axis=0, keepdims=True)
                    held = held * pair_of(low_row, kept, h)
                    kept_sums = kept_sums + dot(
                        jnp.broadcast_to(held, (8, LANES)), to_head.astype(F32), HIGHEST
                    )
            direct_sums = direct_sums + dot((d_scaled * values).astype(BF16), to_head)
            d_values = d_scaled * steps + cw_ref[5:6, columns] * d_out
            cg_ref[5:6, columns] += jnp.sum(d_out * values, axis=0, keepdims=True)
            d_here = d_values * (gate * (1.0 + pre * (1.0 - gate)))
            d_pre[start : start + CHUNK, columns] = d_here
            d_in = cw_ref[3:4, columns] * d_here
            cg_ref[3:4, columns] += jnp.sum(inputs * d_here, axis=0, keepdims=True)
            for delay in range(1, 4):
                shifted = d_pre[start + delay : start + delay + CHUNK, columns]
                shifted = jnp.where(ahead[delay - 1], shifted, 0.0)
                d_in = d_in + cw_ref[3 - delay : 4 - delay, columns] * shifted
                cg_ref[3 - delay : 4 - delay, columns] += jnp.sum(
                    inputs * shifted, axis=0, keepdims=True
                )
            du_ref[start : start + CHUNK, columns] = d_in.astype(BF16)
            cg_ref[4:5, columns] += jnp.sum(d_here, axis=0, keepdims=True)
        d_scores = jnp.where(allowed, d_scores, 0.0)
        d_keys = dot(d_scores.astype(BF16), queries)
        d_queries = dot(d_scores.T.astype(BF16), keys)
        d_running = (
            jnp.concatenate([later_sums, jnp.zeros((CHUNK - 16, CHUNK), F32)], axis=0).T
            - early_sums
            + out_sums
            - source_sums
        )
        if has_later:
            d_keys = d_keys + dot_nt(source_in[...], d_state[...].astype(BF16))
            at_end = jnp.sum(source_sums, axis=0, keepdims=True) + kept_sums[0:1, :]
            d_running = d_running + jnp.where(row == CHUNK - 1, at_end, 0.0)
        if ci:
            d_queries = d_queries + dot_nt(out_in[...], st_ref[0, ci - 1])
            queries_t = queries.astype(F32).T.astype(BF16)
            for pair in range(heads // 2):
                columns = slice(pair * LANES, (pair + 1) * LANES)
                fresh = dot(queries_t, out_in[:, columns])
                if has_later:
                    fresh = fresh + d_state[:, columns] * pair_of(low_row, kept, first_head + 2 * pair)
                d_state[:, columns] = fresh
        here = slice(start, start + CHUNK)
        mine = jnp.where(is_high, d_queries, d_keys)
        other = jnp.where(is_high, d_keys, d_queries)
        if added:
            mine, other = mine + added[0][here, :], other + added[1][here, :]
        mine_ref[here, :] = mine.astype(mine_ref.dtype)
        other_ref[here, :] = other.astype(other_ref.dtype)
        d_rate = dot((row <= column).astype(F32), d_running, HIGHEST)
        d_step = direct_sums - jnp.exp(hp_ref[1:2, :]) * d_rate
        d_raw = d_step * sigmoid(raw)
        ddt_ref[start : start + CHUNK, :] = d_raw.astype(BF16)
        hg_ref[0:1, :] += jnp.sum(d_raw, axis=0, keepdims=True)
        hg_ref[1:2, :] += jnp.sum(d_rate * rate, axis=0, keepdims=True)


def prepare_first_kernel(heads, size, state, at_ref, in_ref, mine_ref, other_ref):
    x, core = at_ref[0], at_ref[1]
    width = heads * size
    inner = 4 * width
    steps_at = 2 * inner + 2 * state
    steps = in_ref[:, steps_at : steps_at + 4 * heads].astype(F32)
    rows = steps.shape[0]
    steps = jnp.concatenate([steps, jnp.zeros((rows, LANES - 4 * heads), F32)], axis=1)
    column = lax.broadcasted_iota(jnp.int32, (rows, LANES), 1)
    for ref, c in ((mine_ref, core), (other_ref, 1 - core)):
        p = 2 * x + c
        values_at = pl.multiple_of(inner + p * width, LANES)
        ref[:, :width] = in_ref[:, pl.ds(values_at, width)]
        drawn = pltpu.roll(steps, lax.rem(LANES - heads * p, LANES), 1)
        ref[:, width : width + LANES] = jnp.where(column < heads, drawn, 0.0).astype(BF16)
        keys_at = pl.multiple_of(2 * inner + c * state, LANES)
        ref[:, width + LANES : width + LANES + state] = in_ref[:, pl.ds(keys_at, state)]


def prepare_last_kernel(width, at_ref, in_ref, out_ref, mine_ref, other_ref):
    x, core = at_ref[0], at_ref[1]
    for ref, c in ((mine_ref, core), (other_ref, 1 - core)):
        at = pl.multiple_of((2 * x + c) * width, LANES)
        ref[:, :width] = in_ref[:, pl.ds(at, width)]
        ref[:, width:] = out_ref[:, pl.ds(at, width)]


def prepare_call(kernel, columns, place, *weights):
    rows = weights[0].shape[0]
    return pl.pallas_call(
        kernel,
        in_specs=[pl.BlockSpec(memory_space=pltpu.SMEM)]
        + [pl.BlockSpec(memory_space=pltpu.VMEM)] * len(weights),
        out_specs=[pl.BlockSpec(memory_space=pltpu.VMEM)] * 2,
        out_shape=[jax.ShapeDtypeStruct((rows, columns), BF16)] * 2,
        compiler_params=pltpu.CompilerParams(vmem_limit_bytes=24 * 1024 * 1024),
        name="prepare",
    )(place, *weights)


def unpack_kernel(sizes, heads, size, state, at_ref, small_ref, n_ref, conv_ref, head_ref, kq_ref, all_ref):
    conv_size, gate_size, norm_size, head_size = sizes
    x, c = at_ref[0], at_ref[1]
    p = 2 * x + c
    shards = small_ref.shape[0] // 8
    width = heads * size

    def joined(first_row, rows, at, part, columns):
        padded = -(-columns // LANES) * LANES
        lanes = -(-part // LANES) * LANES
        lane = lax.broadcasted_iota(jnp.int32, (8, lanes), 1)
        result = jnp.zeros((8, padded), F32)
        for f in range(shards):
            rows_here = small_ref[8 * f : 8 * f + 8, at : at + lanes].astype(F32)
            rows_here = jnp.where(lane < part, rows_here, 0.0)
            if padded > lanes:
                rows_here = jnp.concatenate(
                    [rows_here, jnp.zeros((8, padded - lanes), F32)], axis=1
                )
            result = result + pltpu.roll(rows_here, (part * f) % padded, 1)
        return result[first_row : first_row + rows]

    conv_all = joined(0, 5, 0, conv_size, conv_size * shards)
    gate_all = joined(5, 1, 0, gate_size, gate_size * shards)
    norm_all = joined(6, 1, 0, norm_size, norm_size * shards)
    n_ref[...] = jnp.broadcast_to(norm_all, n_ref.shape)
    all_ref[...] = jnp.zeros_like(all_ref)
    all_ref[0:5, : conv_all.shape[1]] = conv_all
    all_ref[6:7, : gate_all.shape[1]] = gate_all
    conv_ref[...] = all_ref[:, pl.ds(pl.multiple_of(p * width, LANES), width)]
    kq_at = 4 * width + c * state
    kq_ref[...] = all_ref[:, pl.ds(pl.multiple_of(kq_at, LANES), state)]
    column = lax.broadcasted_iota(jnp.int32, (8, LANES), 1)
    head_ref[...] = jnp.zeros_like(head_ref)
    for row in range(3):
        values = joined(7, 1, row * LANES, head_size, head_size * shards)
        values = jnp.broadcast_to(values, (8, LANES))
        values = pltpu.roll(values, lax.rem(LANES - heads * p, LANES), 1)
        head_ref[row : row + 1, :] = jnp.where(column < heads, values, 0.0)[0:1]
    row_at, column_at = iotas(LANES, width)
    spread = (row_at == column_at // size).astype(F32)
    conv_ref[5:6, :] = dot(head_ref[...], spread, HIGHEST)[2:3]


def unpack_call(sizes, heads, size, state, place, small):
    shards = small.shape[0] // 8
    depth, width = sizes[2] * shards, heads * size
    columns = -(-sizes[0] * shards // LANES) * LANES
    return pl.pallas_call(
        functools.partial(unpack_kernel, sizes, heads, size, state),
        in_specs=[
            pl.BlockSpec(memory_space=pltpu.SMEM),
            pl.BlockSpec(memory_space=pltpu.VMEM),
        ],
        out_specs=[pl.BlockSpec(memory_space=pltpu.VMEM)] * 4,
        out_shape=[
            jax.ShapeDtypeStruct((8, depth), F32),
            jax.ShapeDtypeStruct((8, width), F32),
            jax.ShapeDtypeStruct((8, LANES), F32),
            jax.ShapeDtypeStruct((8, state), F32),
        ],
        scratch_shapes=[pltpu.VMEM((8, columns), F32)],
        compiler_params=pltpu.CompilerParams(vmem_limit_bytes=24 * 1024 * 1024),
        name="unpack",
    )(place, small)


def assemble_rows(links_shape, at_ref, own_ref, core_ref, pieces, whole_ref):
    sides, groups = links_shape
    a, g, c = at_ref[0], at_ref[1], at_ref[2]
    rows = own_ref.shape[0]
    part = 2 * rows // sides
    base = g * (2 * rows)
    whole_ref[pl.ds(pl.multiple_of(base + c * rows, 16), rows), :] = own_ref[...]
    whole_ref[pl.ds(pl.multiple_of(base + (1 - c) * rows, 16), rows), :] = core_ref[...]
    for k in range(1, groups):
        base = lax.rem(g + groups - k, groups) * (2 * rows)
        for j in range(sides):
            at = base + lax.rem(a + sides - j, sides) * part
            piece = pieces[(k - 1) * sides + j]
            whole_ref[pl.ds(pl.multiple_of(at, 16), part), :] = piece[...]


def project_kernel(links_shape, at_ref, own_ref, core_ref, *refs):
    pieces, (rows_ref, whole_ref, out_ref) = refs[:-3], refs[-3:]

    @pl.when(pl.program_id(0) == 0)
    def _():
        assemble_rows(links_shape, at_ref, own_ref, core_ref, pieces, whole_ref)

    out_ref[...] = dot(rows_ref[...], whole_ref[...]).astype(out_ref.dtype)


def whole_spec(array):
    return pl.BlockSpec(array.shape, lambda b: (0,) * array.ndim)


def columns_spec(array, width, index):
    if array.shape[1] == width:
        index = 0
    return pl.BlockSpec((array.shape[0], width), lambda b: (0, index))


def project_call(links_shape, width, index, blocks, tokens, kind, place, parts, rows):
    depth = rows.shape[1]
    return pl.pallas_call(
        functools.partial(project_kernel, links_shape),
        grid=(blocks,),
        in_specs=[pl.BlockSpec(memory_space=pltpu.SMEM)]
        + [columns_spec(array, width, index) for array in parts]
        + [pl.BlockSpec((tokens, depth), lambda b: (b, 0))],
        out_specs=[
            pl.BlockSpec((depth, width), lambda b: (0, 0)),
            pl.BlockSpec((tokens, width), lambda b: (b, 0)),
        ],
        out_shape=[
            jax.ShapeDtypeStruct((depth, width), BF16),
            jax.ShapeDtypeStruct((blocks * tokens, width), kind),
        ],
        compiler_params=pltpu.CompilerParams(vmem_limit_bytes=40 * 1024 * 1024),
        cost_estimate=pl.CostEstimate(
            flops=2 * rows.size * width, bytes_accessed=2 * rows.size, transcendentals=0
        ),
        name="project",
    )(place, *parts, rows)


def branch_back_kernel(links_shape, counts, at_ref, own_ref, core_ref, *refs):
    pieces, rows_refs = refs[: -6 - sum(counts)], list(refs[-6 - sum(counts) : -6])
    gate_ref, ssd_ref, cw_ref, whole_ref, out_ref, sums_ref = refs[-6:]
    block = pl.program_id(0)

    @pl.when(block == 0)
    def _():
        assemble_rows(links_shape, at_ref, own_ref, core_ref, pieces, whole_ref)

    for at, count in enumerate(counts):
        parts = [rows_refs.pop(0) for _ in range(count)]

        @pl.when(block == at)
        def _():
            first_row = 0
            for part in parts:
                stop = first_row + part.shape[0]
                out_ref[first_row:stop, :] = dot(part[...], whole_ref[...])
                first_row = stop

    tokens, width = out_ref.shape
    sums_ref[...] = jnp.zeros_like(sums_ref)
    for start in range(0, tokens, CHUNK):
        squares = jnp.zeros((CHUNK, LANES), F32)
        products = jnp.zeros((CHUNK, LANES), F32)
        for left in range(0, width, LANES):
            tile = (slice(start, start + CHUNK), slice(left, left + LANES))
            gate = gate_ref[tile].astype(F32)
            gated = ssd_ref[tile] * (gate * sigmoid(gate))
            squares = squares + gated * gated
            products = products + gated * (cw_ref[6:7, left : left + LANES] * out_ref[tile])
        sums_ref[0:1, start : start + CHUNK] = jnp.sum(squares.T, axis=0, keepdims=True)
        sums_ref[1:2, start : start + CHUNK] = jnp.sum(products.T, axis=0, keepdims=True)


def branch_back_call(links_shape, width, index, place, parts, rows, gate, ssd_out, conv_rows):
    tokens, depth = ssd_out.shape[0] // 4, rows[0][0].shape[1]
    counts = [len(block) for block in rows]
    rows = [part for block in rows for part in block]
    block = pl.BlockSpec((tokens, width), lambda b: (b, 0))
    return pl.pallas_call(
        functools.partial(branch_back_kernel, links_shape, counts),
        grid=(4,),
        in_specs=[pl.BlockSpec(memory_space=pltpu.SMEM)]
        + [columns_spec(array, width, index) for array in parts]
        + [whole_spec(array) for array in rows]
        + [block, block, pl.BlockSpec((8, width), lambda b: (0, 0))],
        out_specs=[
            pl.BlockSpec((depth, width), lambda b: (0, 0)),
            block,
            pl.BlockSpec((8, tokens), lambda b: (0, b)),
        ],
        out_shape=[
            jax.ShapeDtypeStruct((depth, width), BF16),
            jax.ShapeDtypeStruct((4 * tokens, width), F32),
            jax.ShapeDtypeStruct((8, 4 * tokens), F32),
        ],
        compiler_params=pltpu.CompilerParams(vmem_limit_bytes=56 * 1024 * 1024),
        cost_estimate=pl.CostEstimate(
            flops=8 * tokens * depth * width, bytes_accessed=8 * tokens * depth, transcendentals=0
        ),
        name="branch_back",
    )(place, *parts, *rows, gate, ssd_out, conv_rows)


def gating_back_kernel(
    inner, sums_ref, core_ref, side_ref, both_ref, gate_ref, ssd_ref, db_ref, cw_ref,
    branch_ref, dgate_ref, dssd_ref, gain_ref
):
    @pl.when(pl.program_id(0) == 0)
    def _():
        gain_ref[...] = jnp.zeros_like(gain_ref)

    sums = sums_ref[...] + core_ref[...] + side_ref[...] + both_ref[...]
    scale_row = lax.rsqrt(sums[0:1, :] * (1.0 / inner) + EPS)
    cross_row = scale_row * scale_row * scale_row * (sums[1:2, :] * (1.0 / inner))
    tokens, width = gate_ref.shape
    for start in range(0, tokens, CHUNK):
        stacked = jnp.concatenate(
            [scale_row[:, start : start + CHUNK], cross_row[:, start : start + CHUNK],
             jnp.zeros((CHUNK - 2, CHUNK), F32)], axis=0
        ).T
        scale, cross = stacked[:, 0:1], stacked[:, 1:2]
        for left in range(0, width, LANES):
            columns = slice(left, left + LANES)
            tile = (slice(start, start + CHUNK), columns)
            gate, ssd, d_branch = gate_ref[tile].astype(F32), ssd_ref[tile], db_ref[tile]
            gain = cw_ref[6:7, columns]
            sig = sigmoid(gate)
            act = gate * sig
            gated = ssd * act
            scaled = gated * scale
            branch_ref[tile] = (scaled * gain).astype(BF16)
            gain_ref[0:1, columns] += jnp.sum(d_branch * scaled, axis=0, keepdims=True)
            d_gated = scale * (gain * d_branch) - gated * cross
            dssd_ref[tile] = d_gated * act
            dgate_ref[tile] = (d_gated * ssd * (sig * (1.0 + gate * (1.0 - sig)))).astype(BF16)


def gating_back_call(inner, sums, gate, ssd_out, d_branch, conv_rows):
    rows, columns = gate.shape
    tokens = rows // 4
    block = pl.BlockSpec((tokens, columns), lambda b: (b, 0))
    order = [lambda b: (0, b)]
    order.append(lambda b: (0, b + 1 - 2 * lax.rem(b, 2)))
    order.append(lambda b: (0, lax.rem(b + 2, 4)))
    order.append(lambda b: (0, 3 - b))
    return pl.pallas_call(
        functools.partial(gating_back_kernel, inner),
        grid=(4,),
        in_specs=[pl.BlockSpec((8, tokens), index) for index in order]
        + [block, block, block, pl.BlockSpec((8, columns), lambda b: (0, 0))],
        out_specs=[block, block, block, pl.BlockSpec((8, columns), lambda b: (0, 0))],
        out_shape=[
            jax.ShapeDtypeStruct((rows, columns), BF16),
            jax.ShapeDtypeStruct((rows, columns), BF16),
            jax.ShapeDtypeStruct((rows, columns), F32),
            jax.ShapeDtypeStruct((8, columns), F32),
        ],
        compiler_params=pltpu.CompilerParams(vmem_limit_bytes=40 * 1024 * 1024),
        cost_estimate=pl.CostEstimate(
            flops=20 * rows * columns, bytes_accessed=20 * rows * columns, transcendentals=0
        ),
        name="gating_back",
    )(*sums, gate, ssd_out, d_branch, conv_rows)


def normalize_kernel(*refs):
    rows_refs, (gain_ref, normed_ref, scale_ref) = refs[:4], refs[4:]
    for at, rows_ref in enumerate(rows_refs):

        @pl.when(pl.program_id(0) == at)
        def _():
            depth = rows_ref.shape[1]
            for start in range(0, rows_ref.shape[0], 64):
                rows = rows_ref[start : start + 64, :].astype(F32)
                mean = jnp.sum(rows * rows, axis=1, keepdims=True) * (1.0 / depth)
                scale = lax.rsqrt(mean + EPS)
                normed = rows * scale * gain_ref[0:1, :]
                normed_ref[start : start + 64, :] = normed.astype(BF16)
                scale_ref[start : start + 64, :] = jnp.broadcast_to(scale, (64, LANES))


def normalize_call(blocks, gain):
    tokens, depth = blocks[0].shape
    return pl.pallas_call(
        normalize_kernel,
        grid=(4,),
        in_specs=[whole_spec(block) for block in blocks] + [whole_spec(gain)],
        out_specs=[
            pl.BlockSpec((tokens, depth), lambda b: (b, 0)),
            pl.BlockSpec((tokens, LANES), lambda b: (b, 0)),
        ],
        out_shape=[
            jax.ShapeDtypeStruct((4 * tokens, depth), BF16),
            jax.ShapeDtypeStruct((4 * tokens, LANES), F32),
        ],
        compiler_params=pltpu.CompilerParams(vmem_limit_bytes=40 * 1024 * 1024),
        name="normalize",
    )(*blocks, gain)


def weight_grad_kernel(links_shape, groups_of_terms, over_a, at_ref, *refs):
    sides, groups = links_shape
    count = sum(len(terms) for terms in groups_of_terms)
    left_count = 1 + max(left_at for terms in groups_of_terms for left_at, _ in terms)
    lefts, rights = refs[:left_count], refs[left_count : left_count + count]
    outs, scratch = refs[left_count + count : -1], refs[-1]
    at_column, at_term = 0, 0
    for terms in groups_of_terms:
        result = None
        for left_at, first_row in terms:
            right = rights[at_term][...]
            term = lax.dot_general(
                lefts[left_at][first_row : first_row + right.shape[0], :],
                right,
                (((0,), (0,)), ((), ())),
                preferred_element_type=F32,
            )
            result = term if result is None else result + term
            at_term += 1
        width = result.shape[1]
        scratch[:, at_column : at_column + width] = result.astype(BF16)
        at_column += width
    if over_a:
        chips, part = outs[0].shape[0], outs[0].shape[1]
        for chip in range(chips):
            for j, out in enumerate(outs):
                at = (chip * sides + lax.rem(at_ref[0] + j, sides)) * part
                out[chip] = scratch[pl.ds(pl.multiple_of(at, 16), part), :]
        return
    rows = outs[0].shape[0]
    chips = scratch.shape[0] // rows
    for chip in range(chips):
        turn = lax.rem(pl.program_id(0) * chips + chip + groups - at_ref[1], groups)
        for k, out in enumerate(outs):

            @pl.when(turn == k)
            def _():
                out[...] = scratch[chip * rows : (chip + 1) * rows, :]


def weight_grad_call(links_shape, over_a, place, groups_of_terms):
    sides, groups = links_shape
    terms = [term for group in groups_of_terms for term in group]
    depth = terms[0][0].shape[1]
    columns = sum(group[0][5] for group in groups_of_terms)
    rows = depth // groups
    part = rows // sides
    chips = 1
    while chips * rows % LANES:
        chips += 1
    lefts = []
    for term in terms:
        if not any(term[0] is left for left in lefts):
            lefts.append(term[0])

    def left_at(term):
        return [term[0] is left for left in lefts].index(True)

    def left_spec(left):
        return pl.BlockSpec((left.shape[0], chips * rows), lambda b: (0, b))

    def right_spec(term):
        return pl.BlockSpec((term[1], term[5]), lambda b: (term[4], term[6]))

    if over_a:
        out_specs = [pl.BlockSpec((chips, part, columns), lambda b: (b, 0, 0))] * sides
        out_shape = [jax.ShapeDtypeStruct((groups, part, columns), BF16)] * sides
    else:
        out_specs = [pl.BlockSpec((rows, columns), lambda b: (0, 0))] * groups
        out_shape = [jax.ShapeDtypeStruct((rows, columns), BF16)] * groups
    shapes = tuple(
        tuple((left_at(term), term[1] * term[2]) for term in group) for group in groups_of_terms
    )
    return pl.pallas_call(
        functools.partial(weight_grad_kernel, links_shape, shapes, over_a),
        grid=(groups // chips,),
        in_specs=[pl.BlockSpec(memory_space=pltpu.SMEM)]
        + [left_spec(left) for left in lefts]
        + [right_spec(term) for term in terms],
        out_specs=out_specs,
        out_shape=out_shape,
        scratch_shapes=[pltpu.VMEM((chips * rows, columns), BF16)],
        compiler_params=pltpu.CompilerParams(vmem_limit_bytes=48 * 1024 * 1024),
        cost_estimate=pl.CostEstimate(
            flops=2 * terms[0][1] * depth * columns,
            bytes_accessed=2 * terms[0][1] * depth,
            transcendentals=0,
        ),
        name="weight_grad",
    )(place, *lefts, *[term[3] for term in terms])


def combine_kernel(groups, at_ref, *refs):
    parts, outs = refs[:-groups], refs[-groups:]
    result = parts[0][0].astype(F32)
    for part in parts[1:]:
        result = result + part[0].astype(F32)
    turn = lax.rem(pl.program_id(0) + groups - at_ref[1], groups)
    for k, out in enumerate(outs):

        @pl.when(turn == k)
        def _():
            out[...] = result.astype(BF16)


def combine_call(groups, place, parts):
    rows, columns = parts[0].shape[1:]
    return pl.pallas_call(
        functools.partial(combine_kernel, groups),
        grid=(groups,),
        in_specs=[pl.BlockSpec(memory_space=pltpu.SMEM)]
        + [pl.BlockSpec((1, rows, columns), lambda b: (b, 0, 0))] * len(parts),
        out_specs=[pl.BlockSpec((rows, columns), lambda b: (0, 0))] * groups,
        out_shape=[jax.ShapeDtypeStruct((rows, columns), BF16)] * groups,
        compiler_params=pltpu.CompilerParams(vmem_limit_bytes=24 * 1024 * 1024),
        name="combine",
    )(place, *parts)


def keys_front_kernel(len_ref, in_ref, rows_ref, out_ref):
    tokens, columns = in_ref.shape[0] // 2, in_ref.shape[1]
    position = lax.broadcasted_iota(jnp.int32, (tokens, columns), 0)
    row, lane = iotas(16, columns)
    counts = jnp.zeros((16, columns), jnp.int32)
    for block in range(2):
        first = len_ref[block, 0]
        both = first + len_ref[block, 1]
        begin = begin_of(position, first, both)
        inputs = in_ref[block * tokens : (block + 1) * tokens, :]
        pre = rows_ref[4:5, :] + rows_ref[3:4, :] * inputs
        for delay in range(1, 4):
            shifted = jnp.where(position - delay >= begin, pltpu.roll(inputs, delay, 0), 0.0)
            pre = pre + rows_ref[3 - delay : 4 - delay, :] * shifted
        out_ref[block * tokens : (block + 1) * tokens, :] = (pre * sigmoid(pre)).astype(BF16)
        for sequence in range(2):
            length = len_ref[block, sequence]
            here = row == block
            counts = jnp.where(here & (lane == 2 * sequence), lax.div(length, 32), counts)
            counts = jnp.where(here & (lane == 2 * sequence + 1), lax.rem(length, 32), counts)
    out_ref[2 * tokens :, :] = counts.astype(F32).astype(BF16)


def keys_front_call(lengths, inputs, rows):
    total, columns = inputs.shape
    return pl.pallas_call(
        keys_front_kernel,
        in_specs=[
            pl.BlockSpec(memory_space=pltpu.SMEM),
            pl.BlockSpec(memory_space=pltpu.VMEM),
            pl.BlockSpec(memory_space=pltpu.VMEM),
        ],
        out_specs=pl.BlockSpec(memory_space=pltpu.VMEM),
        out_shape=jax.ShapeDtypeStruct((total + 16, columns), BF16),
        compiler_params=pltpu.CompilerParams(vmem_limit_bytes=24 * 1024 * 1024),
        name="keys_front",
    )(lengths, inputs, rows)


def norm_back_kernel(keep_ref, core_ref, *refs):
    far_refs, (hidden_ref, back_ref, scale_ref, gain_ref, out_ref) = refs[:3], refs[3:]
    block = pl.program_id(0)
    far = jnp.where(block == 0, far_refs[0][...], far_refs[1][...])
    far = jnp.where(block <= 1, far, far_refs[2][...]).astype(F32)
    hidden, scale = hidden_ref[...].astype(F32), scale_ref[:, 0:1]
    weighted = gain_ref[0:1, :] * (keep_ref[...] + core_ref[...].astype(F32) + far)
    mean = jnp.sum(hidden * weighted, axis=1, keepdims=True) * (1.0 / hidden.shape[1])
    cross = scale * scale * scale * mean
    out_ref[...] = back_ref[...].astype(F32) + scale * weighted - hidden * cross


def norm_back_call(keep, core, far, hidden, back, scale, gain):
    tokens, depth = keep.shape
    rows = tokens // 4
    block = pl.BlockSpec((rows, depth), lambda b: (b, 0))
    quarter = pl.BlockSpec((rows, depth), lambda b: (0, 0))
    later = pl.BlockSpec((rows, depth), lambda b: (jnp.maximum(b - 2, 0), 0))
    return pl.pallas_call(
        norm_back_kernel,
        grid=(4,),
        in_specs=[
            block, block, quarter, quarter, later, block, block,
            pl.BlockSpec((rows, LANES), lambda b: (b, 0)),
            whole_spec(gain),
        ],
        out_specs=block,
        out_shape=jax.ShapeDtypeStruct((tokens, depth), F32),
        compiler_params=pltpu.CompilerParams(vmem_limit_bytes=32 * 1024 * 1024),
        cost_estimate=pl.CostEstimate(
            flops=4_000_000_000, bytes_accessed=12_000_000, transcendentals=0
        ),
        name="norm_back",
    )(keep, core, *far, hidden, back, scale, gain)


def keys_back_kernel(len_ref, mine_ref, core_ref, side_ref, in_ref, rows_ref, d_ref, grads_ref):
    block = pl.program_id(0)
    first = len_ref[block, 0]
    both = first + len_ref[block, 1]
    tokens, columns = in_ref.shape
    position = lax.broadcasted_iota(jnp.int32, (tokens, columns), 0)
    begin = begin_of(position, first, both)
    inside = [position - delay >= begin for delay in range(1, 4)]
    inputs = [in_ref[...]]
    for delay in range(1, 4):
        shifted = pltpu.roll(inputs[0], delay, 0)
        inputs.append(jnp.where(inside[delay - 1], shifted, 0.0))
    pre = rows_ref[4:5, :] + rows_ref[3:4, :] * inputs[0]
    for delay in range(1, 4):
        pre = pre + rows_ref[3 - delay : 4 - delay, :] * inputs[delay]
    sig = sigmoid(pre)
    d_out = mine_ref[...] + core_ref[...].astype(F32) + side_ref[...].astype(F32)
    d_pre = d_out * (sig * (1.0 + pre * (1.0 - sig)))
    d_in = rows_ref[3:4, :] * d_pre
    for delay in range(1, 4):
        moved = pltpu.roll(jnp.where(inside[delay - 1], d_pre, 0.0), tokens - delay, 0)
        d_in = d_in + rows_ref[3 - delay : 4 - delay, :] * moved
    d_ref[...] = d_in.astype(BF16)

    @pl.when(block == 0)
    def _():
        grads_ref[...] = jnp.zeros_like(grads_ref)

    for delay in range(4):
        grads_ref[3 - delay : 4 - delay, :] += jnp.sum(
            inputs[delay] * d_pre, axis=0, keepdims=True
        )
    grads_ref[4:5, :] += jnp.sum(d_pre, axis=0, keepdims=True)


def keys_back_call(lengths, parts, inputs, rows):
    total, columns = inputs.shape
    block = pl.BlockSpec((total // 2, columns), lambda b: (b, 0))
    small = pl.BlockSpec((8, columns), lambda b: (0, 0))
    return pl.pallas_call(
        keys_back_kernel,
        grid=(2,),
        in_specs=[pl.BlockSpec(memory_space=pltpu.SMEM)] + [block] * 4 + [small],
        out_specs=[block, small],
        out_shape=[
            jax.ShapeDtypeStruct((total, columns), BF16),
            jax.ShapeDtypeStruct((8, columns), F32),
        ],
        compiler_params=pltpu.CompilerParams(vmem_limit_bytes=24 * 1024 * 1024),
        name="keys_back",
    )(lengths, *parts, inputs, rows)


def small_kernel(heads, size, at_ref, *refs):
    convs, head_refs, (gain_ref, kq_ref, out_ref) = refs[:3], refs[3:6], refs[6:]
    p = 2 * at_ref[0] + at_ref[1]
    width = heads * size
    most, less = convs[0].shape[1], convs[1].shape[1]
    out_ref[...] = jnp.zeros_like(out_ref)
    rest = convs[1][...] + convs[2][...]
    at = pl.multiple_of(p * width, LANES)
    out_ref[0:5, pl.ds(at, most)] = convs[0][0:5, :]
    out_ref[0:5, pl.ds(pl.multiple_of(at + most, LANES), less)] = rest[0:5, :]
    kq_at = pl.multiple_of(4 * width + at_ref[1] * kq_ref.shape[1], LANES)
    out_ref[0:5, pl.ds(kq_at, kq_ref.shape[1])] = kq_ref[0:5, :]
    out_ref[5:6, pl.ds(at, width)] = gain_ref[0:1, :]
    skip = jnp.concatenate([convs[0][...], rest], axis=1)
    row, column = iotas(width, LANES)
    skip = dot(skip, (row // size == column).astype(F32), HIGHEST)
    sums = head_refs[0][...] + head_refs[1][...] + head_refs[2][...]
    for field, values in enumerate((sums[0:1], sums[1:2], skip[5:6])):
        values = jnp.broadcast_to(values, (8, LANES))
        lane = lax.broadcasted_iota(jnp.int32, (8, LANES), 1)
        values = pltpu.roll(jnp.where(lane < heads, values, 0.0), heads * p, 1)
        out_ref[7:8, field * LANES : (field + 1) * LANES] = values[0:1]


def small_call(heads, size, channels, place, convs, head_grads, gains, kq_grads):
    operands = [*convs, *head_grads, gains, kq_grads]
    return pl.pallas_call(
        functools.partial(small_kernel, heads, size),
        in_specs=[pl.BlockSpec(memory_space=pltpu.SMEM)]
        + [pl.BlockSpec(memory_space=pltpu.VMEM)] * len(operands),
        out_specs=pl.BlockSpec(memory_space=pltpu.VMEM),
        out_shape=jax.ShapeDtypeStruct((8, channels), F32),
        compiler_params=pltpu.CompilerParams(vmem_limit_bytes=24 * 1024 * 1024),
        name="small_gradients",
    )(place, *operands)


def final_kernel(heads, size, most, by_g, at_ref, *refs):
    first_both, first_other, held_mine, held_core, last_mine, last_core = refs[:6]
    weight_ref, gain_ref, in_ref, out_ref, norm_ref = refs[6:]
    far, high = at_ref[0] == 1, at_ref[1] == 1
    width = heads * size
    less = width - most
    rows = in_ref.shape[0]
    at_values, at_keys = 4 * width, 8 * width
    state = last_mine.shape[1] - 2 * (less + LANES)
    at_steps = at_keys + 2 * state
    norm = jnp.zeros((rows, 1), F32)

    def put(at, values):
        stop = at + values.shape[1]
        in_ref[:, at:stop] = values
        weight = weight_ref[:, at:stop].astype(F32)
        return jnp.sum(values * weight, axis=1, keepdims=True)

    def share(both, other, p, count, start, stop):
        columns = slice((p % 2) * count + start, (p % 2) * count + stop)
        take_other = far if p < 2 else jnp.logical_not(far)
        return jnp.where(take_other, other[:, columns], both[:, columns]).astype(F32)

    def core_share(mine, other, core, start, stop):
        take_other = high if core == 0 else jnp.logical_not(high)
        columns = slice(start, stop)
        return jnp.where(take_other, other[:, columns], mine[:, columns]).astype(F32)

    last_share = functools.partial(core_share, last_mine, last_core)
    held_share = functools.partial(core_share, held_mine, held_core)

    steps = jnp.zeros((rows, LANES), F32)
    lane = lax.broadcasted_iota(jnp.int32, (rows, LANES), 1)
    for p in range(4):
        first = functools.partial(share, first_both, first_other, p, 2 * width - by_g)
        norm = norm + put(p * width, first(0, width))
        left = (p // 2) * (by_g + most)
        out_ref[:, p * width : p * width + by_g] = held_share(p % 2, left, left + by_g)
        out_ref[:, p * width + by_g : (p + 1) * width] = first(width, 2 * width - by_g)
        at = at_values + p * width
        norm = norm + put(at, held_share(p % 2, left + by_g, left + by_g + most))
        left = (p // 2) * (less + LANES)
        norm = norm + put(at + most, last_share(p % 2, left, left + less))
        drawn = last_share(p % 2, left + less, left + less + LANES)
        steps = steps + pltpu.roll(jnp.where(lane < heads, drawn, 0.0), heads * p, 1)
    for core in range(2):
        at = 2 * (less + LANES)
        norm = norm + put(at_keys + core * state, last_share(core, at, at + state))
    norm = norm + put(at_steps, steps[:, : 4 * heads])
    norm_ref[...] = norm / gain_ref[...]


def final_call(heads, size, most, by_g, place, shares, weight, gain):
    rows, columns = weight.shape
    operands = [*shares, weight, gain]
    return pl.pallas_call(
        functools.partial(final_kernel, heads, size, most, by_g),
        in_specs=[pl.BlockSpec(memory_space=pltpu.SMEM)]
        + [pl.BlockSpec(memory_space=pltpu.VMEM)] * len(operands),
        out_specs=[pl.BlockSpec(memory_space=pltpu.VMEM)] * 3,
        out_shape=[
            jax.ShapeDtypeStruct((rows, columns), F32),
            jax.ShapeDtypeStruct((rows, 4 * heads * size), F32),
            jax.ShapeDtypeStruct((rows, 1), F32),
        ],
        compiler_params=pltpu.CompilerParams(vmem_limit_bytes=40 * 1024 * 1024),
        cost_estimate=pl.CostEstimate(
            flops=5_000_000_000, bytes_accessed=16_000_000, transcendentals=0
        ),
        name="owner_gradients",
    )(place, *operands)


def forward_call(
    heads, size, first_block, blocks, lengths, conv_in, keys_queries, conv_rows, head_rows, before=()
):
    total = conv_in.shape[0]
    tokens = total // lengths.shape[0]
    width = heads * size
    state = keys_queries.shape[1] // 2
    boundaries = tokens // CHUNK - 1
    return pl.pallas_call(
        functools.partial(forward_kernel, heads, size, first_block),
        grid=(blocks,),
        in_specs=[
            pl.BlockSpec(memory_space=pltpu.SMEM),
            pl.BlockSpec((tokens, width), lambda b: (first_block + b, 0)),
            pl.BlockSpec((tokens, LANES), lambda b: (first_block + b, width // LANES)),
            pl.BlockSpec((tokens, 2 * state), lambda b: (first_block + b, 0)),
            pl.BlockSpec((8, width), lambda b: (0, 0)),
            pl.BlockSpec((8, LANES), lambda b: (0, 0)),
        ]
        + [pl.BlockSpec(memory_space=pl.ANY)] * len(before),
        out_specs=[
            pl.BlockSpec((tokens, width), lambda b: (first_block + b, 0)),
            pl.BlockSpec((1, boundaries, state, width), lambda b: (first_block + b, 0, 0, 0)),
            pl.BlockSpec((tokens, width), lambda b: (first_block + b, 0)),
        ],
        out_shape=[
            jax.ShapeDtypeStruct((total, width), F32),
            jax.ShapeDtypeStruct((lengths.shape[0], boundaries, state, width), BF16),
            jax.ShapeDtypeStruct((total, width), F32),
        ],
        scratch_shapes=[pltpu.VMEM((state, width), F32)],
        input_output_aliases={6 + at: at for at in range(len(before))},
        compiler_params=pltpu.CompilerParams(vmem_limit_bytes=40 * 1024 * 1024),
        cost_estimate=pl.CostEstimate(
            flops=blocks * 3_000_000_000, bytes_accessed=blocks * 8_000_000, transcendentals=0
        ),
        name="ssd_forward",
    )(lengths, conv_in, conv_in, keys_queries, conv_rows, head_rows, *before)


def backward_call(
    heads, size, first_head, first_block, blocks,
    lengths, place, conv_in, conv_pre, keys_queries, d_out, states, conv_rows, head_rows, before=()
):
    tokens = conv_in.shape[0] // lengths.shape[0]
    total = blocks * tokens
    width = heads * size
    part = first_head * size // width
    steps_at = d_out.shape[1] // LANES
    state = keys_queries.shape[1] // 2
    boundaries = tokens // CHUNK - 1

    def rows_of(columns, index):
        return pl.BlockSpec((tokens, columns), lambda b: (first_block + b, index))

    def swapped(b):
        return b + 1 - 2 * lax.rem(b, 2)

    return pl.pallas_call(
        functools.partial(backward_kernel, heads, size, first_head, first_block),
        grid=(blocks,),
        in_specs=[
            pl.BlockSpec(memory_space=pltpu.SMEM),
            pl.BlockSpec(memory_space=pltpu.SMEM),
            rows_of(width, part),
            rows_of(width, part),
            rows_of(LANES, steps_at),
            rows_of(2 * state, 0),
            rows_of(width, part),
            pl.BlockSpec(
                (1, boundaries, state, width), lambda b: (first_block + b, 0, 0, part)
            ),
            pl.BlockSpec((8, width), lambda b: (0, part)),
            pl.BlockSpec((8, LANES), lambda b: (0, 0)),
        ]
        + [
            rows_of(state, 0),
            pl.BlockSpec((tokens, state), lambda b: (swapped(first_block + b), 0)),
        ][: len(before)],
        out_specs=[
            pl.BlockSpec((tokens, width), lambda b: (b, 0)),
            pl.BlockSpec((tokens, LANES), lambda b: (b, 0)),
            pl.BlockSpec((tokens, state), lambda b: (b, 0)),
            pl.BlockSpec((tokens, state), lambda b: (swapped(b), 0)),
            pl.BlockSpec((8, width), lambda b: (0, 0)),
            pl.BlockSpec((8, LANES), lambda b: (0, 0)),
        ],
        out_shape=[
            jax.ShapeDtypeStruct((total, width), BF16),
            jax.ShapeDtypeStruct((total, LANES), BF16),
            jax.ShapeDtypeStruct((total, state), F32),
            jax.ShapeDtypeStruct((total, state), BF16 if before else F32),
            jax.ShapeDtypeStruct((8, width), F32),
            jax.ShapeDtypeStruct((8, LANES), F32),
        ],
        scratch_shapes=[
            pltpu.VMEM((state, width), F32),
            pltpu.VMEM((tokens + 8, width), F32),
            pltpu.VMEM((CHUNK, width), BF16),
            pltpu.VMEM((CHUNK, width), BF16),
        ],
        compiler_params=pltpu.CompilerParams(vmem_limit_bytes=48 * 1024 * 1024),
        cost_estimate=pl.CostEstimate(
            flops=blocks * heads * 1_000_000_000,
            bytes_accessed=blocks * 8_000_000,
            transcendentals=0,
        ),
        name="ssd_backward",
    )(lengths, place, conv_in, conv_pre, conv_in, keys_queries, d_out, states, conv_rows, head_rows, *before)


def after(values):
    return lax.optimization_barrier(values)


def phase(sends, work=None, arguments=(), until=None):
    values, arguments = after(([value for _, value in sends], arguments))
    moved = [send(value) for (send, _), value in zip(sends, values)]
    done = work(*arguments) if work else ()
    moved, done, until = after((moved, done, until))
    return (moved, done) if until is None else (moved, done, until)


def total(first, others):
    result = first.astype(F32)
    for other in others:
        result = result + other.astype(F32)
    return result


class Links:
    def __init__(self, reps, shards):
        self.reps, self.shards = reps, shards
        self.sides, self.groups = reps // 2, shards // 2
        rep, shard = lax.axis_index("rep"), lax.axis_index("fsdp")
        self.rep, self.shard = rep, shard
        self.a, self.x = rep // 2, rep % 2
        self.g, self.c = shard // 2, shard % 2

    def send(self, value, target):
        pairs = []
        for r in range(self.reps):
            for f in range(self.shards):
                to_r, to_f = target(r, f)
                pairs.append((r * self.shards + f, to_r * self.shards + to_f))
        return lax.ppermute(value, ("rep", "fsdp"), pairs)

    def core(self, value):
        return self.send(value, lambda r, f: (r, f ^ 1))

    def side(self, value):
        return self.send(value, lambda r, f: (r ^ 1, f))

    def corner(self, value):
        return self.send(value, lambda r, f: (r ^ 1, f ^ 1))

    def along_a(self, value, by):
        return self.send(value, lambda r, f: (((r // 2 + by) % self.sides) * 2 + r % 2, f))

    def along_g(self, value, by):
        return self.send(value, lambda r, f: (r, ((f // 2 + by) % self.groups) * 2 + f % 2))

    def diagonal(self, value, by):
        return self.send(
            value, lambda r, f: (((r // 2 + by) % self.sides) * 2 + (r % 2 ^ 1), f)
        )

    def flip(self, value, bit_of_rep, bit_of_shard):
        return self.send(value, lambda r, f: (r ^ bit_of_rep, f ^ bit_of_shard))

    def round_g(self, piece):
        return [self.along_g(piece, k) for k in range(1, self.groups)]

    def piece_of(self, mine, from_core):
        if self.sides == 2:
            return jnp.where(self.a == self.c, mine, from_core)
        is_high = self.c == 1
        chip = jnp.concatenate(
            [jnp.where(is_high, from_core, mine), jnp.where(is_high, mine, from_core)], axis=0
        )
        part = chip.shape[0] // self.sides
        return lax.dynamic_slice_in_dim(chip, self.a * part, part, 0)

    def round_a(self, joined):
        return [self.along_a(joined, j) for j in range(1, self.sides)]

    def assemble(self, mine, from_core, joined, rounds):
        rows, columns = mine.shape
        part = 2 * rows // self.sides
        whole = jnp.zeros((rows * self.shards, columns), mine.dtype)
        base = self.g * 2 * rows
        whole = lax.dynamic_update_slice_in_dim(whole, mine, base + self.c * rows, 0)
        whole = lax.dynamic_update_slice_in_dim(whole, from_core, base + (1 - self.c) * rows, 0)
        for k in range(1, self.groups):
            base = ((self.g - k) % self.groups) * 2 * rows
            for j, pieces in enumerate([joined] + rounds):
                piece = pieces[(k - 1) * part : k * part]
                at = base + ((self.a - j) % self.sides) * part
                whole = lax.dynamic_update_slice_in_dim(whole, piece, at, 0)
        return whole

    def parts_for_a(self, view):
        axis = view.ndim - 3
        mine = lax.dynamic_index_in_dim(view, self.a, axis, keepdims=False)
        others = [
            lax.dynamic_index_in_dim(view, (self.a + j) % self.sides, axis, keepdims=False)
            for j in range(1, self.sides)
        ]
        return mine, others

    def parts_for_g(self, view):
        mine = lax.dynamic_index_in_dim(view, self.g, 0, keepdims=False)
        others = [
            lax.dynamic_index_in_dim(view, (self.g + k) % self.groups, 0, keepdims=False)
            for k in range(1, self.groups)
        ]
        return mine, others

    def send_a(self, others):
        return [self.along_a(part, j + 1) for j, part in enumerate(others)]

    def send_g(self, others):
        return [self.along_g(part, k + 1) for k, part in enumerate(others)]

    def chips_of(self, partial):
        rows = partial.shape[0] // (self.groups * self.sides)
        return partial.reshape(self.groups, self.sides, rows, partial.shape[1])

    def spread_a(self, piece):
        return [self.along_a(piece, j) for j in range(1, self.sides)]

    def join_a(self, piece, others):
        if self.sides == 2:
            is_high = self.a == 1
            return jnp.concatenate(
                [jnp.where(is_high, others[0], piece), jnp.where(is_high, piece, others[0])],
                axis=0,
            )
        part = piece.shape[0]
        chip = jnp.zeros((part * self.sides, piece.shape[1]), piece.dtype)
        for j, value in enumerate([piece] + others):
            at = ((self.a - j) % self.sides) * part
            chip = lax.dynamic_update_slice_in_dim(chip, value, at, 0)
        return chip

    def join_x(self, piece, other):
        is_far = self.x == 1
        return jnp.concatenate(
            [jnp.where(is_far, other, piece), jnp.where(is_far, piece, other)], axis=1
        )

    def rows_of_core(self, chip):
        rows = chip.shape[0] // 2
        is_high = self.c == 1
        mine = jnp.where(is_high, chip[rows:], chip[:rows])
        return mine, jnp.where(is_high, chip[:rows], chip[rows:])

    def shares(self, mine, from_core):
        columns = mine.shape[1] // 2
        is_high = self.c == 1
        low = jnp.where(is_high, from_core, mine)
        high = jnp.where(is_high, mine, from_core)
        return [low[:, :columns], high[:, :columns], low[:, columns:], high[:, columns:]]

    def sum_all(self, value):
        bit = 1
        while bit < self.shards:
            value = value + self.flip(value, 0, bit)
            bit *= 2
        bit = 1
        while bit < self.reps:
            value = value + self.flip(value, bit, 0)
            bit *= 2
        return value

    def group_blocks(self, value):
        far = self.side(value)
        return [value, self.core(value), far, self.core(far)]

    def core_sum(self, partials, link_type):
        tokens = partials.shape[0] // 2
        return partials[:tokens].astype(F32) + self.core(
            partials[tokens:].astype(link_type)
        ).astype(F32)


def per_device(
    reps,
    shards,
    hidden_in,
    lengths,
    norm_gain,
    in_weight,
    conv_weight,
    conv_bias,
    dt_bias,
    a_log,
    skip_gain,
    gate_gain,
    out_weight,
    cotangent,
):
    links = Links(reps, shards)
    tokens, depth = hidden_in.shape
    inner = gate_gain.shape[0] * shards
    channels = conv_bias.shape[0] * shards
    all_heads = dt_bias.shape[0] * shards
    state = (channels - inner) // 2
    size = inner // all_heads
    heads, width = all_heads // 4, inner // 4
    x, c = links.x, links.c
    p = 2 * x + c

    is_high, is_far = c == 1, x == 1
    far_hidden = links.side(hidden_in)
    ends = jnp.cumsum(lengths[0])
    positions = jnp.arange(tokens, dtype=jnp.int32)
    is_valid = (positions < ends[1])[:, None]
    back_own = jnp.where(is_valid, cotangent, jnp.zeros_like(cotangent))
    sides, groups = links.sides, links.groups
    links_shape = (sides, groups)
    place = jnp.stack([links.a, links.g, c]).astype(jnp.int32)

    lanes = max(conv_weight.shape[1], gate_gain.shape[0], norm_gain.shape[0], 3 * LANES)
    lanes = -(-lanes // LANES) * LANES

    def pack(conv_weight, conv_bias, gate_gain, norm_gain, *head_values):
        heads_row = jnp.concatenate(
            [jnp.pad(v, (0, LANES - v.shape[0])) for v in head_values]
        )
        rows = [conv_bias, gate_gain, norm_gain, heads_row[:lanes]]
        rows = [jnp.pad(row, (0, lanes - row.shape[0]))[None] for row in rows]
        taps_rows = jnp.pad(conv_weight, ((0, 0), (0, lanes - conv_weight.shape[1])))
        return jnp.concatenate([taps_rows, *rows], axis=0)

    small_in = (conv_weight, conv_bias, gate_gain, norm_gain, dt_bias, a_log, skip_gain)
    sizes = (conv_bias.shape[0], gate_gain.shape[0], norm_gain.shape[0], dt_bias.shape[0])

    first_columns, last_columns = width + LANES + state, 2 * width
    core_place = jnp.stack([x, c]).astype(jnp.int32)
    mine_a, for_core_a = prepare_call(
        functools.partial(prepare_first_kernel, heads, size, state),
        first_columns,
        core_place,
        in_weight,
    )

    def hops(pieces, stage):
        sends = [(stage, 1, pieces[stage - 1])]
        if groups - stage != stage:
            sends.append((groups - stage, groups - 1, pieces[(groups - stage + 1) % groups]))
        return sends

    def hop_sends(pieces, stage):
        return [
            ((lambda value, by=by: links.along_g(value, by)), value)
            for _, by, value in hops(pieces, stage)
        ]

    def landed(pieces, stage, values):
        at = [k for k, _, _ in hops(pieces, stage)]
        return {**pieces, **dict(zip(at, values))}

    def rounds(piece):
        return [(lambda value, j=j: links.along_a(value, j), piece) for j in range(1, sides)]

    def doubled(value, bit, other):
        upper = (links.shard // bit) % 2 == 1
        return jnp.concatenate(
            [jnp.where(upper, other, value), jnp.where(upper, value, other)], axis=0
        )

    def swap(bit):
        return lambda value: links.flip(value, 0, bit)

    (from_core_a,), _ = phase([(links.core, for_core_a)])
    pieces_a = {0: links.piece_of(mine_a, from_core_a)}

    def prepare_last(small_in, in_weight, out_weight):
        packed = pack(*small_in)
        small_pair = doubled(packed, 1, links.core(packed))
        small_four = doubled(small_pair, 2, links.flip(small_pair, 0, 2))
        kernel = functools.partial(prepare_last_kernel, width)
        last = prepare_call(kernel, last_columns, core_place, in_weight, out_weight)
        return small_four, last

    moved, (small_all, (mine_b, for_core_b)) = phase(
        hop_sends(pieces_a, 1) + [(links.core, lengths)],
        prepare_last,
        (small_in, in_weight, out_weight.T),
    )
    lengths_core = moved[-1]
    pieces_a = landed(pieces_a, 1, moved[:-1])
    firsts = [k for k in pieces_a if k]
    early, late = firsts[:1], firsts[1:]
    early_sends = [send for k in early for send in rounds(pieces_a[k])]
    moved, _ = phase(
        hop_sends(pieces_a, 2)
        + [(swap(4), small_all), (links.core, for_core_b)]
        + early_sends
    )
    hop_count = len(hops(pieces_a, 2))
    small_all = doubled(small_all, 4, moved[hop_count])
    from_core_b = moved[hop_count + 1]
    y_moved = moved[hop_count + 2 :]
    pieces_a = landed(pieces_a, 2, moved[:hop_count])
    pieces_b = {0: links.piece_of(mine_b, from_core_b)}
    bit = 8
    while bit < shards:
        small_all = doubled(small_all, bit, links.flip(small_all, 0, bit))
        bit *= 2
    for stage in range(3, groups // 2 + 1):
        values = [send(value) for send, value in hop_sends(pieces_a, stage)]
        pieces_a = landed(pieces_a, stage, values)
    pieces_a, pieces_b, far_hidden = after((pieces_a, pieces_b, far_hidden))
    late = late + [k for k in pieces_a if k and k not in firsts]
    late_sends = [send for k in late for send in rounds(pieces_a[k])]
    b_firsts = [send(value) for send, value in hop_sends(pieces_b, 1)]
    moved, parameters_here = phase(
        late_sends + [(links.core, hidden_in), (links.core, far_hidden)],
        functools.partial(unpack_call, sizes, heads, size, state, core_place),
        (small_all,),
    )
    core_hidden, far_core_hidden = moved[-2:]
    y_moved = y_moved + moved[:-2]
    y_a = {
        k: y_moved[at * (sides - 1) : (at + 1) * (sides - 1)] for at, k in enumerate(early + late)
    }
    n_rows, conv_rows, head_rows, kq_rows = parameters_here

    def parts_of(mine, from_core, pieces, rounds_of):
        parts = [mine, from_core]
        for k in range(1, groups):
            parts += [pieces[k], *rounds_of[k]]
        return parts

    parts_a = parts_of(mine_a, from_core_a, pieces_a, y_a)
    pair_lengths = jnp.concatenate([lengths, lengths_core], axis=0)
    normed, scale = normalize_call([hidden_in, core_hidden, far_hidden, far_core_hidden], n_rows)
    kq_index = (width + LANES) // state
    w_kq, kq_in = project_call(
        links_shape, state, kq_index, 2, tokens, F32, place, parts_a, normed
    )
    kq_near = keys_front_call(pair_lengths, kq_in, kq_rows)
    half, quarter = tokens // 2, tokens // 4
    cuts = [slice(0, half), slice(half, half + quarter), slice(half + quarter, tokens)]
    moved, (w_values, conv_in), b_firsts = phase(
        [
            (links.side, kq_near),
            (links.side, back_own[cuts[1]]),
        ],
        functools.partial(project_call, links_shape, width + LANES, 0, 4, tokens, F32, place),
        (parts_a, normed),
        b_firsts,
    )
    pieces_b = landed(pieces_b, 1, b_firsts)
    kq_far, far_back = moved[0], [None, moved[1]]
    counts_at = slice(2 * tokens, 2 * tokens + 2)
    all_counts = jnp.concatenate([kq_near[counts_at, :4], kq_far[counts_at, :4]], axis=0)
    all_counts = all_counts.astype(jnp.int32)
    all_lengths = all_counts[:, 0::2] * 32 + all_counts[:, 1::2]
    kq_half = jnp.concatenate([kq_near[: 2 * tokens], kq_far[: 2 * tokens]], axis=0)

    (kq_core,), _ = phase([(links.core, kq_half)])
    kq_core = kq_core.reshape(2, 2, tokens, state)[:, ::-1].reshape(4 * tokens, state)
    keys_queries = jnp.concatenate(
        [jnp.where(is_high, kq_core, kq_half), jnp.where(is_high, kq_half, kq_core)], axis=1
    )
    firsts = [k for k in pieces_b if k]
    hop_count = len(hops(pieces_b, 2))
    moved, before = phase(
        hop_sends(pieces_b, 2)
        + rounds(pieces_b[firsts[0]])
        + [(links.side, back_own[cuts[0]]), (links.core, back_own)],
        functools.partial(forward_call, heads, size, 0, 2),
        (all_lengths, conv_in, keys_queries, conv_rows, head_rows),
    )
    y_b = {firsts[0]: moved[hop_count:-2]}
    far_back[0] = moved[-2]
    core_back = moved[-1]
    pieces_b = landed(pieces_b, 2, moved[:hop_count])
    for stage in range(3, groups // 2 + 1):
        values = [send(value) for send, value in hop_sends(pieces_b, stage)]
        pieces_b = landed(pieces_b, stage, values)
    rest = [k for k in pieces_b if k and k not in firsts]
    moved, (ssd_out, states, conv_pre) = phase(
        [send for k in firsts[1:] for send in rounds(pieces_b[k])]
        + [(links.side, back_own[cuts[2]])],
        functools.partial(forward_call, heads, size, 2, 2),
        (all_lengths, conv_in, keys_queries, conv_rows, head_rows, before),
    )
    far_back.append(moved[-1])
    for at, k in enumerate(firsts[1:]):
        y_b[k] = moved[at * (sides - 1) : (at + 1) * (sides - 1)]
    gate_sends = [send for k in rest for send in rounds(pieces_b[k][:, :width])]
    out_sends = [send for k in rest for send in rounds(pieces_b[k][:, width:])]
    moved, _ = phase(gate_sends + [(links.core, part) for part in far_back])
    gate_moved, far_core_back = moved[: len(gate_sends)], moved[len(gate_sends) :]

    def last_parts(values):
        latest = {k: values[at * (sides - 1) : (at + 1) * (sides - 1)] for at, k in enumerate(rest)}
        return parts_of(mine_b, from_core_b, pieces_b, {**y_b, **latest})

    out_moved, (w_gate, gate) = phase(
        out_sends,
        functools.partial(project_call, links_shape, width, 0, 4, tokens, F32, place),
        (last_parts(gate_moved), normed),
    )
    back_blocks = [[back_own], [core_back], far_back, far_core_back]
    w_out, d_branch, sums = branch_back_call(
        links_shape, width, 1, place, last_parts(out_moved), back_blocks, gate, ssd_out, conv_rows
    )
    moved, _ = phase([(links.core, sums), (links.side, sums), (links.corner, sums)])
    branch, d_gate, d_ssd, gain_rows = gating_back_call(
        inner, [sums, *moved], gate, ssd_out, d_branch, conv_rows
    )

    by_g = width // (3 * LANES) * 2 * LANES
    most = heads // 3 * 2
    less = heads - most
    most_width, less_width = most * size, less * size
    rows_all = 4 * tokens

    def backward(first_head, count, first_block, blocks, d_out, *before):
        return backward_call(
            count, size, first_head, first_block, blocks, all_lengths, core_place,
            conv_in, conv_pre, keys_queries, d_out, states, conv_rows, head_rows, before,
        )

    def turn(k):
        return lambda value: links.along_g(value, k)

    def a_sends(parts):
        return [
            (lambda value, j=j: links.along_a(value, j + 1), part) for j, part in enumerate(parts)
        ]

    def g_sends(parts):
        return [(turn(k + 1), part) for k, part in enumerate(parts)]

    def start(sends):
        return [send(value) for send, value in sends]

    count_a, count_g = sides - 1, groups - 1
    mixed_parts = dot_nt(branch, w_out).astype(BF16).reshape(2, 2, tokens, depth)
    mixed_keep, mixed_send = mixed_parts[:, 0], mixed_parts[:, 1]

    def first_grads(normed, d_gate, back_blocks, branch):
        def out_terms(columns, index):
            terms, first_row = [], 0
            for part in [part for block in back_blocks for part in block]:
                rows = part.shape[0]
                terms.append((part, rows, 0, branch, first_row // rows, columns, index))
                first_row += rows
            return terms

        first = weight_grad_call(
            links_shape, True, place,
            [
                [(normed, rows_all, 0, d_gate, 0, width, 0)],
                out_terms(width - by_g, by_g // (width - by_g)),
            ],
        )
        return first, weight_grad_call(links_shape, False, place, [out_terms(by_g, 0)])

    moved, (first_parts, out_parts) = phase(
        [(links.core, mixed_send)], first_grads, (normed, d_gate, back_blocks, branch)
    )
    mixed_core = moved[0]
    mixed_far = (mixed_keep[1].astype(F32) + mixed_core[1].astype(F32)).astype(BF16)
    moved, (d_in_0, d_steps_0, kq_mine_0, kq_other_0, conv_grads_0, head_grads_0) = phase(
        a_sends(first_parts[1:])
        + g_sends(out_parts[1:])
        + [(links.side, mixed_far)],
        functools.partial(backward, 0, most, 0, 4),
        (d_ssd,),
    )
    mixed_side = moved[-1]
    first_held = combine_call(groups, place, [first_parts[0], *moved[:count_a]])
    values_0 = weight_grad_call(
        links_shape, True, place, [[(normed, rows_all, 0, d_in_0, 0, most_width, 0)]]
    )
    out_chip = total(out_parts[0], moved[count_a:-1]).astype(BF16)
    out_mine, out_others = links.parts_for_a(out_chip.reshape(sides, -1, by_g))
    first_held, values_0, d_ssd, out_mine, out_others = after(
        (first_held, values_0, d_ssd, out_mine, out_others)
    )
    first_sends = g_sends(first_held[1:])
    first_sends = first_sends[:1] + first_sends[-1:] + first_sends[1:-1]

    def back_project(first_row, d_in_1, d_steps):
        rows = slice(first_row, first_row + 2 * tokens)
        d_rest = jnp.concatenate([d_in_0[rows], d_in_1, d_steps], axis=1)
        return dot_nt(d_gate[rows], w_gate) + dot_nt(d_rest, w_values)

    def far_work(d_ssd):
        results = backward(most, less, 2, 2, d_ssd, kq_mine_0, kq_other_0)
        d_steps = d_steps_0[2 * tokens :] + results[1]
        return results, d_steps, back_project(2 * tokens, results[0], d_steps).astype(BF16)

    moved, (results, d_steps_far, d_far_parts) = phase(
        a_sends(values_0[1:]) + first_sends[:2], far_work, (d_ssd,)
    )
    first_far = moved[count_a:]
    d_in_far, _, kq_far_mine, kq_far_core, conv_grads_far, head_grads_far = results
    held_0 = combine_call(groups, place, [values_0[0], *moved[:count_a]])
    held_sends = g_sends(held_0[1:])
    held_sends = held_sends[:1] + held_sends[-1:] + held_sends[1:-1]

    moved, _ = phase([(links.core, kq_far_core), (links.core, d_far_parts[tokens:])])
    kq_far_sum = (kq_far_mine + moved[0].astype(F32)).astype(BF16)
    d_far = (d_far_parts[:tokens].astype(F32) + moved[1].astype(F32)).astype(BF16)
    moved, results = phase(
        [(links.side, kq_far_sum)]
        + first_sends[2:]
        + [(links.side, d_far[:quarter])]
        + a_sends(out_others),
        functools.partial(backward, most, less, 0, 2),
        (d_ssd, kq_mine_0, kq_other_0),
    )
    d_in_near, d_steps_near, kq_near_mine, kq_near_core, conv_grads_near, head_grads_near = results
    kq_from_side = moved[0]
    first_far = first_far + moved[1 : count_g - 1]
    far_d = [moved[count_g - 1]]
    out_piece = total(out_mine, moved[count_g:]).astype(BF16)
    first_piece = total(first_held[0], first_far).astype(BF16)
    d_steps_near = d_steps_0[: 2 * tokens] + d_steps_near
    d_steps = jnp.concatenate([d_steps_near, d_steps_far], axis=0)
    moved, d_near = phase(
        [(links.core, kq_near_core), (links.side, d_far[quarter:half])] + held_sends[:1],
        functools.partial(back_project, 0),
        (d_in_near, d_steps_near),
    )
    far_d.append(moved[1])
    held_far = moved[2:]
    d_kq_in, kq_grads = keys_back_call(
        all_lengths, [kq_near_mine, moved[0], kq_from_side], kq_in, kq_rows
    )
    half_rows = 2 * tokens

    def last_grads(normed, d_in_near, d_in_far, d_steps, d_kq_in):
        last = weight_grad_call(
            links_shape, True, place,
            [
                [
                    (normed, half_rows, 0, d_in_near, 0, less_width, 0),
                    (normed, half_rows, 1, d_in_far, 0, less_width, 0),
                ],
                [
                    (normed, half_rows, 0, d_steps, 0, LANES, 0),
                    (normed, half_rows, 1, d_steps, 1, LANES, 0),
                ],
                [(normed, half_rows, 0, d_kq_in, 0, state, 0)],
            ],
        )
        return last

    moved, last_parts_here = phase(
        rounds(first_piece)
        + held_sends[1:]
        + [(links.side, d_far[half:])],
        last_grads,
        (normed, d_in_near, d_in_far, d_steps, d_kq_in),
    )
    first_y = moved[:count_a]
    held_far = held_far + moved[count_a:-1]
    far_d.append(moved[-1])
    held_piece = total(held_0[0], held_far).astype(BF16)
    held_piece = jnp.concatenate([out_piece, held_piece], axis=1)
    first_rows = links.rows_of_core(links.join_a(first_piece, first_y))
    d_near_keep = d_near[:tokens] + dot_nt(d_kq_in[:tokens], w_kq)
    d_near_send = (d_near[tokens:] + dot_nt(d_kq_in[tokens:], w_kq)).astype(BF16)
    small = small_call(
        heads, size, channels, core_place,
        [conv_grads_0, conv_grads_far, conv_grads_near],
        [head_grads_0, head_grads_far, head_grads_near],
        gain_rows, kq_grads,
    )
    def finish_mixed(keep, core, side):
        mixed = hidden_in.astype(F32) + keep.astype(F32) + core.astype(F32) + side.astype(F32)
        return jnp.where(is_valid, mixed, 0.0).astype(BF16)

    moved, mixed = phase(
        a_sends(last_parts_here[1:])
        + [(links.core, d_near_send)]
        + [(links.core, first_rows[1]), (links.side, held_piece), (links.core, small)],
        finish_mixed,
        (mixed_keep[0], mixed_core[0], mixed_side),
    )
    d_near_core = moved[count_a]
    first_mine, first_core = first_rows[0], moved[count_a + 1]
    held_both = links.join_x(held_piece, moved[count_a + 2])
    small = small + moved[-1]
    first_both = jnp.concatenate(
        [jnp.where(is_high, first_core, first_mine), jnp.where(is_high, first_mine, first_core)],
        axis=1,
    )
    last_held = combine_call(groups, place, [last_parts_here[0], *moved[:count_a]])

    moved, grad_hidden = phase(
        g_sends(last_held[1:])
        + [(links.side, first_both)]
        + rounds(held_both)
        + [(swap(2), small)],
        norm_back_call,
        (d_near_keep, d_near_core, far_d, hidden_in, back_own, scale, n_rows),
    )
    first_other = moved[count_g]
    held_rows = links.rows_of_core(links.join_a(held_both, moved[count_g + 1 : -1]))
    small = small + moved[-1]
    last_piece = total(last_held[0], moved[:count_g]).astype(BF16)
    diagonals = [(lambda value, j=j: links.diagonal(value, j), last_piece) for j in range(1, sides)]
    moved, _ = phase(
        rounds(last_piece)
        + [(links.side, last_piece), (links.core, held_rows[1]), (swap(4), small)]
        + diagonals
    )
    same_x = links.join_a(last_piece, moved[:count_a])
    held_core, small = moved[count_a + 1], small + moved[count_a + 2]
    other_x = links.join_a(moved[count_a], moved[count_a + 3 :])
    bit = 8
    while bit < shards:
        small = small + links.flip(small, 0, bit)
        bit *= 2
    at_kq = less_width + LANES
    kq_both = same_x[:, at_kq:].astype(F32) + other_x[:, at_kq:].astype(F32)
    last_rows = links.rows_of_core(
        jnp.concatenate(
            [
                jnp.where(is_far, other_x, same_x)[:, :at_kq],
                jnp.where(is_far, same_x, other_x)[:, :at_kq],
                kq_both.astype(BF16),
            ],
            axis=1,
        )
    )
    (last_core,), _ = phase([(links.core, last_rows[1])])
    held_rows_pair = [held_rows[0], held_core]
    moved, (grad_in, grad_out, grad_norm) = phase(
        [(links.side, small)]
        + rounds(small)
        + [(lambda value, j=j: links.diagonal(value, j), small) for j in range(1, sides)],
        functools.partial(final_call, heads, size, most_width, by_g, core_place),
        (
            [first_both, first_other, *held_rows_pair, last_rows[0], last_core],
            in_weight,
            norm_gain.astype(F32)[:, None],
        ),
    )
    small = total(small, moved)

    def own_slice(array, count):
        return lax.dynamic_slice_in_dim(array, links.shard * count, count, array.ndim - 1)

    grad_conv = own_slice(small[:5], channels // shards)
    grad_heads = [
        own_slice(small[7, field * LANES : field * LANES + all_heads], all_heads // shards)
        for field in range(3)
    ]
    return (
        mixed,
        grad_hidden,
        grad_norm[:, 0],
        grad_in,
        grad_conv[:4],
        grad_conv[4],
        grad_heads[0],
        grad_heads[1],
        grad_heads[2],
        own_slice(small[5, :inner], inner // shards),
        grad_out.T,
    )


def solution(mesh):
    return jax.shard_map(
        functools.partial(per_device, mesh.shape["rep"], mesh.shape["fsdp"]),
        mesh=mesh,
        in_specs=(
            P(("rep", "fsdp"), None),
            P(("rep", "fsdp"), None),
            P("fsdp"),
            P("fsdp", None),
            P(None, "fsdp"),
            P("fsdp"),
            P("fsdp"),
            P("fsdp"),
            P("fsdp"),
            P("fsdp"),
            P(None, "fsdp"),
            P(("rep", "fsdp"), None),
        ),
        out_specs=(
            P(("rep", "fsdp"), None),
            P(("rep", "fsdp"), None),
            P("fsdp"),
            P("fsdp", None),
            P(None, "fsdp"),
            P("fsdp"),
            P("fsdp"),
            P("fsdp"),
            P("fsdp"),
            P("fsdp"),
            P(None, "fsdp"),
        ),
        check_vma=False,
    )
```

```python
import functools

import jax
import jax.numpy as jnp
from jax import lax
from jax.experimental import pallas as pl
from jax.experimental.pallas import tpu as pltpu
from jax.sharding import PartitionSpec as P

EPS = 1e-05
CHUNK = 128
LANES = 128
HIGHEST = lax.Precision.HIGHEST
F32 = jnp.float32
BF16 = jnp.bfloat16


def dot(left, right, precision=None):
    return lax.dot_general(
        left, right, (((1,), (0,)), ((), ())), precision=precision, preferred_element_type=F32
    )


def dot_nt(left, right):
    return lax.dot_general(left, right, (((1,), (1,)), ((), ())), preferred_element_type=F32)


def sigmoid(v):
    return 0.5 * jnp.tanh(0.5 * v) + 0.5


def softplus(v):
    return jnp.maximum(v, 0.0) + jnp.log1p(jnp.exp(-jnp.abs(v)))


def begin_of(position, first, both):
    return jnp.where(position >= both, both, jnp.where(position >= first, first, 0))


def iotas(rows, columns):
    return (
        lax.broadcasted_iota(jnp.int32, (rows, columns), 0),
        lax.broadcasted_iota(jnp.int32, (rows, columns), 1),
    )


def conv_tile(u_ref, cw_ref, start, columns, masks):
    inputs = [u_ref[start : start + CHUNK, columns]]
    for delay in range(1, 4):
        if start:
            shifted = u_ref[start - delay : start - delay + CHUNK, columns]
        else:
            shifted = pltpu.roll(inputs[0], delay, 0)
        inputs.append(jnp.where(masks[delay - 1], shifted, 0.0))
    pre = cw_ref[4:5, columns] + cw_ref[3:4, columns] * inputs[0]
    for delay in range(1, 4):
        pre = pre + cw_ref[3 - delay : 4 - delay, columns] * inputs[delay]
    return pre


def chunk_rates(dt_ref, hp_ref, start):
    raw = dt_ref[start : start + CHUNK, :] + hp_ref[0:1, :]
    step = softplus(raw)
    rate = -jnp.exp(hp_ref[1:2, :]) * step
    row, column = iotas(CHUNK, CHUNK)
    running = dot((row >= column).astype(F32), rate, HIGHEST)
    return raw, step, rate, running


def pair_of(low, matrix, head):
    return jnp.where(low, matrix[:, head : head + 1], matrix[:, head + 1 : head + 2])


def keys_queries_of(is_high, mine_ref, other_ref, start):
    here = slice(start, start + CHUNK)
    mine, other = mine_ref[here, :], other_ref[here, :]
    return jnp.where(is_high, other, mine), jnp.where(is_high, mine, other)


def forward_kernel(
    heads, size, first_block, len_ref, at_ref, u_ref, dt_ref, kq_ref, kq_other_ref, cw_ref, hp_ref, *refs
):
    y_ref, st_ref, pre_ref, state = refs[-4:]
    block = first_block + pl.program_id(0)
    first = len_ref[block, 0]
    both = first + len_ref[block, 1]
    tokens = u_ref.shape[0]
    chunks = tokens // CHUNK
    row, column = iotas(CHUNK, CHUNK)
    low = column < size
    low_row = low[0:1, :]
    for ci in range(chunks):
        start = ci * CHUNK
        position = row + start
        begin = begin_of(position, first, both)
        masks = [position - delay >= begin for delay in range(1, 4)]
        raw, step, rate, running = chunk_rates(dt_ref, hp_ref, start)
        running_t = running.T
        keys, queries = keys_queries_of(at_ref[1] == 1, kq_ref, kq_other_ref, start)
        keys_t = keys.astype(F32).T.astype(BF16)
        allowed = (column <= row) & (column + start >= begin)
        scores = jnp.where(allowed, dot_nt(queries, keys), 0.0)
        last_begin = begin_of(start + CHUNK - 1, first, both)
        source = position >= last_begin
        reached = begin < start
        ending = running[CHUNK - 1 : CHUNK, :]
        kept = jnp.where(last_begin < start, jnp.exp(ending), 0.0)
        for pair in range(heads // 2):
            h = 2 * pair
            columns = slice(pair * LANES, (pair + 1) * LANES)
            pre = conv_tile(u_ref, cw_ref, start, columns, masks)
            pre_ref[start : start + CHUNK, columns] = pre
            values = pre * sigmoid(pre)
            scaled = values * pair_of(low, step, h)
            weights = []
            for head in (h, h + 1):
                gap = running[:, head : head + 1] - running_t[head : head + 1, :]
                weights.append((scores * jnp.exp(jnp.minimum(gap, 0.0))).astype(BF16))
            stacked = jnp.concatenate(
                [jnp.where(low, scaled, 0.0), jnp.where(low, 0.0, scaled)], axis=0
            ).astype(BF16)
            out = dot(jnp.concatenate(weights, axis=1), stacked)
            out = out + cw_ref[5:6, columns] * values
            across = pair_of(low, running, h)
            if ci:
                carried = dot(queries, state[:, columns].astype(BF16))
                out = out + jnp.where(reached, carried * jnp.exp(across), 0.0)
            y_ref[start : start + CHUNK, columns] = out
            if ci < chunks - 1:
                left = pair_of(low_row, ending, h) - across
                source_in = jnp.where(source, scaled * jnp.exp(left), 0.0).astype(BF16)
                fresh = dot(keys_t, source_in)
                if ci:
                    fresh = fresh + state[:, columns] * pair_of(low_row, kept, h)
                state[:, columns] = fresh
                st_ref[0, ci, :, columns] = fresh.astype(BF16)


def backward_kernel(
    heads,
    size,
    first_head,
    first_block,
    len_ref,
    at_ref,
    u_ref,
    pre_ref,
    dt_ref,
    kq_ref,
    kq_other_ref,
    dy_ref,
    st_ref,
    cw_ref,
    hp_ref,
    *refs,
):
    added = refs[:-10]
    du_ref, ddt_ref, mine_ref, other_ref, cg_ref, hg_ref = refs[-10:-4]
    d_state, d_pre, out_in, source_in = refs[-4:]
    is_high = at_ref[1] == 1
    block = pl.program_id(0)
    first = len_ref[first_block + block, 0]
    both = first + len_ref[first_block + block, 1]
    tokens, width = u_ref.shape
    chunks = tokens // CHUNK
    row, column = iotas(CHUNK, CHUNK)
    low = column < size
    low_row = low[0:1, :]
    wide_row, wide_column = iotas(2 * CHUNK, LANES)
    pick_row, pick_column = iotas(16, 2 * CHUNK)

    @pl.when(block == 0)
    def _():
        cg_ref[...] = jnp.zeros_like(cg_ref)
        hg_ref[...] = jnp.zeros_like(hg_ref)

    d_pre[tokens : tokens + 8, :] = jnp.zeros((8, width), F32)
    for ci in reversed(range(chunks)):
        start = ci * CHUNK
        has_later = ci < chunks - 1
        position = row + start
        begin = begin_of(position, first, both)
        ahead = [begin_of(position + delay, first, both) <= position for delay in range(1, 4)]
        raw, step, rate, running = chunk_rates(dt_ref, hp_ref, start)
        running_t = running.T
        keys, queries = keys_queries_of(is_high, kq_ref, kq_other_ref, start)
        allowed = (row <= column) & (position >= begin_of(column + start, first, both))
        scores = jnp.where(allowed, dot_nt(keys, queries), 0.0)
        last_begin = begin_of(start + CHUNK - 1, first, both)
        source = position >= last_begin
        reached = begin < start
        ending = running[CHUNK - 1 : CHUNK, :]
        kept = jnp.where(last_begin < start, jnp.exp(ending), 0.0)
        d_scores = jnp.zeros((CHUNK, CHUNK), F32)
        later_sums = jnp.zeros((16, CHUNK), F32)
        early_sums = jnp.zeros((CHUNK, LANES), F32)
        out_sums = jnp.zeros((CHUNK, LANES), F32)
        source_sums = jnp.zeros((CHUNK, LANES), F32)
        direct_sums = jnp.zeros((CHUNK, LANES), F32)
        kept_sums = jnp.zeros((8, LANES), F32)
        for pair in range(heads // 2):
            h = first_head + 2 * pair
            columns = slice(pair * LANES, (pair + 1) * LANES)
            to_head = (column == h + (row >= size).astype(jnp.int32)).astype(BF16)
            pre = pre_ref[start : start + CHUNK, columns]
            inputs = u_ref[start : start + CHUNK, columns]
            gate = sigmoid(pre)
            values = pre * gate
            steps = pair_of(low, step, h)
            scaled = values * steps
            d_out = dy_ref[start : start + CHUNK, columns].astype(F32)
            d_low = d_out.astype(BF16)
            stacked = jnp.concatenate(
                [jnp.where(low, scaled, 0.0), jnp.where(low, 0.0, scaled)], axis=0
            ).astype(BF16)
            d_weights = dot_nt(stacked, d_low)
            weights, products = [], []
            for at, head in enumerate((h, h + 1)):
                gap = running_t[head : head + 1, :] - running[:, head : head + 1]
                decay = jnp.exp(jnp.minimum(gap, 0.0))
                d_decayed = decay * d_weights[at * CHUNK : (at + 1) * CHUNK]
                d_scores = d_scores + d_decayed
                products.append((scores * d_decayed).astype(BF16))
                weights.append((scores * decay).astype(BF16))
            early = wide_column == h + (wide_row >= CHUNK).astype(jnp.int32)
            early_sums = early_sums + dot(jnp.concatenate(products, axis=1), early.astype(BF16))
            later = pick_row == h + (pick_column >= CHUNK).astype(jnp.int32)
            later_sums = later_sums + dot(later.astype(BF16), jnp.concatenate(products, axis=0))
            d_stacked = jnp.concatenate(
                [jnp.where(low, d_out, 0.0), jnp.where(low, 0.0, d_out)], axis=0
            ).astype(BF16)
            d_scaled = dot(jnp.concatenate(weights, axis=1), d_stacked)
            across = pair_of(low, running, h)
            if has_later:
                left = jnp.exp(pair_of(low_row, ending, h) - across)
                left = jnp.where(source, left, 0.0)
                d_state_here = d_state[:, columns]
                d_source = dot(keys, d_state_here.astype(BF16)) * left
                d_scaled = d_scaled + d_source
                source_sums = source_sums + dot((scaled * d_source).astype(BF16), to_head)
                source_in[:, columns] = (scaled * left).astype(BF16)
            if ci:
                before = st_ref[0, ci - 1, :, columns]
                d_reach = jnp.where(reached, d_out * jnp.exp(across), 0.0)
                out_sums = out_sums + dot((d_reach * dot(queries, before)).astype(BF16), to_head)
                out_in[:, columns] = d_reach.astype(BF16)
                if has_later:
                    held = jnp.sum(d_state_here * before.astype(F32), axis=0, keepdims=True)
                    held = held * pair_of(low_row, kept, h)
                    kept_sums = kept_sums + dot(
                        jnp.broadcast_to(held, (8, LANES)), to_head.astype(F32), HIGHEST
                    )
            direct_sums = direct_sums + dot((d_scaled * values).astype(BF16), to_head)
            d_values = d_scaled * steps + cw_ref[5:6, columns] * d_out
            cg_ref[5:6, columns] += jnp.sum(d_out * values, axis=0, keepdims=True)
            d_here = d_values * (gate * (1.0 + pre * (1.0 - gate)))
            d_pre[start : start + CHUNK, columns] = d_here
            d_in = cw_ref[3:4, columns] * d_here
            cg_ref[3:4, columns] += jnp.sum(inputs * d_here, axis=0, keepdims=True)
            for delay in range(1, 4):
                shifted = d_pre[start + delay : start + delay + CHUNK, columns]
                shifted = jnp.where(ahead[delay - 1], shifted, 0.0)
                d_in = d_in + cw_ref[3 - delay : 4 - delay, columns] * shifted
                cg_ref[3 - delay : 4 - delay, columns] += jnp.sum(
                    inputs * shifted, axis=0, keepdims=True
                )
            du_ref[start : start + CHUNK, columns] = d_in.astype(BF16)
            cg_ref[4:5, columns] += jnp.sum(d_here, axis=0, keepdims=True)
        d_scores = jnp.where(allowed, d_scores, 0.0)
        d_keys = dot(d_scores.astype(BF16), queries)
        d_queries = dot(d_scores.T.astype(BF16), keys)
        d_running = (
            jnp.concatenate([later_sums, jnp.zeros((CHUNK - 16, CHUNK), F32)], axis=0).T
            - early_sums
            + out_sums
            - source_sums
        )
        if has_later:
            d_keys = d_keys + dot_nt(source_in[...], d_state[...].astype(BF16))
            at_end = jnp.sum(source_sums, axis=0, keepdims=True) + kept_sums[0:1, :]
            d_running = d_running + jnp.where(row == CHUNK - 1, at_end, 0.0)
        if ci:
            d_queries = d_queries + dot_nt(out_in[...], st_ref[0, ci - 1])
            queries_t = queries.astype(F32).T.astype(BF16)
            for pair in range(heads // 2):
                columns = slice(pair * LANES, (pair + 1) * LANES)
                fresh = dot(queries_t, out_in[:, columns])
                if has_later:
                    fresh = fresh + d_state[:, columns] * pair_of(low_row, kept, first_head + 2 * pair)
                d_state[:, columns] = fresh
        here = slice(start, start + CHUNK)
        mine = jnp.where(is_high, d_queries, d_keys)
        other = jnp.where(is_high, d_keys, d_queries)
        if added:
            mine, other = mine + added[0][here, :], other + added[1][here, :]
        mine_ref[here, :] = mine.astype(mine_ref.dtype)
        other_ref[here, :] = other.astype(other_ref.dtype)
        d_rate = dot((row <= column).astype(F32), d_running, HIGHEST)
        d_step = direct_sums - jnp.exp(hp_ref[1:2, :]) * d_rate
        d_raw = d_step * sigmoid(raw)
        ddt_ref[start : start + CHUNK, :] = d_raw.astype(BF16)
        hg_ref[0:1, :] += jnp.sum(d_raw, axis=0, keepdims=True)
        hg_ref[1:2, :] += jnp.sum(d_rate * rate, axis=0, keepdims=True)


def prepare_first_kernel(heads, size, state, at_ref, in_ref, mine_ref, other_ref):
    x, core = at_ref[0], at_ref[1]
    width = heads * size
    inner = 4 * width
    steps_at = 2 * inner + 2 * state
    steps = in_ref[:, steps_at : steps_at + 4 * heads].astype(F32)
    rows = steps.shape[0]
    steps = jnp.concatenate([steps, jnp.zeros((rows, LANES - 4 * heads), F32)], axis=1)
    column = lax.broadcasted_iota(jnp.int32, (rows, LANES), 1)
    for ref, c in ((mine_ref, core), (other_ref, 1 - core)):
        p = 2 * x + c
        values_at = pl.multiple_of(inner + p * width, LANES)
        ref[:, :width] = in_ref[:, pl.ds(values_at, width)]
        drawn = pltpu.roll(steps, lax.rem(LANES - heads * p, LANES), 1)
        ref[:, width : width + LANES] = jnp.where(column < heads, drawn, 0.0).astype(BF16)
        keys_at = pl.multiple_of(2 * inner + c * state, LANES)
        ref[:, width + LANES : width + LANES + state] = in_ref[:, pl.ds(keys_at, state)]


def prepare_last_kernel(width, at_ref, in_ref, out_ref, mine_ref, other_ref):
    x, core = at_ref[0], at_ref[1]
    for ref, c in ((mine_ref, core), (other_ref, 1 - core)):
        at = pl.multiple_of((2 * x + c) * width, LANES)
        ref[:, :width] = in_ref[:, pl.ds(at, width)]
        ref[:, width:] = out_ref[:, pl.ds(at, width)]


def prepare_call(kernel, columns, place, *weights):
    rows = weights[0].shape[0]
    return pl.pallas_call(
        kernel,
        in_specs=[pl.BlockSpec(memory_space=pltpu.SMEM)]
        + [pl.BlockSpec(memory_space=pltpu.VMEM)] * len(weights),
        out_specs=[pl.BlockSpec(memory_space=pltpu.VMEM)] * 2,
        out_shape=[jax.ShapeDtypeStruct((rows, columns), BF16)] * 2,
        compiler_params=pltpu.CompilerParams(vmem_limit_bytes=24 * 1024 * 1024),
        name="prepare",
    )(place, *weights)


def unpack_kernel(sizes, heads, size, state, at_ref, small_ref, n_ref, conv_ref, head_ref, kq_ref, all_ref):
    conv_size, gate_size, norm_size, head_size = sizes
    x, c = at_ref[0], at_ref[1]
    p = 2 * x + c
    shards = small_ref.shape[0] // 8
    width = heads * size

    def joined(first_row, rows, at, part, columns):
        padded = -(-columns // LANES) * LANES
        lanes = -(-part // LANES) * LANES
        lane = lax.broadcasted_iota(jnp.int32, (8, lanes), 1)
        result = jnp.zeros((8, padded), F32)
        for f in range(shards):
            rows_here = small_ref[8 * f : 8 * f + 8, at : at + lanes].astype(F32)
            rows_here = jnp.where(lane < part, rows_here, 0.0)
            if padded > lanes:
                rows_here = jnp.concatenate(
                    [rows_here, jnp.zeros((8, padded - lanes), F32)], axis=1
                )
            result = result + pltpu.roll(rows_here, (part * f) % padded, 1)
        return result[first_row : first_row + rows]

    conv_all = joined(0, 5, 0, conv_size, conv_size * shards)
    gate_all = joined(5, 1, 0, gate_size, gate_size * shards)
    norm_all = joined(6, 1, 0, norm_size, norm_size * shards)
    n_ref[...] = jnp.broadcast_to(norm_all, n_ref.shape)
    all_ref[...] = jnp.zeros_like(all_ref)
    all_ref[0:5, : conv_all.shape[1]] = conv_all
    all_ref[6:7, : gate_all.shape[1]] = gate_all
    conv_ref[...] = all_ref[:, pl.ds(pl.multiple_of(p * width, LANES), width)]
    kq_at = 4 * width + c * state
    kq_ref[...] = all_ref[:, pl.ds(pl.multiple_of(kq_at, LANES), state)]
    column = lax.broadcasted_iota(jnp.int32, (8, LANES), 1)
    head_ref[...] = jnp.zeros_like(head_ref)
    for row in range(3):
        values = joined(7, 1, row * LANES, head_size, head_size * shards)
        values = jnp.broadcast_to(values, (8, LANES))
        values = pltpu.roll(values, lax.rem(LANES - heads * p, LANES), 1)
        head_ref[row : row + 1, :] = jnp.where(column < heads, values, 0.0)[0:1]
    row_at, column_at = iotas(LANES, width)
    spread = (row_at == column_at // size).astype(F32)
    conv_ref[5:6, :] = dot(head_ref[...], spread, HIGHEST)[2:3]


def unpack_call(sizes, heads, size, state, place, small):
    shards = small.shape[0] // 8
    depth, width = sizes[2] * shards, heads * size
    columns = -(-sizes[0] * shards // LANES) * LANES
    return pl.pallas_call(
        functools.partial(unpack_kernel, sizes, heads, size, state),
        in_specs=[
            pl.BlockSpec(memory_space=pltpu.SMEM),
            pl.BlockSpec(memory_space=pltpu.VMEM),
        ],
        out_specs=[pl.BlockSpec(memory_space=pltpu.VMEM)] * 4,
        out_shape=[
            jax.ShapeDtypeStruct((8, depth), F32),
            jax.ShapeDtypeStruct((8, width), F32),
            jax.ShapeDtypeStruct((8, LANES), F32),
            jax.ShapeDtypeStruct((8, state), F32),
        ],
        scratch_shapes=[pltpu.VMEM((8, columns), F32)],
        compiler_params=pltpu.CompilerParams(vmem_limit_bytes=24 * 1024 * 1024),
        name="unpack",
    )(place, small)


def assemble_rows(links_shape, at_ref, own_ref, core_ref, pieces, whole_ref):
    sides, groups = links_shape
    a, g, c = at_ref[0], at_ref[1], at_ref[2]
    rows = own_ref.shape[0]
    part = 2 * rows // sides
    base = g * (2 * rows)
    whole_ref[pl.ds(pl.multiple_of(base + c * rows, 16), rows), :] = own_ref[...]
    whole_ref[pl.ds(pl.multiple_of(base + (1 - c) * rows, 16), rows), :] = core_ref[...]
    for k in range(1, groups):
        base = lax.rem(g + groups - k, groups) * (2 * rows)
        for j in range(sides):
            at = base + lax.rem(a + sides - j, sides) * part
            piece = pieces[(k - 1) * sides + j]
            whole_ref[pl.ds(pl.multiple_of(at, 16), part), :] = piece[...]


def project_kernel(links_shape, at_ref, own_ref, core_ref, *refs):
    pieces, (rows_ref, whole_ref, out_ref) = refs[:-3], refs[-3:]

    @pl.when(pl.program_id(0) == 0)
    def _():
        assemble_rows(links_shape, at_ref, own_ref, core_ref, pieces, whole_ref)

    out_ref[...] = dot(rows_ref[...], whole_ref[...]).astype(out_ref.dtype)


def whole_spec(array):
    return pl.BlockSpec(array.shape, lambda b: (0,) * array.ndim)


def columns_spec(array, width, index):
    if array.shape[1] == width:
        index = 0
    return pl.BlockSpec((array.shape[0], width), lambda b: (0, index))


def project_call(links_shape, width, index, blocks, tokens, kind, place, parts, rows):
    depth = rows.shape[1]
    return pl.pallas_call(
        functools.partial(project_kernel, links_shape),
        grid=(blocks,),
        in_specs=[pl.BlockSpec(memory_space=pltpu.SMEM)]
        + [columns_spec(array, width, index) for array in parts]
        + [pl.BlockSpec((tokens, depth), lambda b: (b, 0))],
        out_specs=[
            pl.BlockSpec((depth, width), lambda b: (0, 0)),
            pl.BlockSpec((tokens, width), lambda b: (b, 0)),
        ],
        out_shape=[
            jax.ShapeDtypeStruct((depth, width), BF16),
            jax.ShapeDtypeStruct((blocks * tokens, width), kind),
        ],
        compiler_params=pltpu.CompilerParams(vmem_limit_bytes=40 * 1024 * 1024),
        cost_estimate=pl.CostEstimate(
            flops=2 * rows.size * width, bytes_accessed=2 * rows.size, transcendentals=0
        ),
        name="project",
    )(place, *parts, rows)


def branch_back_kernel(links_shape, counts, at_ref, own_ref, core_ref, *refs):
    pieces, rows_refs = refs[: -6 - sum(counts)], list(refs[-6 - sum(counts) : -6])
    gate_ref, ssd_ref, cw_ref, whole_ref, out_ref, sums_ref = refs[-6:]
    block = pl.program_id(0)

    @pl.when(block == 0)
    def _():
        assemble_rows(links_shape, at_ref, own_ref, core_ref, pieces, whole_ref)

    for at, count in enumerate(counts):
        parts = [rows_refs.pop(0) for _ in range(count)]

        @pl.when(block == at)
        def _():
            first_row = 0
            for part in parts:
                stop = first_row + part.shape[0]
                out_ref[first_row:stop, :] = dot(part[...], whole_ref[...])
                first_row = stop

    tokens, width = out_ref.shape
    sums_ref[...] = jnp.zeros_like(sums_ref)
    for start in range(0, tokens, CHUNK):
        squares = jnp.zeros((CHUNK, LANES), F32)
        products = jnp.zeros((CHUNK, LANES), F32)
        for left in range(0, width, LANES):
            tile = (slice(start, start + CHUNK), slice(left, left + LANES))
            gate = gate_ref[tile].astype(F32)
            gated = ssd_ref[tile] * (gate * sigmoid(gate))
            squares = squares + gated * gated
            products = products + gated * (cw_ref[6:7, left : left + LANES] * out_ref[tile])
        sums_ref[0:1, start : start + CHUNK] = jnp.sum(squares.T, axis=0, keepdims=True)
        sums_ref[1:2, start : start + CHUNK] = jnp.sum(products.T, axis=0, keepdims=True)


def branch_back_call(links_shape, width, index, place, parts, rows, gate, ssd_out, conv_rows):
    tokens, depth = ssd_out.shape[0] // 4, rows[0][0].shape[1]
    counts = [len(block) for block in rows]
    rows = [part for block in rows for part in block]
    block = pl.BlockSpec((tokens, width), lambda b: (b, 0))
    return pl.pallas_call(
        functools.partial(branch_back_kernel, links_shape, counts),
        grid=(4,),
        in_specs=[pl.BlockSpec(memory_space=pltpu.SMEM)]
        + [columns_spec(array, width, index) for array in parts]
        + [whole_spec(array) for array in rows]
        + [block, block, pl.BlockSpec((8, width), lambda b: (0, 0))],
        out_specs=[
            pl.BlockSpec((depth, width), lambda b: (0, 0)),
            block,
            pl.BlockSpec((8, tokens), lambda b: (0, b)),
        ],
        out_shape=[
            jax.ShapeDtypeStruct((depth, width), BF16),
            jax.ShapeDtypeStruct((4 * tokens, width), F32),
            jax.ShapeDtypeStruct((8, 4 * tokens), F32),
        ],
        compiler_params=pltpu.CompilerParams(vmem_limit_bytes=56 * 1024 * 1024),
        cost_estimate=pl.CostEstimate(
            flops=8 * tokens * depth * width, bytes_accessed=8 * tokens * depth, transcendentals=0
        ),
        name="branch_back",
    )(place, *parts, *rows, gate, ssd_out, conv_rows)


def gating_back_kernel(
    inner, sums_ref, core_ref, side_ref, both_ref, gate_ref, ssd_ref, db_ref, cw_ref,
    branch_ref, dgate_ref, dssd_ref, gain_ref
):
    @pl.when(pl.program_id(0) == 0)
    def _():
        gain_ref[...] = jnp.zeros_like(gain_ref)

    sums = sums_ref[...] + core_ref[...] + side_ref[...] + both_ref[...]
    scale_row = lax.rsqrt(sums[0:1, :] * (1.0 / inner) + EPS)
    cross_row = scale_row * scale_row * scale_row * (sums[1:2, :] * (1.0 / inner))
    tokens, width = gate_ref.shape
    for start in range(0, tokens, CHUNK):
        stacked = jnp.concatenate(
            [scale_row[:, start : start + CHUNK], cross_row[:, start : start + CHUNK],
             jnp.zeros((CHUNK - 2, CHUNK), F32)], axis=0
        ).T
        scale, cross = stacked[:, 0:1], stacked[:, 1:2]
        for left in range(0, width, LANES):
            columns = slice(left, left + LANES)
            tile = (slice(start, start + CHUNK), columns)
            gate, ssd, d_branch = gate_ref[tile].astype(F32), ssd_ref[tile], db_ref[tile]
            gain = cw_ref[6:7, columns]
            sig = sigmoid(gate)
            act = gate * sig
            gated = ssd * act
            scaled = gated * scale
            branch_ref[tile] = (scaled * gain).astype(BF16)
            gain_ref[0:1, columns] += jnp.sum(d_branch * scaled, axis=0, keepdims=True)
            d_gated = scale * (gain * d_branch) - gated * cross
            dssd_ref[tile] = d_gated * act
            dgate_ref[tile] = (d_gated * ssd * (sig * (1.0 + gate * (1.0 - sig)))).astype(BF16)


def gating_back_call(inner, sums, gate, ssd_out, d_branch, conv_rows):
    rows, columns = gate.shape
    tokens = rows // 4
    block = pl.BlockSpec((tokens, columns), lambda b: (b, 0))
    order = [lambda b: (0, b)]
    order.append(lambda b: (0, b + 1 - 2 * lax.rem(b, 2)))
    order.append(lambda b: (0, lax.rem(b + 2, 4)))
    order.append(lambda b: (0, 3 - b))
    return pl.pallas_call(
        functools.partial(gating_back_kernel, inner),
        grid=(4,),
        in_specs=[pl.BlockSpec((8, tokens), index) for index in order]
        + [block, block, block, pl.BlockSpec((8, columns), lambda b: (0, 0))],
        out_specs=[block, block, block, pl.BlockSpec((8, columns), lambda b: (0, 0))],
        out_shape=[
            jax.ShapeDtypeStruct((rows, columns), BF16),
            jax.ShapeDtypeStruct((rows, columns), BF16),
            jax.ShapeDtypeStruct((rows, columns), F32),
            jax.ShapeDtypeStruct((8, columns), F32),
        ],
        compiler_params=pltpu.CompilerParams(vmem_limit_bytes=40 * 1024 * 1024),
        cost_estimate=pl.CostEstimate(
            flops=20 * rows * columns, bytes_accessed=20 * rows * columns, transcendentals=0
        ),
        name="gating_back",
    )(*sums, gate, ssd_out, d_branch, conv_rows)


def normalize_kernel(*refs):
    rows_refs, (gain_ref, normed_ref, scale_ref) = refs[:4], refs[4:]
    for at, rows_ref in enumerate(rows_refs):

        @pl.when(pl.program_id(0) == at)
        def _():
            depth = rows_ref.shape[1]
            for start in range(0, rows_ref.shape[0], 64):
                rows = rows_ref[start : start + 64, :].astype(F32)
                mean = jnp.sum(rows * rows, axis=1, keepdims=True) * (1.0 / depth)
                scale = lax.rsqrt(mean + EPS)
                normed = rows * scale * gain_ref[0:1, :]
                normed_ref[start : start + 64, :] = normed.astype(BF16)
                scale_ref[start : start + 64, :] = jnp.broadcast_to(scale, (64, LANES))


def normalize_call(blocks, gain):
    tokens, depth = blocks[0].shape
    return pl.pallas_call(
        normalize_kernel,
        grid=(4,),
        in_specs=[whole_spec(block) for block in blocks] + [whole_spec(gain)],
        out_specs=[
            pl.BlockSpec((tokens, depth), lambda b: (b, 0)),
            pl.BlockSpec((tokens, LANES), lambda b: (b, 0)),
        ],
        out_shape=[
            jax.ShapeDtypeStruct((4 * tokens, depth), BF16),
            jax.ShapeDtypeStruct((4 * tokens, LANES), F32),
        ],
        compiler_params=pltpu.CompilerParams(vmem_limit_bytes=40 * 1024 * 1024),
        name="normalize",
    )(*blocks, gain)


def weight_grad_kernel(links_shape, groups_of_terms, over_a, at_ref, *refs):
    sides, groups = links_shape
    count = sum(len(terms) for terms in groups_of_terms)
    left_count = 1 + max(left_at for terms in groups_of_terms for left_at, _ in terms)
    lefts, rights = refs[:left_count], refs[left_count : left_count + count]
    outs, scratch = refs[left_count + count : -1], refs[-1]
    at_column, at_term = 0, 0
    for terms in groups_of_terms:
        result = None
        for left_at, first_row in terms:
            right = rights[at_term][...]
            term = lax.dot_general(
                lefts[left_at][first_row : first_row + right.shape[0], :],
                right,
                (((0,), (0,)), ((), ())),
                preferred_element_type=F32,
            )
            result = term if result is None else result + term
            at_term += 1
        width = result.shape[1]
        scratch[:, at_column : at_column + width] = result.astype(BF16)
        at_column += width
    if over_a:
        chips, part = outs[0].shape[0], outs[0].shape[1]
        for chip in range(chips):
            for j, out in enumerate(outs):
                at = (chip * sides + lax.rem(at_ref[0] + j, sides)) * part
                out[chip] = scratch[pl.ds(pl.multiple_of(at, 16), part), :]
        return
    rows = outs[0].shape[0]
    chips = scratch.shape[0] // rows
    for chip in range(chips):
        turn = lax.rem(pl.program_id(0) * chips + chip + groups - at_ref[1], groups)
        for k, out in enumerate(outs):

            @pl.when(turn == k)
            def _():
                out[...] = scratch[chip * rows : (chip + 1) * rows, :]


def weight_grad_call(links_shape, over_a, place, groups_of_terms):
    sides, groups = links_shape
    terms = [term for group in groups_of_terms for term in group]
    depth = terms[0][0].shape[1]
    columns = sum(group[0][5] for group in groups_of_terms)
    rows = depth // groups
    part = rows // sides
    chips = 1
    while chips * rows % LANES:
        chips += 1
    lefts = []
    for term in terms:
        if not any(term[0] is left for left in lefts):
            lefts.append(term[0])

    def left_at(term):
        return [term[0] is left for left in lefts].index(True)

    def left_spec(left):
        return pl.BlockSpec((left.shape[0], chips * rows), lambda b: (0, b))

    def right_spec(term):
        return pl.BlockSpec((term[1], term[5]), lambda b: (term[4], term[6]))

    if over_a:
        out_specs = [pl.BlockSpec((chips, part, columns), lambda b: (b, 0, 0))] * sides
        out_shape = [jax.ShapeDtypeStruct((groups, part, columns), BF16)] * sides
    else:
        out_specs = [pl.BlockSpec((rows, columns), lambda b: (0, 0))] * groups
        out_shape = [jax.ShapeDtypeStruct((rows, columns), BF16)] * groups
    shapes = tuple(
        tuple((left_at(term), term[1] * term[2]) for term in group) for group in groups_of_terms
    )
    return pl.pallas_call(
        functools.partial(weight_grad_kernel, links_shape, shapes, over_a),
        grid=(groups // chips,),
        in_specs=[pl.BlockSpec(memory_space=pltpu.SMEM)]
        + [left_spec(left) for left in lefts]
        + [right_spec(term) for term in terms],
        out_specs=out_specs,
        out_shape=out_shape,
        scratch_shapes=[pltpu.VMEM((chips * rows, columns), BF16)],
        compiler_params=pltpu.CompilerParams(vmem_limit_bytes=48 * 1024 * 1024),
        cost_estimate=pl.CostEstimate(
            flops=2 * terms[0][1] * depth * columns,
            bytes_accessed=2 * terms[0][1] * depth,
            transcendentals=0,
        ),
        name="weight_grad",
    )(place, *lefts, *[term[3] for term in terms])


def combine_kernel(groups, at_ref, *refs):
    parts, outs = refs[:-groups], refs[-groups:]
    result = parts[0][0].astype(F32)
    for part in parts[1:]:
        result = result + part[0].astype(F32)
    turn = lax.rem(pl.program_id(0) + groups - at_ref[1], groups)
    for k, out in enumerate(outs):

        @pl.when(turn == k)
        def _():
            out[...] = result.astype(BF16)


def combine_call(groups, place, parts):
    rows, columns = parts[0].shape[1:]
    return pl.pallas_call(
        functools.partial(combine_kernel, groups),
        grid=(groups,),
        in_specs=[pl.BlockSpec(memory_space=pltpu.SMEM)]
        + [pl.BlockSpec((1, rows, columns), lambda b: (b, 0, 0))] * len(parts),
        out_specs=[pl.BlockSpec((rows, columns), lambda b: (0, 0))] * groups,
        out_shape=[jax.ShapeDtypeStruct((rows, columns), BF16)] * groups,
        compiler_params=pltpu.CompilerParams(vmem_limit_bytes=24 * 1024 * 1024),
        name="combine",
    )(place, *parts)


def keys_front_kernel(len_ref, in_ref, rows_ref, out_ref):
    tokens, columns = in_ref.shape[0] // 2, in_ref.shape[1]
    position = lax.broadcasted_iota(jnp.int32, (tokens, columns), 0)
    row, lane = iotas(16, columns)
    counts = jnp.zeros((16, columns), jnp.int32)
    for block in range(2):
        first = len_ref[block, 0]
        both = first + len_ref[block, 1]
        begin = begin_of(position, first, both)
        inputs = in_ref[block * tokens : (block + 1) * tokens, :]
        pre = rows_ref[4:5, :] + rows_ref[3:4, :] * inputs
        for delay in range(1, 4):
            shifted = jnp.where(position - delay >= begin, pltpu.roll(inputs, delay, 0), 0.0)
            pre = pre + rows_ref[3 - delay : 4 - delay, :] * shifted
        out_ref[block * tokens : (block + 1) * tokens, :] = (pre * sigmoid(pre)).astype(BF16)
        for sequence in range(2):
            length = len_ref[block, sequence]
            here = row == block
            counts = jnp.where(here & (lane == 2 * sequence), lax.div(length, 32), counts)
            counts = jnp.where(here & (lane == 2 * sequence + 1), lax.rem(length, 32), counts)
    out_ref[2 * tokens :, :] = counts.astype(F32).astype(BF16)


def keys_front_call(lengths, inputs, rows):
    total, columns = inputs.shape
    return pl.pallas_call(
        keys_front_kernel,
        in_specs=[
            pl.BlockSpec(memory_space=pltpu.SMEM),
            pl.BlockSpec(memory_space=pltpu.VMEM),
            pl.BlockSpec(memory_space=pltpu.VMEM),
        ],
        out_specs=pl.BlockSpec(memory_space=pltpu.VMEM),
        out_shape=jax.ShapeDtypeStruct((total + 16, columns), BF16),
        compiler_params=pltpu.CompilerParams(vmem_limit_bytes=24 * 1024 * 1024),
        name="keys_front",
    )(lengths, inputs, rows)


def norm_back_kernel(keep_ref, core_ref, *refs):
    far_refs, (hidden_ref, back_ref, scale_ref, gain_ref, out_ref) = refs[:3], refs[3:]
    block = pl.program_id(0)
    far = jnp.where(block == 0, far_refs[0][...], far_refs[1][...])
    far = jnp.where(block <= 1, far, far_refs[2][...]).astype(F32)
    hidden, scale = hidden_ref[...].astype(F32), scale_ref[:, 0:1]
    weighted = gain_ref[0:1, :] * (keep_ref[...] + core_ref[...].astype(F32) + far)
    mean = jnp.sum(hidden * weighted, axis=1, keepdims=True) * (1.0 / hidden.shape[1])
    cross = scale * scale * scale * mean
    out_ref[...] = back_ref[...].astype(F32) + scale * weighted - hidden * cross


def norm_back_call(keep, core, far, hidden, back, scale, gain):
    tokens, depth = keep.shape
    rows = tokens // 4
    block = pl.BlockSpec((rows, depth), lambda b: (b, 0))
    quarter = pl.BlockSpec((rows, depth), lambda b: (0, 0))
    later = pl.BlockSpec((rows, depth), lambda b: (jnp.maximum(b - 2, 0), 0))
    return pl.pallas_call(
        norm_back_kernel,
        grid=(4,),
        in_specs=[
            block, block, quarter, quarter, later, block, block,
            pl.BlockSpec((rows, LANES), lambda b: (b, 0)),
            whole_spec(gain),
        ],
        out_specs=block,
        out_shape=jax.ShapeDtypeStruct((tokens, depth), F32),
        compiler_params=pltpu.CompilerParams(vmem_limit_bytes=32 * 1024 * 1024),
        cost_estimate=pl.CostEstimate(
            flops=4_000_000_000, bytes_accessed=12_000_000, transcendentals=0
        ),
        name="norm_back",
    )(keep, core, *far, hidden, back, scale, gain)


def keys_back_kernel(len_ref, mine_ref, core_ref, side_ref, in_ref, rows_ref, d_ref, grads_ref):
    block = pl.program_id(0)
    first = len_ref[block, 0]
    both = first + len_ref[block, 1]
    tokens, columns = in_ref.shape
    position = lax.broadcasted_iota(jnp.int32, (tokens, columns), 0)
    begin = begin_of(position, first, both)
    inside = [position - delay >= begin for delay in range(1, 4)]
    inputs = [in_ref[...]]
    for delay in range(1, 4):
        shifted = pltpu.roll(inputs[0], delay, 0)
        inputs.append(jnp.where(inside[delay - 1], shifted, 0.0))
    pre = rows_ref[4:5, :] + rows_ref[3:4, :] * inputs[0]
    for delay in range(1, 4):
        pre = pre + rows_ref[3 - delay : 4 - delay, :] * inputs[delay]
    sig = sigmoid(pre)
    d_out = mine_ref[...] + core_ref[...].astype(F32) + side_ref[...].astype(F32)
    d_pre = d_out * (sig * (1.0 + pre * (1.0 - sig)))
    d_in = rows_ref[3:4, :] * d_pre
    for delay in range(1, 4):
        moved = pltpu.roll(jnp.where(inside[delay - 1], d_pre, 0.0), tokens - delay, 0)
        d_in = d_in + rows_ref[3 - delay : 4 - delay, :] * moved
    d_ref[...] = d_in.astype(BF16)

    @pl.when(block == 0)
    def _():
        grads_ref[...] = jnp.zeros_like(grads_ref)

    for delay in range(4):
        grads_ref[3 - delay : 4 - delay, :] += jnp.sum(
            inputs[delay] * d_pre, axis=0, keepdims=True
        )
    grads_ref[4:5, :] += jnp.sum(d_pre, axis=0, keepdims=True)


def keys_back_call(lengths, parts, inputs, rows):
    total, columns = inputs.shape
    block = pl.BlockSpec((total // 2, columns), lambda b: (b, 0))
    small = pl.BlockSpec((8, columns), lambda b: (0, 0))
    return pl.pallas_call(
        keys_back_kernel,
        grid=(2,),
        in_specs=[pl.BlockSpec(memory_space=pltpu.SMEM)] + [block] * 4 + [small],
        out_specs=[block, small],
        out_shape=[
            jax.ShapeDtypeStruct((total, columns), BF16),
            jax.ShapeDtypeStruct((8, columns), F32),
        ],
        compiler_params=pltpu.CompilerParams(vmem_limit_bytes=24 * 1024 * 1024),
        name="keys_back",
    )(lengths, *parts, inputs, rows)


def small_kernel(heads, size, at_ref, *refs):
    convs, head_refs, (gain_ref, kq_ref, out_ref) = refs[:3], refs[3:6], refs[6:]
    p = 2 * at_ref[0] + at_ref[1]
    width = heads * size
    most, less = convs[0].shape[1], convs[1].shape[1]
    out_ref[...] = jnp.zeros_like(out_ref)
    rest = convs[1][...] + convs[2][...]
    at = pl.multiple_of(p * width, LANES)
    out_ref[0:5, pl.ds(at, most)] = convs[0][0:5, :]
    out_ref[0:5, pl.ds(pl.multiple_of(at + most, LANES), less)] = rest[0:5, :]
    kq_at = pl.multiple_of(4 * width + at_ref[1] * kq_ref.shape[1], LANES)
    out_ref[0:5, pl.ds(kq_at, kq_ref.shape[1])] = kq_ref[0:5, :]
    out_ref[5:6, pl.ds(at, width)] = gain_ref[0:1, :]
    skip = jnp.concatenate([convs[0][...], rest], axis=1)
    row, column = iotas(width, LANES)
    skip = dot(skip, (row // size == column).astype(F32), HIGHEST)
    sums = head_refs[0][...] + head_refs[1][...] + head_refs[2][...]
    for field, values in enumerate((sums[0:1], sums[1:2], skip[5:6])):
        values = jnp.broadcast_to(values, (8, LANES))
        lane = lax.broadcasted_iota(jnp.int32, (8, LANES), 1)
        values = pltpu.roll(jnp.where(lane < heads, values, 0.0), heads * p, 1)
        out_ref[7:8, field * LANES : (field + 1) * LANES] = values[0:1]


def small_call(heads, size, channels, place, convs, head_grads, gains, kq_grads):
    operands = [*convs, *head_grads, gains, kq_grads]
    return pl.pallas_call(
        functools.partial(small_kernel, heads, size),
        in_specs=[pl.BlockSpec(memory_space=pltpu.SMEM)]
        + [pl.BlockSpec(memory_space=pltpu.VMEM)] * len(operands),
        out_specs=pl.BlockSpec(memory_space=pltpu.VMEM),
        out_shape=jax.ShapeDtypeStruct((8, channels), F32),
        compiler_params=pltpu.CompilerParams(vmem_limit_bytes=24 * 1024 * 1024),
        name="small_gradients",
    )(place, *operands)


def final_kernel(heads, size, most, by_g, at_ref, *refs):
    first_both, first_other, held_mine, held_core, last_mine, last_core = refs[:6]
    weight_ref, gain_ref, in_ref, out_ref, norm_ref = refs[6:]
    far, high = at_ref[0] == 1, at_ref[1] == 1
    width = heads * size
    less = width - most
    rows = in_ref.shape[0]
    at_values, at_keys = 4 * width, 8 * width
    state = last_mine.shape[1] - 2 * (less + LANES)
    at_steps = at_keys + 2 * state
    norm = jnp.zeros((rows, 1), F32)

    def put(at, values):
        stop = at + values.shape[1]
        in_ref[:, at:stop] = values
        weight = weight_ref[:, at:stop].astype(F32)
        return jnp.sum(values * weight, axis=1, keepdims=True)

    def share(both, other, p, count, start, stop):
        columns = slice((p % 2) * count + start, (p % 2) * count + stop)
        take_other = far if p < 2 else jnp.logical_not(far)
        return jnp.where(take_other, other[:, columns], both[:, columns]).astype(F32)

    def core_share(mine, other, core, start, stop):
        take_other = high if core == 0 else jnp.logical_not(high)
        columns = slice(start, stop)
        return jnp.where(take_other, other[:, columns], mine[:, columns]).astype(F32)

    last_share = functools.partial(core_share, last_mine, last_core)
    held_share = functools.partial(core_share, held_mine, held_core)

    steps = jnp.zeros((rows, LANES), F32)
    lane = lax.broadcasted_iota(jnp.int32, (rows, LANES), 1)
    for p in range(4):
        first = functools.partial(share, first_both, first_other, p, 2 * width - by_g)
        norm = norm + put(p * width, first(0, width))
        left = (p // 2) * (by_g + most)
        out_ref[:, p * width : p * width + by_g] = held_share(p % 2, left, left + by_g)
        out_ref[:, p * width + by_g : (p + 1) * width] = first(width, 2 * width - by_g)
        at = at_values + p * width
        norm = norm + put(at, held_share(p % 2, left + by_g, left + by_g + most))
        left = (p // 2) * (less + LANES)
        norm = norm + put(at + most, last_share(p % 2, left, left + less))
        drawn = last_share(p % 2, left + less, left + less + LANES)
        steps = steps + pltpu.roll(jnp.where(lane < heads, drawn, 0.0), heads * p, 1)
    for core in range(2):
        at = 2 * (less + LANES)
        norm = norm + put(at_keys + core * state, last_share(core, at, at + state))
    norm = norm + put(at_steps, steps[:, : 4 * heads])
    norm_ref[...] = norm / gain_ref[...]


def final_call(heads, size, most, by_g, place, shares, weight, gain):
    rows, columns = weight.shape
    operands = [*shares, weight, gain]
    return pl.pallas_call(
        functools.partial(final_kernel, heads, size, most, by_g),
        in_specs=[pl.BlockSpec(memory_space=pltpu.SMEM)]
        + [pl.BlockSpec(memory_space=pltpu.VMEM)] * len(operands),
        out_specs=[pl.BlockSpec(memory_space=pltpu.VMEM)] * 3,
        out_shape=[
            jax.ShapeDtypeStruct((rows, columns), F32),
            jax.ShapeDtypeStruct((rows, 4 * heads * size), F32),
            jax.ShapeDtypeStruct((rows, 1), F32),
        ],
        compiler_params=pltpu.CompilerParams(vmem_limit_bytes=40 * 1024 * 1024),
        cost_estimate=pl.CostEstimate(
            flops=5_000_000_000, bytes_accessed=16_000_000, transcendentals=0
        ),
        name="owner_gradients",
    )(place, *operands)


def forward_call(
    heads, size, first_block, blocks, lengths, place, conv_in, keys_queries, conv_rows, head_rows, before=()
):
    total = conv_in.shape[0]
    tokens = total // lengths.shape[0]
    width = heads * size
    state = keys_queries[0].shape[1]
    boundaries = tokens // CHUNK - 1
    return pl.pallas_call(
        functools.partial(forward_kernel, heads, size, first_block),
        grid=(blocks,),
        in_specs=[
            pl.BlockSpec(memory_space=pltpu.SMEM),
            pl.BlockSpec(memory_space=pltpu.SMEM),
            pl.BlockSpec((tokens, width), lambda b: (first_block + b, 0)),
            pl.BlockSpec((tokens, LANES), lambda b: (first_block + b, width // LANES)),
            pl.BlockSpec((tokens, state), lambda b: (first_block + b, 0)),
            pl.BlockSpec((tokens, state), lambda b: (first_block + b + 1 - 2 * lax.rem(b, 2), 0)),
            pl.BlockSpec((8, width), lambda b: (0, 0)),
            pl.BlockSpec((8, LANES), lambda b: (0, 0)),
        ]
        + [pl.BlockSpec(memory_space=pl.ANY)] * len(before),
        out_specs=[
            pl.BlockSpec((tokens, width), lambda b: (first_block + b, 0)),
            pl.BlockSpec((1, boundaries, state, width), lambda b: (first_block + b, 0, 0, 0)),
            pl.BlockSpec((tokens, width), lambda b: (first_block + b, 0)),
        ],
        out_shape=[
            jax.ShapeDtypeStruct((total, width), F32),
            jax.ShapeDtypeStruct((lengths.shape[0], boundaries, state, width), BF16),
            jax.ShapeDtypeStruct((total, width), F32),
        ],
        scratch_shapes=[pltpu.VMEM((state, width), F32)],
        input_output_aliases={8 + at: at for at in range(len(before))},
        compiler_params=pltpu.CompilerParams(vmem_limit_bytes=40 * 1024 * 1024),
        cost_estimate=pl.CostEstimate(
            flops=blocks * 3_000_000_000, bytes_accessed=blocks * 8_000_000, transcendentals=0
        ),
        name="ssd_forward",
    )(lengths, place, conv_in, conv_in, *keys_queries, conv_rows, head_rows, *before)


def backward_call(
    heads, size, first_head, first_block, blocks,
    lengths, place, conv_in, conv_pre, keys_queries, d_out, states, conv_rows, head_rows, before=()
):
    tokens = conv_in.shape[0] // lengths.shape[0]
    total = blocks * tokens
    width = heads * size
    part = first_head * size // width
    steps_at = d_out.shape[1] // LANES
    state = keys_queries[0].shape[1]
    boundaries = tokens // CHUNK - 1

    def rows_of(columns, index):
        return pl.BlockSpec((tokens, columns), lambda b: (first_block + b, index))

    def swapped(b):
        return b + 1 - 2 * lax.rem(b, 2)

    return pl.pallas_call(
        functools.partial(backward_kernel, heads, size, first_head, first_block),
        grid=(blocks,),
        in_specs=[
            pl.BlockSpec(memory_space=pltpu.SMEM),
            pl.BlockSpec(memory_space=pltpu.SMEM),
            rows_of(width, part),
            rows_of(width, part),
            rows_of(LANES, steps_at),
            rows_of(state, 0),
            pl.BlockSpec((tokens, state), lambda b: (swapped(first_block + b), 0)),
            rows_of(width, part),
            pl.BlockSpec(
                (1, boundaries, state, width), lambda b: (first_block + b, 0, 0, part)
            ),
            pl.BlockSpec((8, width), lambda b: (0, part)),
            pl.BlockSpec((8, LANES), lambda b: (0, 0)),
        ]
        + [
            rows_of(state, 0),
            pl.BlockSpec((tokens, state), lambda b: (swapped(first_block + b), 0)),
        ][: len(before)],
        out_specs=[
            pl.BlockSpec((tokens, width), lambda b: (b, 0)),
            pl.BlockSpec((tokens, LANES), lambda b: (b, 0)),
            pl.BlockSpec((tokens, state), lambda b: (b, 0)),
            pl.BlockSpec((tokens, state), lambda b: (swapped(b), 0)),
            pl.BlockSpec((8, width), lambda b: (0, 0)),
            pl.BlockSpec((8, LANES), lambda b: (0, 0)),
        ],
        out_shape=[
            jax.ShapeDtypeStruct((total, width), BF16),
            jax.ShapeDtypeStruct((total, LANES), BF16),
            jax.ShapeDtypeStruct((total, state), F32),
            jax.ShapeDtypeStruct((total, state), BF16 if before else F32),
            jax.ShapeDtypeStruct((8, width), F32),
            jax.ShapeDtypeStruct((8, LANES), F32),
        ],
        scratch_shapes=[
            pltpu.VMEM((state, width), F32),
            pltpu.VMEM((tokens + 8, width), F32),
            pltpu.VMEM((CHUNK, width), BF16),
            pltpu.VMEM((CHUNK, width), BF16),
        ],
        compiler_params=pltpu.CompilerParams(vmem_limit_bytes=48 * 1024 * 1024),
        cost_estimate=pl.CostEstimate(
            flops=blocks * heads * 1_000_000_000,
            bytes_accessed=blocks * 8_000_000,
            transcendentals=0,
        ),
        name="ssd_backward",
    )(lengths, place, conv_in, conv_pre, conv_in, *keys_queries, d_out, states, conv_rows, head_rows, *before)


def after(values):
    return lax.optimization_barrier(values)


def phase(sends, work=None, arguments=(), until=None):
    values, arguments = after(([value for _, value in sends], arguments))
    moved = [send(value) for (send, _), value in zip(sends, values)]
    done = work(*arguments) if work else ()
    moved, done, until = after((moved, done, until))
    return (moved, done) if until is None else (moved, done, until)


def total(first, others):
    result = first.astype(F32)
    for other in others:
        result = result + other.astype(F32)
    return result


class Links:
    def __init__(self, reps, shards):
        self.reps, self.shards = reps, shards
        self.sides, self.groups = reps // 2, shards // 2
        rep, shard = lax.axis_index("rep"), lax.axis_index("fsdp")
        self.rep, self.shard = rep, shard
        self.a, self.x = rep // 2, rep % 2
        self.g, self.c = shard // 2, shard % 2

    def send(self, value, target):
        pairs = []
        for r in range(self.reps):
            for f in range(self.shards):
                to_r, to_f = target(r, f)
                pairs.append((r * self.shards + f, to_r * self.shards + to_f))
        return lax.ppermute(value, ("rep", "fsdp"), pairs)

    def core(self, value):
        return self.send(value, lambda r, f: (r, f ^ 1))

    def side(self, value):
        return self.send(value, lambda r, f: (r ^ 1, f))

    def corner(self, value):
        return self.send(value, lambda r, f: (r ^ 1, f ^ 1))

    def along_a(self, value, by):
        return self.send(value, lambda r, f: (((r // 2 + by) % self.sides) * 2 + r % 2, f))

    def along_g(self, value, by):
        return self.send(value, lambda r, f: (r, ((f // 2 + by) % self.groups) * 2 + f % 2))

    def diagonal(self, value, by):
        return self.send(
            value, lambda r, f: (((r // 2 + by) % self.sides) * 2 + (r % 2 ^ 1), f)
        )

    def flip(self, value, bit_of_rep, bit_of_shard):
        return self.send(value, lambda r, f: (r ^ bit_of_rep, f ^ bit_of_shard))

    def round_g(self, piece):
        return [self.along_g(piece, k) for k in range(1, self.groups)]

    def piece_of(self, mine, from_core):
        if self.sides == 2:
            return jnp.where(self.a == self.c, mine, from_core)
        is_high = self.c == 1
        chip = jnp.concatenate(
            [jnp.where(is_high, from_core, mine), jnp.where(is_high, mine, from_core)], axis=0
        )
        part = chip.shape[0] // self.sides
        return lax.dynamic_slice_in_dim(chip, self.a * part, part, 0)

    def round_a(self, joined):
        return [self.along_a(joined, j) for j in range(1, self.sides)]

    def assemble(self, mine, from_core, joined, rounds):
        rows, columns = mine.shape
        part = 2 * rows // self.sides
        whole = jnp.zeros((rows * self.shards, columns), mine.dtype)
        base = self.g * 2 * rows
        whole = lax.dynamic_update_slice_in_dim(whole, mine, base + self.c * rows, 0)
        whole = lax.dynamic_update_slice_in_dim(whole, from_core, base + (1 - self.c) * rows, 0)
        for k in range(1, self.groups):
            base = ((self.g - k) % self.groups) * 2 * rows
            for j, pieces in enumerate([joined] + rounds):
                piece = pieces[(k - 1) * part : k * part]
                at = base + ((self.a - j) % self.sides) * part
                whole = lax.dynamic_update_slice_in_dim(whole, piece, at, 0)
        return whole

    def parts_for_a(self, view):
        axis = view.ndim - 3
        mine = lax.dynamic_index_in_dim(view, self.a, axis, keepdims=False)
        others = [
            lax.dynamic_index_in_dim(view, (self.a + j) % self.sides, axis, keepdims=False)
            for j in range(1, self.sides)
        ]
        return mine, others

    def parts_for_g(self, view):
        mine = lax.dynamic_index_in_dim(view, self.g, 0, keepdims=False)
        others = [
            lax.dynamic_index_in_dim(view, (self.g + k) % self.groups, 0, keepdims=False)
            for k in range(1, self.groups)
        ]
        return mine, others

    def send_a(self, others):
        return [self.along_a(part, j + 1) for j, part in enumerate(others)]

    def send_g(self, others):
        return [self.along_g(part, k + 1) for k, part in enumerate(others)]

    def chips_of(self, partial):
        rows = partial.shape[0] // (self.groups * self.sides)
        return partial.reshape(self.groups, self.sides, rows, partial.shape[1])

    def spread_a(self, piece):
        return [self.along_a(piece, j) for j in range(1, self.sides)]

    def join_a(self, piece, others):
        if self.sides == 2:
            is_high = self.a == 1
            return jnp.concatenate(
                [jnp.where(is_high, others[0], piece), jnp.where(is_high, piece, others[0])],
                axis=0,
            )
        part = piece.shape[0]
        chip = jnp.zeros((part * self.sides, piece.shape[1]), piece.dtype)
        for j, value in enumerate([piece] + others):
            at = ((self.a - j) % self.sides) * part
            chip = lax.dynamic_update_slice_in_dim(chip, value, at, 0)
        return chip

    def join_x(self, piece, other):
        is_far = self.x == 1
        return jnp.concatenate(
            [jnp.where(is_far, other, piece), jnp.where(is_far, piece, other)], axis=1
        )

    def rows_of_core(self, chip):
        rows = chip.shape[0] // 2
        is_high = self.c == 1
        mine = jnp.where(is_high, chip[rows:], chip[:rows])
        return mine, jnp.where(is_high, chip[:rows], chip[rows:])

    def shares(self, mine, from_core):
        columns = mine.shape[1] // 2
        is_high = self.c == 1
        low = jnp.where(is_high, from_core, mine)
        high = jnp.where(is_high, mine, from_core)
        return [low[:, :columns], high[:, :columns], low[:, columns:], high[:, columns:]]

    def sum_all(self, value):
        bit = 1
        while bit < self.shards:
            value = value + self.flip(value, 0, bit)
            bit *= 2
        bit = 1
        while bit < self.reps:
            value = value + self.flip(value, bit, 0)
            bit *= 2
        return value

    def group_blocks(self, value):
        far = self.side(value)
        return [value, self.core(value), far, self.core(far)]

    def core_sum(self, partials, link_type):
        tokens = partials.shape[0] // 2
        return partials[:tokens].astype(F32) + self.core(
            partials[tokens:].astype(link_type)
        ).astype(F32)


def per_device(
    reps,
    shards,
    hidden_in,
    lengths,
    norm_gain,
    in_weight,
    conv_weight,
    conv_bias,
    dt_bias,
    a_log,
    skip_gain,
    gate_gain,
    out_weight,
    cotangent,
):
    links = Links(reps, shards)
    tokens, depth = hidden_in.shape
    inner = gate_gain.shape[0] * shards
    channels = conv_bias.shape[0] * shards
    all_heads = dt_bias.shape[0] * shards
    state = (channels - inner) // 2
    size = inner // all_heads
    heads, width = all_heads // 4, inner // 4
    x, c = links.x, links.c
    p = 2 * x + c

    is_high, is_far = c == 1, x == 1
    far_hidden = links.side(hidden_in)
    ends = jnp.cumsum(lengths[0])
    positions = jnp.arange(tokens, dtype=jnp.int32)
    is_valid = (positions < ends[1])[:, None]
    back_own = jnp.where(is_valid, cotangent, jnp.zeros_like(cotangent))
    sides, groups = links.sides, links.groups
    links_shape = (sides, groups)
    place = jnp.stack([links.a, links.g, c]).astype(jnp.int32)

    lanes = max(conv_weight.shape[1], gate_gain.shape[0], norm_gain.shape[0], 3 * LANES)
    lanes = -(-lanes // LANES) * LANES

    def pack(conv_weight, conv_bias, gate_gain, norm_gain, *head_values):
        heads_row = jnp.concatenate(
            [jnp.pad(v, (0, LANES - v.shape[0])) for v in head_values]
        )
        rows = [conv_bias, gate_gain, norm_gain, heads_row[:lanes]]
        rows = [jnp.pad(row, (0, lanes - row.shape[0]))[None] for row in rows]
        taps_rows = jnp.pad(conv_weight, ((0, 0), (0, lanes - conv_weight.shape[1])))
        return jnp.concatenate([taps_rows, *rows], axis=0)

    small_in = (conv_weight, conv_bias, gate_gain, norm_gain, dt_bias, a_log, skip_gain)
    sizes = (conv_bias.shape[0], gate_gain.shape[0], norm_gain.shape[0], dt_bias.shape[0])

    first_columns, last_columns = width + LANES + state, 2 * width
    core_place = jnp.stack([x, c]).astype(jnp.int32)
    mine_a, for_core_a = prepare_call(
        functools.partial(prepare_first_kernel, heads, size, state),
        first_columns,
        core_place,
        in_weight,
    )

    def hops(pieces, stage):
        sends = [(stage, 1, pieces[stage - 1])]
        if groups - stage != stage:
            sends.append((groups - stage, groups - 1, pieces[(groups - stage + 1) % groups]))
        return sends

    def hop_sends(pieces, stage):
        return [
            ((lambda value, by=by: links.along_g(value, by)), value)
            for _, by, value in hops(pieces, stage)
        ]

    def landed(pieces, stage, values):
        at = [k for k, _, _ in hops(pieces, stage)]
        return {**pieces, **dict(zip(at, values))}

    def rounds(piece):
        return [(lambda value, j=j: links.along_a(value, j), piece) for j in range(1, sides)]

    def doubled(value, bit, other):
        upper = (links.shard // bit) % 2 == 1
        return jnp.concatenate(
            [jnp.where(upper, other, value), jnp.where(upper, value, other)], axis=0
        )

    def swap(bit):
        return lambda value: links.flip(value, 0, bit)

    (from_core_a,), _ = phase([(links.core, for_core_a)])
    pieces_a = {0: links.piece_of(mine_a, from_core_a)}

    def prepare_last(small_in, in_weight, out_weight):
        packed = pack(*small_in)
        small_pair = doubled(packed, 1, links.core(packed))
        small_four = doubled(small_pair, 2, links.flip(small_pair, 0, 2))
        kernel = functools.partial(prepare_last_kernel, width)
        last = prepare_call(kernel, last_columns, core_place, in_weight, out_weight)
        return small_four, last

    moved, (small_all, (mine_b, for_core_b)) = phase(
        hop_sends(pieces_a, 1) + [(links.core, lengths)],
        prepare_last,
        (small_in, in_weight, out_weight.T),
    )
    lengths_core = moved[-1]
    pieces_a = landed(pieces_a, 1, moved[:-1])
    firsts = [k for k in pieces_a if k]
    early, late = firsts[:1], firsts[1:]
    early_sends = [send for k in early for send in rounds(pieces_a[k])]
    moved, _ = phase(
        hop_sends(pieces_a, 2)
        + [(swap(4), small_all), (links.core, for_core_b)]
        + early_sends
    )
    hop_count = len(hops(pieces_a, 2))
    small_all = doubled(small_all, 4, moved[hop_count])
    from_core_b = moved[hop_count + 1]
    y_moved = moved[hop_count + 2 :]
    pieces_a = landed(pieces_a, 2, moved[:hop_count])
    pieces_b = {0: links.piece_of(mine_b, from_core_b)}
    bit = 8
    while bit < shards:
        small_all = doubled(small_all, bit, links.flip(small_all, 0, bit))
        bit *= 2
    for stage in range(3, groups // 2 + 1):
        values = [send(value) for send, value in hop_sends(pieces_a, stage)]
        pieces_a = landed(pieces_a, stage, values)
    pieces_a, pieces_b, far_hidden = after((pieces_a, pieces_b, far_hidden))
    late = late + [k for k in pieces_a if k and k not in firsts]
    late_sends = [send for k in late for send in rounds(pieces_a[k])]
    b_firsts = [send(value) for send, value in hop_sends(pieces_b, 1)]
    moved, parameters_here = phase(
        late_sends + [(links.core, hidden_in), (links.core, far_hidden)],
        functools.partial(unpack_call, sizes, heads, size, state, core_place),
        (small_all,),
    )
    core_hidden, far_core_hidden = moved[-2:]
    y_moved = y_moved + moved[:-2]
    y_a = {
        k: y_moved[at * (sides - 1) : (at + 1) * (sides - 1)] for at, k in enumerate(early + late)
    }
    n_rows, conv_rows, head_rows, kq_rows = parameters_here

    def parts_of(mine, from_core, pieces, rounds_of):
        parts = [mine, from_core]
        for k in range(1, groups):
            parts += [pieces[k], *rounds_of[k]]
        return parts

    parts_a = parts_of(mine_a, from_core_a, pieces_a, y_a)
    pair_lengths = jnp.concatenate([lengths, lengths_core], axis=0)
    normed, scale = normalize_call([hidden_in, core_hidden, far_hidden, far_core_hidden], n_rows)
    kq_index = (width + LANES) // state
    w_kq, kq_in = project_call(
        links_shape, state, kq_index, 2, tokens, F32, place, parts_a, normed
    )
    kq_near = keys_front_call(pair_lengths, kq_in, kq_rows)
    half, quarter = tokens // 2, tokens // 4
    cuts = [slice(0, half), slice(half, half + quarter), slice(half + quarter, tokens)]
    moved, (w_values, conv_in), b_firsts = phase(
        [
            (links.side, kq_near),
            (links.side, back_own[cuts[1]]),
        ],
        functools.partial(project_call, links_shape, width + LANES, 0, 4, tokens, F32, place),
        (parts_a, normed),
        b_firsts,
    )
    pieces_b = landed(pieces_b, 1, b_firsts)
    kq_far, far_back = moved[0], [None, moved[1]]
    counts_at = slice(2 * tokens, 2 * tokens + 2)
    all_counts = jnp.concatenate([kq_near[counts_at, :4], kq_far[counts_at, :4]], axis=0)
    all_counts = all_counts.astype(jnp.int32)
    all_lengths = all_counts[:, 0::2] * 32 + all_counts[:, 1::2]
    kq_half = jnp.concatenate([kq_near[: 2 * tokens], kq_far[: 2 * tokens]], axis=0)

    (kq_core,), _ = phase([(links.core, kq_half)])
    keys_queries = [kq_half, kq_core]
    firsts = [k for k in pieces_b if k]
    hop_count = len(hops(pieces_b, 2))
    moved, before = phase(
        hop_sends(pieces_b, 2)
        + rounds(pieces_b[firsts[0]])
        + [(links.side, back_own[cuts[0]]), (links.core, back_own)],
        functools.partial(forward_call, heads, size, 0, 2),
        (all_lengths, core_place, conv_in, keys_queries, conv_rows, head_rows),
    )
    y_b = {firsts[0]: moved[hop_count:-2]}
    far_back[0] = moved[-2]
    core_back = moved[-1]
    pieces_b = landed(pieces_b, 2, moved[:hop_count])
    for stage in range(3, groups // 2 + 1):
        values = [send(value) for send, value in hop_sends(pieces_b, stage)]
        pieces_b = landed(pieces_b, stage, values)
    rest = [k for k in pieces_b if k and k not in firsts]
    moved, (ssd_out, states, conv_pre) = phase(
        [send for k in firsts[1:] for send in rounds(pieces_b[k])]
        + [(links.side, back_own[cuts[2]])],
        functools.partial(forward_call, heads, size, 2, 2),
        (all_lengths, core_place, conv_in, keys_queries, conv_rows, head_rows, before),
    )
    far_back.append(moved[-1])
    for at, k in enumerate(firsts[1:]):
        y_b[k] = moved[at * (sides - 1) : (at + 1) * (sides - 1)]
    gate_sends = [send for k in rest for send in rounds(pieces_b[k][:, :width])]
    out_sends = [send for k in rest for send in rounds(pieces_b[k][:, width:])]
    moved, _ = phase(gate_sends + [(links.core, part) for part in far_back])
    gate_moved, far_core_back = moved[: len(gate_sends)], moved[len(gate_sends) :]

    def last_parts(values):
        latest = {k: values[at * (sides - 1) : (at + 1) * (sides - 1)] for at, k in enumerate(rest)}
        return parts_of(mine_b, from_core_b, pieces_b, {**y_b, **latest})

    out_moved, (w_gate, gate) = phase(
        out_sends,
        functools.partial(project_call, links_shape, width, 0, 4, tokens, F32, place),
        (last_parts(gate_moved), normed),
    )
    back_blocks = [[back_own], [core_back], far_back, far_core_back]
    w_out, d_branch, sums = branch_back_call(
        links_shape, width, 1, place, last_parts(out_moved), back_blocks, gate, ssd_out, conv_rows
    )
    moved, _ = phase([(links.core, sums), (links.side, sums), (links.corner, sums)])
    branch, d_gate, d_ssd, gain_rows = gating_back_call(
        inner, [sums, *moved], gate, ssd_out, d_branch, conv_rows
    )

    by_g = width // (3 * LANES) * 2 * LANES
    most = heads // 3 * 2
    less = heads - most
    most_width, less_width = most * size, less * size
    rows_all = 4 * tokens

    def backward(first_head, count, first_block, blocks, d_out, *before):
        return backward_call(
            count, size, first_head, first_block, blocks, all_lengths, core_place,
            conv_in, conv_pre, keys_queries, d_out, states, conv_rows, head_rows, before,
        )

    def turn(k):
        return lambda value: links.along_g(value, k)

    def a_sends(parts):
        return [
            (lambda value, j=j: links.along_a(value, j + 1), part) for j, part in enumerate(parts)
        ]

    def g_sends(parts):
        return [(turn(k + 1), part) for k, part in enumerate(parts)]

    def start(sends):
        return [send(value) for send, value in sends]

    count_a, count_g = sides - 1, groups - 1
    mixed_parts = dot_nt(branch, w_out).astype(BF16).reshape(2, 2, tokens, depth)
    mixed_keep, mixed_send = mixed_parts[:, 0], mixed_parts[:, 1]

    def first_grads(normed, d_gate, back_blocks, branch):
        def out_terms(columns, index):
            terms, first_row = [], 0
            for part in [part for block in back_blocks for part in block]:
                rows = part.shape[0]
                terms.append((part, rows, 0, branch, first_row // rows, columns, index))
                first_row += rows
            return terms

        first = weight_grad_call(
            links_shape, True, place,
            [
                [(normed, rows_all, 0, d_gate, 0, width, 0)],
                out_terms(width - by_g, by_g // (width - by_g)),
            ],
        )
        return first, weight_grad_call(links_shape, False, place, [out_terms(by_g, 0)])

    moved, (first_parts, out_parts) = phase(
        [(links.core, mixed_send)], first_grads, (normed, d_gate, back_blocks, branch)
    )
    mixed_core = moved[0]
    mixed_far = (mixed_keep[1].astype(F32) + mixed_core[1].astype(F32)).astype(BF16)
    moved, (d_in_0, d_steps_0, kq_mine_0, kq_other_0, conv_grads_0, head_grads_0) = phase(
        a_sends(first_parts[1:])
        + g_sends(out_parts[1:])
        + [(links.side, mixed_far)],
        functools.partial(backward, 0, most, 0, 4),
        (d_ssd,),
    )
    mixed_side = moved[-1]
    first_held = combine_call(groups, place, [first_parts[0], *moved[:count_a]])
    values_0 = weight_grad_call(
        links_shape, True, place, [[(normed, rows_all, 0, d_in_0, 0, most_width, 0)]]
    )
    out_chip = total(out_parts[0], moved[count_a:-1]).astype(BF16)
    out_mine, out_others = links.parts_for_a(out_chip.reshape(sides, -1, by_g))
    first_held, values_0, d_ssd, out_mine, out_others = after(
        (first_held, values_0, d_ssd, out_mine, out_others)
    )
    first_sends = g_sends(first_held[1:])
    first_sends = first_sends[:1] + first_sends[-1:] + first_sends[1:-1]

    def back_project(first_row, d_in_1, d_steps):
        rows = slice(first_row, first_row + 2 * tokens)
        d_rest = jnp.concatenate([d_in_0[rows], d_in_1, d_steps], axis=1)
        return dot_nt(d_gate[rows], w_gate) + dot_nt(d_rest, w_values)

    def far_work(d_ssd):
        results = backward(most, less, 2, 2, d_ssd, kq_mine_0, kq_other_0)
        d_steps = d_steps_0[2 * tokens :] + results[1]
        return results, d_steps, back_project(2 * tokens, results[0], d_steps).astype(BF16)

    moved, (results, d_steps_far, d_far_parts) = phase(
        a_sends(values_0[1:]) + first_sends[:2], far_work, (d_ssd,)
    )
    first_far = moved[count_a:]
    d_in_far, _, kq_far_mine, kq_far_core, conv_grads_far, head_grads_far = results
    held_0 = combine_call(groups, place, [values_0[0], *moved[:count_a]])
    held_sends = g_sends(held_0[1:])
    held_sends = held_sends[:1] + held_sends[-1:] + held_sends[1:-1]

    moved, _ = phase([(links.core, kq_far_core), (links.core, d_far_parts[tokens:])])
    kq_far_sum = (kq_far_mine + moved[0].astype(F32)).astype(BF16)
    d_far = (d_far_parts[:tokens].astype(F32) + moved[1].astype(F32)).astype(BF16)
    moved, results = phase(
        [(links.side, kq_far_sum)]
        + first_sends[2:]
        + [(links.side, d_far[:quarter])]
        + a_sends(out_others),
        functools.partial(backward, most, less, 0, 2),
        (d_ssd, kq_mine_0, kq_other_0),
    )
    d_in_near, d_steps_near, kq_near_mine, kq_near_core, conv_grads_near, head_grads_near = results
    kq_from_side = moved[0]
    first_far = first_far + moved[1 : count_g - 1]
    far_d = [moved[count_g - 1]]
    out_piece = total(out_mine, moved[count_g:]).astype(BF16)
    first_piece = total(first_held[0], first_far).astype(BF16)
    d_steps_near = d_steps_0[: 2 * tokens] + d_steps_near
    d_steps = jnp.concatenate([d_steps_near, d_steps_far], axis=0)
    moved, d_near = phase(
        [(links.core, kq_near_core), (links.side, d_far[quarter:half])] + held_sends[:1],
        functools.partial(back_project, 0),
        (d_in_near, d_steps_near),
    )
    far_d.append(moved[1])
    held_far = moved[2:]
    d_kq_in, kq_grads = keys_back_call(
        all_lengths, [kq_near_mine, moved[0], kq_from_side], kq_in, kq_rows
    )
    half_rows = 2 * tokens

    def last_grads(normed, d_in_near, d_in_far, d_steps, d_kq_in):
        last = weight_grad_call(
            links_shape, True, place,
            [
                [
                    (normed, half_rows, 0, d_in_near, 0, less_width, 0),
                    (normed, half_rows, 1, d_in_far, 0, less_width, 0),
                ],
                [
                    (normed, half_rows, 0, d_steps, 0, LANES, 0),
                    (normed, half_rows, 1, d_steps, 1, LANES, 0),
                ],
                [(normed, half_rows, 0, d_kq_in, 0, state, 0)],
            ],
        )
        return last

    moved, last_parts_here = phase(
        rounds(first_piece)
        + held_sends[1:]
        + [(links.side, d_far[half:])],
        last_grads,
        (normed, d_in_near, d_in_far, d_steps, d_kq_in),
    )
    first_y = moved[:count_a]
    held_far = held_far + moved[count_a:-1]
    far_d.append(moved[-1])
    held_piece = total(held_0[0], held_far).astype(BF16)
    held_piece = jnp.concatenate([out_piece, held_piece], axis=1)
    first_rows = links.rows_of_core(links.join_a(first_piece, first_y))
    d_near_keep = d_near[:tokens] + dot_nt(d_kq_in[:tokens], w_kq)
    d_near_send = (d_near[tokens:] + dot_nt(d_kq_in[tokens:], w_kq)).astype(BF16)
    small = small_call(
        heads, size, channels, core_place,
        [conv_grads_0, conv_grads_far, conv_grads_near],
        [head_grads_0, head_grads_far, head_grads_near],
        gain_rows, kq_grads,
    )
    def finish_mixed(keep, core, side):
        mixed = hidden_in.astype(F32) + keep.astype(F32) + core.astype(F32) + side.astype(F32)
        return jnp.where(is_valid, mixed, 0.0).astype(BF16)

    moved, mixed = phase(
        a_sends(last_parts_here[1:])
        + [(links.core, d_near_send)]
        + [(links.core, first_rows[1]), (links.side, held_piece), (links.core, small)],
        finish_mixed,
        (mixed_keep[0], mixed_core[0], mixed_side),
    )
    d_near_core = moved[count_a]
    first_mine, first_core = first_rows[0], moved[count_a + 1]
    held_both = links.join_x(held_piece, moved[count_a + 2])
    small = small + moved[-1]
    first_both = jnp.concatenate(
        [jnp.where(is_high, first_core, first_mine), jnp.where(is_high, first_mine, first_core)],
        axis=1,
    )
    last_held = combine_call(groups, place, [last_parts_here[0], *moved[:count_a]])

    moved, grad_hidden = phase(
        g_sends(last_held[1:])
        + [(links.side, first_both)]
        + rounds(held_both)
        + [(swap(2), small)],
        norm_back_call,
        (d_near_keep, d_near_core, far_d, hidden_in, back_own, scale, n_rows),
    )
    first_other = moved[count_g]
    held_rows = links.rows_of_core(links.join_a(held_both, moved[count_g + 1 : -1]))
    small = small + moved[-1]
    last_piece = total(last_held[0], moved[:count_g]).astype(BF16)
    diagonals = [(lambda value, j=j: links.diagonal(value, j), last_piece) for j in range(1, sides)]
    moved, _ = phase(
        rounds(last_piece)
        + [(links.side, last_piece), (links.core, held_rows[1]), (swap(4), small)]
        + diagonals
    )
    same_x = links.join_a(last_piece, moved[:count_a])
    held_core, small = moved[count_a + 1], small + moved[count_a + 2]
    other_x = links.join_a(moved[count_a], moved[count_a + 3 :])
    bit = 8
    while bit < shards:
        small = small + links.flip(small, 0, bit)
        bit *= 2
    at_kq = less_width + LANES
    kq_both = same_x[:, at_kq:].astype(F32) + other_x[:, at_kq:].astype(F32)
    last_rows = links.rows_of_core(
        jnp.concatenate(
            [
                jnp.where(is_far, other_x, same_x)[:, :at_kq],
                jnp.where(is_far, same_x, other_x)[:, :at_kq],
                kq_both.astype(BF16),
            ],
            axis=1,
        )
    )
    (last_core,), _ = phase([(links.core, last_rows[1])])
    held_rows_pair = [held_rows[0], held_core]
    moved, (grad_in, grad_out, grad_norm) = phase(
        [(links.side, small)]
        + rounds(small)
        + [(lambda value, j=j: links.diagonal(value, j), small) for j in range(1, sides)],
        functools.partial(final_call, heads, size, most_width, by_g, core_place),
        (
            [first_both, first_other, *held_rows_pair, last_rows[0], last_core],
            in_weight,
            norm_gain.astype(F32)[:, None],
        ),
    )
    small = total(small, moved)

    def own_slice(array, count):
        return lax.dynamic_slice_in_dim(array, links.shard * count, count, array.ndim - 1)

    grad_conv = own_slice(small[:5], channels // shards)
    grad_heads = [
        own_slice(small[7, field * LANES : field * LANES + all_heads], all_heads // shards)
        for field in range(3)
    ]
    return (
        mixed,
        grad_hidden,
        grad_norm[:, 0],
        grad_in,
        grad_conv[:4],
        grad_conv[4],
        grad_heads[0],
        grad_heads[1],
        grad_heads[2],
        own_slice(small[5, :inner], inner // shards),
        grad_out.T,
    )


def solution(mesh):
    return jax.shard_map(
        functools.partial(per_device, mesh.shape["rep"], mesh.shape["fsdp"]),
        mesh=mesh,
        in_specs=(
            P(("rep", "fsdp"), None),
            P(("rep", "fsdp"), None),
            P("fsdp"),
            P("fsdp", None),
            P(None, "fsdp"),
            P("fsdp"),
            P("fsdp"),
            P("fsdp"),
            P("fsdp"),
            P("fsdp"),
            P(None, "fsdp"),
            P(("rep", "fsdp"), None),
        ),
        out_specs=(
            P(("rep", "fsdp"), None),
            P(("rep", "fsdp"), None),
            P("fsdp"),
            P("fsdp", None),
            P(None, "fsdp"),
            P("fsdp"),
            P("fsdp"),
            P("fsdp"),
            P("fsdp"),
            P("fsdp"),
            P(None, "fsdp"),
        ),
        check_vma=False,
    )
```

```python
import functools

import jax
import jax.numpy as jnp
from jax import lax
from jax.experimental import pallas as pl
from jax.experimental.pallas import tpu as pltpu
from jax.sharding import PartitionSpec as P

EPS = 1e-05
CHUNK = 128
LANES = 128
HIGHEST = lax.Precision.HIGHEST
F32 = jnp.float32
BF16 = jnp.bfloat16


def dot(left, right, precision=None):
    return lax.dot_general(
        left, right, (((1,), (0,)), ((), ())), precision=precision, preferred_element_type=F32
    )


def dot_nt(left, right):
    return lax.dot_general(left, right, (((1,), (1,)), ((), ())), preferred_element_type=F32)


def sigmoid(v):
    return 0.5 * jnp.tanh(0.5 * v) + 0.5


def softplus(v):
    return jnp.maximum(v, 0.0) + jnp.log1p(jnp.exp(-jnp.abs(v)))


def begin_of(position, first, both):
    return jnp.where(position >= both, both, jnp.where(position >= first, first, 0))


def iotas(rows, columns):
    return (
        lax.broadcasted_iota(jnp.int32, (rows, columns), 0),
        lax.broadcasted_iota(jnp.int32, (rows, columns), 1),
    )


def conv_tile(u_ref, cw_ref, start, columns, masks):
    inputs = [u_ref[start : start + CHUNK, columns]]
    for delay in range(1, 4):
        if start:
            shifted = u_ref[start - delay : start - delay + CHUNK, columns]
        else:
            shifted = pltpu.roll(inputs[0], delay, 0)
        inputs.append(jnp.where(masks[delay - 1], shifted, 0.0))
    pre = cw_ref[4:5, columns] + cw_ref[3:4, columns] * inputs[0]
    for delay in range(1, 4):
        pre = pre + cw_ref[3 - delay : 4 - delay, columns] * inputs[delay]
    return pre


def chunk_rates(dt_ref, hp_ref, start):
    raw = dt_ref[start : start + CHUNK, :] + hp_ref[0:1, :]
    step = softplus(raw)
    rate = -jnp.exp(hp_ref[1:2, :]) * step
    row, column = iotas(CHUNK, CHUNK)
    running = dot((row >= column).astype(F32), rate, HIGHEST)
    return raw, step, rate, running


def pair_of(low, matrix, head):
    return jnp.where(low, matrix[:, head : head + 1], matrix[:, head + 1 : head + 2])


def keys_queries_of(is_high, mine_ref, other_ref, start):
    here = slice(start, start + CHUNK)
    mine, other = mine_ref[here, :], other_ref[here, :]
    return jnp.where(is_high, other, mine), jnp.where(is_high, mine, other)


def forward_kernel(
    heads, size, first_block, len_ref, at_ref, u_ref, dt_ref, kq_ref, kq_other_ref, cw_ref, hp_ref, *refs
):
    y_ref, st_ref, pre_ref, state = refs[-4:]
    block = first_block + pl.program_id(0)
    first = len_ref[block, 0]
    both = first + len_ref[block, 1]
    tokens = u_ref.shape[0]
    chunks = tokens // CHUNK
    row, column = iotas(CHUNK, CHUNK)
    low = column < size
    low_row = low[0:1, :]
    for ci in range(chunks):
        start = ci * CHUNK
        position = row + start
        begin = begin_of(position, first, both)
        masks = [position - delay >= begin for delay in range(1, 4)]
        raw, step, rate, running = chunk_rates(dt_ref, hp_ref, start)
        running_t = running.T
        keys, queries = keys_queries_of(at_ref[1] == 1, kq_ref, kq_other_ref, start)
        keys_t = keys.astype(F32).T.astype(BF16)
        allowed = (column <= row) & (column + start >= begin)
        scores = jnp.where(allowed, dot_nt(queries, keys), 0.0)
        last_begin = begin_of(start + CHUNK - 1, first, both)
        source = position >= last_begin
        reached = begin < start
        ending = running[CHUNK - 1 : CHUNK, :]
        kept = jnp.where(last_begin < start, jnp.exp(ending), 0.0)
        for pair in range(heads // 2):
            h = 2 * pair
            columns = slice(pair * LANES, (pair + 1) * LANES)
            pre = conv_tile(u_ref, cw_ref, start, columns, masks)
            pre_ref[start : start + CHUNK, columns] = pre
            values = pre * sigmoid(pre)
            scaled = values * pair_of(low, step, h)
            weights = []
            for head in (h, h + 1):
                gap = running[:, head : head + 1] - running_t[head : head + 1, :]
                weights.append((scores * jnp.exp(jnp.minimum(gap, 0.0))).astype(BF16))
            stacked = jnp.concatenate(
                [jnp.where(low, scaled, 0.0), jnp.where(low, 0.0, scaled)], axis=0
            ).astype(BF16)
            out = dot(jnp.concatenate(weights, axis=1), stacked)
            out = out + cw_ref[5:6, columns] * values
            across = pair_of(low, running, h)
            if ci:
                carried = dot(queries, state[:, columns].astype(BF16))
                out = out + jnp.where(reached, carried * jnp.exp(across), 0.0)
            y_ref[start : start + CHUNK, columns] = out
            if ci < chunks - 1:
                left = pair_of(low_row, ending, h) - across
                source_in = jnp.where(source, scaled * jnp.exp(left), 0.0).astype(BF16)
                fresh = dot(keys_t, source_in)
                if ci:
                    fresh = fresh + state[:, columns] * pair_of(low_row, kept, h)
                state[:, columns] = fresh
                st_ref[0, ci, :, columns] = fresh.astype(BF16)


def backward_kernel(
    heads,
    size,
    first_head,
    first_block,
    len_ref,
    at_ref,
    u_ref,
    pre_ref,
    dt_ref,
    kq_ref,
    kq_other_ref,
    dy_ref,
    st_ref,
    cw_ref,
    hp_ref,
    *refs,
):
    added = refs[:-10]
    du_ref, ddt_ref, mine_ref, other_ref, cg_ref, hg_ref = refs[-10:-4]
    d_state, d_pre, out_in, source_in = refs[-4:]
    is_high = at_ref[1] == 1
    block = pl.program_id(0)
    first = len_ref[first_block + block, 0]
    both = first + len_ref[first_block + block, 1]
    tokens, width = u_ref.shape
    chunks = tokens // CHUNK
    row, column = iotas(CHUNK, CHUNK)
    low = column < size
    low_row = low[0:1, :]
    wide_row, wide_column = iotas(2 * CHUNK, LANES)
    pick_row, pick_column = iotas(16, 2 * CHUNK)

    @pl.when(block == 0)
    def _():
        cg_ref[...] = jnp.zeros_like(cg_ref)
        hg_ref[...] = jnp.zeros_like(hg_ref)

    d_pre[tokens : tokens + 8, :] = jnp.zeros((8, width), F32)
    for ci in reversed(range(chunks)):
        start = ci * CHUNK
        has_later = ci < chunks - 1
        position = row + start
        begin = begin_of(position, first, both)
        ahead = [begin_of(position + delay, first, both) <= position for delay in range(1, 4)]
        raw, step, rate, running = chunk_rates(dt_ref, hp_ref, start)
        running_t = running.T
        keys, queries = keys_queries_of(is_high, kq_ref, kq_other_ref, start)
        allowed = (row <= column) & (position >= begin_of(column + start, first, both))
        scores = jnp.where(allowed, dot_nt(keys, queries), 0.0)
        last_begin = begin_of(start + CHUNK - 1, first, both)
        source = position >= last_begin
        reached = begin < start
        ending = running[CHUNK - 1 : CHUNK, :]
        kept = jnp.where(last_begin < start, jnp.exp(ending), 0.0)
        d_scores = jnp.zeros((CHUNK, CHUNK), F32)
        later_sums = jnp.zeros((16, CHUNK), F32)
        early_sums = jnp.zeros((CHUNK, LANES), F32)
        out_sums = jnp.zeros((CHUNK, LANES), F32)
        source_sums = jnp.zeros((CHUNK, LANES), F32)
        direct_sums = jnp.zeros((CHUNK, LANES), F32)
        kept_sums = jnp.zeros((8, LANES), F32)
        for pair in range(heads // 2):
            h = first_head + 2 * pair
            columns = slice(pair * LANES, (pair + 1) * LANES)
            to_head = (column == h + (row >= size).astype(jnp.int32)).astype(BF16)
            pre = pre_ref[start : start + CHUNK, columns]
            inputs = u_ref[start : start + CHUNK, columns]
            gate = sigmoid(pre)
            values = pre * gate
            steps = pair_of(low, step, h)
            scaled = values * steps
            d_out = dy_ref[start : start + CHUNK, columns].astype(F32)
            d_low = d_out.astype(BF16)
            stacked = jnp.concatenate(
                [jnp.where(low, scaled, 0.0), jnp.where(low, 0.0, scaled)], axis=0
            ).astype(BF16)
            d_weights = dot_nt(stacked, d_low)
            weights, products = [], []
            for at, head in enumerate((h, h + 1)):
                gap = running_t[head : head + 1, :] - running[:, head : head + 1]
                decay = jnp.exp(jnp.minimum(gap, 0.0))
                d_decayed = decay * d_weights[at * CHUNK : (at + 1) * CHUNK]
                d_scores = d_scores + d_decayed
                products.append((scores * d_decayed).astype(BF16))
                weights.append((scores * decay).astype(BF16))
            early = wide_column == h + (wide_row >= CHUNK).astype(jnp.int32)
            early_sums = early_sums + dot(jnp.concatenate(products, axis=1), early.astype(BF16))
            later = pick_row == h + (pick_column >= CHUNK).astype(jnp.int32)
            later_sums = later_sums + dot(later.astype(BF16), jnp.concatenate(products, axis=0))
            d_stacked = jnp.concatenate(
                [jnp.where(low, d_out, 0.0), jnp.where(low, 0.0, d_out)], axis=0
            ).astype(BF16)
            d_scaled = dot(jnp.concatenate(weights, axis=1), d_stacked)
            across = pair_of(low, running, h)
            if has_later:
                left = jnp.exp(pair_of(low_row, ending, h) - across)
                left = jnp.where(source, left, 0.0)
                d_state_here = d_state[:, columns]
                d_source = dot(keys, d_state_here.astype(BF16)) * left
                d_scaled = d_scaled + d_source
                source_sums = source_sums + dot((scaled * d_source).astype(BF16), to_head)
                source_in[:, columns] = (scaled * left).astype(BF16)
            if ci:
                before = st_ref[0, ci - 1, :, columns]
                d_reach = jnp.where(reached, d_out * jnp.exp(across), 0.0)
                out_sums = out_sums + dot((d_reach * dot(queries, before)).astype(BF16), to_head)
                out_in[:, columns] = d_reach.astype(BF16)
                if has_later:
                    held = jnp.sum(d_state_here * before.astype(F32), axis=0, keepdims=True)
                    held = held * pair_of(low_row, kept, h)
                    kept_sums = kept_sums + dot(
                        jnp.broadcast_to(held, (8, LANES)), to_head.astype(F32), HIGHEST
                    )
            direct_sums = direct_sums + dot((d_scaled * values).astype(BF16), to_head)
            d_values = d_scaled * steps + cw_ref[5:6, columns] * d_out
            cg_ref[5:6, columns] += jnp.sum(d_out * values, axis=0, keepdims=True)
            d_here = d_values * (gate * (1.0 + pre * (1.0 - gate)))
            d_pre[start : start + CHUNK, columns] = d_here
            d_in = cw_ref[3:4, columns] * d_here
            cg_ref[3:4, columns] += jnp.sum(inputs * d_here, axis=0, keepdims=True)
            for delay in range(1, 4):
                shifted = d_pre[start + delay : start + delay + CHUNK, columns]
                shifted = jnp.where(ahead[delay - 1], shifted, 0.0)
                d_in = d_in + cw_ref[3 - delay : 4 - delay, columns] * shifted
                cg_ref[3 - delay : 4 - delay, columns] += jnp.sum(
                    inputs * shifted, axis=0, keepdims=True
                )
            du_ref[start : start + CHUNK, columns] = d_in.astype(BF16)
            cg_ref[4:5, columns] += jnp.sum(d_here, axis=0, keepdims=True)
        d_scores = jnp.where(allowed, d_scores, 0.0)
        d_keys = dot(d_scores.astype(BF16), queries)
        d_queries = dot(d_scores.T.astype(BF16), keys)
        d_running = (
            jnp.concatenate([later_sums, jnp.zeros((CHUNK - 16, CHUNK), F32)], axis=0).T
            - early_sums
            + out_sums
            - source_sums
        )
        if has_later:
            d_keys = d_keys + dot_nt(source_in[...], d_state[...].astype(BF16))
            at_end = jnp.sum(source_sums, axis=0, keepdims=True) + kept_sums[0:1, :]
            d_running = d_running + jnp.where(row == CHUNK - 1, at_end, 0.0)
        if ci:
            d_queries = d_queries + dot_nt(out_in[...], st_ref[0, ci - 1])
            queries_t = queries.astype(F32).T.astype(BF16)
            for pair in range(heads // 2):
                columns = slice(pair * LANES, (pair + 1) * LANES)
                fresh = dot(queries_t, out_in[:, columns])
                if has_later:
                    fresh = fresh + d_state[:, columns] * pair_of(low_row, kept, first_head + 2 * pair)
                d_state[:, columns] = fresh
        here = slice(start, start + CHUNK)
        mine = jnp.where(is_high, d_queries, d_keys)
        other = jnp.where(is_high, d_keys, d_queries)
        if added:
            mine, other = mine + added[0][here, :], other + added[1][here, :]
        mine_ref[here, :] = mine.astype(mine_ref.dtype)
        other_ref[here, :] = other.astype(other_ref.dtype)
        d_rate = dot((row <= column).astype(F32), d_running, HIGHEST)
        d_step = direct_sums - jnp.exp(hp_ref[1:2, :]) * d_rate
        d_raw = d_step * sigmoid(raw)
        ddt_ref[start : start + CHUNK, :] = d_raw.astype(BF16)
        hg_ref[0:1, :] += jnp.sum(d_raw, axis=0, keepdims=True)
        hg_ref[1:2, :] += jnp.sum(d_rate * rate, axis=0, keepdims=True)


def prepare_first_kernel(heads, size, state, at_ref, in_ref, mine_ref, other_ref):
    x, core = at_ref[0], at_ref[1]
    width = heads * size
    inner = 4 * width
    steps_at = 2 * inner + 2 * state
    steps = in_ref[:, steps_at : steps_at + 4 * heads].astype(F32)
    rows = steps.shape[0]
    steps = jnp.concatenate([steps, jnp.zeros((rows, LANES - 4 * heads), F32)], axis=1)
    column = lax.broadcasted_iota(jnp.int32, (rows, LANES), 1)
    for ref, c in ((mine_ref, core), (other_ref, 1 - core)):
        p = 2 * x + c
        values_at = pl.multiple_of(inner + p * width, LANES)
        ref[:, :width] = in_ref[:, pl.ds(values_at, width)]
        drawn = pltpu.roll(steps, lax.rem(LANES - heads * p, LANES), 1)
        ref[:, width : width + LANES] = jnp.where(column < heads, drawn, 0.0).astype(BF16)
        keys_at = pl.multiple_of(2 * inner + c * state, LANES)
        ref[:, width + LANES : width + LANES + state] = in_ref[:, pl.ds(keys_at, state)]


def prepare_last_kernel(width, at_ref, in_ref, out_ref, mine_ref, other_ref):
    x, core = at_ref[0], at_ref[1]
    for ref, c in ((mine_ref, core), (other_ref, 1 - core)):
        at = pl.multiple_of((2 * x + c) * width, LANES)
        ref[:, :width] = in_ref[:, pl.ds(at, width)]
        ref[:, width:] = out_ref[:, pl.ds(at, width)]


def prepare_call(kernel, columns, place, *weights):
    rows = weights[0].shape[0]
    return pl.pallas_call(
        kernel,
        in_specs=[pl.BlockSpec(memory_space=pltpu.SMEM)]
        + [pl.BlockSpec(memory_space=pltpu.VMEM)] * len(weights),
        out_specs=[pl.BlockSpec(memory_space=pltpu.VMEM)] * 2,
        out_shape=[jax.ShapeDtypeStruct((rows, columns), BF16)] * 2,
        compiler_params=pltpu.CompilerParams(vmem_limit_bytes=24 * 1024 * 1024),
        name="prepare",
    )(place, *weights)


def unpack_kernel(sizes, heads, size, state, at_ref, small_ref, n_ref, conv_ref, head_ref, kq_ref, all_ref):
    conv_size, gate_size, norm_size, head_size = sizes
    x, c = at_ref[0], at_ref[1]
    p = 2 * x + c
    shards = small_ref.shape[0] // 8
    width = heads * size

    def joined(first_row, rows, at, part, columns):
        padded = -(-columns // LANES) * LANES
        lanes = -(-part // LANES) * LANES
        lane = lax.broadcasted_iota(jnp.int32, (8, lanes), 1)
        result = jnp.zeros((8, padded), F32)
        for f in range(shards):
            rows_here = small_ref[8 * f : 8 * f + 8, at : at + lanes].astype(F32)
            rows_here = jnp.where(lane < part, rows_here, 0.0)
            if padded > lanes:
                rows_here = jnp.concatenate(
                    [rows_here, jnp.zeros((8, padded - lanes), F32)], axis=1
                )
            result = result + pltpu.roll(rows_here, (part * f) % padded, 1)
        return result[first_row : first_row + rows]

    conv_all = joined(0, 5, 0, conv_size, conv_size * shards)
    gate_all = joined(5, 1, 0, gate_size, gate_size * shards)
    norm_all = joined(6, 1, 0, norm_size, norm_size * shards)
    n_ref[...] = jnp.broadcast_to(norm_all, n_ref.shape)
    all_ref[...] = jnp.zeros_like(all_ref)
    all_ref[0:5, : conv_all.shape[1]] = conv_all
    all_ref[6:7, : gate_all.shape[1]] = gate_all
    conv_ref[...] = all_ref[:, pl.ds(pl.multiple_of(p * width, LANES), width)]
    kq_at = 4 * width + c * state
    kq_ref[...] = all_ref[:, pl.ds(pl.multiple_of(kq_at, LANES), state)]
    column = lax.broadcasted_iota(jnp.int32, (8, LANES), 1)
    head_ref[...] = jnp.zeros_like(head_ref)
    for row in range(3):
        values = joined(7, 1, row * LANES, head_size, head_size * shards)
        values = jnp.broadcast_to(values, (8, LANES))
        values = pltpu.roll(values, lax.rem(LANES - heads * p, LANES), 1)
        head_ref[row : row + 1, :] = jnp.where(column < heads, values, 0.0)[0:1]
    row_at, column_at = iotas(LANES, width)
    spread = (row_at == column_at // size).astype(F32)
    conv_ref[5:6, :] = dot(head_ref[...], spread, HIGHEST)[2:3]


def unpack_call(sizes, heads, size, state, place, small):
    shards = small.shape[0] // 8
    depth, width = sizes[2] * shards, heads * size
    columns = -(-sizes[0] * shards // LANES) * LANES
    return pl.pallas_call(
        functools.partial(unpack_kernel, sizes, heads, size, state),
        in_specs=[
            pl.BlockSpec(memory_space=pltpu.SMEM),
            pl.BlockSpec(memory_space=pltpu.VMEM),
        ],
        out_specs=[pl.BlockSpec(memory_space=pltpu.VMEM)] * 4,
        out_shape=[
            jax.ShapeDtypeStruct((8, depth), F32),
            jax.ShapeDtypeStruct((8, width), F32),
            jax.ShapeDtypeStruct((8, LANES), F32),
            jax.ShapeDtypeStruct((8, state), F32),
        ],
        scratch_shapes=[pltpu.VMEM((8, columns), F32)],
        compiler_params=pltpu.CompilerParams(vmem_limit_bytes=24 * 1024 * 1024),
        name="unpack",
    )(place, small)


def assemble_rows(links_shape, at_ref, own_ref, core_ref, pieces, whole_ref):
    sides, groups = links_shape
    a, g, c = at_ref[0], at_ref[1], at_ref[2]
    rows = own_ref.shape[0]
    part = 2 * rows // sides
    base = g * (2 * rows)
    whole_ref[pl.ds(pl.multiple_of(base + c * rows, 16), rows), :] = own_ref[...]
    whole_ref[pl.ds(pl.multiple_of(base + (1 - c) * rows, 16), rows), :] = core_ref[...]
    for k in range(1, groups):
        base = lax.rem(g + groups - k, groups) * (2 * rows)
        for j in range(sides):
            at = base + lax.rem(a + sides - j, sides) * part
            piece = pieces[(k - 1) * sides + j]
            whole_ref[pl.ds(pl.multiple_of(at, 16), part), :] = piece[...]


def project_kernel(links_shape, at_ref, own_ref, core_ref, *refs):
    pieces, (rows_ref, whole_ref, out_ref) = refs[:-3], refs[-3:]

    @pl.when(pl.program_id(0) == 0)
    def _():
        assemble_rows(links_shape, at_ref, own_ref, core_ref, pieces, whole_ref)

    out_ref[...] = dot(rows_ref[...], whole_ref[...]).astype(out_ref.dtype)


def whole_spec(array):
    return pl.BlockSpec(array.shape, lambda b: (0,) * array.ndim)


def columns_spec(array, width, index):
    if array.shape[1] == width:
        index = 0
    return pl.BlockSpec((array.shape[0], width), lambda b: (0, index))


def project_call(links_shape, width, index, blocks, tokens, kind, place, parts, rows):
    depth = rows.shape[1]
    return pl.pallas_call(
        functools.partial(project_kernel, links_shape),
        grid=(blocks,),
        in_specs=[pl.BlockSpec(memory_space=pltpu.SMEM)]
        + [columns_spec(array, width, index) for array in parts]
        + [pl.BlockSpec((tokens, depth), lambda b: (b, 0))],
        out_specs=[
            pl.BlockSpec((depth, width), lambda b: (0, 0)),
            pl.BlockSpec((tokens, width), lambda b: (b, 0)),
        ],
        out_shape=[
            jax.ShapeDtypeStruct((depth, width), BF16),
            jax.ShapeDtypeStruct((blocks * tokens, width), kind),
        ],
        compiler_params=pltpu.CompilerParams(vmem_limit_bytes=40 * 1024 * 1024),
        cost_estimate=pl.CostEstimate(
            flops=2 * rows.size * width, bytes_accessed=2 * rows.size, transcendentals=0
        ),
        name="project",
    )(place, *parts, rows)


def branch_back_kernel(links_shape, counts, at_ref, own_ref, core_ref, *refs):
    pieces, rows_refs = refs[: -6 - sum(counts)], list(refs[-6 - sum(counts) : -6])
    gate_ref, ssd_ref, cw_ref, whole_ref, out_ref, sums_ref = refs[-6:]
    block = pl.program_id(0)

    @pl.when(block == 0)
    def _():
        assemble_rows(links_shape, at_ref, own_ref, core_ref, pieces, whole_ref)

    for at, count in enumerate(counts):
        parts = [rows_refs.pop(0) for _ in range(count)]

        @pl.when(block == at)
        def _():
            first_row = 0
            for part in parts:
                stop = first_row + part.shape[0]
                out_ref[first_row:stop, :] = dot(part[...], whole_ref[...])
                first_row = stop

    tokens, width = out_ref.shape
    sums_ref[...] = jnp.zeros_like(sums_ref)
    for start in range(0, tokens, CHUNK):
        squares = jnp.zeros((CHUNK, LANES), F32)
        products = jnp.zeros((CHUNK, LANES), F32)
        for left in range(0, width, LANES):
            tile = (slice(start, start + CHUNK), slice(left, left + LANES))
            gate = gate_ref[tile].astype(F32)
            gated = ssd_ref[tile] * (gate * sigmoid(gate))
            squares = squares + gated * gated
            products = products + gated * (cw_ref[6:7, left : left + LANES] * out_ref[tile])
        sums_ref[0:1, start : start + CHUNK] = jnp.sum(squares.T, axis=0, keepdims=True)
        sums_ref[1:2, start : start + CHUNK] = jnp.sum(products.T, axis=0, keepdims=True)


def branch_back_call(links_shape, width, index, place, parts, rows, gate, ssd_out, conv_rows):
    tokens, depth = ssd_out.shape[0] // 4, rows[0][0].shape[1]
    counts = [len(block) for block in rows]
    rows = [part for block in rows for part in block]
    block = pl.BlockSpec((tokens, width), lambda b: (b, 0))
    return pl.pallas_call(
        functools.partial(branch_back_kernel, links_shape, counts),
        grid=(4,),
        in_specs=[pl.BlockSpec(memory_space=pltpu.SMEM)]
        + [columns_spec(array, width, index) for array in parts]
        + [whole_spec(array) for array in rows]
        + [block, block, pl.BlockSpec((8, width), lambda b: (0, 0))],
        out_specs=[
            pl.BlockSpec((depth, width), lambda b: (0, 0)),
            block,
            pl.BlockSpec((8, tokens), lambda b: (0, b)),
        ],
        out_shape=[
            jax.ShapeDtypeStruct((depth, width), BF16),
            jax.ShapeDtypeStruct((4 * tokens, width), F32),
            jax.ShapeDtypeStruct((8, 4 * tokens), F32),
        ],
        compiler_params=pltpu.CompilerParams(vmem_limit_bytes=56 * 1024 * 1024),
        cost_estimate=pl.CostEstimate(
            flops=8 * tokens * depth * width, bytes_accessed=8 * tokens * depth, transcendentals=0
        ),
        name="branch_back",
    )(place, *parts, *rows, gate, ssd_out, conv_rows)


def gating_back_kernel(
    inner, sums_ref, core_ref, side_ref, both_ref, gate_ref, ssd_ref, db_ref, cw_ref,
    branch_ref, dgate_ref, dssd_ref, gain_ref
):
    @pl.when(pl.program_id(0) == 0)
    def _():
        gain_ref[...] = jnp.zeros_like(gain_ref)

    sums = sums_ref[...] + core_ref[...] + side_ref[...] + both_ref[...]
    scale_row = lax.rsqrt(sums[0:1, :] * (1.0 / inner) + EPS)
    cross_row = scale_row * scale_row * scale_row * (sums[1:2, :] * (1.0 / inner))
    tokens, width = gate_ref.shape
    for start in range(0, tokens, CHUNK):
        stacked = jnp.concatenate(
            [scale_row[:, start : start + CHUNK], cross_row[:, start : start + CHUNK],
             jnp.zeros((CHUNK - 2, CHUNK), F32)], axis=0
        ).T
        scale, cross = stacked[:, 0:1], stacked[:, 1:2]
        for left in range(0, width, LANES):
            columns = slice(left, left + LANES)
            tile = (slice(start, start + CHUNK), columns)
            gate, ssd, d_branch = gate_ref[tile].astype(F32), ssd_ref[tile], db_ref[tile]
            gain = cw_ref[6:7, columns]
            sig = sigmoid(gate)
            act = gate * sig
            gated = ssd * act
            scaled = gated * scale
            branch_ref[tile] = (scaled * gain).astype(BF16)
            gain_ref[0:1, columns] += jnp.sum(d_branch * scaled, axis=0, keepdims=True)
            d_gated = scale * (gain * d_branch) - gated * cross
            dssd_ref[tile] = d_gated * act
            dgate_ref[tile] = (d_gated * ssd * (sig * (1.0 + gate * (1.0 - sig)))).astype(BF16)


def gating_back_call(inner, sums, gate, ssd_out, d_branch, conv_rows):
    rows, columns = gate.shape
    tokens = rows // 4
    block = pl.BlockSpec((tokens, columns), lambda b: (b, 0))
    order = [lambda b: (0, b)]
    order.append(lambda b: (0, b + 1 - 2 * lax.rem(b, 2)))
    order.append(lambda b: (0, lax.rem(b + 2, 4)))
    order.append(lambda b: (0, 3 - b))
    return pl.pallas_call(
        functools.partial(gating_back_kernel, inner),
        grid=(4,),
        in_specs=[pl.BlockSpec((8, tokens), index) for index in order]
        + [block, block, block, pl.BlockSpec((8, columns), lambda b: (0, 0))],
        out_specs=[block, block, block, pl.BlockSpec((8, columns), lambda b: (0, 0))],
        out_shape=[
            jax.ShapeDtypeStruct((rows, columns), BF16),
            jax.ShapeDtypeStruct((rows, columns), BF16),
            jax.ShapeDtypeStruct((rows, columns), F32),
            jax.ShapeDtypeStruct((8, columns), F32),
        ],
        compiler_params=pltpu.CompilerParams(vmem_limit_bytes=40 * 1024 * 1024),
        cost_estimate=pl.CostEstimate(
            flops=20 * rows * columns, bytes_accessed=20 * rows * columns, transcendentals=0
        ),
        name="gating_back",
    )(*sums, gate, ssd_out, d_branch, conv_rows)


def normalize_kernel(*refs):
    rows_refs, (gain_ref, normed_ref, scale_ref) = refs[:4], refs[4:]
    for at, rows_ref in enumerate(rows_refs):

        @pl.when(pl.program_id(0) == at)
        def _():
            depth = rows_ref.shape[1]
            for start in range(0, rows_ref.shape[0], 64):
                rows = rows_ref[start : start + 64, :].astype(F32)
                mean = jnp.sum(rows * rows, axis=1, keepdims=True) * (1.0 / depth)
                scale = lax.rsqrt(mean + EPS)
                normed = rows * scale * gain_ref[0:1, :]
                normed_ref[start : start + 64, :] = normed.astype(BF16)
                scale_ref[start : start + 64, :] = jnp.broadcast_to(scale, (64, LANES))


def normalize_call(blocks, gain):
    tokens, depth = blocks[0].shape
    return pl.pallas_call(
        normalize_kernel,
        grid=(4,),
        in_specs=[whole_spec(block) for block in blocks] + [whole_spec(gain)],
        out_specs=[
            pl.BlockSpec((tokens, depth), lambda b: (b, 0)),
            pl.BlockSpec((tokens, LANES), lambda b: (b, 0)),
        ],
        out_shape=[
            jax.ShapeDtypeStruct((4 * tokens, depth), BF16),
            jax.ShapeDtypeStruct((4 * tokens, LANES), F32),
        ],
        compiler_params=pltpu.CompilerParams(vmem_limit_bytes=40 * 1024 * 1024),
        name="normalize",
    )(*blocks, gain)


def weight_grad_kernel(links_shape, groups_of_terms, over_a, at_ref, *refs):
    sides, groups = links_shape
    count = sum(len(terms) for terms in groups_of_terms)
    left_count = 1 + max(left_at for terms in groups_of_terms for left_at, _ in terms)
    lefts, rights = refs[:left_count], refs[left_count : left_count + count]
    outs, scratch = refs[left_count + count : -1], refs[-1]
    at_column, at_term = 0, 0
    for terms in groups_of_terms:
        result = None
        for left_at, first_row in terms:
            right = rights[at_term][...]
            term = lax.dot_general(
                lefts[left_at][first_row : first_row + right.shape[0], :],
                right,
                (((0,), (0,)), ((), ())),
                preferred_element_type=F32,
            )
            result = term if result is None else result + term
            at_term += 1
        width = result.shape[1]
        scratch[:, at_column : at_column + width] = result.astype(BF16)
        at_column += width
    if over_a:
        chips, part = outs[0].shape[0], outs[0].shape[1]
        for chip in range(chips):
            for j, out in enumerate(outs):
                at = (chip * sides + lax.rem(at_ref[0] + j, sides)) * part
                out[chip] = scratch[pl.ds(pl.multiple_of(at, 16), part), :]
        return
    rows = outs[0].shape[0]
    chips = scratch.shape[0] // rows
    for chip in range(chips):
        turn = lax.rem(pl.program_id(0) * chips + chip + groups - at_ref[1], groups)
        for k, out in enumerate(outs):

            @pl.when(turn == k)
            def _():
                out[...] = scratch[chip * rows : (chip + 1) * rows, :]


def weight_grad_call(links_shape, over_a, place, groups_of_terms):
    sides, groups = links_shape
    terms = [term for group in groups_of_terms for term in group]
    depth = terms[0][0].shape[1]
    columns = sum(group[0][5] for group in groups_of_terms)
    rows = depth // groups
    part = rows // sides
    chips = 1
    while chips * rows % LANES:
        chips += 1
    lefts = []
    for term in terms:
        if not any(term[0] is left for left in lefts):
            lefts.append(term[0])

    def left_at(term):
        return [term[0] is left for left in lefts].index(True)

    def left_spec(left):
        return pl.BlockSpec((left.shape[0], chips * rows), lambda b: (0, b))

    def right_spec(term):
        return pl.BlockSpec((term[1], term[5]), lambda b: (term[4], term[6]))

    if over_a:
        out_specs = [pl.BlockSpec((chips, part, columns), lambda b: (b, 0, 0))] * sides
        out_shape = [jax.ShapeDtypeStruct((groups, part, columns), BF16)] * sides
    else:
        out_specs = [pl.BlockSpec((rows, columns), lambda b: (0, 0))] * groups
        out_shape = [jax.ShapeDtypeStruct((rows, columns), BF16)] * groups
    shapes = tuple(
        tuple((left_at(term), term[1] * term[2]) for term in group) for group in groups_of_terms
    )
    return pl.pallas_call(
        functools.partial(weight_grad_kernel, links_shape, shapes, over_a),
        grid=(groups // chips,),
        in_specs=[pl.BlockSpec(memory_space=pltpu.SMEM)]
        + [left_spec(left) for left in lefts]
        + [right_spec(term) for term in terms],
        out_specs=out_specs,
        out_shape=out_shape,
        scratch_shapes=[pltpu.VMEM((chips * rows, columns), BF16)],
        compiler_params=pltpu.CompilerParams(vmem_limit_bytes=48 * 1024 * 1024),
        cost_estimate=pl.CostEstimate(
            flops=2 * terms[0][1] * depth * columns,
            bytes_accessed=2 * terms[0][1] * depth,
            transcendentals=0,
        ),
        name="weight_grad",
    )(place, *lefts, *[term[3] for term in terms])


def combine_kernel(groups, at_ref, *refs):
    parts, outs = refs[:-groups], refs[-groups:]
    result = parts[0][0].astype(F32)
    for part in parts[1:]:
        result = result + part[0].astype(F32)
    turn = lax.rem(pl.program_id(0) + groups - at_ref[1], groups)
    for k, out in enumerate(outs):

        @pl.when(turn == k)
        def _():
            out[...] = result.astype(BF16)


def combine_call(groups, place, parts):
    rows, columns = parts[0].shape[1:]
    return pl.pallas_call(
        functools.partial(combine_kernel, groups),
        grid=(groups,),
        in_specs=[pl.BlockSpec(memory_space=pltpu.SMEM)]
        + [pl.BlockSpec((1, rows, columns), lambda b: (b, 0, 0))] * len(parts),
        out_specs=[pl.BlockSpec((rows, columns), lambda b: (0, 0))] * groups,
        out_shape=[jax.ShapeDtypeStruct((rows, columns), BF16)] * groups,
        compiler_params=pltpu.CompilerParams(vmem_limit_bytes=24 * 1024 * 1024),
        name="combine",
    )(place, *parts)


def keys_front_kernel(len_ref, in_ref, rows_ref, out_ref):
    tokens, columns = in_ref.shape[0] // 2, in_ref.shape[1]
    position = lax.broadcasted_iota(jnp.int32, (tokens, columns), 0)
    row, lane = iotas(16, columns)
    counts = jnp.zeros((16, columns), jnp.int32)
    for block in range(2):
        first = len_ref[block, 0]
        both = first + len_ref[block, 1]
        begin = begin_of(position, first, both)
        inputs = in_ref[block * tokens : (block + 1) * tokens, :]
        pre = rows_ref[4:5, :] + rows_ref[3:4, :] * inputs
        for delay in range(1, 4):
            shifted = jnp.where(position - delay >= begin, pltpu.roll(inputs, delay, 0), 0.0)
            pre = pre + rows_ref[3 - delay : 4 - delay, :] * shifted
        out_ref[block * tokens : (block + 1) * tokens, :] = (pre * sigmoid(pre)).astype(BF16)
        for sequence in range(2):
            length = len_ref[block, sequence]
            here = row == block
            counts = jnp.where(here & (lane == 2 * sequence), lax.div(length, 32), counts)
            counts = jnp.where(here & (lane == 2 * sequence + 1), lax.rem(length, 32), counts)
    out_ref[2 * tokens :, :] = counts.astype(F32).astype(BF16)


def keys_front_call(lengths, inputs, rows):
    total, columns = inputs.shape
    return pl.pallas_call(
        keys_front_kernel,
        in_specs=[
            pl.BlockSpec(memory_space=pltpu.SMEM),
            pl.BlockSpec(memory_space=pltpu.VMEM),
            pl.BlockSpec(memory_space=pltpu.VMEM),
        ],
        out_specs=pl.BlockSpec(memory_space=pltpu.VMEM),
        out_shape=jax.ShapeDtypeStruct((total + 16, columns), BF16),
        compiler_params=pltpu.CompilerParams(vmem_limit_bytes=24 * 1024 * 1024),
        name="keys_front",
    )(lengths, inputs, rows)


def norm_back_kernel(keep_ref, core_ref, *refs):
    far_refs, (hidden_ref, back_ref, scale_ref, gain_ref, out_ref) = refs[:3], refs[3:]
    block = pl.program_id(0)
    far = jnp.where(block == 0, far_refs[0][...], far_refs[1][...])
    far = jnp.where(block <= 1, far, far_refs[2][...]).astype(F32)
    hidden, scale = hidden_ref[...].astype(F32), scale_ref[:, 0:1]
    weighted = gain_ref[0:1, :] * (keep_ref[...] + core_ref[...].astype(F32) + far)
    mean = jnp.sum(hidden * weighted, axis=1, keepdims=True) * (1.0 / hidden.shape[1])
    cross = scale * scale * scale * mean
    out_ref[...] = back_ref[...].astype(F32) + scale * weighted - hidden * cross


def norm_back_call(keep, core, far, hidden, back, scale, gain):
    tokens, depth = keep.shape
    rows = tokens // 4
    block = pl.BlockSpec((rows, depth), lambda b: (b, 0))
    quarter = pl.BlockSpec((rows, depth), lambda b: (0, 0))
    later = pl.BlockSpec((rows, depth), lambda b: (jnp.maximum(b - 2, 0), 0))
    return pl.pallas_call(
        norm_back_kernel,
        grid=(4,),
        in_specs=[
            block, block, quarter, quarter, later, block, block,
            pl.BlockSpec((rows, LANES), lambda b: (b, 0)),
            whole_spec(gain),
        ],
        out_specs=block,
        out_shape=jax.ShapeDtypeStruct((tokens, depth), F32),
        compiler_params=pltpu.CompilerParams(vmem_limit_bytes=32 * 1024 * 1024),
        cost_estimate=pl.CostEstimate(
            flops=4_000_000_000, bytes_accessed=12_000_000, transcendentals=0
        ),
        name="norm_back",
    )(keep, core, *far, hidden, back, scale, gain)


def keys_back_kernel(len_ref, mine_ref, core_ref, side_ref, in_ref, rows_ref, d_ref, grads_ref):
    block = pl.program_id(0)
    first = len_ref[block, 0]
    both = first + len_ref[block, 1]
    tokens, columns = in_ref.shape
    position = lax.broadcasted_iota(jnp.int32, (tokens, columns), 0)
    begin = begin_of(position, first, both)
    inside = [position - delay >= begin for delay in range(1, 4)]
    inputs = [in_ref[...]]
    for delay in range(1, 4):
        shifted = pltpu.roll(inputs[0], delay, 0)
        inputs.append(jnp.where(inside[delay - 1], shifted, 0.0))
    pre = rows_ref[4:5, :] + rows_ref[3:4, :] * inputs[0]
    for delay in range(1, 4):
        pre = pre + rows_ref[3 - delay : 4 - delay, :] * inputs[delay]
    sig = sigmoid(pre)
    d_out = mine_ref[...] + core_ref[...].astype(F32) + side_ref[...].astype(F32)
    d_pre = d_out * (sig * (1.0 + pre * (1.0 - sig)))
    d_in = rows_ref[3:4, :] * d_pre
    for delay in range(1, 4):
        moved = pltpu.roll(jnp.where(inside[delay - 1], d_pre, 0.0), tokens - delay, 0)
        d_in = d_in + rows_ref[3 - delay : 4 - delay, :] * moved
    d_ref[...] = d_in.astype(BF16)

    @pl.when(block == 0)
    def _():
        grads_ref[...] = jnp.zeros_like(grads_ref)

    for delay in range(4):
        grads_ref[3 - delay : 4 - delay, :] += jnp.sum(
            inputs[delay] * d_pre, axis=0, keepdims=True
        )
    grads_ref[4:5, :] += jnp.sum(d_pre, axis=0, keepdims=True)


def keys_back_call(lengths, parts, inputs, rows):
    total, columns = inputs.shape
    block = pl.BlockSpec((total // 2, columns), lambda b: (b, 0))
    small = pl.BlockSpec((8, columns), lambda b: (0, 0))
    return pl.pallas_call(
        keys_back_kernel,
        grid=(2,),
        in_specs=[pl.BlockSpec(memory_space=pltpu.SMEM)] + [block] * 4 + [small],
        out_specs=[block, small],
        out_shape=[
            jax.ShapeDtypeStruct((total, columns), BF16),
            jax.ShapeDtypeStruct((8, columns), F32),
        ],
        compiler_params=pltpu.CompilerParams(vmem_limit_bytes=24 * 1024 * 1024),
        name="keys_back",
    )(lengths, *parts, inputs, rows)


def small_kernel(heads, size, at_ref, *refs):
    convs, head_refs, (gain_ref, kq_ref, out_ref) = refs[:3], refs[3:6], refs[6:]
    p = 2 * at_ref[0] + at_ref[1]
    width = heads * size
    most, less = convs[0].shape[1], convs[1].shape[1]
    out_ref[...] = jnp.zeros_like(out_ref)
    rest = convs[1][...] + convs[2][...]
    at = pl.multiple_of(p * width, LANES)
    out_ref[0:5, pl.ds(at, most)] = convs[0][0:5, :]
    out_ref[0:5, pl.ds(pl.multiple_of(at + most, LANES), less)] = rest[0:5, :]
    kq_at = pl.multiple_of(4 * width + at_ref[1] * kq_ref.shape[1], LANES)
    out_ref[0:5, pl.ds(kq_at, kq_ref.shape[1])] = kq_ref[0:5, :]
    out_ref[5:6, pl.ds(at, width)] = gain_ref[0:1, :]
    skip = jnp.concatenate([convs[0][...], rest], axis=1)
    row, column = iotas(width, LANES)
    skip = dot(skip, (row // size == column).astype(F32), HIGHEST)
    sums = head_refs[0][...] + head_refs[1][...] + head_refs[2][...]
    for field, values in enumerate((sums[0:1], sums[1:2], skip[5:6])):
        values = jnp.broadcast_to(values, (8, LANES))
        lane = lax.broadcasted_iota(jnp.int32, (8, LANES), 1)
        values = pltpu.roll(jnp.where(lane < heads, values, 0.0), heads * p, 1)
        out_ref[7:8, field * LANES : (field + 1) * LANES] = values[0:1]


def small_call(heads, size, channels, place, convs, head_grads, gains, kq_grads):
    operands = [*convs, *head_grads, gains, kq_grads]
    return pl.pallas_call(
        functools.partial(small_kernel, heads, size),
        in_specs=[pl.BlockSpec(memory_space=pltpu.SMEM)]
        + [pl.BlockSpec(memory_space=pltpu.VMEM)] * len(operands),
        out_specs=pl.BlockSpec(memory_space=pltpu.VMEM),
        out_shape=jax.ShapeDtypeStruct((8, channels), F32),
        compiler_params=pltpu.CompilerParams(vmem_limit_bytes=24 * 1024 * 1024),
        name="small_gradients",
    )(place, *operands)


def final_kernel(heads, size, most, by_g, at_ref, *refs):
    first_both, first_other, held_mine, held_core, last_mine, last_core = refs[:6]
    weight_ref, gain_ref, in_ref, out_ref, norm_ref = refs[6:]
    far, high = at_ref[0] == 1, at_ref[1] == 1
    width = heads * size
    less = width - most
    rows = in_ref.shape[0]
    at_values, at_keys = 4 * width, 8 * width
    state = last_mine.shape[1] - 2 * (less + LANES)
    at_steps = at_keys + 2 * state
    norm = jnp.zeros((rows, 1), F32)

    def put(at, values):
        stop = at + values.shape[1]
        in_ref[:, at:stop] = values
        weight = weight_ref[:, at:stop].astype(F32)
        return jnp.sum(values * weight, axis=1, keepdims=True)

    def share(both, other, p, count, start, stop):
        columns = slice((p % 2) * count + start, (p % 2) * count + stop)
        take_other = far if p < 2 else jnp.logical_not(far)
        return jnp.where(take_other, other[:, columns], both[:, columns]).astype(F32)

    def core_share(mine, other, core, start, stop):
        take_other = high if core == 0 else jnp.logical_not(high)
        columns = slice(start, stop)
        return jnp.where(take_other, other[:, columns], mine[:, columns]).astype(F32)

    last_share = functools.partial(core_share, last_mine, last_core)
    held_share = functools.partial(core_share, held_mine, held_core)

    steps = jnp.zeros((rows, LANES), F32)
    lane = lax.broadcasted_iota(jnp.int32, (rows, LANES), 1)
    for p in range(4):
        first = functools.partial(share, first_both, first_other, p, 2 * width - by_g)
        norm = norm + put(p * width, first(0, width))
        left = (p // 2) * (by_g + most)
        out_ref[:, p * width : p * width + by_g] = held_share(p % 2, left, left + by_g)
        out_ref[:, p * width + by_g : (p + 1) * width] = first(width, 2 * width - by_g)
        at = at_values + p * width
        norm = norm + put(at, held_share(p % 2, left + by_g, left + by_g + most))
        left = (p // 2) * (less + LANES)
        norm = norm + put(at + most, last_share(p % 2, left, left + less))
        drawn = last_share(p % 2, left + less, left + less + LANES)
        steps = steps + pltpu.roll(jnp.where(lane < heads, drawn, 0.0), heads * p, 1)
    for core in range(2):
        at = 2 * (less + LANES)
        norm = norm + put(at_keys + core * state, last_share(core, at, at + state))
    norm = norm + put(at_steps, steps[:, : 4 * heads])
    norm_ref[...] = norm / gain_ref[...]


def final_call(heads, size, most, by_g, place, shares, weight, gain):
    rows, columns = weight.shape
    operands = [*shares, weight, gain]
    return pl.pallas_call(
        functools.partial(final_kernel, heads, size, most, by_g),
        in_specs=[pl.BlockSpec(memory_space=pltpu.SMEM)]
        + [pl.BlockSpec(memory_space=pltpu.VMEM)] * len(operands),
        out_specs=[pl.BlockSpec(memory_space=pltpu.VMEM)] * 3,
        out_shape=[
            jax.ShapeDtypeStruct((rows, columns), F32),
            jax.ShapeDtypeStruct((rows, 4 * heads * size), F32),
            jax.ShapeDtypeStruct((rows, 1), F32),
        ],
        compiler_params=pltpu.CompilerParams(vmem_limit_bytes=40 * 1024 * 1024),
        cost_estimate=pl.CostEstimate(
            flops=5_000_000_000, bytes_accessed=16_000_000, transcendentals=0
        ),
        name="owner_gradients",
    )(place, *operands)


def forward_call(
    heads, size, first_block, blocks, lengths, place, conv_in, keys_queries, conv_rows, head_rows, before=()
):
    total = conv_in.shape[0]
    tokens = total // lengths.shape[0]
    width = heads * size
    state = keys_queries[0].shape[1]
    boundaries = tokens // CHUNK - 1
    return pl.pallas_call(
        functools.partial(forward_kernel, heads, size, first_block),
        grid=(blocks,),
        in_specs=[
            pl.BlockSpec(memory_space=pltpu.SMEM),
            pl.BlockSpec(memory_space=pltpu.SMEM),
            pl.BlockSpec((tokens, width), lambda b: (first_block + b, 0)),
            pl.BlockSpec((tokens, LANES), lambda b: (first_block + b, width // LANES)),
            pl.BlockSpec((tokens, state), lambda b: (first_block + b, 0)),
            pl.BlockSpec((tokens, state), lambda b: (first_block + b + 1 - 2 * lax.rem(b, 2), 0)),
            pl.BlockSpec((8, width), lambda b: (0, 0)),
            pl.BlockSpec((8, LANES), lambda b: (0, 0)),
        ]
        + [pl.BlockSpec(memory_space=pl.ANY)] * len(before),
        out_specs=[
            pl.BlockSpec((tokens, width), lambda b: (first_block + b, 0)),
            pl.BlockSpec((1, boundaries, state, width), lambda b: (first_block + b, 0, 0, 0)),
            pl.BlockSpec((tokens, width), lambda b: (first_block + b, 0)),
        ],
        out_shape=[
            jax.ShapeDtypeStruct((total, width), F32),
            jax.ShapeDtypeStruct((lengths.shape[0], boundaries, state, width), BF16),
            jax.ShapeDtypeStruct((total, width), F32),
        ],
        scratch_shapes=[pltpu.VMEM((state, width), F32)],
        input_output_aliases={8 + at: at for at in range(len(before))},
        compiler_params=pltpu.CompilerParams(vmem_limit_bytes=40 * 1024 * 1024),
        cost_estimate=pl.CostEstimate(
            flops=blocks * 3_000_000_000, bytes_accessed=blocks * 8_000_000, transcendentals=0
        ),
        name="ssd_forward",
    )(lengths, place, conv_in, conv_in, *keys_queries, conv_rows, head_rows, *before)


def backward_call(
    heads, size, first_head, first_block, blocks,
    lengths, place, conv_in, conv_pre, keys_queries, d_out, states, conv_rows, head_rows, before=()
):
    tokens = conv_in.shape[0] // lengths.shape[0]
    total = blocks * tokens
    width = heads * size
    part = first_head * size // width
    steps_at = d_out.shape[1] // LANES
    state = keys_queries[0].shape[1]
    boundaries = tokens // CHUNK - 1

    def rows_of(columns, index):
        return pl.BlockSpec((tokens, columns), lambda b: (first_block + b, index))

    def swapped(b):
        return b + 1 - 2 * lax.rem(b, 2)

    return pl.pallas_call(
        functools.partial(backward_kernel, heads, size, first_head, first_block),
        grid=(blocks,),
        in_specs=[
            pl.BlockSpec(memory_space=pltpu.SMEM),
            pl.BlockSpec(memory_space=pltpu.SMEM),
            rows_of(width, part),
            rows_of(width, part),
            rows_of(LANES, steps_at),
            rows_of(state, 0),
            pl.BlockSpec((tokens, state), lambda b: (swapped(first_block + b), 0)),
            rows_of(width, part),
            pl.BlockSpec(
                (1, boundaries, state, width), lambda b: (first_block + b, 0, 0, part)
            ),
            pl.BlockSpec((8, width), lambda b: (0, part)),
            pl.BlockSpec((8, LANES), lambda b: (0, 0)),
        ]
        + [
            rows_of(state, 0),
            pl.BlockSpec((tokens, state), lambda b: (swapped(first_block + b), 0)),
        ][: len(before)],
        out_specs=[
            pl.BlockSpec((tokens, width), lambda b: (b, 0)),
            pl.BlockSpec((tokens, LANES), lambda b: (b, 0)),
            pl.BlockSpec((tokens, state), lambda b: (b, 0)),
            pl.BlockSpec((tokens, state), lambda b: (swapped(b), 0)),
            pl.BlockSpec((8, width), lambda b: (0, 0)),
            pl.BlockSpec((8, LANES), lambda b: (0, 0)),
        ],
        out_shape=[
            jax.ShapeDtypeStruct((total, width), BF16),
            jax.ShapeDtypeStruct((total, LANES), BF16),
            jax.ShapeDtypeStruct((total, state), F32),
            jax.ShapeDtypeStruct((total, state), BF16 if before else F32),
            jax.ShapeDtypeStruct((8, width), F32),
            jax.ShapeDtypeStruct((8, LANES), F32),
        ],
        scratch_shapes=[
            pltpu.VMEM((state, width), F32),
            pltpu.VMEM((tokens + 8, width), F32),
            pltpu.VMEM((CHUNK, width), BF16),
            pltpu.VMEM((CHUNK, width), BF16),
        ],
        compiler_params=pltpu.CompilerParams(vmem_limit_bytes=48 * 1024 * 1024),
        cost_estimate=pl.CostEstimate(
            flops=blocks * heads * 1_000_000_000,
            bytes_accessed=blocks * 8_000_000,
            transcendentals=0,
        ),
        name="ssd_backward",
    )(lengths, place, conv_in, conv_pre, conv_in, *keys_queries, d_out, states, conv_rows, head_rows, *before)


def after(values):
    return lax.optimization_barrier(values)


def phase(sends, work=None, arguments=(), until=None):
    values, arguments = after(([value for _, value in sends], arguments))
    moved = [send(value) for (send, _), value in zip(sends, values)]
    done = work(*arguments) if work else ()
    moved, done, until = after((moved, done, until))
    return (moved, done) if until is None else (moved, done, until)


def total(first, others):
    result = first.astype(F32)
    for other in others:
        result = result + other.astype(F32)
    return result


class Links:
    def __init__(self, reps, shards):
        self.reps, self.shards = reps, shards
        self.sides, self.groups = reps // 2, shards // 2
        rep, shard = lax.axis_index("rep"), lax.axis_index("fsdp")
        self.rep, self.shard = rep, shard
        self.a, self.x = rep // 2, rep % 2
        self.g, self.c = shard // 2, shard % 2

    def send(self, value, target):
        pairs = []
        for r in range(self.reps):
            for f in range(self.shards):
                to_r, to_f = target(r, f)
                pairs.append((r * self.shards + f, to_r * self.shards + to_f))
        return lax.ppermute(value, ("rep", "fsdp"), pairs)

    def core(self, value):
        return self.send(value, lambda r, f: (r, f ^ 1))

    def side(self, value):
        return self.send(value, lambda r, f: (r ^ 1, f))

    def corner(self, value):
        return self.send(value, lambda r, f: (r ^ 1, f ^ 1))

    def along_a(self, value, by):
        return self.send(value, lambda r, f: (((r // 2 + by) % self.sides) * 2 + r % 2, f))

    def along_g(self, value, by):
        return self.send(value, lambda r, f: (r, ((f // 2 + by) % self.groups) * 2 + f % 2))

    def diagonal(self, value, by):
        return self.send(
            value, lambda r, f: (((r // 2 + by) % self.sides) * 2 + (r % 2 ^ 1), f)
        )

    def flip(self, value, bit_of_rep, bit_of_shard):
        return self.send(value, lambda r, f: (r ^ bit_of_rep, f ^ bit_of_shard))

    def round_g(self, piece):
        return [self.along_g(piece, k) for k in range(1, self.groups)]

    def piece_of(self, mine, from_core):
        if self.sides == 2:
            return jnp.where(self.a == self.c, mine, from_core)
        is_high = self.c == 1
        chip = jnp.concatenate(
            [jnp.where(is_high, from_core, mine), jnp.where(is_high, mine, from_core)], axis=0
        )
        part = chip.shape[0] // self.sides
        return lax.dynamic_slice_in_dim(chip, self.a * part, part, 0)

    def round_a(self, joined):
        return [self.along_a(joined, j) for j in range(1, self.sides)]

    def assemble(self, mine, from_core, joined, rounds):
        rows, columns = mine.shape
        part = 2 * rows // self.sides
        whole = jnp.zeros((rows * self.shards, columns), mine.dtype)
        base = self.g * 2 * rows
        whole = lax.dynamic_update_slice_in_dim(whole, mine, base + self.c * rows, 0)
        whole = lax.dynamic_update_slice_in_dim(whole, from_core, base + (1 - self.c) * rows, 0)
        for k in range(1, self.groups):
            base = ((self.g - k) % self.groups) * 2 * rows
            for j, pieces in enumerate([joined] + rounds):
                piece = pieces[(k - 1) * part : k * part]
                at = base + ((self.a - j) % self.sides) * part
                whole = lax.dynamic_update_slice_in_dim(whole, piece, at, 0)
        return whole

    def parts_for_a(self, view):
        axis = view.ndim - 3
        mine = lax.dynamic_index_in_dim(view, self.a, axis, keepdims=False)
        others = [
            lax.dynamic_index_in_dim(view, (self.a + j) % self.sides, axis, keepdims=False)
            for j in range(1, self.sides)
        ]
        return mine, others

    def parts_for_g(self, view):
        mine = lax.dynamic_index_in_dim(view, self.g, 0, keepdims=False)
        others = [
            lax.dynamic_index_in_dim(view, (self.g + k) % self.groups, 0, keepdims=False)
            for k in range(1, self.groups)
        ]
        return mine, others

    def send_a(self, others):
        return [self.along_a(part, j + 1) for j, part in enumerate(others)]

    def send_g(self, others):
        return [self.along_g(part, k + 1) for k, part in enumerate(others)]

    def chips_of(self, partial):
        rows = partial.shape[0] // (self.groups * self.sides)
        return partial.reshape(self.groups, self.sides, rows, partial.shape[1])

    def spread_a(self, piece):
        return [self.along_a(piece, j) for j in range(1, self.sides)]

    def join_a(self, piece, others):
        if self.sides == 2:
            is_high = self.a == 1
            return jnp.concatenate(
                [jnp.where(is_high, others[0], piece), jnp.where(is_high, piece, others[0])],
                axis=0,
            )
        part = piece.shape[0]
        chip = jnp.zeros((part * self.sides, piece.shape[1]), piece.dtype)
        for j, value in enumerate([piece] + others):
            at = ((self.a - j) % self.sides) * part
            chip = lax.dynamic_update_slice_in_dim(chip, value, at, 0)
        return chip

    def join_x(self, piece, other):
        is_far = self.x == 1
        return jnp.concatenate(
            [jnp.where(is_far, other, piece), jnp.where(is_far, piece, other)], axis=1
        )

    def rows_of_core(self, chip):
        rows = chip.shape[0] // 2
        is_high = self.c == 1
        mine = jnp.where(is_high, chip[rows:], chip[:rows])
        return mine, jnp.where(is_high, chip[:rows], chip[rows:])

    def shares(self, mine, from_core):
        columns = mine.shape[1] // 2
        is_high = self.c == 1
        low = jnp.where(is_high, from_core, mine)
        high = jnp.where(is_high, mine, from_core)
        return [low[:, :columns], high[:, :columns], low[:, columns:], high[:, columns:]]

    def sum_all(self, value):
        bit = 1
        while bit < self.shards:
            value = value + self.flip(value, 0, bit)
            bit *= 2
        bit = 1
        while bit < self.reps:
            value = value + self.flip(value, bit, 0)
            bit *= 2
        return value

    def group_blocks(self, value):
        far = self.side(value)
        return [value, self.core(value), far, self.core(far)]

    def core_sum(self, partials, link_type):
        tokens = partials.shape[0] // 2
        return partials[:tokens].astype(F32) + self.core(
            partials[tokens:].astype(link_type)
        ).astype(F32)


def per_device(
    reps,
    shards,
    hidden_in,
    lengths,
    norm_gain,
    in_weight,
    conv_weight,
    conv_bias,
    dt_bias,
    a_log,
    skip_gain,
    gate_gain,
    out_weight,
    cotangent,
):
    links = Links(reps, shards)
    tokens, depth = hidden_in.shape
    inner = gate_gain.shape[0] * shards
    channels = conv_bias.shape[0] * shards
    all_heads = dt_bias.shape[0] * shards
    state = (channels - inner) // 2
    size = inner // all_heads
    heads, width = all_heads // 4, inner // 4
    x, c = links.x, links.c
    p = 2 * x + c

    is_high, is_far = c == 1, x == 1
    far_hidden = links.side(hidden_in)
    ends = jnp.cumsum(lengths[0])
    positions = jnp.arange(tokens, dtype=jnp.int32)
    is_valid = (positions < ends[1])[:, None]
    sides, groups = links.sides, links.groups
    links_shape = (sides, groups)
    place = jnp.stack([links.a, links.g, c]).astype(jnp.int32)

    lanes = max(conv_weight.shape[1], gate_gain.shape[0], norm_gain.shape[0], 3 * LANES)
    lanes = -(-lanes // LANES) * LANES

    def pack(conv_weight, conv_bias, gate_gain, norm_gain, *head_values):
        heads_row = jnp.concatenate(
            [jnp.pad(v, (0, LANES - v.shape[0])) for v in head_values]
        )
        rows = [conv_bias, gate_gain, norm_gain, heads_row[:lanes]]
        rows = [jnp.pad(row, (0, lanes - row.shape[0]))[None] for row in rows]
        taps_rows = jnp.pad(conv_weight, ((0, 0), (0, lanes - conv_weight.shape[1])))
        return jnp.concatenate([taps_rows, *rows], axis=0)

    small_in = (conv_weight, conv_bias, gate_gain, norm_gain, dt_bias, a_log, skip_gain)
    sizes = (conv_bias.shape[0], gate_gain.shape[0], norm_gain.shape[0], dt_bias.shape[0])

    first_columns, last_columns = width + LANES + state, 2 * width
    core_place = jnp.stack([x, c]).astype(jnp.int32)
    mine_a, for_core_a = prepare_call(
        functools.partial(prepare_first_kernel, heads, size, state),
        first_columns,
        core_place,
        in_weight,
    )

    def hops(pieces, stage):
        sends = [(stage, 1, pieces[stage - 1])]
        if groups - stage != stage:
            sends.append((groups - stage, groups - 1, pieces[(groups - stage + 1) % groups]))
        return sends

    def hop_sends(pieces, stage):
        return [
            ((lambda value, by=by: links.along_g(value, by)), value)
            for _, by, value in hops(pieces, stage)
        ]

    def landed(pieces, stage, values):
        at = [k for k, _, _ in hops(pieces, stage)]
        return {**pieces, **dict(zip(at, values))}

    def rounds(piece):
        return [(lambda value, j=j: links.along_a(value, j), piece) for j in range(1, sides)]

    def doubled(value, bit, other):
        upper = (links.shard // bit) % 2 == 1
        return jnp.concatenate(
            [jnp.where(upper, other, value), jnp.where(upper, value, other)], axis=0
        )

    def swap(bit):
        return lambda value: links.flip(value, 0, bit)

    (from_core_a,), _ = phase([(links.core, for_core_a)])
    pieces_a = {0: links.piece_of(mine_a, from_core_a)}

    half, quarter = tokens // 2, tokens // 4
    cuts = [slice(0, half), slice(half, half + quarter), slice(half + quarter, tokens)]

    def prepare_last(small_in, in_weight, out_weight, cotangent):
        back = jnp.where(is_valid, cotangent, jnp.zeros_like(cotangent))
        packed = pack(*small_in)
        small_pair = doubled(packed, 1, links.core(packed))
        small_four = doubled(small_pair, 2, links.flip(small_pair, 0, 2))
        kernel = functools.partial(prepare_last_kernel, width)
        last = prepare_call(kernel, last_columns, core_place, in_weight, out_weight)
        return small_four, last, back, [back[cut] for cut in cuts]

    moved, (small_all, (mine_b, for_core_b), back_own, back_parts) = phase(
        hop_sends(pieces_a, 1) + [(links.core, lengths)],
        prepare_last,
        (small_in, in_weight, out_weight.T, cotangent),
    )
    lengths_core = moved[-1]
    pieces_a = landed(pieces_a, 1, moved[:-1])
    firsts = [k for k in pieces_a if k]
    early, late = firsts[:1], firsts[1:]
    early_sends = [send for k in early for send in rounds(pieces_a[k])]
    moved, _ = phase(
        hop_sends(pieces_a, 2)
        + [(swap(4), small_all), (links.core, for_core_b)]
        + early_sends
    )
    hop_count = len(hops(pieces_a, 2))
    small_all = doubled(small_all, 4, moved[hop_count])
    from_core_b = moved[hop_count + 1]
    y_moved = moved[hop_count + 2 :]
    pieces_a = landed(pieces_a, 2, moved[:hop_count])
    pieces_b = {0: links.piece_of(mine_b, from_core_b)}
    bit = 8
    while bit < shards:
        small_all = doubled(small_all, bit, links.flip(small_all, 0, bit))
        bit *= 2
    for stage in range(3, groups // 2 + 1):
        values = [send(value) for send, value in hop_sends(pieces_a, stage)]
        pieces_a = landed(pieces_a, stage, values)
    pieces_a, pieces_b, far_hidden = after((pieces_a, pieces_b, far_hidden))
    late = late + [k for k in pieces_a if k and k not in firsts]
    late_sends = [send for k in late for send in rounds(pieces_a[k])]
    b_firsts = [send(value) for send, value in hop_sends(pieces_b, 1)]
    moved, parameters_here = phase(
        late_sends + [(links.core, hidden_in), (links.core, far_hidden)],
        functools.partial(unpack_call, sizes, heads, size, state, core_place),
        (small_all,),
    )
    core_hidden, far_core_hidden = moved[-2:]
    y_moved = y_moved + moved[:-2]
    y_a = {
        k: y_moved[at * (sides - 1) : (at + 1) * (sides - 1)] for at, k in enumerate(early + late)
    }
    n_rows, conv_rows, head_rows, kq_rows = parameters_here

    def parts_of(mine, from_core, pieces, rounds_of):
        parts = [mine, from_core]
        for k in range(1, groups):
            parts += [pieces[k], *rounds_of[k]]
        return parts

    parts_a = parts_of(mine_a, from_core_a, pieces_a, y_a)
    pair_lengths = jnp.concatenate([lengths, lengths_core], axis=0)
    normed, scale = normalize_call([hidden_in, core_hidden, far_hidden, far_core_hidden], n_rows)
    kq_index = (width + LANES) // state
    w_kq, kq_in = project_call(
        links_shape, state, kq_index, 2, tokens, F32, place, parts_a, normed
    )
    kq_near = keys_front_call(pair_lengths, kq_in, kq_rows)
    moved, (w_values, conv_in), b_firsts = phase(
        [
            (links.side, kq_near),
            (links.side, back_parts[1]),
        ],
        functools.partial(project_call, links_shape, width + LANES, 0, 4, tokens, F32, place),
        (parts_a, normed),
        b_firsts,
    )
    pieces_b = landed(pieces_b, 1, b_firsts)
    kq_far, far_back = moved[0], [None, moved[1]]
    counts_at = slice(2 * tokens, 2 * tokens + 2)
    all_counts = jnp.concatenate([kq_near[counts_at, :4], kq_far[counts_at, :4]], axis=0)
    all_counts = all_counts.astype(jnp.int32)
    all_lengths = all_counts[:, 0::2] * 32 + all_counts[:, 1::2]
    kq_half = jnp.concatenate([kq_near[: 2 * tokens], kq_far[: 2 * tokens]], axis=0)

    (kq_core,), _ = phase([(links.core, kq_half)])
    keys_queries = [kq_half, kq_core]
    firsts = [k for k in pieces_b if k]
    hop_count = len(hops(pieces_b, 2))
    moved, before = phase(
        hop_sends(pieces_b, 2)
        + rounds(pieces_b[firsts[0]])
        + [(links.side, back_parts[0]), (links.core, back_own)],
        functools.partial(forward_call, heads, size, 0, 2),
        (all_lengths, core_place, conv_in, keys_queries, conv_rows, head_rows),
    )
    y_b = {firsts[0]: moved[hop_count:-2]}
    far_back[0] = moved[-2]
    core_back = moved[-1]
    pieces_b = landed(pieces_b, 2, moved[:hop_count])
    for stage in range(3, groups // 2 + 1):
        values = [send(value) for send, value in hop_sends(pieces_b, stage)]
        pieces_b = landed(pieces_b, stage, values)
    rest = [k for k in pieces_b if k and k not in firsts]
    moved, (ssd_out, states, conv_pre) = phase(
        [send for k in firsts[1:] for send in rounds(pieces_b[k])]
        + [(links.side, back_parts[2])],
        functools.partial(forward_call, heads, size, 2, 2),
        (all_lengths, core_place, conv_in, keys_queries, conv_rows, head_rows, before),
    )
    far_back.append(moved[-1])
    for at, k in enumerate(firsts[1:]):
        y_b[k] = moved[at * (sides - 1) : (at + 1) * (sides - 1)]
    gate_sends = [send for k in rest for send in rounds(pieces_b[k][:, :width])]
    out_sends = [send for k in rest for send in rounds(pieces_b[k][:, width:])]
    moved, _ = phase(gate_sends + [(links.core, part) for part in far_back])
    gate_moved, far_core_back = moved[: len(gate_sends)], moved[len(gate_sends) :]

    def last_parts(values):
        latest = {k: values[at * (sides - 1) : (at + 1) * (sides - 1)] for at, k in enumerate(rest)}
        return parts_of(mine_b, from_core_b, pieces_b, {**y_b, **latest})

    out_moved, (w_gate, gate) = phase(
        out_sends,
        functools.partial(project_call, links_shape, width, 0, 4, tokens, F32, place),
        (last_parts(gate_moved), normed),
    )
    back_blocks = [[back_own], [core_back], far_back, far_core_back]
    w_out, d_branch, sums = branch_back_call(
        links_shape, width, 1, place, last_parts(out_moved), back_blocks, gate, ssd_out, conv_rows
    )
    moved, _ = phase([(links.core, sums), (links.side, sums), (links.corner, sums)])
    branch, d_gate, d_ssd, gain_rows = gating_back_call(
        inner, [sums, *moved], gate, ssd_out, d_branch, conv_rows
    )

    by_g = width // (3 * LANES) * 2 * LANES
    most = heads // 3 * 2
    less = heads - most
    most_width, less_width = most * size, less * size
    rows_all = 4 * tokens

    def backward(first_head, count, first_block, blocks, d_out, *before):
        return backward_call(
            count, size, first_head, first_block, blocks, all_lengths, core_place,
            conv_in, conv_pre, keys_queries, d_out, states, conv_rows, head_rows, before,
        )

    def turn(k):
        return lambda value: links.along_g(value, k)

    def a_sends(parts):
        return [
            (lambda value, j=j: links.along_a(value, j + 1), part) for j, part in enumerate(parts)
        ]

    def g_sends(parts):
        return [(turn(k + 1), part) for k, part in enumerate(parts)]

    def start(sends):
        return [send(value) for send, value in sends]

    count_a, count_g = sides - 1, groups - 1
    mixed_parts = dot_nt(branch, w_out).astype(BF16).reshape(2, 2, tokens, depth)
    mixed_keep, mixed_send = mixed_parts[:, 0], mixed_parts[:, 1]

    def first_grads(normed, d_gate, back_blocks, branch):
        def out_terms(columns, index):
            terms, first_row = [], 0
            for part in [part for block in back_blocks for part in block]:
                rows = part.shape[0]
                terms.append((part, rows, 0, branch, first_row // rows, columns, index))
                first_row += rows
            return terms

        first = weight_grad_call(
            links_shape, True, place,
            [
                [(normed, rows_all, 0, d_gate, 0, width, 0)],
                out_terms(width - by_g, by_g // (width - by_g)),
            ],
        )
        return first, weight_grad_call(links_shape, False, place, [out_terms(by_g, 0)])

    moved, (first_parts, out_parts) = phase(
        [(links.core, mixed_send)], first_grads, (normed, d_gate, back_blocks, branch)
    )
    mixed_core = moved[0]
    mixed_far = (mixed_keep[1].astype(F32) + mixed_core[1].astype(F32)).astype(BF16)
    moved, (d_in_0, d_steps_0, kq_mine_0, kq_other_0, conv_grads_0, head_grads_0) = phase(
        a_sends(first_parts[1:])
        + g_sends(out_parts[1:])
        + [(links.side, mixed_far)],
        functools.partial(backward, 0, most, 0, 4),
        (d_ssd,),
    )
    mixed_side = moved[-1]
    first_held = combine_call(groups, place, [first_parts[0], *moved[:count_a]])
    values_0 = weight_grad_call(
        links_shape, True, place, [[(normed, rows_all, 0, d_in_0, 0, most_width, 0)]]
    )
    out_chip = total(out_parts[0], moved[count_a:-1]).astype(BF16)
    out_mine, out_others = links.parts_for_a(out_chip.reshape(sides, -1, by_g))
    first_held, values_0, d_ssd, out_mine, out_others = after(
        (first_held, values_0, d_ssd, out_mine, out_others)
    )
    first_sends = g_sends(first_held[1:])
    first_sends = first_sends[:1] + first_sends[-1:] + first_sends[1:-1]

    def back_project(first_row, d_in_1, d_steps):
        rows = slice(first_row, first_row + 2 * tokens)
        d_rest = jnp.concatenate([d_in_0[rows], d_in_1, d_steps], axis=1)
        return dot_nt(d_gate[rows], w_gate) + dot_nt(d_rest, w_values)

    def far_work(d_ssd):
        results = backward(most, less, 2, 2, d_ssd, kq_mine_0, kq_other_0)
        d_steps = d_steps_0[2 * tokens :] + results[1]
        return results, d_steps, back_project(2 * tokens, results[0], d_steps).astype(BF16)

    moved, (results, d_steps_far, d_far_parts) = phase(
        a_sends(values_0[1:]) + first_sends[:2], far_work, (d_ssd,)
    )
    first_far = moved[count_a:]
    d_in_far, _, kq_far_mine, kq_far_core, conv_grads_far, head_grads_far = results
    held_0 = combine_call(groups, place, [values_0[0], *moved[:count_a]])
    held_sends = g_sends(held_0[1:])
    held_sends = held_sends[:1] + held_sends[-1:] + held_sends[1:-1]

    moved, _ = phase([(links.core, kq_far_core), (links.core, d_far_parts[tokens:])])
    kq_far_sum = (kq_far_mine + moved[0].astype(F32)).astype(BF16)
    d_far = (d_far_parts[:tokens].astype(F32) + moved[1].astype(F32)).astype(BF16)
    moved, results = phase(
        [(links.side, kq_far_sum)]
        + first_sends[2:]
        + [(links.side, d_far[:quarter])]
        + a_sends(out_others),
        functools.partial(backward, most, less, 0, 2),
        (d_ssd, kq_mine_0, kq_other_0),
    )
    d_in_near, d_steps_near, kq_near_mine, kq_near_core, conv_grads_near, head_grads_near = results
    kq_from_side = moved[0]
    first_far = first_far + moved[1 : count_g - 1]
    far_d = [moved[count_g - 1]]
    out_piece = total(out_mine, moved[count_g:]).astype(BF16)
    first_piece = total(first_held[0], first_far).astype(BF16)
    d_steps_near = d_steps_0[: 2 * tokens] + d_steps_near
    d_steps = jnp.concatenate([d_steps_near, d_steps_far], axis=0)
    moved, d_near = phase(
        [(links.core, kq_near_core), (links.side, d_far[quarter:half])] + held_sends[:1],
        functools.partial(back_project, 0),
        (d_in_near, d_steps_near),
    )
    far_d.append(moved[1])
    held_far = moved[2:]
    d_kq_in, kq_grads = keys_back_call(
        all_lengths, [kq_near_mine, moved[0], kq_from_side], kq_in, kq_rows
    )
    half_rows = 2 * tokens

    def last_grads(normed, d_in_near, d_in_far, d_steps, d_kq_in):
        last = weight_grad_call(
            links_shape, True, place,
            [
                [
                    (normed, half_rows, 0, d_in_near, 0, less_width, 0),
                    (normed, half_rows, 1, d_in_far, 0, less_width, 0),
                ],
                [
                    (normed, half_rows, 0, d_steps, 0, LANES, 0),
                    (normed, half_rows, 1, d_steps, 1, LANES, 0),
                ],
                [(normed, half_rows, 0, d_kq_in, 0, state, 0)],
            ],
        )
        return last

    moved, last_parts_here = phase(
        rounds(first_piece)
        + held_sends[1:]
        + [(links.side, d_far[half:])],
        last_grads,
        (normed, d_in_near, d_in_far, d_steps, d_kq_in),
    )
    first_y = moved[:count_a]
    held_far = held_far + moved[count_a:-1]
    far_d.append(moved[-1])
    held_piece = total(held_0[0], held_far).astype(BF16)
    held_piece = jnp.concatenate([out_piece, held_piece], axis=1)
    first_rows = links.rows_of_core(links.join_a(first_piece, first_y))
    d_near_keep = d_near[:tokens] + dot_nt(d_kq_in[:tokens], w_kq)
    d_near_send = (d_near[tokens:] + dot_nt(d_kq_in[tokens:], w_kq)).astype(BF16)
    small = small_call(
        heads, size, channels, core_place,
        [conv_grads_0, conv_grads_far, conv_grads_near],
        [head_grads_0, head_grads_far, head_grads_near],
        gain_rows, kq_grads,
    )
    def finish_mixed(keep, core, side):
        mixed = hidden_in.astype(F32) + keep.astype(F32) + core.astype(F32) + side.astype(F32)
        return jnp.where(is_valid, mixed, 0.0).astype(BF16)

    moved, mixed = phase(
        a_sends(last_parts_here[1:])
        + [(links.core, d_near_send)]
        + [(links.core, first_rows[1]), (links.side, held_piece), (links.core, small)],
        finish_mixed,
        (mixed_keep[0], mixed_core[0], mixed_side),
    )
    d_near_core = moved[count_a]
    first_mine, first_core = first_rows[0], moved[count_a + 1]
    held_both = links.join_x(held_piece, moved[count_a + 2])
    small = small + moved[-1]
    first_both = jnp.concatenate(
        [jnp.where(is_high, first_core, first_mine), jnp.where(is_high, first_mine, first_core)],
        axis=1,
    )
    last_held = combine_call(groups, place, [last_parts_here[0], *moved[:count_a]])

    moved, grad_hidden = phase(
        g_sends(last_held[1:])
        + [(links.side, first_both)]
        + rounds(held_both)
        + [(swap(2), small)],
        norm_back_call,
        (d_near_keep, d_near_core, far_d, hidden_in, back_own, scale, n_rows),
    )
    first_other = moved[count_g]
    held_rows = links.rows_of_core(links.join_a(held_both, moved[count_g + 1 : -1]))
    small = small + moved[-1]
    last_piece = total(last_held[0], moved[:count_g]).astype(BF16)
    diagonals = [(lambda value, j=j: links.diagonal(value, j), last_piece) for j in range(1, sides)]
    moved, _ = phase(
        rounds(last_piece)
        + [(links.side, last_piece), (links.core, held_rows[1]), (swap(4), small)]
        + diagonals
    )
    same_x = links.join_a(last_piece, moved[:count_a])
    held_core, small = moved[count_a + 1], small + moved[count_a + 2]
    other_x = links.join_a(moved[count_a], moved[count_a + 3 :])
    bit = 8
    while bit < shards:
        small = small + links.flip(small, 0, bit)
        bit *= 2
    at_kq = less_width + LANES
    kq_both = same_x[:, at_kq:].astype(F32) + other_x[:, at_kq:].astype(F32)
    last_rows = links.rows_of_core(
        jnp.concatenate(
            [
                jnp.where(is_far, other_x, same_x)[:, :at_kq],
                jnp.where(is_far, same_x, other_x)[:, :at_kq],
                kq_both.astype(BF16),
            ],
            axis=1,
        )
    )
    (last_core,), _ = phase([(links.core, last_rows[1])])
    held_rows_pair = [held_rows[0], held_core]
    moved, (grad_in, grad_out, grad_norm) = phase(
        [(links.side, small)]
        + rounds(small)
        + [(lambda value, j=j: links.diagonal(value, j), small) for j in range(1, sides)],
        functools.partial(final_call, heads, size, most_width, by_g, core_place),
        (
            [first_both, first_other, *held_rows_pair, last_rows[0], last_core],
            in_weight,
            norm_gain.astype(F32)[:, None],
        ),
    )
    small = total(small, moved)

    def own_slice(array, count):
        return lax.dynamic_slice_in_dim(array, links.shard * count, count, array.ndim - 1)

    grad_conv = own_slice(small[:5], channels // shards)
    grad_heads = [
        own_slice(small[7, field * LANES : field * LANES + all_heads], all_heads // shards)
        for field in range(3)
    ]
    return (
        mixed,
        grad_hidden,
        grad_norm[:, 0],
        grad_in,
        grad_conv[:4],
        grad_conv[4],
        grad_heads[0],
        grad_heads[1],
        grad_heads[2],
        own_slice(small[5, :inner], inner // shards),
        grad_out.T,
    )


def solution(mesh):
    return jax.shard_map(
        functools.partial(per_device, mesh.shape["rep"], mesh.shape["fsdp"]),
        mesh=mesh,
        in_specs=(
            P(("rep", "fsdp"), None),
            P(("rep", "fsdp"), None),
            P("fsdp"),
            P("fsdp", None),
            P(None, "fsdp"),
            P("fsdp"),
            P("fsdp"),
            P("fsdp"),
            P("fsdp"),
            P("fsdp"),
            P(None, "fsdp"),
            P(("rep", "fsdp"), None),
        ),
        out_specs=(
            P(("rep", "fsdp"), None),
            P(("rep", "fsdp"), None),
            P("fsdp"),
            P("fsdp", None),
            P(None, "fsdp"),
            P("fsdp"),
            P("fsdp"),
            P("fsdp"),
            P("fsdp"),
            P("fsdp"),
            P(None, "fsdp"),
        ),
        check_vma=False,
    )
```
